32 devices in a mesh: batch: 4 (over z), seq: 8 (over y, x, core).
Axes of the slice: x: 2, y: 2, z: 4, core: 2. Of those that a mesh axis runs over, the one named last changes fastest.
Arguments:
- inputs: float32 [4, 1536, 512], P('batch', 'seq'), may hold values from -6 to 6
- cotangent: float32 [4, 1536, 512], P('batch', 'seq'), may hold values from -6 to 6
- full_gain_attn: float32 [512], replicated, may hold values from 0.5 to 1.5
- full_query: bfloat16 [512, 512], replicated, may hold values from -0.25 to 0.25
- full_key: bfloat16 [512, 512], replicated, may hold values from -0.25 to 0.25
- full_value: bfloat16 [512, 512], replicated, may hold values from -0.25 to 0.25
- full_output: bfloat16 [512, 512], replicated, may hold values from -2.5 to 2.5
- full_gain_ffn: float32 [512], replicated, may hold values from 0.5 to 1.5
- full_expand: bfloat16 [512, 2048], replicated, may hold values from -0.25 to 0.25
- full_contract: bfloat16 [2048, 512], replicated, may hold values from -0.125 to 0.125
- short_gain_attn: float32 [512], replicated, may hold values from 0.5 to 1.5
- short_query: bfloat16 [512, 512], replicated, may hold values from -0.25 to 0.25
- short_key: bfloat16 [512, 512], replicated, may hold values from -0.25 to 0.25
- short_value: bfloat16 [512, 512], replicated, may hold values from -0.25 to 0.25
- short_output: bfloat16 [512, 512], replicated, may hold values from -1.5 to 1.5
- short_gain_ffn: float32 [512], replicated, may hold values from 0.5 to 1.5
- short_expand: bfloat16 [512, 2048], replicated, may hold values from -0.25 to 0.25
- short_contract: bfloat16 [2048, 512], replicated, may hold values from -0.125 to 0.125
Outputs:
- output: float32 [4, 1536, 512], P('batch', 'seq')
- input_grad: float32 [4, 1536, 512], P('batch', 'seq')
- grad_full_gain_attn: float32 [512], replicated
- grad_full_query: float32 [512, 512], replicated
- grad_full_key: float32 [512, 512], replicated
- grad_full_value: float32 [512, 512], replicated
- grad_full_output: float32 [512, 512], replicated
- grad_full_gain_ffn: float32 [512], replicated
- grad_full_expand: float32 [512, 2048], replicated
- grad_full_contract: float32 [2048, 512], replicated
- grad_short_gain_attn: float32 [512], replicated
- grad_short_query: float32 [512, 512], replicated
- grad_short_key: float32 [512, 512], replicated
- grad_short_value: float32 [512, 512], replicated
- grad_short_output: float32 [512, 512], replicated
- grad_short_gain_ffn: float32 [512], replicated
- grad_short_expand: float32 [512, 2048], replicated
- grad_short_contract: float32 [2048, 512], replicated
The draws below stay inside these ranges and needn't reach their ends.
All inputs are finite; a program needn't handle non-finite values.
Results may differ from the reference program's by a relative error of at most 0.025.
Values may be sent and summed in bfloat16 or wider, within the bound.
No kernel may reach another device: no remote copies, remote signals or barrier semaphores. Data moves between devices by JAX's collectives and lax.ppermute only.
A program may use at most 384 MiB of HBM per device.

```python
import jax
import jax.numpy as jnp
from jax import lax

D = 512
HEADS = 8
HEAD = 64
FF = 2048
LENGTH = 1536
SEQS = 4


def block_levels(rng, dims, shards, smallest, high):
    level, own = 1.0, jax.random.fold_in(rng, 6)
    for axis_at, parts in shards:
        draws = jnp.exp(jax.random.uniform(jax.random.fold_in(own, axis_at), (parts,), jnp.float32, smallest / len(shards), high / len(shards)))
        level = level * jnp.repeat(draws, dims[axis_at] // parts).reshape([-1 if axis == axis_at else 1 for axis in range(len(dims))])
    return level


def bell_draw(own_key, shape, scale, most, cuts=(), kind=jnp.bfloat16):
    entries = jax.random.normal(own_key, shape, jnp.float32) * scale
    if len(cuts) > 0:
        entries = block_levels(own_key, shape, cuts, -0.22, 0.18) * entries
    return jnp.clip(entries, min=-most, max=most).astype(kind)


def setup_inputs(seed: int = 0) -> dict:
    splits = jax.random.split(jax.random.key(seed), 19)
    return {
        "inputs": bell_draw(splits[0], (SEQS, LENGTH, D), 1.0, 6.0, ((0, 4), (1, 8)), jnp.float32),
        "cotangent": bell_draw(splits[1], (SEQS, LENGTH, D), 1.0, 6.0, ((0, 4), (1, 8)), jnp.float32),
        "full_gain_attn": jnp.clip(1.0 + 0.1 * jax.random.normal(splits[2], (D,), jnp.float32), 0.5, 1.5),
        "full_query": bell_draw(splits[3], (D, D), D ** -0.5, 0.25),
        "full_key": bell_draw(splits[4], (D, D), D ** -0.5, 0.25),
        "full_value": bell_draw(splits[5], (D, D), D ** -0.5, 0.25),
        "full_output": bell_draw(splits[6], (D, D), (D * 16 // LENGTH) ** -0.5, 2.5),
        "full_gain_ffn": jnp.clip(1.0 + 0.1 * jax.random.normal(splits[7], (D,), jnp.float32), 0.5, 1.5),
        "full_expand": bell_draw(splits[8], (D, FF), D ** -0.5, 0.25),
        "full_contract": bell_draw(splits[9], (FF, D), FF ** -0.5, 0.125),
        "short_gain_attn": jnp.clip(1.0 + 0.1 * jax.random.normal(splits[10], (D,), jnp.float32), 0.5, 1.5),
        "short_query": bell_draw(splits[11], (D, D), D ** -0.5, 0.25),
        "short_key": bell_draw(splits[12], (D, D), D ** -0.5, 0.25),
        "short_value": bell_draw(splits[13], (D, D), D ** -0.5, 0.25),
        "short_output": bell_draw(splits[14], (D, D), (D * 48 // LENGTH) ** -0.5, 1.5),
        "short_gain_ffn": jnp.clip(1.0 + 0.1 * jax.random.normal(splits[15], (D,), jnp.float32), 0.5, 1.5),
        "short_expand": bell_draw(splits[16], (D, FF), D ** -0.5, 0.25),
        "short_contract": bell_draw(splits[17], (FF, D), FF ** -0.5, 0.125),
    }


norm_eps = 1e-05
highest = lax.Precision.HIGHEST

@jax.custom_vjp
def low(v):
    return lax.optimization_barrier(v.astype(jnp.bfloat16)).astype(jnp.float32)

@jax.custom_vjp
def low_back(v):
    return v

def low_keep(v):
    return (low(v), None)

def low_pass(kept, grad):
    return (grad,)

def back_keep(v):
    return (v, None)

def back_low(kept, grad):
    return (low(grad),)
low.defvjp(low_keep, low_pass)
low_back.defvjp(back_keep, back_low)

def normalize(stream, gain):
    row_mean = lax.optimization_barrier(jnp.mean(stream, axis=-1, keepdims=True))
    centered = stream - row_mean
    spread = lax.optimization_barrier(jnp.mean(centered * centered, axis=-1, keepdims=True))
    return centered * lax.rsqrt(spread + norm_eps) * gain

def rope_table(positions):
    half_size = HEAD // 2
    frequency = jnp.power(10000.0, -jnp.arange(half_size, dtype=jnp.float32) * 2.0 / HEAD)
    angles = positions.astype(jnp.float32)[:, None] * frequency[None, :]
    return (jnp.cos(angles)[:, None, :], jnp.sin(angles)[:, None, :])

def rotate(values, angle_cos, angle_sin):
    first_half, second_half = jnp.split(values, 2, axis=-1)
    return jnp.concatenate([first_half * angle_cos - second_half * angle_sin, first_half * angle_sin + second_half * angle_cos], axis=-1)

def product(left_side, right_side):
    return jnp.dot(left_side, right_side, precision=highest)

def layer(stream, params, positions):
    gain_attn, w_query, w_key, w_value, w_output, gain_ffn, w_expand, w_contract = params
    row_count = stream.shape[0]
    score_scale = HEAD ** (-0.5)
    angle_cos, angle_sin = rope_table(positions)
    normed_in = low(normalize(stream, gain_attn))

    def heads_of(matrix):
        return low_back(product(normed_in, matrix)).reshape(row_count, HEADS, HEAD)
    queries = low(rotate(heads_of(w_query), angle_cos, angle_sin))
    keys_all = low(rotate(heads_of(w_key), angle_cos, angle_sin))
    values_all = low(heads_of(w_value))
    block_rows = 512 if row_count % 512 == 0 else row_count
    block_count = row_count // block_rows

    def one_block(pieces):
        query_block, place_block = pieces
        scores = low_back(jnp.einsum('nhe,mhe->hnm', query_block, keys_all, precision=highest) * score_scale)
        allowed = positions[None, None, :] <= place_block[None, :, None]
        scores = jnp.where(allowed, scores, -1e+30)
        soft_weights = jax.nn.softmax(scores, axis=-1)
        return jnp.einsum('hnm,mhe->nhe', low(soft_weights), values_all, precision=highest)
    attended = lax.map(jax.checkpoint(one_block), (queries.reshape(block_count, block_rows, HEADS, HEAD), positions.reshape(block_count, block_rows)))
    attended = low(low_back(attended.reshape(row_count, HEADS * HEAD)))
    middle = stream + low_back(product(attended, w_output))
    normed_mid = low(normalize(middle, gain_ffn))
    hidden_pre = low_back(product(normed_mid, w_expand))
    hidden_low = low(jax.nn.gelu(hidden_pre, approximate=True))
    return middle + low_back(product(hidden_low, w_contract))

def block(weights, sequence):
    row_count, width = sequence.shape
    residual = layer(sequence, weights[:8], jnp.arange(row_count, dtype=jnp.int32))
    shifted = jnp.concatenate([jnp.zeros((2, width), jnp.float32), residual[:row_count - 2]], axis=0)
    pooled = lax.optimization_barrier(jnp.mean(shifted.reshape(row_count // 3, 3, width), axis=1))
    short_out = layer(pooled, weights[8:], jnp.arange(row_count // 3, dtype=jnp.int32))
    return residual + jnp.repeat(short_out, 3, axis=0)

def reference(inputs, cotangent, full_gain_attn, full_query, full_key, full_value, full_output, full_gain_ffn, full_expand, full_contract, short_gain_attn, short_query, short_key, short_value, short_output, short_gain_ffn, short_expand, short_contract):
    weights = tuple((matrix.astype(jnp.float32) for matrix in (full_gain_attn, full_query, full_key, full_value, full_output, full_gain_ffn, full_expand, full_contract, short_gain_attn, short_query, short_key, short_value, short_output, short_gain_ffn, short_expand, short_contract)))

    def one_sequence(running, pieces):
        sequence, grad_sequence = pieces
        result, pull = jax.vjp(block, weights, sequence)
        grad_weights, grad_input = pull(grad_sequence)
        return (tuple((total + added for total, added in zip(running, grad_weights))), (result, grad_input))
    start_totals = tuple((jnp.zeros(matrix.shape, jnp.float32) for matrix in weights))
    totals, (outputs, grad_inputs) = lax.scan(one_sequence, start_totals, (inputs, cotangent))
    return (outputs, grad_inputs, totals[0], totals[1], totals[2], totals[3], totals[4], totals[5], totals[6], totals[7], totals[8], totals[9], totals[10], totals[11], totals[12], totals[13], totals[14], totals[15])
```

```python
from functools import partial

import jax
import jax.numpy as jnp
import numpy as np
from jax import lax
from jax.experimental import pallas as pl
from jax.experimental.pallas import tpu as pltpu
from jax.sharding import PartitionSpec as P

HEADS = 8
HEAD = 64
LANES = 128
BLOCK = 256
F32 = jnp.float32
BF16 = jnp.bfloat16


norm_eps = 1e-05


def dot_nn(left, right):
    return jnp.dot(left, right, preferred_element_type=F32)


def dot_nt(left, right):
    return lax.dot_general(left, right, (((1,), (1,)), ((), ())), preferred_element_type=F32)


def dot_tn(left, right):
    return lax.dot_general(left, right, (((0,), (0,)), ((), ())), preferred_element_type=F32)


def lower_half(rows):
    return lax.broadcasted_iota(jnp.int32, (rows, LANES), 1) < HEAD


def turn(values):
    return pltpu.roll(values, HEAD, 1)


def swap_pairs(values):
    lane = lax.broadcasted_iota(jnp.int32, values.shape, 1)
    return jnp.where(
        lane % HEAD < HEAD // 2,
        pltpu.roll(values, LANES - HEAD // 2, 1),
        pltpu.roll(values, HEAD // 2, 1),
    )


def rope(values, table):
    return values * table[:, :LANES] + swap_pairs(values) * table[:, LANES:]


def rope_back(grads, table):
    return grads * table[:, :LANES] - swap_pairs(grads) * table[:, LANES:]


def rope_constants(rows):
    frequency = np.power(
        np.float32(10000.0), -np.arange(HEAD // 2, dtype=np.float32) * np.float32(2.0 / HEAD)
    ).astype(np.float32)
    angles = np.arange(rows, dtype=np.float32)[:, None] * frequency[None, :]
    cosine, sine = np.cos(angles), np.sin(angles)
    table = np.concatenate([cosine] * 4 + [-sine, sine] * 2, axis=1)
    return jnp.asarray(table, F32)


def norm_parts(stream):
    centered = stream - jnp.mean(stream, axis=-1, keepdims=True)
    spread = jnp.mean(centered * centered, axis=-1, keepdims=True)
    scale = lax.rsqrt(spread + norm_eps)
    return centered * scale, scale


def norm_back(grad, gain, unit, scale):
    grad_unit = grad * gain
    inner = jnp.mean(grad_unit * unit, axis=-1, keepdims=True)
    return scale * (grad_unit - jnp.mean(grad_unit, axis=-1, keepdims=True) - unit * inner)


GELU_SCALE = 0.7978845608028654
GELU_CUBE = 0.044715


def gelu_both(pre):
    square = pre * pre
    tanh = jnp.tanh(GELU_SCALE * pre * (1.0 + GELU_CUBE * square))
    half = 0.5 * (1.0 + tanh)
    slope = half + 0.5 * pre * (1.0 - tanh * tanh) * (
        GELU_SCALE * (1.0 + 3.0 * GELU_CUBE * square)
    )
    return pre * half, slope


def gelu_value(pre):
    tanh = jnp.tanh(GELU_SCALE * pre * (1.0 + GELU_CUBE * pre * pre))
    return 0.5 * pre * (1.0 + tanh)


def causal(scores, first_row, first_key):
    row = lax.broadcasted_iota(jnp.int32, scores.shape, 0) + first_row
    key = lax.broadcasted_iota(jnp.int32, scores.shape, 1) + first_key
    return jnp.where(key <= row, scores, -1e30)


def fold_rows(values):
    half = values.shape[0] // 2
    return jnp.where(lower_half(half), values[:half], turn(values[half:]))


def unfold_rows(folded):
    low = lower_half(folded.shape[0])
    return jnp.where(low, folded, 0.0), jnp.where(low, turn(folded), 0.0)


def rows_at(start, size, multiple):
    return pl.ds(pl.multiple_of(start, multiple), size)


def project_kernel(place, x, cot, gain, w_q, w_k, w_v, table, *refs):
    pieces, bundle, heads, chunks = refs[:HEADS], refs[HEADS], refs[HEADS + 1], refs[HEADS + 2]
    rows, width = x.shape
    me = place[0]
    unit, _ = norm_parts(x[...])
    normed = (unit * gain[...]).astype(BF16)
    own = table[rows_at(me * rows, rows, 16), :]
    q = dot_nn(normed, w_q[...])
    k = dot_nn(normed, w_k[...])
    v = dot_nn(normed, w_v[...])
    low = lower_half(rows)
    low_half = lower_half(rows // 2)
    for chunk in range(width // LANES):
        cut = slice(chunk * LANES, (chunk + 1) * LANES)
        q_chunk = rope(q[:, cut], own) * HEAD**-0.5
        k_chunk = rope(k[:, cut], own)
        v_chunk = v[:, cut]
        first, later = q_chunk[: rows // 2], q_chunk[rows // 2 :]
        heads[2 * chunk, :rows] = jnp.where(low, k_chunk, turn(v_chunk)).astype(BF16)
        heads[2 * chunk + 1, :rows] = jnp.where(low, turn(k_chunk), v_chunk).astype(BF16)
        heads[2 * chunk, rows:] = jnp.where(low_half, first, turn(later)).astype(BF16)
        heads[2 * chunk + 1, rows:] = jnp.where(low_half, turn(first), later).astype(BF16)
    for step in range(HEADS):
        pieces[step][...] = heads[me ^ step]
    bundle[:rows] = normed
    bundle[rows : 2 * rows] = cot[...].astype(BF16)
    for chunk in range(width // LANES):
        cut = slice(chunk * LANES, (chunk + 1) * LANES)
        chunks[chunk] = cot[:, cut]
        total = sum(chunks[chunk, pl.ds(s, rows // 3, stride=3), :] for s in range(3))
        bundle[2 * rows :, cut] = total.astype(BF16)


def attend_kernel(place, *refs):
    pieces, outs = refs[:HEADS], refs[HEADS : 2 * HEADS]
    q_all, kv_all, lse_o = refs[2 * HEADS : 2 * HEADS + 3]
    me = place[0]
    rows = outs[0].shape[0] * 2
    for step in range(HEADS):
        start = (me ^ step) * rows
        kv_all[rows_at(start, rows, 16), :] = pieces[step][:rows]
        first, later = unfold_rows(pieces[step][rows:].astype(F32))
        q_all[rows_at(start, rows // 2, 16), :] = first.astype(BF16)
        q_all[rows_at(start + rows // 2, rows // 2, 16), :] = later.astype(BF16)
    low = lower_half(BLOCK)
    for block in range(q_all.shape[0] // BLOCK):
        cut = slice(block * BLOCK, (block + 1) * BLOCK)
        seen = kv_all[: (block + 1) * BLOCK]
        scores = causal(dot_nt(q_all[cut], seen), block * BLOCK, 0)
        most = jnp.max(scores, axis=-1, keepdims=True)
        weights = jnp.exp(scores - most)
        total = jnp.sum(weights, axis=-1, keepdims=True)
        attended = dot_nn(weights.astype(BF16), seen) / total
        lse_o[cut] = jnp.where(low, most + jnp.log(total), attended)
    for step in range(HEADS):
        own = lse_o[rows_at((me ^ step) * rows, rows, 16), :]
        outs[step][...] = jnp.where(
            lower_half(rows // 2), turn(own[: rows // 2]), own[rows // 2 :]
        ).astype(BF16)


def finish_kernel(place, x, gain, w_o, w_e, w_c, *refs):
    pieces = refs[:HEADS]
    result_out, middle_out, att_out, normed_out, pooled_out, heads, chunks = refs[HEADS:]
    rows, width = x.shape
    me = place[0]
    for step in range(HEADS):
        heads[me ^ step] = pieces[step][...].astype(F32)
    low = lower_half(rows // 2)
    for chunk in range(width // LANES):
        cut = slice(chunk * LANES, (chunk + 1) * LANES)
        even, odd = heads[2 * chunk], heads[2 * chunk + 1]
        att_out[: rows // 2, cut] = jnp.where(low, even, turn(odd)).astype(BF16)
        att_out[rows // 2 :, cut] = jnp.where(low, turn(even), odd).astype(BF16)
    middle = x[...] + dot_nn(att_out[...], w_o[...])
    middle_out[...] = middle
    unit, _ = norm_parts(middle)
    normed = (unit * gain[...]).astype(BF16)
    normed_out[...] = normed
    hidden = gelu_value(dot_nn(normed, w_e[...])).astype(BF16)
    result = middle + dot_nn(hidden, w_c[...])
    result_out[...] = result
    short = rows // 3
    for chunk in range(width // LANES):
        cut = slice(chunk * LANES, (chunk + 1) * LANES)
        chunks[chunk, :8] = jnp.zeros((8, LANES), F32)
        chunks[chunk, 8:] = result[:, cut]
        total = sum(chunks[chunk, pl.ds(s, short, stride=3), :] for s in (6, 7, 8))
        pooled_out[:short, cut] = (total / 3.0).astype(BF16)
    tail = (result[rows - 1 :] + result[rows - 2 : rows - 1]) / 3.0
    extra = pooled_out.shape[0] - short
    pooled_out[short:] = jnp.broadcast_to(tail, (extra, width)).astype(BF16)


def short_kernel(
    place, residual, cot, gathered, table, gain_a, w_q, w_k, w_v, w_o, gain_f, w_e, w_c, *refs
):
    pieces = refs[:HEADS]
    output, grad_own, grad_all = refs[HEADS : HEADS + 3]
    batch = (len(refs) - HEADS - 3) - 22
    share_pieces = refs[HEADS + 3 : HEADS + 3 + batch]
    (
        pooled,
        extra,
        normed_a,
        q_s,
        k_s,
        v_s,
        o_s,
        lse_s,
        att,
        middle,
        normed_f,
        hidden,
        grad_pre,
        grad_normed,
        grad_low,
        do_s,
        dq_s,
        dk_s,
        dv_s,
        wide,
        share,
        wo_s,
    ) = refs[HEADS + 3 + batch :]
    me, seat = place[0], place[1]
    rows, width = residual.shape
    count = pooled.shape[0]
    short = rows // 3
    full = rows * HEADS
    chunk_count = width // LANES
    stride = 2 * rows + short
    ff = w_e.shape[1]
    ff_own = ff // HEADS

    for step in range(HEADS):
        other = me ^ step
        pooled[rows_at(other * short, short, 16), :] = pieces[step][:short].astype(F32)
        extra[pl.ds(other, 1), :] = pieces[step][short:].astype(F32)[:1]
    for part in range(1, HEADS):
        at = slice(part * short, part * short + 1)
        pooled[at] = pooled[at] + extra[part - 1 : part]

    unit, _ = norm_parts(pooled[...])
    normed_a[...] = (unit * gain_a[...]).astype(BF16)
    low = lower_half(count)
    turns = table[:count, :]
    q = dot_nn(normed_a[...], w_q[...])
    for chunk in range(chunk_count):
        q_chunk = rope(q[:, chunk * LANES : (chunk + 1) * LANES], turns) * HEAD**-0.5
        q_s[2 * chunk] = jnp.where(low, q_chunk, 0.0).astype(BF16)
        q_s[2 * chunk + 1] = jnp.where(low, 0.0, q_chunk).astype(BF16)
    k = dot_nn(normed_a[...], w_k[...])
    for chunk in range(chunk_count):
        k_s[chunk] = rope(k[:, chunk * LANES : (chunk + 1) * LANES], turns).astype(BF16)
    v = dot_nn(normed_a[...], w_v[...])
    for chunk in range(chunk_count):
        v_s[chunk] = v[:, chunk * LANES : (chunk + 1) * LANES].astype(BF16)

    low_block = lower_half(BLOCK)

    def attend_chunk(chunk, carry):
        for block in range(count // BLOCK):
            cut = slice(block * BLOCK, (block + 1) * BLOCK)
            seen = slice(0, (block + 1) * BLOCK)
            results = []
            for half in range(2):
                scores = dot_nt(q_s[2 * chunk + half, cut, :], k_s[chunk, seen, :])
                scores = causal(scores, block * BLOCK, 0)
                most = jnp.max(scores, axis=-1, keepdims=True)
                weights = jnp.exp(scores - most)
                total = jnp.sum(weights, axis=-1, keepdims=True)
                attended = dot_nn(weights.astype(BF16), v_s[chunk, seen, :]) / total
                results.append((attended, most + jnp.log(total)))
            both = jnp.where(low_block, results[0][0], results[1][0])
            o_s[chunk, cut, :] = both
            lse_s[chunk, cut, :] = jnp.where(low_block, results[0][1], results[1][1])
            att[cut, rows_at(chunk * LANES, LANES, LANES)] = both.astype(BF16)
        return carry

    lax.fori_loop(0, chunk_count, attend_chunk, 0)
    middle[...] = pooled[...] + dot_nn(att[...], w_o[...])
    unit, scale = norm_parts(middle[...])
    normed_f[...] = (unit * gain_f[...]).astype(BF16)

    for part in range(HEADS):
        at = part * stride + 2 * rows
        grad_low[part * short : (part + 1) * short] = gathered[at : at + short]

    ff_part = ff // 4
    grad_normed[...] = jnp.zeros(grad_normed.shape, F32)

    def feed_forward(part, carry):
        cut = rows_at(part * ff_part, ff_part, ff_part)
        pre = dot_nn(normed_f[...], w_e[:, cut])
        value, slope = gelu_both(pre)
        hidden[:, cut] = value.astype(BF16)
        grad_hidden = dot_nt(grad_low[...], w_c[cut, :])
        low_grad = (grad_hidden * slope).astype(BF16)
        grad_pre[:, cut] = low_grad
        grad_normed[...] += dot_nt(low_grad, w_e[:, cut])
        return carry

    lax.fori_loop(0, 4, feed_forward, 0)

    mine = rows_at(me * short, short, 16)
    short_out = middle[mine, :] + dot_nn(hidden[mine, :], w_c[...])
    for chunk in range(chunk_count):
        cut = slice(chunk * LANES, (chunk + 1) * LANES)
        for s in range(3):
            wide[chunk, pl.ds(s, short, stride=3), :] = short_out[:, cut]
        output[:, cut] = residual[:, cut] + wide[chunk, :rows]

    own_ff = rows_at(me * ff_own, ff_own, ff_own)
    share[:ff_own] = dot_tn(hidden[:, own_ff], grad_low[...]).astype(BF16)
    expand = dot_tn(normed_f[...], grad_pre[:, own_ff]).astype(BF16)
    share[ff_own : 2 * ff_own, : width // 2] = expand[: width // 2]
    share[ff_own : 2 * ff_own, width // 2 :] = expand[width // 2 :]

    unit, scale = norm_parts(middle[...])
    grad_middle = grad_low[...].astype(F32) + norm_back(grad_normed[...], gain_f[...], unit, scale)
    middle[...] = grad_middle
    g1 = grad_middle.astype(BF16)
    d_att = dot_nt(g1, w_o[...])
    for chunk in range(chunk_count):
        do_chunk = d_att[:, chunk * LANES : (chunk + 1) * LANES]
        do_s[2 * chunk] = jnp.where(low, do_chunk, 0.0).astype(BF16)
        do_s[2 * chunk + 1] = jnp.where(low, 0.0, do_chunk).astype(BF16)
    own_chunk = rows_at((me // 2) * LANES, LANES, LANES)
    wo_s[...] = dot_tn(att[:, own_chunk], g1)

    def attend_back(chunk, carry):
        dk = [None] * (count // BLOCK)
        dv = [None] * (count // BLOCK)
        columns = rows_at(chunk * LANES, LANES, LANES)
        for block in range(count // BLOCK):
            cut = slice(block * BLOCK, (block + 1) * BLOCK)
            dq = []
            for half in range(2):
                head = 2 * chunk + half
                q_block, do_block = q_s[head, cut, :], do_s[head, cut, :]
                lse = lse_s[chunk, cut, :][:, half * HEAD : half * HEAD + 1]
                delta = jnp.sum(
                    do_block.astype(F32) * o_s[chunk, cut, :], axis=-1, keepdims=True
                )
                dq_half = None
                for key in range(block + 1):
                    key_cut = slice(key * BLOCK, (key + 1) * BLOCK)
                    k_block, v_block = k_s[chunk, key_cut, :], v_s[chunk, key_cut, :]
                    scores = dot_nt(q_block, k_block)
                    if key == block:
                        scores = causal(scores, 0, 0)
                    probs = jnp.exp(scores - lse)
                    grad_probs = dot_nt(do_block, v_block)
                    ds = (probs * (grad_probs - delta)).astype(BF16)
                    term = dot_nn(ds, k_block)
                    dq_half = term if dq_half is None else dq_half + term
                    term = dot_tn(ds, q_block)
                    dk[key] = term if dk[key] is None else dk[key] + term
                    term = dot_tn(probs.astype(BF16), do_block)
                    dv[key] = term if dv[key] is None else dv[key] + term
                dq.append(dq_half)
            both = jnp.where(low_block, dq[0], dq[1]) * HEAD**-0.5
            dq_s[cut, columns] = rope_back(both, table[cut, :]).astype(BF16)
        for key in range(count // BLOCK):
            key_cut = slice(key * BLOCK, (key + 1) * BLOCK)
            dk_s[key_cut, columns] = rope_back(dk[key], table[key_cut, :]).astype(BF16)
            dv_s[key_cut, columns] = dv[key].astype(BF16)
        return carry

    lax.fori_loop(0, chunk_count, attend_back, 0)
    grad_a = dot_nt(dq_s[...], w_q[...])
    grad_a += dot_nt(dk_s[...], w_k[...])
    grad_a += dot_nt(dv_s[...], w_v[...])
    unit, scale = norm_parts(pooled[...])
    grad_pooled = middle[...] + norm_back(grad_a, gain_a[...], unit, scale)

    odd = me % 2 == 1
    low_width = lower_half(width)
    share_q = dot_tn(normed_a[...], dq_s[:, own_chunk])
    share_k = dot_tn(normed_a[...], dk_s[:, own_chunk])
    share_v = dot_tn(normed_a[...], dv_s[:, own_chunk])
    share_q = jnp.where(odd, turn(share_q), share_q)
    share_k = jnp.where(odd, share_k, turn(share_k))
    share_v = jnp.where(odd, turn(share_v), share_v)
    pack_attention(share, 2 * ff_own, jnp.where(low_width, share_q, share_k), fold_rows(share_v),
                   wo_s[rows_at((me % 2) * HEAD, HEAD, HEAD), :])
    ff_rows = 2 * ff_own // batch
    more_rows = share_pieces[0].shape[0] - ff_rows
    for step in range(batch):
        peer = seat ^ step
        share_pieces[step][:ff_rows] = share[rows_at(peer * ff_rows, ff_rows, 16), :]
        share_pieces[step][ff_rows:] = share[
            rows_at(2 * ff_own + peer * more_rows, more_rows, 16), :
        ]

    for chunk in range(chunk_count):
        cut = slice(chunk * LANES, (chunk + 1) * LANES)
        third = grad_pooled[:, cut] / 3.0
        for s in range(3):
            wide[chunk, pl.ds(6 + s, count, stride=3), :] = third
        wide[chunk, full + 6 : full + 8] = jnp.zeros((2, LANES), F32)
        grad_own[:, cut] = cot[:, cut] + wide[chunk, rows_at(me * rows + 8, rows, 8), :]
        for part in range(HEADS):
            at = part * stride + rows
            more = wide[chunk, 8 + part * rows : 8 + (part + 1) * rows, :]
            grad_all[part * rows : (part + 1) * rows, cut] = (
                gathered[at : at + rows, cut].astype(F32) + more
            ).astype(BF16)


def pack_attention(share, first, both_qk, folded_v, head_rows):
    half = both_qk.shape[0] // 2
    share[first : first + half, :LANES] = both_qk[:half].astype(BF16)
    share[first : first + half, LANES : 2 * LANES] = both_qk[half:].astype(BF16)
    share[first : first + half, 2 * LANES : 3 * LANES] = folded_v.astype(BF16)
    size = head_rows.shape[0]
    for chunk in range(head_rows.shape[1] // LANES):
        share[first + chunk * size : first + (chunk + 1) * size, 3 * LANES :] = head_rows[
            :, chunk * LANES : (chunk + 1) * LANES
        ].astype(BF16)


def finish_back_kernel(place, grad, middle, att, normed, gain, w_o, w_e, w_c, *refs):
    grad_middle_out, pieces, heads = refs[0], refs[1 : 1 + HEADS], refs[1 + HEADS]
    me = place[0]
    rows, width = grad.shape
    _, slope = gelu_both(dot_nn(normed[...], w_e[...]))
    grad_hidden = dot_nt(grad[...].astype(BF16), w_c[...])
    grad_pre = (grad_hidden * slope).astype(BF16)
    grad_normed = dot_nt(grad_pre, w_e[...])
    unit, scale = norm_parts(middle[...])
    grad_middle = grad[...] + norm_back(grad_normed, gain[...], unit, scale)
    grad_middle_out[...] = grad_middle
    g1 = grad_middle.astype(BF16)
    d_att = dot_nt(g1, w_o[...])
    grad_w = dot_tn(att[...], g1)
    half = rows // 2
    low = lower_half(half)
    for chunk in range(width // LANES):
        do_chunk = d_att[:, chunk * LANES : (chunk + 1) * LANES]
        first, later = do_chunk[:half], do_chunk[half:]
        heads[2 * chunk, :half] = jnp.where(low, first, turn(later)).astype(BF16)
        heads[2 * chunk + 1, :half] = jnp.where(low, turn(first), later).astype(BF16)
    for head in range(HEADS):
        for chunk in range(width // LANES):
            at = half + chunk * HEAD
            heads[head, at : at + HEAD] = grad_w[
                head * HEAD : (head + 1) * HEAD, chunk * LANES : (chunk + 1) * LANES
            ].astype(BF16)
    for step in range(HEADS):
        pieces[step][...] = heads[me ^ step]


def feed_forward_share_kernel(place, normed, grad, w_e, w_c, *refs):
    pieces, share = refs[:-1], refs[-1]
    seat = place[1]
    width, ff_own = w_e.shape
    value, slope = gelu_both(dot_nn(normed[...], w_e[...]))
    grad_hidden = dot_nt(grad[...], w_c[...])
    grad_pre = (grad_hidden * slope).astype(BF16)
    share[:ff_own] = dot_tn(value.astype(BF16), grad[...]).astype(BF16)
    expand = dot_tn(normed[...], grad_pre).astype(BF16)
    share[ff_own:, : width // 2] = expand[: width // 2]
    share[ff_own:, width // 2 :] = expand[width // 2 :]
    part_rows = pieces[0].shape[0]
    for step in range(len(pieces)):
        pieces[step][...] = share[rows_at((seat ^ step) * part_rows, part_rows, 16), :]


def attend_back_kernel(place, q_all, kv_all, lse_o, table, *refs):
    pieces, outs = refs[:HEADS], refs[HEADS : 2 * HEADS]
    dq_all, dkv_all, grad_wo, do_all, dkv_sum = refs[2 * HEADS :]
    me = place[0]
    rows = q_all.shape[0] // HEADS
    half = rows // 2
    low_half = lower_half(half)
    total = None
    for step in range(HEADS):
        start = (me ^ step) * rows
        folded = pieces[step][:half].astype(F32)
        do_all[rows_at(start, half, 16), :] = jnp.where(low_half, 0.0, turn(folded)).astype(BF16)
        do_all[rows_at(start + half, half, 16), :] = jnp.where(low_half, 0.0, folded).astype(BF16)
        term = pieces[step][half:].astype(F32)
        total = term if total is None else total + term
    grad_wo[...] = total
    dkv_sum[...] = jnp.zeros(dkv_sum.shape, F32)
    for block in range(q_all.shape[0] // BLOCK):
        cut = slice(block * BLOCK, (block + 1) * BLOCK)
        q_block, do_block = q_all[cut], do_all[cut]
        lse = lse_o[cut][:, :1]
        delta = jnp.sum(do_block.astype(F32) * lse_o[cut], axis=-1, keepdims=True)
        dq = None
        for key in range(block + 1):
            key_cut = slice(key * BLOCK, (key + 1) * BLOCK)
            kv_block = kv_all[key_cut]
            scores = dot_nt(q_block, kv_block)
            if key == block:
                scores = causal(scores, 0, 0)
            probs = jnp.exp(scores - lse)
            grad_probs = dot_nt(do_block, kv_block)
            ds = (probs * (grad_probs - delta)).astype(BF16)
            term = dot_nn(ds, kv_block)
            dq = term if dq is None else dq + term
            dkv_sum[key_cut] += dot_tn(ds, q_block) + dot_tn(probs.astype(BF16), do_block)
        dq_all[cut] = rope_back(dq * HEAD**-0.5, table[cut, :]).astype(BF16)
    low = lower_half(BLOCK)
    for block in range(q_all.shape[0] // BLOCK):
        cut = slice(block * BLOCK, (block + 1) * BLOCK)
        dkv = dkv_sum[cut]
        dkv_all[cut] = jnp.where(low, rope_back(dkv, table[cut, :]), dkv).astype(BF16)
    for step in range(HEADS):
        own = rows_at((me ^ step) * rows, rows, 16)
        outs[step][:rows] = dkv_all[own, :]
        outs[step][rows:] = fold_rows(dq_all[own, :].astype(F32)).astype(BF16)


def attention_share_kernel(place, gathered, dq_all, dkv_all, grad_wo, *refs):
    pieces, share = refs[:-1], refs[-1]
    seat = place[1]
    total = dq_all.shape[0]
    rows = total // HEADS
    stride = gathered.shape[0] // HEADS
    width = gathered.shape[1]
    grad_q = jnp.zeros((width, LANES), F32)
    grad_kv = jnp.zeros((width, LANES), F32)
    for part in range(HEADS):
        normed = gathered[part * stride : part * stride + rows]
        grad_q += dot_tn(normed, dq_all[part * rows : (part + 1) * rows])
        grad_kv += dot_tn(normed, dkv_all[part * rows : (part + 1) * rows])
    both = jnp.where(lower_half(width), grad_q, turn(grad_kv))
    half = width // 2
    folded_v = jnp.where(lower_half(half), turn(grad_kv[:half]), grad_kv[half:])
    share[:half, :LANES] = both[:half].astype(BF16)
    share[:half, LANES : 2 * LANES] = both[half:].astype(BF16)
    share[:half, 2 * LANES : 3 * LANES] = folded_v.astype(BF16)
    share[:half, 3 * LANES :] = grad_wo[...].astype(BF16)
    part_rows = pieces[0].shape[0]
    for step in range(len(pieces)):
        pieces[step][...] = share[rows_at((seat ^ step) * part_rows, part_rows, 16), :]


def start_back_kernel(place, x, grad_middle, gain, w_q, w_k, w_v, *refs):
    pieces = refs[:HEADS]
    grad_in, heads, dq, dk, dv = refs[HEADS:]
    me = place[0]
    rows, width = x.shape
    half = rows // 2
    for step in range(HEADS):
        heads[me ^ step] = pieces[step][...]
    low, low_half = lower_half(rows), lower_half(half)
    for chunk in range(width // LANES):
        cut = slice(chunk * LANES, (chunk + 1) * LANES)
        even, odd = heads[2 * chunk].astype(F32), heads[2 * chunk + 1].astype(F32)
        dk[:, cut] = jnp.where(low, even[:rows], turn(odd[:rows])).astype(BF16)
        dv[:, cut] = jnp.where(low, turn(even[:rows]), odd[:rows]).astype(BF16)
        dq[:half, cut] = jnp.where(low_half, even[rows:], turn(odd[rows:])).astype(BF16)
        dq[half:, cut] = jnp.where(low_half, turn(even[rows:]), odd[rows:]).astype(BF16)
    grad_a = dot_nt(dq[...], w_q[...]) + dot_nt(dk[...], w_k[...]) + dot_nt(dv[...], w_v[...])
    unit, scale = norm_parts(x[...])
    grad_in[...] = grad_middle[...] + norm_back(grad_a, gain[...], unit, scale)


def column_to_row(column):
    return jnp.transpose(jnp.broadcast_to(column, (column.shape[0], LANES)))[:1]


def feed_forward_grads_kernel(place, gathered, w_e, gain, contract, expand, grad_gain, share, acc):
    seat = place[1]
    step = pl.program_id(0)
    batch, _, width = gathered.shape[1:]
    ff_own = w_e.shape[1]
    part_rows = 2 * ff_own // batch
    for peer in range(batch):
        share[rows_at((seat ^ peer) * part_rows, part_rows, 16), :] = gathered[0, peer, :part_rows]
    contract[...] = share[:ff_own].astype(F32)
    half = width // 2
    first = share[ff_own:, :half].astype(F32)
    later = share[ff_own:, half:].astype(F32)
    expand[:half] = first
    expand[half:] = later

    @pl.when(step == 0)
    def _():
        acc[...] = jnp.zeros(acc.shape, F32)

    weights = w_e[...].astype(F32)
    acc[:half] += fold_lanes(weights[:half] * first)
    acc[half:] += fold_lanes(weights[half:] * later)

    @pl.when(step == pl.num_programs(0) - 1)
    def _():
        total = jnp.sum(acc[...], axis=-1, keepdims=True)
        grad_gain[...] = column_to_row(total) / gain[...]


def fold_lanes(values):
    return sum(
        values[:, at : at + LANES] for at in range(0, values.shape[1], LANES)
    )


def attention_grads_kernel(
    place, gathered, w_q, w_k, w_v, gain, grad_q, grad_k, grad_v, grad_o, grad_gain, share, acc
):
    seat = place[1]
    step = pl.program_id(0)
    _, batch, all_rows, width = gathered.shape
    half = width // 2
    part_rows = half // batch
    for side in range(2):
        for peer in range(batch):
            share[side, rows_at((seat ^ peer) * part_rows, part_rows, 16), :] = gathered[
                side, peer, all_rows - part_rows :
            ]
    low = lower_half(half)
    for part in range(2):
        rows = slice(part * half, (part + 1) * half)
        even = share[0, :, part * LANES : (part + 1) * LANES].astype(F32)
        odd = share[1, :, part * LANES : (part + 1) * LANES].astype(F32)
        grad_q[rows] = jnp.where(low, even, turn(odd))
        grad_k[rows] = jnp.where(low, turn(even), odd)
    even = share[0, :, 2 * LANES : 3 * LANES].astype(F32)
    odd = share[1, :, 2 * LANES : 3 * LANES].astype(F32)
    grad_v[:half] = jnp.where(low, even, turn(odd))
    grad_v[half:] = jnp.where(low, turn(even), odd)
    for side in range(2):
        for chunk in range(width // LANES):
            grad_o[side * HEAD : (side + 1) * HEAD, chunk * LANES : (chunk + 1) * LANES] = share[
                side, chunk * HEAD : (chunk + 1) * HEAD, 3 * LANES :
            ].astype(F32)

    @pl.when(step == 0)
    def _():
        acc[...] = jnp.zeros(acc.shape, F32)

    acc[...] += (
        w_q[...].astype(F32) * grad_q[...]
        + w_k[...].astype(F32) * grad_k[...]
        + w_v[...].astype(F32) * grad_v[...]
    )

    @pl.when(step == pl.num_programs(0) - 1)
    def _():
        total = jnp.sum(acc[...], axis=-1, keepdims=True)
        grad_gain[...] = column_to_row(total) / gain[...]


def call(kernel, out_shape, scratch, arguments, flops, limit=32):
    specs = [pl.BlockSpec(memory_space=pltpu.SMEM)]
    specs += [pl.BlockSpec(memory_space=pltpu.VMEM)] * (len(arguments) - 1)
    return pl.pallas_call(
        kernel,
        out_shape=[jax.ShapeDtypeStruct(shape, kind) for shape, kind in out_shape],
        in_specs=specs,
        out_specs=[pl.BlockSpec(memory_space=pltpu.VMEM)] * len(out_shape),
        scratch_shapes=[pltpu.VMEM(shape, kind) for shape, kind in scratch],
        compiler_params=pltpu.CompilerParams(vmem_limit_bytes=limit * 2**20),
        cost_estimate=pl.CostEstimate(flops=int(flops), bytes_accessed=2**20, transcendentals=0),
    )(*arguments)


def exchange(pieces, axis):
    devices = range(lax.axis_size(axis))
    moved = {
        step: lax.ppermute(pieces[step], axis, [(i, i ^ step) for i in devices])
        for step in reversed(range(1, len(pieces)))
    }
    return [pieces[0]] + [moved[step] for step in range(1, len(pieces))]


def sum_over_batch(pieces):
    arrived = exchange(pieces, "batch")
    total = sum(piece.astype(F32) for piece in arrived).astype(BF16)
    return jnp.stack(exchange([total] * len(pieces), "batch"))


def gather(block):
    return lax.all_gather(block, "seq", axis=0, tiled=True)


def feed_forward_grads(place, gathered, params):
    parts, batch, rows, width = gathered.shape
    ff = params[6].shape[1]
    ff_own = ff // parts
    return pl.pallas_call(
        feed_forward_grads_kernel,
        grid_spec=pltpu.PrefetchScalarGridSpec(
            num_scalar_prefetch=1,
            grid=(parts,),
            in_specs=[
                pl.BlockSpec((1, batch, rows, width), lambda i, s: (i, 0, 0, 0)),
                pl.BlockSpec((width, ff_own), lambda i, s: (0, i)),
                pl.BlockSpec((1, width), lambda i, s: (0, 0)),
            ],
            out_specs=[
                pl.BlockSpec((ff_own, width), lambda i, s: (i, 0)),
                pl.BlockSpec((width, ff_own), lambda i, s: (0, i)),
                pl.BlockSpec((1, width), lambda i, s: (0, 0)),
            ],
            scratch_shapes=[
                pltpu.VMEM((2 * ff_own, width), BF16),
                pltpu.VMEM((width, LANES), F32),
            ],
        ),
        out_shape=[
            jax.ShapeDtypeStruct((ff, width), F32),
            jax.ShapeDtypeStruct((width, ff), F32),
            jax.ShapeDtypeStruct((1, width), F32),
        ],
        cost_estimate=pl.CostEstimate(flops=10**9, bytes_accessed=2**23, transcendentals=0),
    )(place, gathered, params[6], params[5])


def attention_grads(place, gathered, params):
    parts, batch, rows, width = gathered.shape
    column = pl.BlockSpec((width, LANES), lambda i, s: (0, i))
    row = pl.BlockSpec((1, width), lambda i, s: (0, 0))
    square = jax.ShapeDtypeStruct((width, width), F32)
    return pl.pallas_call(
        attention_grads_kernel,
        grid_spec=pltpu.PrefetchScalarGridSpec(
            num_scalar_prefetch=1,
            grid=(parts // 2,),
            in_specs=[
                pl.BlockSpec((2, batch, rows, width), lambda i, s: (i, 0, 0, 0)),
                column,
                column,
                column,
                row,
            ],
            out_specs=[
                column,
                column,
                column,
                pl.BlockSpec((LANES, width), lambda i, s: (i, 0)),
                row,
            ],
            scratch_shapes=[
                pltpu.VMEM((2, width // 2, width), BF16),
                pltpu.VMEM((width, LANES), F32),
            ],
        ),
        out_shape=[square, square, square, square, jax.ShapeDtypeStruct((1, width), F32)],
        cost_estimate=pl.CostEstimate(flops=10**9, bytes_accessed=2**22, transcendentals=0),
    )(place, gathered, params[1], params[2], params[3], params[0])


def by_heads(inputs, cotangent, *weights):
    full = (weights[0][None],) + weights[1:5] + (weights[5][None],) + weights[6:8]
    brief = (weights[8][None],) + weights[9:13] + (weights[13][None],) + weights[14:16]
    x, cot = inputs[0], cotangent[0]
    rows, width = x.shape
    short, half, total = rows // 3, rows // 2, rows * HEADS
    batch = lax.axis_size("batch")
    ff = full[6].shape[1]
    ff_own = ff // HEADS
    count = short * HEADS
    chunks = width // LANES
    unit = 2.0 * rows * width * width
    place = jnp.stack([lax.axis_index("seq"), lax.axis_index("batch")]).astype(jnp.int32)
    table = rope_constants(total)
    block = rows + half

    outs = call(
        project_kernel,
        [((block, LANES), BF16)] * HEADS + [((2 * rows + short, width), BF16)],
        [((HEADS, block, LANES), BF16), ((chunks, rows, LANES), F32)],
        (place, x, cot, full[0], full[1], full[2], full[3], table),
        3 * unit,
    )
    pieces, bundle = exchange(outs[:HEADS], "seq"), outs[HEADS]
    gathered = gather(bundle)

    outs = call(
        attend_kernel,
        [((half, LANES), BF16)] * HEADS
        + [((total, LANES), BF16), ((total, LANES), BF16), ((total, LANES), F32)],
        [],
        (place, *pieces),
        12 * unit,
    )
    pieces = exchange(outs[:HEADS], "seq")
    q_all, kv_all, lse_o = outs[HEADS:]

    residual, middle, att, normed_f, pooled = call(
        finish_kernel,
        [
            ((rows, width), F32),
            ((rows, width), F32),
            ((rows, width), BF16),
            ((rows, width), BF16),
            ((short + 16, width), BF16),
        ],
        [((HEADS, half, LANES), F32), ((chunks, rows + 8, LANES), F32)],
        (place, x, full[5], full[4], full[6], full[7], *pieces),
        9 * unit,
    )
    pieces = exchange([pooled] * HEADS, "seq")
    normed_all = gather(normed_f)

    part_rows = (2 * ff_own + width // 2) // batch
    outs = call(
        short_kernel,
        [((rows, width), F32), ((rows, width), F32), ((total, width), BF16)]
        + [((part_rows, width), BF16)] * batch,
        [
            ((count, width), F32),
            ((HEADS, width), F32),
            ((count, width), BF16),
            ((HEADS, count, LANES), BF16),
            ((chunks, count, LANES), BF16),
            ((chunks, count, LANES), BF16),
            ((chunks, count, LANES), F32),
            ((chunks, count, LANES), F32),
            ((count, width), BF16),
            ((count, width), F32),
            ((count, width), BF16),
            ((count, ff), BF16),
            ((count, ff), BF16),
            ((count, width), F32),
            ((count, width), BF16),
            ((HEADS, count, LANES), BF16),
            ((count, width), BF16),
            ((count, width), BF16),
            ((count, width), BF16),
            ((chunks, total + 16, LANES), F32),
            ((2 * ff_own + width // 2, width), BF16),
            ((LANES, width), F32),
        ],
        (place, residual, cot, gathered, table) + brief + tuple(pieces),
        60 * unit,
        60,
    )
    output, grad_own, grad_all = outs[:3]
    short_share = gather(sum_over_batch(outs[3:])[None])

    outs = call(
        finish_back_kernel,
        [((rows, width), F32)] + [((half + 4 * HEAD, LANES), BF16)] * HEADS,
        [((HEADS, half + 4 * HEAD, LANES), BF16)],
        (place, grad_own, middle, att, normed_f, full[5], full[4], full[6], full[7]),
        14 * unit,
    )
    grad_middle = outs[0]
    pieces = exchange(outs[1:], "seq")

    whole = pl.BlockSpec((total, width), lambda i, s: (0, 0))
    piece = pl.BlockSpec((2 * ff_own // batch, width), lambda i, s: (0, 0))
    outs = pl.pallas_call(
        feed_forward_share_kernel,
        grid_spec=pltpu.PrefetchScalarGridSpec(
            num_scalar_prefetch=1,
            grid=(1,),
            in_specs=[
                whole,
                whole,
                pl.BlockSpec((width, ff_own), lambda i, s: (0, s[0])),
                pl.BlockSpec((ff_own, width), lambda i, s: (s[0], 0)),
            ],
            out_specs=[piece] * batch,
            scratch_shapes=[pltpu.VMEM((2 * ff_own, width), BF16)],
        ),
        out_shape=[jax.ShapeDtypeStruct((2 * ff_own // batch, width), BF16)] * batch,
        compiler_params=pltpu.CompilerParams(vmem_limit_bytes=32 * 2**20),
        cost_estimate=pl.CostEstimate(
            flops=int(20 * unit), bytes_accessed=2**22, transcendentals=0
        ),
    )(place, normed_all, grad_all, full[6], full[7])
    ff_share = gather(sum_over_batch(outs)[None])

    outs = call(
        attend_back_kernel,
        [((block, LANES), BF16)] * HEADS
        + [((total, LANES), BF16), ((total, LANES), BF16), ((4 * HEAD, LANES), F32)],
        [((total, LANES), BF16), ((total, LANES), F32)],
        (place, q_all, kv_all, lse_o, table, *pieces),
        20 * unit,
    )
    pieces = exchange(outs[:HEADS], "seq")
    dq_all, dkv_all, grad_wo = outs[HEADS:]
    outs = call(
        attention_share_kernel,
        [((width // 2 // batch, width), BF16)] * batch,
        [((width // 2, width), BF16)],
        (place, gathered, dq_all, dkv_all, grad_wo),
        8 * unit,
    )
    attention_share = gather(sum_over_batch(outs)[None])

    (grad_in,) = call(
        start_back_kernel,
        [((rows, width), F32)],
        [((HEADS, block, LANES), BF16)] + [((rows, width), BF16)] * 3,
        (place, x, grad_middle, full[0], full[1], full[2], full[3], *pieces),
        6 * unit,
    )

    def arranged(attention, feed_forward):
        grad_q, grad_k, grad_v, grad_o, grad_gain_a = attention
        contract, expand, grad_gain_f = feed_forward
        return (grad_gain_a[0], grad_q, grad_k, grad_v, grad_o, grad_gain_f[0], expand, contract)

    short_grads = arranged(
        attention_grads(place, short_share, brief), feed_forward_grads(place, short_share, brief)
    )
    full_grads = arranged(
        attention_grads(place, attention_share, full), feed_forward_grads(place, ff_share, full)
    )
    return (output[None], grad_in[None]) + full_grads + short_grads


def from_behind(block, axis, distance):
    devices = range(lax.axis_size(axis))
    route = [(i - distance, i) for i in devices if i - distance in devices]
    return lax.ppermute(block, axis, route)


def normalize(stream, gain):
    row_mean = jnp.mean(stream, axis=-1, keepdims=True)
    centered = stream - row_mean
    spread = jnp.mean(centered * centered, axis=-1, keepdims=True)
    return centered * lax.rsqrt(spread + norm_eps) * gain


def rope_table(positions):
    half_size = HEAD // 2
    frequency = jnp.power(10000.0, -jnp.arange(half_size, dtype=jnp.float32) * 2.0 / HEAD)
    angles = positions.astype(jnp.float32)[:, None] * frequency[None, :]
    return (jnp.cos(angles)[:, None, :], jnp.sin(angles)[:, None, :])


def rotate(values, angle_cos, angle_sin):
    first_half, second_half = jnp.split(values, 2, axis=-1)
    return jnp.concatenate(
        [
            first_half * angle_cos - second_half * angle_sin,
            first_half * angle_sin + second_half * angle_cos,
        ],
        axis=-1,
    )


def rotate_back(grads, angle_cos, angle_sin):
    first_half, second_half = jnp.split(grads, 2, axis=-1)
    return jnp.concatenate(
        [
            first_half * angle_cos + second_half * angle_sin,
            second_half * angle_cos - first_half * angle_sin,
        ],
        axis=-1,
    )


def split_heads(matrix):
    return matrix.reshape(matrix.shape[0], HEADS, HEAD)


def project(stream, params, angle_cos, angle_sin):
    normed_in = normalize(stream, params[0]).astype(jnp.bfloat16)

    def heads_of(matrix):
        return split_heads(jnp.dot(normed_in, matrix, preferred_element_type=jnp.float32))

    queries = rotate(heads_of(params[1]), angle_cos, angle_sin).astype(jnp.bfloat16)
    keys_here = rotate(heads_of(params[2]), angle_cos, angle_sin).astype(jnp.bfloat16)
    values_here = heads_of(params[3]).astype(jnp.bfloat16)
    return (normed_in, queries, keys_here, values_here)


def masked_scores(queries, keys_all, query_places, key_places):
    scores = jnp.einsum(
        "nhe,mhe->hnm", queries, keys_all, preferred_element_type=jnp.float32
    ) * HEAD ** (-0.5)
    allowed = key_places[None, None, :] <= query_places[None, :, None]
    return jnp.where(allowed, scores, -1e30)


def attend(queries, keys_all, values_all, query_places, key_places):
    scores = masked_scores(queries, keys_all, query_places, key_places)
    highest_score = jnp.max(scores, axis=-1, keepdims=True)
    log_total = highest_score + jnp.log(
        jnp.sum(jnp.exp(scores - highest_score), axis=-1, keepdims=True)
    )
    prob_low = jnp.exp(scores - log_total).astype(jnp.bfloat16)
    attended = jnp.einsum("hnm,mhe->nhe", prob_low, values_all, preferred_element_type=jnp.float32)
    return (attended, log_total)


def attend_back(queries, keys_all, values_all, query_places, key_places, log_total, grad_attended):
    scores = masked_scores(queries, keys_all, query_places, key_places)
    probs_full = jnp.exp(scores - log_total)
    grad_probs = jnp.einsum(
        "nhe,mhe->hnm", grad_attended, values_all, preferred_element_type=jnp.float32
    )
    row_inner = jnp.sum(probs_full * grad_probs, axis=-1, keepdims=True)
    grad_scores = (probs_full * (grad_probs - row_inner)).astype(jnp.bfloat16)
    grad_queries = jnp.einsum(
        "hnm,mhe->nhe", grad_scores, keys_all, preferred_element_type=jnp.float32
    ) * HEAD ** (-0.5)
    return (grad_queries, grad_scores, probs_full.astype(jnp.bfloat16), row_inner)


def finish(stream, attended, params):
    row_count, width = stream.shape
    attended_low = attended.reshape(row_count, width).astype(jnp.bfloat16)
    middle = stream + jnp.dot(attended_low, params[4], preferred_element_type=jnp.float32)
    normed_mid = normalize(middle, params[5]).astype(jnp.bfloat16)
    hidden_pre = jnp.dot(normed_mid, params[6], preferred_element_type=jnp.float32)
    hidden_low = jax.nn.gelu(hidden_pre, approximate=True).astype(jnp.bfloat16)
    result = middle + jnp.dot(hidden_low, params[7], preferred_element_type=jnp.float32)
    return (result, (attended_low, middle, normed_mid, hidden_pre, hidden_low))


def finish_back(grad_result, finish_saved, params):
    attended_low, middle, normed_mid, hidden_pre, hidden_low = finish_saved
    grad_low = grad_result.astype(jnp.bfloat16)
    grad_contract = jnp.einsum(
        "nf,nd->fd", hidden_low, grad_low, preferred_element_type=jnp.float32
    )
    grad_hidden = jnp.einsum("nd,fd->nf", grad_low, params[7], preferred_element_type=jnp.float32)
    gelu_value, gelu_pull = jax.vjp(partial(jax.nn.gelu, approximate=True), hidden_pre)
    grad_pre = gelu_pull(grad_hidden)[0].astype(jnp.bfloat16)
    grad_expand = jnp.einsum("nd,nf->df", normed_mid, grad_pre, preferred_element_type=jnp.float32)
    grad_normed = jnp.einsum("nf,df->nd", grad_pre, params[6], preferred_element_type=jnp.float32)
    norm_value, norm_pull = jax.vjp(normalize, middle, params[5])
    grad_norm_in, grad_gain_ffn = norm_pull(grad_normed)
    grad_middle = grad_result + grad_norm_in
    middle_low = grad_middle.astype(jnp.bfloat16)
    grad_output_w = jnp.einsum(
        "nc,nd->cd", attended_low, middle_low, preferred_element_type=jnp.float32
    )
    grad_attended = split_heads(
        jnp.einsum("nd,cd->nc", middle_low, params[4], preferred_element_type=jnp.float32).astype(
            jnp.bfloat16
        )
    )
    return (grad_middle, grad_attended, grad_output_w, grad_expand, grad_contract, grad_gain_ffn)


def start_back(
    grad_queries, grad_keys, grad_values, stream, params, normed_in, angle_cos, angle_sin
):
    row_count, width = stream.shape
    query_low = (
        rotate_back(grad_queries, angle_cos, angle_sin)
        .reshape(row_count, width)
        .astype(jnp.bfloat16)
    )
    key_low = (
        rotate_back(grad_keys, angle_cos, angle_sin).reshape(row_count, width).astype(jnp.bfloat16)
    )
    value_low = grad_values.reshape(row_count, width).astype(jnp.bfloat16)
    grad_query = jnp.einsum("nd,nc->dc", normed_in, query_low, preferred_element_type=jnp.float32)
    grad_key = jnp.einsum("nd,nc->dc", normed_in, key_low, preferred_element_type=jnp.float32)
    grad_value = jnp.einsum("nd,nc->dc", normed_in, value_low, preferred_element_type=jnp.float32)
    grad_normed = (
        jnp.einsum("nc,dc->nd", query_low, params[1], preferred_element_type=jnp.float32)
        + jnp.einsum("nc,dc->nd", key_low, params[2], preferred_element_type=jnp.float32)
        + jnp.einsum("nc,dc->nd", value_low, params[3], preferred_element_type=jnp.float32)
    )
    norm_value, norm_pull = jax.vjp(normalize, stream, params[0])
    grad_stream, grad_gain_attn = norm_pull(grad_normed)
    return (grad_stream, grad_gain_attn, grad_query, grad_key, grad_value)


def local_forward(stream, places, params, fetch):
    angle_cos, angle_sin = rope_table(places)
    normed_in, queries, keys_here, values_here = project(stream, params, angle_cos, angle_sin)
    row_count, width = stream.shape
    keys_local = keys_here.reshape(row_count, width)
    values_local = values_here.reshape(row_count, width)
    keys_flat, values_flat = fetch(keys_local, values_local)
    key_places = jnp.arange(keys_flat.shape[0], dtype=jnp.int32)
    attended, log_total = attend(
        queries, split_heads(keys_flat), split_heads(values_flat), places, key_places
    )
    result, finish_saved = finish(stream, attended, params)
    return (
        result,
        (
            normed_in,
            queries,
            keys_local,
            values_local,
            keys_flat,
            values_flat,
            log_total,
            angle_cos,
            angle_sin,
            finish_saved,
        ),
    )


def local_backward(grad_result, stream, places, params, saved, keys_flat, values_flat, key_sum):
    normed_in, queries = (saved[0], saved[1])
    log_total, angle_cos, angle_sin, finish_saved = (saved[6], saved[7], saved[8], saved[9])
    grad_middle, grad_attended, grad_output_w, grad_expand, grad_contract, grad_gain_ffn = (
        finish_back(grad_result, finish_saved, params)
    )
    row_count, width = stream.shape
    key_places = jnp.arange(keys_flat.shape[0], dtype=jnp.int32)
    grad_queries, grad_scores, prob_low, row_inner = attend_back(
        queries,
        split_heads(keys_flat),
        split_heads(values_flat),
        places,
        key_places,
        log_total,
        grad_attended,
    )

    def contribution(first_row, term_rows):
        grad_keys = jnp.einsum(
            "hnm,nhe->mhe", grad_scores, queries, preferred_element_type=jnp.float32
        ) * HEAD ** (-0.5)
        grad_values = jnp.einsum(
            "hnm,nhe->mhe", prob_low, grad_attended, preferred_element_type=jnp.float32
        )
        return jnp.concatenate(
            [grad_keys.reshape(term_rows, width), grad_values.reshape(term_rows, width)], axis=1
        )

    both_grads = key_sum(contribution, row_count, (queries, grad_attended, log_total, row_inner))
    grad_stream, grad_gain_attn, grad_query, grad_key, grad_value = start_back(
        grad_queries,
        split_heads(both_grads[:, :width]),
        split_heads(both_grads[:, width:]),
        stream,
        params,
        normed_in,
        angle_cos,
        angle_sin,
    )
    return (
        grad_middle + grad_stream,
        (
            grad_gain_attn,
            grad_query,
            grad_key,
            grad_value,
            grad_output_w,
            grad_gain_ffn,
            grad_expand,
            grad_contract,
        ),
    )


def whole_forward(stream, params):
    row_count, width = stream.shape
    places = jnp.arange(row_count, dtype=jnp.int32)
    angle_cos, angle_sin = rope_table(places)
    normed_in, queries, keys_here, values_here = project(stream, params, angle_cos, angle_sin)
    block_rows = 512
    block_count = row_count // block_rows

    def one_block(pieces):
        return attend(pieces[0], keys_here, values_here, pieces[1], places)

    attended, log_total = lax.map(
        one_block,
        (
            queries.reshape(block_count, block_rows, HEADS, HEAD),
            places.reshape(block_count, block_rows),
        ),
    )
    result, finish_saved = finish(stream, attended.reshape(row_count, HEADS, HEAD), params)
    return (
        result,
        (normed_in, queries, keys_here, values_here, log_total, angle_cos, angle_sin, finish_saved),
    )


def whole_backward(grad_result, stream, params, saved):
    normed_in, queries, keys_here, values_here, log_total, angle_cos, angle_sin, finish_saved = (
        saved
    )
    grad_middle, grad_attended, grad_output_w, grad_expand, grad_contract, grad_gain_ffn = (
        finish_back(grad_result, finish_saved, params)
    )
    row_count, width = stream.shape
    places = jnp.arange(row_count, dtype=jnp.int32)
    block_rows = 512
    block_count = row_count // block_rows

    def one_block(running, pieces):
        query_block, place_block, total_block, grad_block = pieces
        grad_queries, grad_scores, prob_low, row_inner = attend_back(
            query_block, keys_here, values_here, place_block, places, total_block, grad_block
        )
        grad_keys = running[0] + jnp.einsum(
            "hnm,nhe->mhe", grad_scores, query_block, preferred_element_type=jnp.float32
        ) * HEAD ** (-0.5)
        grad_values = running[1] + jnp.einsum(
            "hnm,nhe->mhe", prob_low, grad_block, preferred_element_type=jnp.float32
        )
        return ((grad_keys, grad_values), grad_queries)

    zero_grads = jnp.zeros((row_count, HEADS, HEAD), jnp.float32)
    (grad_keys, grad_values), grad_queries = lax.scan(
        one_block,
        (zero_grads, zero_grads),
        (
            queries.reshape(block_count, block_rows, HEADS, HEAD),
            places.reshape(block_count, block_rows),
            log_total,
            grad_attended.reshape(block_count, block_rows, HEADS, HEAD),
        ),
    )
    grad_stream, grad_gain_attn, grad_query, grad_key, grad_value = start_back(
        grad_queries.reshape(row_count, HEADS, HEAD),
        grad_keys,
        grad_values,
        stream,
        params,
        normed_in,
        angle_cos,
        angle_sin,
    )
    return (
        grad_middle + grad_stream,
        (
            grad_gain_attn,
            grad_query,
            grad_key,
            grad_value,
            grad_output_w,
            grad_gain_ffn,
            grad_expand,
            grad_contract,
        ),
    )


def by_rows(
    inputs,
    cotangent,
    full_gain_attn,
    full_query,
    full_key,
    full_value,
    full_output,
    full_gain_ffn,
    full_expand,
    full_contract,
    short_gain_attn,
    short_query,
    short_key,
    short_value,
    short_output,
    short_gain_ffn,
    short_expand,
    short_contract,
):
    full_params = (
        full_gain_attn,
        full_query,
        full_key,
        full_value,
        full_output,
        full_gain_ffn,
        full_expand,
        full_contract,
    )
    short_params = (
        short_gain_attn,
        short_query,
        short_key,
        short_value,
        short_output,
        short_gain_ffn,
        short_expand,
        short_contract,
    )
    stream_in = inputs[0]
    row_count, width = stream_in.shape
    own_short = row_count // 3
    position = lax.axis_index("seq")
    seq_parts = lax.axis_size("seq")
    places = position * row_count + jnp.arange(row_count, dtype=jnp.int32)

    def fetch_full(keys_local, values_local):
        return (
            lax.all_gather(keys_local, "seq", axis=0, tiled=True),
            lax.all_gather(values_local, "seq", axis=0, tiled=True),
        )

    residual, full_saved = local_forward(stream_in, places, full_params, fetch_full)
    tail_rows = from_behind(residual[row_count - 2 :], "seq", 1)
    shifted = jnp.concatenate([tail_rows, residual[: row_count - 2]], axis=0)
    pooled = jnp.mean(shifted.reshape(own_short, 3, width), axis=1)
    pooled_all = lax.all_gather(pooled, "seq", axis=0, tiled=True)
    short_all, short_saved = whole_forward(pooled_all, short_params)
    short_result = lax.dynamic_slice_in_dim(short_all, position * own_short, own_short, 0)
    output = residual + jnp.repeat(short_result, 3, axis=0)
    grad_output = cotangent[0]
    grad_short = jnp.sum(grad_output.reshape(own_short, 3, width), axis=1)
    grad_short_all = lax.all_gather(grad_short, "seq", axis=0, tiled=True)
    grad_pooled_all, short_grads = whole_backward(
        grad_short_all, pooled_all, short_params, short_saved
    )
    grad_pooled = lax.dynamic_slice_in_dim(grad_pooled_all, position * own_short, own_short, 0)
    short_grads = tuple(
        (
            lax.dynamic_slice_in_dim(
                gradient,
                position * (gradient.shape[0] // seq_parts),
                gradient.shape[0] // seq_parts,
                0,
            )
            for gradient in short_grads
        )
    )
    grad_shifted = jnp.repeat(grad_pooled / 3.0, 3, axis=0)
    carried = from_behind(grad_shifted[:2], "seq", -1)
    grad_residual = grad_output + jnp.concatenate([grad_shifted[2:], carried], axis=0)
    keys_flat, values_flat = (
        lax.all_gather(full_saved[2], "seq", axis=0, tiled=True),
        lax.all_gather(full_saved[3], "seq", axis=0, tiled=True),
    )

    def full_sum(contribution, term_rows, query_side):
        return lax.psum_scatter(
            contribution(jnp.int32(0), term_rows * lax.axis_size("seq")).astype(jnp.bfloat16),
            "seq",
            scatter_dimension=0,
            tiled=True,
        ).astype(jnp.float32)

    grad_input, full_grads = local_backward(
        grad_residual, stream_in, places, full_params, full_saved, keys_flat, values_flat, full_sum
    )
    full_shares = (
        lax.psum_scatter(
            full_grads[0].astype(jnp.bfloat16), "seq", scatter_dimension=0, tiled=True
        ).astype(jnp.float32),
        lax.psum_scatter(
            full_grads[1].astype(jnp.bfloat16), "seq", scatter_dimension=0, tiled=True
        ).astype(jnp.float32),
        lax.psum_scatter(
            full_grads[2].astype(jnp.bfloat16), "seq", scatter_dimension=0, tiled=True
        ).astype(jnp.float32),
        lax.psum_scatter(
            full_grads[3].astype(jnp.bfloat16), "seq", scatter_dimension=0, tiled=True
        ).astype(jnp.float32),
        lax.psum_scatter(
            full_grads[4].astype(jnp.bfloat16), "seq", scatter_dimension=0, tiled=True
        ).astype(jnp.float32),
        lax.psum_scatter(
            full_grads[5].astype(jnp.bfloat16), "seq", scatter_dimension=0, tiled=True
        ).astype(jnp.float32),
        lax.psum_scatter(
            full_grads[6].astype(jnp.bfloat16), "seq", scatter_dimension=0, tiled=True
        ).astype(jnp.float32),
        lax.psum_scatter(
            full_grads[7].astype(jnp.bfloat16), "seq", scatter_dimension=0, tiled=True
        ).astype(jnp.float32),
    )
    shares = tuple(full_shares) + tuple(short_grads)
    totals = (
        lax.psum(shares[0].astype(jnp.bfloat16), "batch").astype(jnp.float32),
        lax.psum(shares[1].astype(jnp.bfloat16), "batch").astype(jnp.float32),
        lax.psum(shares[2].astype(jnp.bfloat16), "batch").astype(jnp.float32),
        lax.psum(shares[3].astype(jnp.bfloat16), "batch").astype(jnp.float32),
        lax.psum(shares[4].astype(jnp.bfloat16), "batch").astype(jnp.float32),
        lax.psum(shares[5].astype(jnp.bfloat16), "batch").astype(jnp.float32),
        lax.psum(shares[6].astype(jnp.bfloat16), "batch").astype(jnp.float32),
        lax.psum(shares[7].astype(jnp.bfloat16), "batch").astype(jnp.float32),
        lax.psum(shares[8].astype(jnp.bfloat16), "batch").astype(jnp.float32),
        lax.psum(shares[9].astype(jnp.bfloat16), "batch").astype(jnp.float32),
        lax.psum(shares[10].astype(jnp.bfloat16), "batch").astype(jnp.float32),
        lax.psum(shares[11].astype(jnp.bfloat16), "batch").astype(jnp.float32),
        lax.psum(shares[12].astype(jnp.bfloat16), "batch").astype(jnp.float32),
        lax.psum(shares[13].astype(jnp.bfloat16), "batch").astype(jnp.float32),
        lax.psum(shares[14].astype(jnp.bfloat16), "batch").astype(jnp.float32),
        lax.psum(shares[15].astype(jnp.bfloat16), "batch").astype(jnp.float32),
    )
    whole = (
        lax.all_gather(totals[0].astype(jnp.bfloat16), "seq", axis=0, tiled=True).astype(
            jnp.float32
        ),
        lax.all_gather(totals[1].astype(jnp.bfloat16), "seq", axis=0, tiled=True).astype(
            jnp.float32
        ),
        lax.all_gather(totals[2].astype(jnp.bfloat16), "seq", axis=0, tiled=True).astype(
            jnp.float32
        ),
        lax.all_gather(totals[3].astype(jnp.bfloat16), "seq", axis=0, tiled=True).astype(
            jnp.float32
        ),
        lax.all_gather(totals[4].astype(jnp.bfloat16), "seq", axis=0, tiled=True).astype(
            jnp.float32
        ),
        lax.all_gather(totals[5].astype(jnp.bfloat16), "seq", axis=0, tiled=True).astype(
            jnp.float32
        ),
        lax.all_gather(totals[6].astype(jnp.bfloat16), "seq", axis=0, tiled=True).astype(
            jnp.float32
        ),
        lax.all_gather(totals[7].astype(jnp.bfloat16), "seq", axis=0, tiled=True).astype(
            jnp.float32
        ),
        lax.all_gather(totals[8].astype(jnp.bfloat16), "seq", axis=0, tiled=True).astype(
            jnp.float32
        ),
        lax.all_gather(totals[9].astype(jnp.bfloat16), "seq", axis=0, tiled=True).astype(
            jnp.float32
        ),
        lax.all_gather(totals[10].astype(jnp.bfloat16), "seq", axis=0, tiled=True).astype(
            jnp.float32
        ),
        lax.all_gather(totals[11].astype(jnp.bfloat16), "seq", axis=0, tiled=True).astype(
            jnp.float32
        ),
        lax.all_gather(totals[12].astype(jnp.bfloat16), "seq", axis=0, tiled=True).astype(
            jnp.float32
        ),
        lax.all_gather(totals[13].astype(jnp.bfloat16), "seq", axis=0, tiled=True).astype(
            jnp.float32
        ),
        lax.all_gather(totals[14].astype(jnp.bfloat16), "seq", axis=0, tiled=True).astype(
            jnp.float32
        ),
        lax.all_gather(totals[15].astype(jnp.bfloat16), "seq", axis=0, tiled=True).astype(
            jnp.float32
        ),
    )
    return (output[None], grad_input[None]) + tuple(whole)


def solution(mesh):
    sequence = P("batch", "seq", None)
    seq, batch = mesh.shape["seq"], mesh.shape["batch"]
    fits = seq == HEADS and batch & (batch - 1) == 0
    return jax.shard_map(
        by_heads if fits else by_rows,
        mesh=mesh,
        in_specs=(sequence, sequence) + (P(),) * 16,
        out_specs=(sequence, sequence) + (P(),) * 16,
        check_vma=False,
    )
```

```python
from functools import partial

import jax
import jax.numpy as jnp
import numpy as np
from jax import lax
from jax.experimental import pallas as pl
from jax.experimental.pallas import tpu as pltpu
from jax.sharding import PartitionSpec as P

HEADS = 8
HEAD = 64
LANES = 128
BLOCK = 256
F32 = jnp.float32
BF16 = jnp.bfloat16


norm_eps = 1e-05


def dot_nn(left, right):
    return jnp.dot(left, right, preferred_element_type=F32)


def dot_nt(left, right):
    return lax.dot_general(left, right, (((1,), (1,)), ((), ())), preferred_element_type=F32)


def dot_tn(left, right):
    return lax.dot_general(left, right, (((0,), (0,)), ((), ())), preferred_element_type=F32)


def lower_half(rows):
    return lax.broadcasted_iota(jnp.int32, (rows, LANES), 1) < HEAD


def turn(values):
    return pltpu.roll(values, HEAD, 1)


def swap_pairs(values):
    lane = lax.broadcasted_iota(jnp.int32, values.shape, 1)
    return jnp.where(
        lane % HEAD < HEAD // 2,
        pltpu.roll(values, LANES - HEAD // 2, 1),
        pltpu.roll(values, HEAD // 2, 1),
    )


def rope(values, table):
    return values * table[:, :LANES] + swap_pairs(values) * table[:, LANES:]


def rope_back(grads, table):
    return grads * table[:, :LANES] - swap_pairs(grads) * table[:, LANES:]


def rope_constants(rows):
    frequency = np.power(
        np.float32(10000.0), -np.arange(HEAD // 2, dtype=np.float32) * np.float32(2.0 / HEAD)
    ).astype(np.float32)
    angles = np.arange(rows, dtype=np.float32)[:, None] * frequency[None, :]
    cosine, sine = np.cos(angles), np.sin(angles)
    table = np.concatenate([cosine] * 4 + [-sine, sine] * 2, axis=1)
    return jnp.asarray(table, F32)


def norm_parts(stream):
    centered = stream - jnp.mean(stream, axis=-1, keepdims=True)
    spread = jnp.mean(centered * centered, axis=-1, keepdims=True)
    scale = lax.rsqrt(spread + norm_eps)
    return centered * scale, scale


def norm_back(grad, gain, unit, scale):
    grad_unit = grad * gain
    inner = jnp.mean(grad_unit * unit, axis=-1, keepdims=True)
    return scale * (grad_unit - jnp.mean(grad_unit, axis=-1, keepdims=True) - unit * inner)


GELU_SCALE = 0.7978845608028654
GELU_CUBE = 0.044715


def gelu_both(pre):
    square = pre * pre
    tanh = jnp.tanh(GELU_SCALE * pre * (1.0 + GELU_CUBE * square))
    half = 0.5 * (1.0 + tanh)
    slope = half + 0.5 * pre * (1.0 - tanh * tanh) * (
        GELU_SCALE * (1.0 + 3.0 * GELU_CUBE * square)
    )
    return pre * half, slope


def gelu_value(pre):
    tanh = jnp.tanh(GELU_SCALE * pre * (1.0 + GELU_CUBE * pre * pre))
    return 0.5 * pre * (1.0 + tanh)


def causal(scores, first_row, first_key):
    row = lax.broadcasted_iota(jnp.int32, scores.shape, 0) + first_row
    key = lax.broadcasted_iota(jnp.int32, scores.shape, 1) + first_key
    return jnp.where(key <= row, scores, -1e30)


def fold_rows(values):
    half = values.shape[0] // 2
    return jnp.where(lower_half(half), values[:half], turn(values[half:]))


def unfold_rows(folded):
    low = lower_half(folded.shape[0])
    return jnp.where(low, folded, 0.0), jnp.where(low, turn(folded), 0.0)


def rows_at(start, size, multiple):
    return pl.ds(pl.multiple_of(start, multiple), size)


class Late:
    def __init__(self, source, target, semaphore):
        self.copy = pltpu.make_async_copy(source, target, semaphore)
        self.target, self.arrived = target, False
        self.shape = target.shape
        self.copy.start()

    def ready(self):
        if not self.arrived:
            self.copy.wait()
            self.arrived = True
        return self.target

    def __getitem__(self, index):
        return self.ready()[index]


def with_late(kernel, late, argument_count, out_count, *refs):
    arguments, outs = list(refs[:argument_count]), refs[argument_count : argument_count + out_count]
    rest = refs[argument_count + out_count :]
    first = len(rest) - len(late) - 1
    for at, (place, _, part) in enumerate(late):
        source = arguments[place]
        source = source if part is None else part(source, refs[0][0])
        arguments[place] = Late(source, rest[first + at], rest[-1].at[at])
    kernel(*arguments, *outs, *rest[:first])


def paired(refs):
    size = refs[0].shape[0] // 2
    pairs = len(refs) // 2
    return [
        refs[step // 2].at[pl.ds(0, size), :]
        if step % 2 == 0
        else refs[pairs + step // 2].at[pl.ds(size, size), :]
        for step in range(2 * pairs)
    ]


def by_distance(share, pieces, seat):
    rows = pieces[0].shape[0]
    for step in range(len(pieces)):
        pieces[step][...] = share[rows_at((seat ^ step) * rows, rows, 16), :]


def keep_and_send(share, keep, send, seat, parts, first=0):
    rows = share.shape[0] // parts
    stride = keep.shape[0] // (parts // 2)
    for step in range(parts):
        target = keep if step % 2 == 0 else send
        at = (step // 2) * stride + first
        target[at : at + rows] = share[rows_at((seat ^ step) * rows, rows, 16), :]


def load_kernel(place, *refs):
    count = (len(refs) - 1) // 2
    copies = [
        pltpu.make_async_copy(refs[at], refs[count + at], refs[-1].at[at]) for at in range(count)
    ]
    for copy in copies:
        copy.start()
    for copy in copies:
        copy.wait()


def project_kernel(place, x, cot, gain, w_q, w_k, w_v, table, *refs):
    pieces, bundle, heads, chunks = refs[:HEADS], refs[HEADS], refs[HEADS + 1], refs[HEADS + 2]
    rows, width = x.shape
    me = place[0]
    unit, _ = norm_parts(x[...])
    normed = (unit * gain[...]).astype(BF16)
    q = dot_nn(normed, w_q[...])
    k = dot_nn(normed, w_k[...])
    v = dot_nn(normed, w_v[...])
    low = lower_half(rows)
    low_half = lower_half(rows // 2)
    own = table[...]
    for chunk in range(width // LANES):
        cut = slice(chunk * LANES, (chunk + 1) * LANES)
        q_chunk = rope(q[:, cut], own) * HEAD**-0.5
        k_chunk = rope(k[:, cut], own)
        v_chunk = v[:, cut]
        first, later = q_chunk[: rows // 2], q_chunk[rows // 2 :]
        heads[2 * chunk, :rows] = jnp.where(low, k_chunk, turn(v_chunk)).astype(BF16)
        heads[2 * chunk + 1, :rows] = jnp.where(low, turn(k_chunk), v_chunk).astype(BF16)
        heads[2 * chunk, rows:] = jnp.where(low_half, first, turn(later)).astype(BF16)
        heads[2 * chunk + 1, rows:] = jnp.where(low_half, turn(first), later).astype(BF16)
    for step in range(HEADS):
        pieces[step][...] = heads[me ^ step]
    bundle[:rows] = normed
    bundle[rows : 2 * rows] = cot[...].astype(BF16)
    for chunk in range(width // LANES):
        cut = slice(chunk * LANES, (chunk + 1) * LANES)
        chunks[chunk] = cot[:, cut]
        total = sum(chunks[chunk, pl.ds(s, rows // 3, stride=3), :] for s in range(3))
        bundle[2 * rows :, cut] = total.astype(BF16)


def attend_kernel(place, *refs):
    pieces, outs = refs[:HEADS], refs[HEADS : HEADS + HEADS // 2]
    q_all, kv_all, lse_o = refs[HEADS + HEADS // 2 :]
    me = place[0]
    rows = outs[0].shape[0]
    for step in range(HEADS):
        start = (me ^ step) * rows
        kv_all[rows_at(start, rows, 16), :] = pieces[step][:rows]
        first, later = unfold_rows(pieces[step][rows:].astype(F32))
        q_all[rows_at(start, rows // 2, 16), :] = first.astype(BF16)
        q_all[rows_at(start + rows // 2, rows // 2, 16), :] = later.astype(BF16)
    low = lower_half(BLOCK)
    for block in range(q_all.shape[0] // BLOCK):
        cut = slice(block * BLOCK, (block + 1) * BLOCK)
        seen = kv_all[: (block + 1) * BLOCK]
        scores = causal(dot_nt(q_all[cut], seen), block * BLOCK, 0)
        most = jnp.max(scores, axis=-1, keepdims=True)
        weights = jnp.exp(scores - most)
        total = jnp.sum(weights, axis=-1, keepdims=True)
        attended = dot_nn(weights.astype(BF16), seen) / total
        lse_o[cut] = jnp.where(low, most + jnp.log(total), attended)
    for step in range(HEADS):
        own = lse_o[rows_at((me ^ step) * rows, rows, 16), :]
        at = (step % 2) * (rows // 2)
        outs[step // 2][at : at + rows // 2] = jnp.where(
            lower_half(rows // 2), turn(own[: rows // 2]), own[rows // 2 :]
        ).astype(BF16)


def finish_kernel(place, x, gain, w_o, w_e, w_c, *refs):
    pieces = paired(refs[:HEADS])
    result_out, middle_out, att_out, normed_out, pooled_out, heads, chunks = refs[HEADS:]
    rows, width = x.shape
    me = place[0]
    for step in range(HEADS):
        heads[me ^ step] = pieces[step][...].astype(F32)
    low = lower_half(rows // 2)
    for chunk in range(width // LANES):
        cut = slice(chunk * LANES, (chunk + 1) * LANES)
        even, odd = heads[2 * chunk], heads[2 * chunk + 1]
        att_out[: rows // 2, cut] = jnp.where(low, even, turn(odd)).astype(BF16)
        att_out[rows // 2 :, cut] = jnp.where(low, turn(even), odd).astype(BF16)
    middle = x[...] + dot_nn(att_out[...], w_o[...])
    middle_out[...] = middle
    unit, _ = norm_parts(middle)
    normed = (unit * gain[...]).astype(BF16)
    normed_out[...] = normed
    hidden = gelu_value(dot_nn(normed, w_e[...])).astype(BF16)
    result = middle + dot_nn(hidden, w_c[...])
    result_out[...] = result
    short = rows // 3
    for chunk in range(width // LANES):
        cut = slice(chunk * LANES, (chunk + 1) * LANES)
        chunks[chunk, :8] = jnp.zeros((8, LANES), F32)
        chunks[chunk, 8:] = result[:, cut]
        total = sum(chunks[chunk, pl.ds(s, short, stride=3), :] for s in (6, 7, 8))
        pooled_out[:short, cut] = (total / 3.0).astype(BF16)
    tail = (result[rows - 1 :] + result[rows - 2 : rows - 1]) / 3.0
    extra = pooled_out.shape[0] - short
    pooled_out[short:] = jnp.broadcast_to(tail, (extra, width)).astype(BF16)


def short_forward_kernel(
    place, residual, gathered, table, gain_a, w_q, w_k, w_v, w_o, gain_f, w_e, w_c, *refs
):
    pieces, refs = refs[:HEADS], refs[HEADS:]
    output, pooled, normed_a, q_s, k_s, v_s, o_s, lse_s, att, grad_middle = refs[:10]
    share_pieces = refs[10:-9]
    extra, middle, normed_f, hidden, grad_pre, grad_normed, grad_low, wide, share = refs[-9:]
    me, seat = place[0], place[1]
    rows, width = residual.shape
    count = pooled.shape[0]
    short = rows // 3
    chunk_count = width // LANES
    ff = w_e.shape[1]
    ff_own = ff // HEADS

    for step in range(HEADS):
        other = me ^ step
        pooled[rows_at(other * short, short, 16), :] = pieces[step][:short].astype(F32)
        extra[pl.ds(other, 1), :] = pieces[step][short:].astype(F32)[:1]
    for part in range(1, HEADS):
        at = slice(part * short, part * short + 1)
        pooled[at] = pooled[at] + extra[part - 1 : part]

    unit, _ = norm_parts(pooled[...])
    normed_a[...] = (unit * gain_a[...]).astype(BF16)
    low = lower_half(count)
    q = dot_nn(normed_a[...], w_q[...])
    turns = table[...]
    for chunk in range(chunk_count):
        q_chunk = rope(q[:, chunk * LANES : (chunk + 1) * LANES], turns) * HEAD**-0.5
        q_s[2 * chunk] = jnp.where(low, q_chunk, 0.0).astype(BF16)
        q_s[2 * chunk + 1] = jnp.where(low, 0.0, q_chunk).astype(BF16)
    k = dot_nn(normed_a[...], w_k[...])
    for chunk in range(chunk_count):
        k_s[chunk] = rope(k[:, chunk * LANES : (chunk + 1) * LANES], turns).astype(BF16)
    v = dot_nn(normed_a[...], w_v[...])
    for chunk in range(chunk_count):
        v_s[chunk] = v[:, chunk * LANES : (chunk + 1) * LANES].astype(BF16)

    low_block = lower_half(BLOCK)

    def attend_chunk(chunk, carry):
        for block in range(count // BLOCK):
            cut = slice(block * BLOCK, (block + 1) * BLOCK)
            seen = slice(0, (block + 1) * BLOCK)
            results = []
            for half in range(2):
                scores = dot_nt(q_s[2 * chunk + half, cut, :], k_s[chunk, seen, :])
                scores = causal(scores, block * BLOCK, 0)
                most = jnp.max(scores, axis=-1, keepdims=True)
                weights = jnp.exp(scores - most)
                total = jnp.sum(weights, axis=-1, keepdims=True)
                attended = dot_nn(weights.astype(BF16), v_s[chunk, seen, :]) / total
                results.append((attended, most + jnp.log(total)))
            both = jnp.where(low_block, results[0][0], results[1][0])
            o_s[chunk, cut, :] = both
            lse_s[chunk, cut, :] = jnp.where(low_block, results[0][1], results[1][1])
            att[cut, rows_at(chunk * LANES, LANES, LANES)] = both.astype(BF16)
        return carry

    lax.fori_loop(0, chunk_count, attend_chunk, 0)
    middle[...] = pooled[...] + dot_nn(att[...], w_o[...])
    unit, scale = norm_parts(middle[...])
    normed_f[...] = (unit * gain_f[...]).astype(BF16)

    for part in range(HEADS):
        grad_low[part * short : (part + 1) * short] = gathered[part]

    ff_part = ff // 4
    grad_normed[...] = jnp.zeros(grad_normed.shape, F32)
    w_e, w_c = w_e.ready(), w_c.ready()

    def feed_forward(part, carry):
        cut = rows_at(part * ff_part, ff_part, ff_part)
        pre = dot_nn(normed_f[...], w_e[:, cut])
        value, slope = gelu_both(pre)
        hidden[:, cut] = value.astype(BF16)
        grad_hidden = dot_nt(grad_low[...], w_c[cut, :])
        low_grad = (grad_hidden * slope).astype(BF16)
        grad_pre[:, cut] = low_grad
        grad_normed[...] += dot_nt(low_grad, w_e[:, cut])
        return carry

    lax.fori_loop(0, 4, feed_forward, 0)

    own_ff = rows_at(me * ff_own, ff_own, ff_own)
    share[:ff_own] = dot_tn(hidden[:, own_ff], grad_low[...]).astype(BF16)
    expand = dot_tn(normed_f[...], grad_pre[:, own_ff]).astype(BF16)
    share[ff_own : 2 * ff_own, : width // 2] = expand[: width // 2]
    share[ff_own : 2 * ff_own, width // 2 :] = expand[width // 2 :]
    by_distance(share, share_pieces, seat)

    mine = rows_at(me * short, short, 16)
    short_out = middle[mine, :] + dot_nn(hidden[mine, :], w_c[...])
    for chunk in range(chunk_count):
        cut = slice(chunk * LANES, (chunk + 1) * LANES)
        for s in range(3):
            wide[chunk, pl.ds(s, short, stride=3), :] = short_out[:, cut]
        output[:, cut] = residual[:, cut] + wide[chunk]

    unit, scale = norm_parts(middle[...])
    grad_middle[...] = grad_low[...].astype(F32) + norm_back(
        grad_normed[...], gain_f[...], unit, scale
    )


def short_back_kernel(
    place,
    cot,
    gathered,
    table,
    gain_a,
    w_q,
    w_k,
    w_v,
    w_o,
    pooled,
    normed_a,
    q_s,
    k_s,
    v_s,
    o_s,
    lse_s,
    att,
    grad_middle,
    grad_own,
    grad_all,
    share,
    do_s,
    dq_s,
    dk_s,
    dv_s,
    wide,
    wo_s,
):
    me = place[0]
    rows, width = cot.shape
    count = pooled.shape[0]
    full = rows * HEADS
    chunk_count = width // LANES
    low = lower_half(count)
    low_block = lower_half(BLOCK)
    g1 = grad_middle[...].astype(BF16)
    d_att = dot_nt(g1, w_o[...])
    for chunk in range(chunk_count):
        do_chunk = d_att[:, chunk * LANES : (chunk + 1) * LANES]
        do_s[2 * chunk] = jnp.where(low, do_chunk, 0.0).astype(BF16)
        do_s[2 * chunk + 1] = jnp.where(low, 0.0, do_chunk).astype(BF16)
    own_chunk = rows_at((me // 2) * LANES, LANES, LANES)
    wo_s[...] = dot_tn(att[:, own_chunk], g1)
    table = table.ready()

    def attend_back(chunk, carry):
        dk = [None] * (count // BLOCK)
        dv = [None] * (count // BLOCK)
        columns = rows_at(chunk * LANES, LANES, LANES)
        for block in range(count // BLOCK):
            cut = slice(block * BLOCK, (block + 1) * BLOCK)
            dq = []
            for half in range(2):
                head = 2 * chunk + half
                q_block, do_block = q_s[head, cut, :], do_s[head, cut, :]
                lse = lse_s[chunk, cut, :][:, half * HEAD : half * HEAD + 1]
                delta = jnp.sum(
                    do_block.astype(F32) * o_s[chunk, cut, :], axis=-1, keepdims=True
                )
                dq_half = None
                for key in range(block + 1):
                    key_cut = slice(key * BLOCK, (key + 1) * BLOCK)
                    k_block, v_block = k_s[chunk, key_cut, :], v_s[chunk, key_cut, :]
                    scores = dot_nt(q_block, k_block)
                    if key == block:
                        scores = causal(scores, 0, 0)
                    probs = jnp.exp(scores - lse)
                    grad_probs = dot_nt(do_block, v_block)
                    ds = (probs * (grad_probs - delta)).astype(BF16)
                    term = dot_nn(ds, k_block)
                    dq_half = term if dq_half is None else dq_half + term
                    term = dot_tn(ds, q_block)
                    dk[key] = term if dk[key] is None else dk[key] + term
                    term = dot_tn(probs.astype(BF16), do_block)
                    dv[key] = term if dv[key] is None else dv[key] + term
                dq.append(dq_half)
            both = jnp.where(low_block, dq[0], dq[1]) * HEAD**-0.5
            dq_s[cut, columns] = rope_back(both, table[cut, :]).astype(BF16)
        for key in range(count // BLOCK):
            key_cut = slice(key * BLOCK, (key + 1) * BLOCK)
            dk_s[key_cut, columns] = rope_back(dk[key], table[key_cut, :]).astype(BF16)
            dv_s[key_cut, columns] = dv[key].astype(BF16)
        return carry

    lax.fori_loop(0, chunk_count, attend_back, 0)

    odd = me % 2 == 1
    low_width = lower_half(width)
    share_q = dot_tn(normed_a[...], dq_s[:, own_chunk])
    share_k = dot_tn(normed_a[...], dk_s[:, own_chunk])
    share_v = dot_tn(normed_a[...], dv_s[:, own_chunk])
    share_q = jnp.where(odd, turn(share_q), share_q)
    share_k = jnp.where(odd, share_k, turn(share_k))
    share_v = jnp.where(odd, turn(share_v), share_v)
    head_rows = wo_s[rows_at((me % 2) * HEAD, HEAD, HEAD), :]
    pack_attention(share, jnp.where(low_width, share_q, share_k), fold_rows(share_v), head_rows)

    grad_a = dot_nt(dq_s[...], w_q[...])
    grad_a += dot_nt(dk_s[...], w_k[...])
    grad_a += dot_nt(dv_s[...], w_v[...])
    unit, scale = norm_parts(pooled[...])
    grad_pooled = grad_middle[...] + norm_back(grad_a, gain_a[...], unit, scale)
    for chunk in range(chunk_count):
        cut = slice(chunk * LANES, (chunk + 1) * LANES)
        third = grad_pooled[:, cut] / 3.0
        for s in range(3):
            wide[chunk, pl.ds(6 + s, count, stride=3), :] = third
        wide[chunk, full + 6 : full + 8] = jnp.zeros((2, LANES), F32)
        grad_own[:, cut] = cot[:, cut] + wide[chunk, rows_at(me * rows + 8, rows, 8), :]
        for part in range(HEADS):
            more = wide[chunk, 8 + part * rows : 8 + (part + 1) * rows, :]
            grad_all[part * rows : (part + 1) * rows, cut] = (
                gathered[part, :, cut].astype(F32) + more
            ).astype(BF16)


def pack_attention(share, both_qk, folded_v, head_rows):
    half = both_qk.shape[0] // 2
    share[:half, :LANES] = both_qk[:half].astype(BF16)
    share[:half, LANES : 2 * LANES] = both_qk[half:].astype(BF16)
    share[:half, 2 * LANES : 3 * LANES] = folded_v.astype(BF16)
    size = head_rows.shape[0]
    for chunk in range(head_rows.shape[1] // LANES):
        share[chunk * size : (chunk + 1) * size, 3 * LANES :] = head_rows[
            :, chunk * LANES : (chunk + 1) * LANES
        ].astype(BF16)


def finish_back_kernel(place, grad, middle, normed, gain, w_e, w_c, grad_middle_out, g1_out):
    _, slope = gelu_both(dot_nn(normed[...], w_e[...]))
    grad_hidden = dot_nt(grad[...].astype(BF16), w_c[...])
    grad_pre = (grad_hidden * slope).astype(BF16)
    grad_normed = dot_nt(grad_pre, w_e[...])
    unit, scale = norm_parts(middle[...])
    grad_middle = grad[...] + norm_back(grad_normed, gain[...], unit, scale)
    grad_middle_out[...] = grad_middle
    g1_out[...] = grad_middle.astype(BF16)


def feed_forward_share_kernel(parts, place, normed, grad, w_e, w_c, more, keep, send, share):
    seat = place[1]
    width, ff_own = w_e.shape
    value, slope = gelu_both(dot_nn(normed[...], w_e[...]))
    grad_hidden = dot_nt(grad[...], w_c[...])
    grad_pre = (grad_hidden * slope).astype(BF16)
    share[:ff_own] = dot_tn(value.astype(BF16), grad[...]).astype(BF16)
    expand = dot_tn(normed[...], grad_pre).astype(BF16)
    share[ff_own:, : width // 2] = expand[: width // 2]
    share[ff_own:, width // 2 :] = expand[width // 2 :]
    keep_and_send(share, keep, send, seat, parts)
    keep_and_send(more, keep, send, seat, parts, share.shape[0] // parts)


def attend_back_kernel(place, q_all, kv_all, lse_o, table, w_o, *refs):
    pieces, outs = refs[:HEADS], refs[HEADS : 2 * HEADS]
    dq_all, dkv_all, do_all, dkv_sum = refs[2 * HEADS :]
    me = place[0]
    rows = q_all.shape[0] // HEADS
    own_w = w_o[...]
    own_w = jnp.concatenate([jnp.zeros(own_w.shape, BF16), own_w])
    for step in range(HEADS):
        do_all[rows_at((me ^ step) * rows, rows, 16), :] = dot_nt(
            pieces[step][...], own_w
        ).astype(BF16)
    dkv_sum[...] = jnp.zeros(dkv_sum.shape, F32)
    for block in range(q_all.shape[0] // BLOCK):
        cut = slice(block * BLOCK, (block + 1) * BLOCK)
        q_block, do_block = q_all[cut], do_all[cut]
        lse = lse_o[cut][:, :1]
        delta = jnp.sum(do_block.astype(F32) * lse_o[cut], axis=-1, keepdims=True)
        dq = None
        for key in range(block + 1):
            key_cut = slice(key * BLOCK, (key + 1) * BLOCK)
            kv_block = kv_all[key_cut]
            scores = dot_nt(q_block, kv_block)
            if key == block:
                scores = causal(scores, 0, 0)
            probs = jnp.exp(scores - lse)
            grad_probs = dot_nt(do_block, kv_block)
            ds = (probs * (grad_probs - delta)).astype(BF16)
            term = dot_nn(ds, kv_block)
            dq = term if dq is None else dq + term
            dkv_sum[key_cut] += dot_tn(ds, q_block) + dot_tn(probs.astype(BF16), do_block)
        dq_all[cut] = rope_back(dq * HEAD**-0.5, table[cut, :]).astype(BF16)
    low = lower_half(BLOCK)
    for block in range(q_all.shape[0] // BLOCK):
        cut = slice(block * BLOCK, (block + 1) * BLOCK)
        dkv = dkv_sum[cut]
        dkv_all[cut] = jnp.where(low, rope_back(dkv, table[cut, :]), dkv).astype(BF16)
    for step in range(HEADS):
        own = rows_at((me ^ step) * rows, rows, 16)
        outs[step][:rows] = dkv_all[own, :]
        outs[step][rows:] = fold_rows(dq_all[own, :].astype(F32)).astype(BF16)


def attention_share_kernel(
    place, gathered, dq_all, dkv_all, lse_o, *refs
):
    pieces, share_pieces, share = refs[:HEADS], refs[HEADS:-1], refs[-1]
    me, seat = place[0], place[1]
    _, rows, width = gathered.shape
    grad_q = jnp.zeros((width, LANES), F32)
    grad_kv = jnp.zeros((width, LANES), F32)
    for part in range(HEADS):
        normed = gathered[part]
        grad_q += dot_tn(normed, dq_all[part * rows : (part + 1) * rows])
        grad_kv += dot_tn(normed, dkv_all[part * rows : (part + 1) * rows])
    grad_o = jnp.zeros((LANES, width), F32)
    for step in range(HEADS):
        own = lse_o[rows_at((me ^ step) * rows, rows, 16), :].astype(BF16)
        grad_o += dot_tn(own, pieces[step][...])
    grad_o = grad_o[HEAD:]
    half = width // 2
    folded_v = jnp.where(lower_half(half), turn(grad_kv[:half]), grad_kv[half:])
    pack_attention(
        share, jnp.where(lower_half(width), grad_q, turn(grad_kv)), folded_v, grad_o
    )
    by_distance(share, share_pieces, seat)


def start_back_kernel(place, x, grad_middle, gain, w_q, w_k, w_v, *refs):
    pieces = refs[:HEADS]
    grad_in, heads, dq, dk, dv = refs[HEADS:]
    me = place[0]
    rows, width = x.shape
    half = rows // 2
    for step in range(HEADS):
        heads[me ^ step] = pieces[step][...]
    low, low_half = lower_half(rows), lower_half(half)
    for chunk in range(width // LANES):
        cut = slice(chunk * LANES, (chunk + 1) * LANES)
        even, odd = heads[2 * chunk].astype(F32), heads[2 * chunk + 1].astype(F32)
        dk[:, cut] = jnp.where(low, even[:rows], turn(odd[:rows])).astype(BF16)
        dv[:, cut] = jnp.where(low, turn(even[:rows]), odd[:rows]).astype(BF16)
        dq[:half, cut] = jnp.where(low_half, even[rows:], turn(odd[rows:])).astype(BF16)
        dq[half:, cut] = jnp.where(low_half, turn(even[rows:]), odd[rows:]).astype(BF16)
    grad_a = dot_nt(dq[...], w_q[...]) + dot_nt(dk[...], w_k[...]) + dot_nt(dv[...], w_v[...])
    unit, scale = norm_parts(x[...])
    grad_in[...] = grad_middle[...] + norm_back(grad_a, gain[...], unit, scale)


def column_to_row(column):
    return jnp.transpose(jnp.broadcast_to(column, (column.shape[0], LANES)))[:1]


def fold_lanes(values):
    return sum(
        values[:, at : at + LANES] for at in range(0, values.shape[1], LANES)
    )


def part_order(batch):
    order, bit = [0], batch // 2
    while bit >= 1:
        order = order + [step ^ bit for step in order]
        bit //= 2
    return order


def grads_kernel(parts, attention, feed_forward, source_count, place, *refs):
    refs = list(refs)
    sources = [refs.pop(0) for _ in range(source_count)]
    weights = [refs.pop(0) for _ in range(4 * attention + 2 * feed_forward)]
    outs = [refs.pop(0) for _ in range(5 * attention + 3 * feed_forward)]
    me, seat = place[0], place[1]
    batch = parts
    order = part_order(batch)
    copies = []

    def send(source, target, semaphore):
        copy = pltpu.make_async_copy(source, target, semaphore)
        copy.start()
        copies.append(copy)

    def rows_of(step):
        if source_count == 1:
            return sources[0].ready().at[step], step
        return sources[step], me ^ step

    if attention:
        w_q, w_k, w_v, gain_a = weights[:4]
        grad_q, grad_k, grad_v, grad_o, grad_gain_a = outs[:5]
        heads, square, over, acc_a, sems_a = refs[-5:]
        width = grad_q.shape[0]
        half, at_rows = width // 2, width // 2 // batch
        for step in range(HEADS):
            source, owner = rows_of(step)
            part_rows = source.shape[0] // batch
            for at, peer in enumerate(order):
                end = (at + 1) * part_rows
                heads[owner, rows_at((seat ^ peer) * at_rows, at_rows, 16), :] = source[
                    end - at_rows : end
                ]
        low = lower_half(half)
        total = None
        for chunk in range(HEADS // 2):
            cut = slice(chunk * LANES, (chunk + 1) * LANES)
            for part in range(2):
                rows = slice(part * half, (part + 1) * half)
                lanes = slice(part * LANES, (part + 1) * LANES)
                even = heads[2 * chunk, :, lanes].astype(F32)
                odd = heads[2 * chunk + 1, :, lanes].astype(F32)
                square[0, chunk, rows] = jnp.where(low, even, turn(odd))
                square[1, chunk, rows] = jnp.where(low, turn(even), odd)
            even = heads[2 * chunk, :, 2 * LANES : 3 * LANES].astype(F32)
            odd = heads[2 * chunk + 1, :, 2 * LANES : 3 * LANES].astype(F32)
            square[2, chunk, :half] = jnp.where(low, even, turn(odd))
            square[2, chunk, half:] = jnp.where(low, turn(even), odd)
            for side in range(2):
                for lane in range(width // LANES):
                    over[
                        2 * chunk + side, :, lane * LANES : (lane + 1) * LANES
                    ] = heads[
                        2 * chunk + side, lane * HEAD : (lane + 1) * HEAD, 3 * LANES :
                    ].astype(F32)
                head = 2 * chunk + side
                send(over.at[head], grad_o.at[pl.ds(head * HEAD, HEAD), :], sems_a.at[3 + side, chunk])
            for at, target in enumerate((grad_q, grad_k, grad_v)):
                send(square.at[at, chunk], target.at[:, pl.ds(chunk * LANES, LANES)], sems_a.at[at, chunk])
            term = (
                w_q[:, cut].astype(F32) * square[0, chunk]
                + w_k[:, cut].astype(F32) * square[1, chunk]
                + w_v[:, cut].astype(F32) * square[2, chunk]
            )
            total = term if total is None else total + term
        total = jnp.sum(total, axis=-1, keepdims=True)
        grad_gain_a[...] = column_to_row(total) / gain_a[...]

    if feed_forward:
        w_e, gain_f = weights[-2:]
        contract, expand, grad_gain_f = outs[-3:]
        share, acc, sems = refs[:3]
        width = expand.shape[0]
        half = width // 2
        ff_own = contract.shape[0] // HEADS
        ff_rows = 2 * ff_own // batch
        acc[...] = jnp.zeros(acc.shape, F32)
        for step in range(HEADS):
            source, owner = rows_of(step)
            part_rows = source.shape[0] // batch
            for at, peer in enumerate(order):
                share[step, rows_at((seat ^ peer) * ff_rows, ff_rows, 16), :] = source[
                    at * part_rows : at * part_rows + ff_rows
                ].astype(F32)
            own = pl.ds(pl.multiple_of(owner * ff_own, ff_own), ff_own)
            send(share.at[step, pl.ds(0, ff_own), :], contract.at[own, :], sems.at[step, 0])
            for side in range(2):
                lanes = pl.ds(side * half, half)
                send(
                    share.at[step, pl.ds(ff_own, ff_own), lanes],
                    expand.at[pl.ds(side * half, half), own],
                    sems.at[step, 1 + side],
                )
                acc[side * half : (side + 1) * half] += fold_lanes(
                    w_e[side * half : (side + 1) * half, own].astype(F32)
                    * share[step, ff_own:, side * half : (side + 1) * half]
                )
        total = jnp.sum(acc[...], axis=-1, keepdims=True)
        grad_gain_f[...] = column_to_row(total) / gain_f[...]
    for copy in copies:
        copy.wait()


COST = 1.15e9


def call(kernel, out_shape, scratch, arguments, late=(), limit=16, in_hbm=(), near=(), loaded=False, us=5):
    late = [entry if isinstance(entry, tuple) else (entry, None, None) for entry in late]
    specs = [pl.BlockSpec(memory_space=pltpu.SMEM)]
    specs += [pl.BlockSpec(memory_space=pltpu.VMEM)] * (len(arguments) - 1)
    buffers, arguments = [], list(arguments)
    for at, shape, _ in late:
        specs[at] = pl.BlockSpec(memory_space=pltpu.HBM)
        buffers.append(pltpu.VMEM(shape or arguments[at].shape, arguments[at].dtype))
        arguments[at] = pltpu.with_memory_space_constraint(arguments[at], pltpu.HBM)
    for at in near:
        arguments[at] = pltpu.with_memory_space_constraint(arguments[at], pltpu.VMEM)
    semaphores = [pltpu.SemaphoreType.DMA((len(late),))] if late else []
    body = kernel
    if late:
        body = partial(with_late, kernel, late, len(arguments), len(out_shape))
    return pl.pallas_call(
        body,
        out_shape=[
            (pltpu.HBM if at in in_hbm else pltpu.VMEM if loaded else jax.ShapeDtypeStruct)(*entry)
            for at, entry in enumerate(out_shape)
        ],
        in_specs=specs,
        out_specs=[
            pl.BlockSpec(memory_space=pltpu.HBM if at in in_hbm else pltpu.VMEM)
            for at in range(len(out_shape))
        ],
        scratch_shapes=[
            pltpu.VMEM(*entry) if isinstance(entry, tuple) else entry for entry in scratch
        ]
        + buffers
        + semaphores,
        compiler_params=pltpu.CompilerParams(vmem_limit_bytes=limit * 2**20),
        cost_estimate=pl.CostEstimate(
            flops=int(us * COST), bytes_accessed=2**20, transcendentals=0
        ),
    )(*arguments)


def exchange(pieces, axis):
    devices = range(lax.axis_size(axis))
    moved = {
        step: lax.ppermute(pieces[step], axis, [(i, i ^ step) for i in devices])
        for step in reversed(range(1, len(pieces)))
    }
    return [pieces[0]] + [moved[step] for step in range(1, len(pieces))]


def after(values, *others):
    return lax.optimization_barrier((values, others))[0]


def phase(*values):
    return lax.optimization_barrier(values)


def swap(block, axis, step):
    return lax.ppermute(block, axis, [(i, i ^ step) for i in range(lax.axis_size(axis))])


def near_exchange(pairs):
    moved = {step: swap(pairs[step], "seq", 2 * step) for step in reversed(range(1, len(pairs)))}
    first = [pairs[0]] + [moved[step] for step in range(1, len(pairs))]
    return first + [swap(pair, "seq", 1) for pair in first]


def summed(pieces):
    return sum(piece.astype(F32) for piece in pieces).astype(BF16)


def sum_step(keep, arrived, bit):
    total = keep.astype(F32) + arrived.astype(F32)
    parts = lax.axis_size("batch") // (2 * bit)
    if parts <= 1:
        return total.astype(BF16), None
    total = total.reshape(parts // 2, 2, -1, total.shape[1])
    return (
        total[:, 0].reshape(-1, total.shape[-1]),
        total[:, 1].reshape(-1, total.shape[-1]).astype(BF16),
    )


def near_gather(block, *beside):
    found = {0: block}
    for step in (6, 4, 2):
        found[step] = swap(block, "seq", step)
    for step in (0, 2, 4, 6):
        found[step] = after(found[step], *beside) if beside else found[step]
        found[step + 1] = swap(found[step], "seq", 1)
    return [found[step] for step in range(HEADS)]


def gather(block):
    return lax.all_gather(block, "seq", axis=0, tiled=True)


def whole_grads(place, sources, params, batch, attention, feed_forward):
    brief, full = params
    width, ff = full[6].shape
    ff_own = ff // HEADS
    square, row = ((width, width), F32), ((1, width), F32)
    arguments, out_shape, scratch = [place, *sources], [], []
    late = [1] if len(sources) == 1 else []
    in_hbm = []
    if attention:
        first = len(arguments)
        arguments += [brief[1], brief[2], brief[3], brief[0]]
        late += [first, first + 1, first + 2]
        in_hbm += [0, 1, 2, 3]
        out_shape += [square] * 4 + [row]
    if feed_forward:
        late += [len(arguments)]
        arguments += [full[6], full[5]]
        in_hbm += [len(out_shape), len(out_shape) + 1]
        out_shape += [((ff, width), F32), ((width, ff), F32), row]
        scratch += [
            ((HEADS, 2 * ff_own, width), F32),
            ((width, LANES), F32),
            pltpu.SemaphoreType.DMA((HEADS, 3)),
        ]
    if attention:
        scratch += [
            ((HEADS, width // 2, width), BF16),
            ((3, HEADS // 2, width, LANES), F32),
            ((HEADS, HEAD, width), F32),
            ((width, LANES), F32),
            pltpu.SemaphoreType.DMA((5, HEADS // 2)),
        ]
    return call(
        partial(grads_kernel, batch, attention, feed_forward, len(sources)),
        out_shape,
        scratch,
        tuple(arguments),
        late,
        32,
        in_hbm,
    )


def by_heads(inputs, cotangent, *weights):
    full = (weights[0][None],) + weights[1:5] + (weights[5][None],) + weights[6:8]
    brief = (weights[8][None],) + weights[9:13] + (weights[13][None],) + weights[14:16]
    x, cot = inputs[0], cotangent[0]
    rows, width = x.shape
    short, half, total = rows // 3, rows // 2, rows * HEADS
    batch = lax.axis_size("batch")
    ff = full[6].shape[1]
    ff_own = ff // HEADS
    count = short * HEADS
    chunks = width // LANES
    place = jnp.stack([lax.axis_index("seq"), lax.axis_index("batch")]).astype(jnp.int32)
    table = rope_constants(total)
    block = rows + half

    outs = call(
        project_kernel,
        [((block, LANES), BF16)] * HEADS + [((2 * rows + short, width), BF16)],
        [((HEADS, block, LANES), BF16), ((chunks, rows, LANES), F32)],
        (place, x, cot, full[0], full[1], full[2], full[3], table),
        (
            1,
            4,
            5,
            6,
            (7, (rows, 2 * LANES), lambda ref, me: ref.at[rows_at(me * rows, rows, 16), :]),
            2,
        ),
    )
    pieces, bundle = exchange(outs[:HEADS], "seq"), outs[HEADS]
    bundles = gather(bundle).reshape(HEADS, 2 * rows + short, width)

    outs = call(
        attend_kernel,
        [((rows, LANES), BF16)] * (HEADS // 2)
        + [((total, LANES), BF16), ((total, LANES), BF16), ((total, LANES), F32)],
        [],
        (place, *pieces),
    )
    pieces = near_exchange(outs[: HEADS // 2])
    q_all, kv_all, lse_o = outs[HEADS // 2 :]

    residual, middle, att, normed_f, pooled = call(
        finish_kernel,
        [
            ((rows, width), F32),
            ((rows, width), F32),
            ((rows, width), BF16),
            ((rows, width), BF16),
            ((short + 16, width), BF16),
        ],
        [((HEADS, half, LANES), F32), ((chunks, rows + 8, LANES), F32)],
        (place, x, full[5], full[4], full[6], full[7], *pieces),
        (3, 1, 4, 5),
    )
    pieces = near_gather(pooled)
    normed_all = gather(normed_f)

    outs = call(
        short_forward_kernel,
        [
            ((rows, width), F32),
            ((count, width), F32),
            ((count, width), BF16),
            ((HEADS, count, LANES), BF16),
            ((chunks, count, LANES), BF16),
            ((chunks, count, LANES), BF16),
            ((chunks, count, LANES), F32),
            ((chunks, count, LANES), F32),
            ((count, width), BF16),
            ((count, width), F32),
        ]
        + [((2 * ff_own // batch, width), BF16)] * batch,
        [
            ((HEADS, width), F32),
            ((count, width), F32),
            ((count, width), BF16),
            ((count, ff), BF16),
            ((count, ff), BF16),
            ((count, width), F32),
            ((count, width), BF16),
            ((chunks, rows, LANES), F32),
            ((2 * ff_own, width), BF16),
        ],
        (place, residual, bundles, table[:count]) + brief + tuple(pieces),
        (
            5,
            3,
            6,
            7,
            8,
            10,
            11,
            (2, (HEADS, short, width), lambda ref, me: ref.at[:, pl.ds(2 * rows, short), :]),
            1,
        ),
        28,
    )
    output, saved = outs[0], outs[1:10]
    a_at, saved = phase(outs[10:], saved)

    a_at = exchange(a_at, "batch")
    outs = call(
        short_back_kernel,
        [((rows, width), F32), ((total, width), BF16), ((width // 2, width), BF16)],
        [
            ((HEADS, count, LANES), BF16),
            ((count, width), BF16),
            ((count, width), BF16),
            ((count, width), BF16),
            ((chunks, total + 16, LANES), F32),
            ((LANES, width), F32),
        ],
        (place, cot, bundles, table[:count]) + brief[:5] + tuple(saved),
        (
            8,
            3,
            5,
            6,
            7,
            (2, (HEADS, rows, width), lambda ref, me: ref.at[:, pl.ds(rows, rows), :]),
            1,
        ),
        22,
        us=14,
    )
    a_at, (grad_own, grad_all, short_share) = phase(a_at, outs)

    a_all = summed(a_at)
    a_all, grad_all, short_share = phase(a_all, grad_all, short_share)
    a_at = swap(a_all, "batch", 2)
    outs = call(
        partial(feed_forward_share_kernel, batch),
        [((ff_own + width // 4, width), BF16)] * 2,
        [((2 * ff_own, width), BF16)],
        (place, normed_all, grad_all, full[6], full[7], short_share),
        (
            1,
            (3, (width, ff_own), lambda ref, me: ref.at[:, rows_at(me * ff_own, ff_own, ff_own)]),
            2,
            (4, (ff_own, width), lambda ref, me: ref.at[rows_at(me * ff_own, ff_own, ff_own), :]),
        ),
        22,
    )
    a_at, (b_keep, b_send), grad_own = phase(a_at, outs, grad_own)

    a_all = jnp.concatenate([a_all, a_at])
    a_all, b_send, grad_own = phase(a_all, b_send, grad_own)
    a_at = swap(a_all, "batch", 1)
    b_at = swap(b_send, "batch", 1)
    outs = call(
        finish_back_kernel,
        [((rows, width), F32), ((rows, width), BF16)],
        [],
        (place, grad_own, middle, normed_f, full[5], full[6], full[7]),
        (5, 6),
        us=6,
    )
    a_at, b_at, (grad_middle, g1) = phase(a_at, b_at, outs)

    a_all = jnp.concatenate([a_all, a_at])
    b_keep, b_send = sum_step(b_keep, b_at, 1)
    a_all, b_send, g1 = phase(a_all, b_send, g1)
    a_shares = gather(a_all[None])
    b_at = swap(b_send, "batch", 2)
    g1_all = near_gather(g1)
    b_at, g1_all = phase(b_at, g1_all)

    b_all, _ = sum_step(b_keep, b_at, 2)
    b_all, g1_all = phase(b_all, g1_all)
    b_at = swap(b_all, "batch", 2)
    outs = call(
        attend_back_kernel,
        [((block, LANES), BF16)] * HEADS + [((total, LANES), BF16), ((total, LANES), BF16)],
        [((total, LANES), BF16), ((total, LANES), F32)],
        (place, q_all, kv_all, lse_o, table, full[4], *g1_all),
        (
            (5, (HEAD, width), lambda ref, me: ref.at[rows_at(me * HEAD, HEAD, HEAD), :]),
            4,
        ),
        us=9,
    )
    b_at, outs = phase(b_at, outs)
    dq_all, dkv_all = outs[HEADS:]

    b_all = jnp.concatenate([b_all, b_at])
    b_all, pieces, dq_all = phase(b_all, outs[:HEADS], dq_all)
    b_at = swap(b_all, "batch", 1)
    pieces = exchange(pieces, "seq")
    outs = call(
        attention_share_kernel,
        [((width // 2 // batch, width), BF16)] * batch,
        [((width // 2, width), BF16)],
        (place, bundles, dq_all, dkv_all, lse_o, *g1_all),
        ((1, (HEADS, rows, width), lambda ref, me: ref.at[:, pl.ds(0, rows), :]),),
        us=3,
    )
    b_at, pieces, c_at = phase(b_at, pieces, outs)

    b_all = jnp.concatenate([b_all, b_at])
    b_all, pieces, c_at = phase(b_all, pieces, c_at)
    b_shares = gather(b_all[None])
    c_at = exchange(c_at, "batch")
    (grad_in,) = call(
        start_back_kernel,
        [((rows, width), F32)],
        [((HEADS, block, LANES), BF16)] + [((rows, width), BF16)] * 3,
        (place, x, grad_middle, full[0], full[1], full[2], full[3], *pieces),
        (1, 4, 5, 6),
        us=4,
    )
    c_at, grad_in = phase(c_at, grad_in)
    c_all = summed(c_at)
    c_at = swap(c_all, "batch", 2)
    c_all = jnp.concatenate([c_all, c_at])
    c_at = swap(c_all, "batch", 1)
    c_all = jnp.concatenate([c_all, c_at])
    short_ff_grads = whole_grads(
        place, [after(a_shares, grad_in)], (brief, brief), batch, False, True
    )
    c_shares = near_gather(c_all, short_ff_grads[0])
    full_at_grads = whole_grads(place, c_shares, (full, full), batch, True, False)
    both_grads = whole_grads(
        place, [after(b_shares, full_at_grads[0])], (brief, full), batch, True, True
    )
    short_at_grads, full_ff_grads = both_grads[:5], both_grads[5:]

    def arranged(attention, feed_forward):
        grad_q, grad_k, grad_v, grad_o, grad_gain_a = attention
        contract, expand, grad_gain_f = feed_forward
        return (grad_gain_a[0], grad_q, grad_k, grad_v, grad_o, grad_gain_f[0], expand, contract)

    return (
        (output[None], grad_in[None])
        + arranged(full_at_grads, full_ff_grads)
        + arranged(short_at_grads, short_ff_grads)
    )


def from_behind(block, axis, distance):
    devices = range(lax.axis_size(axis))
    route = [(i - distance, i) for i in devices if i - distance in devices]
    return lax.ppermute(block, axis, route)


def normalize(stream, gain):
    row_mean = jnp.mean(stream, axis=-1, keepdims=True)
    centered = stream - row_mean
    spread = jnp.mean(centered * centered, axis=-1, keepdims=True)
    return centered * lax.rsqrt(spread + norm_eps) * gain


def rope_table(positions):
    half_size = HEAD // 2
    frequency = jnp.power(10000.0, -jnp.arange(half_size, dtype=jnp.float32) * 2.0 / HEAD)
    angles = positions.astype(jnp.float32)[:, None] * frequency[None, :]
    return (jnp.cos(angles)[:, None, :], jnp.sin(angles)[:, None, :])


def rotate(values, angle_cos, angle_sin):
    first_half, second_half = jnp.split(values, 2, axis=-1)
    return jnp.concatenate(
        [
            first_half * angle_cos - second_half * angle_sin,
            first_half * angle_sin + second_half * angle_cos,
        ],
        axis=-1,
    )


def rotate_back(grads, angle_cos, angle_sin):
    first_half, second_half = jnp.split(grads, 2, axis=-1)
    return jnp.concatenate(
        [
            first_half * angle_cos + second_half * angle_sin,
            second_half * angle_cos - first_half * angle_sin,
        ],
        axis=-1,
    )


def split_heads(matrix):
    return matrix.reshape(matrix.shape[0], HEADS, HEAD)


def project(stream, params, angle_cos, angle_sin):
    normed_in = normalize(stream, params[0]).astype(jnp.bfloat16)

    def heads_of(matrix):
        return split_heads(jnp.dot(normed_in, matrix, preferred_element_type=jnp.float32))

    queries = rotate(heads_of(params[1]), angle_cos, angle_sin).astype(jnp.bfloat16)
    keys_here = rotate(heads_of(params[2]), angle_cos, angle_sin).astype(jnp.bfloat16)
    values_here = heads_of(params[3]).astype(jnp.bfloat16)
    return (normed_in, queries, keys_here, values_here)


def masked_scores(queries, keys_all, query_places, key_places):
    scores = jnp.einsum(
        "nhe,mhe->hnm", queries, keys_all, preferred_element_type=jnp.float32
    ) * HEAD ** (-0.5)
    allowed = key_places[None, None, :] <= query_places[None, :, None]
    return jnp.where(allowed, scores, -1e30)


def attend(queries, keys_all, values_all, query_places, key_places):
    scores = masked_scores(queries, keys_all, query_places, key_places)
    highest_score = jnp.max(scores, axis=-1, keepdims=True)
    log_total = highest_score + jnp.log(
        jnp.sum(jnp.exp(scores - highest_score), axis=-1, keepdims=True)
    )
    prob_low = jnp.exp(scores - log_total).astype(jnp.bfloat16)
    attended = jnp.einsum("hnm,mhe->nhe", prob_low, values_all, preferred_element_type=jnp.float32)
    return (attended, log_total)


def attend_back(queries, keys_all, values_all, query_places, key_places, log_total, grad_attended):
    scores = masked_scores(queries, keys_all, query_places, key_places)
    probs_full = jnp.exp(scores - log_total)
    grad_probs = jnp.einsum(
        "nhe,mhe->hnm", grad_attended, values_all, preferred_element_type=jnp.float32
    )
    row_inner = jnp.sum(probs_full * grad_probs, axis=-1, keepdims=True)
    grad_scores = (probs_full * (grad_probs - row_inner)).astype(jnp.bfloat16)
    grad_queries = jnp.einsum(
        "hnm,mhe->nhe", grad_scores, keys_all, preferred_element_type=jnp.float32
    ) * HEAD ** (-0.5)
    return (grad_queries, grad_scores, probs_full.astype(jnp.bfloat16), row_inner)


def finish(stream, attended, params):
    row_count, width = stream.shape
    attended_low = attended.reshape(row_count, width).astype(jnp.bfloat16)
    middle = stream + jnp.dot(attended_low, params[4], preferred_element_type=jnp.float32)
    normed_mid = normalize(middle, params[5]).astype(jnp.bfloat16)
    hidden_pre = jnp.dot(normed_mid, params[6], preferred_element_type=jnp.float32)
    hidden_low = jax.nn.gelu(hidden_pre, approximate=True).astype(jnp.bfloat16)
    result = middle + jnp.dot(hidden_low, params[7], preferred_element_type=jnp.float32)
    return (result, (attended_low, middle, normed_mid, hidden_pre, hidden_low))


def finish_back(grad_result, finish_saved, params):
    attended_low, middle, normed_mid, hidden_pre, hidden_low = finish_saved
    grad_low = grad_result.astype(jnp.bfloat16)
    grad_contract = jnp.einsum(
        "nf,nd->fd", hidden_low, grad_low, preferred_element_type=jnp.float32
    )
    grad_hidden = jnp.einsum("nd,fd->nf", grad_low, params[7], preferred_element_type=jnp.float32)
    gelu_value, gelu_pull = jax.vjp(partial(jax.nn.gelu, approximate=True), hidden_pre)
    grad_pre = gelu_pull(grad_hidden)[0].astype(jnp.bfloat16)
    grad_expand = jnp.einsum("nd,nf->df", normed_mid, grad_pre, preferred_element_type=jnp.float32)
    grad_normed = jnp.einsum("nf,df->nd", grad_pre, params[6], preferred_element_type=jnp.float32)
    norm_value, norm_pull = jax.vjp(normalize, middle, params[5])
    grad_norm_in, grad_gain_ffn = norm_pull(grad_normed)
    grad_middle = grad_result + grad_norm_in
    middle_low = grad_middle.astype(jnp.bfloat16)
    grad_output_w = jnp.einsum(
        "nc,nd->cd", attended_low, middle_low, preferred_element_type=jnp.float32
    )
    grad_attended = split_heads(
        jnp.einsum("nd,cd->nc", middle_low, params[4], preferred_element_type=jnp.float32).astype(
            jnp.bfloat16
        )
    )
    return (grad_middle, grad_attended, grad_output_w, grad_expand, grad_contract, grad_gain_ffn)


def start_back(
    grad_queries, grad_keys, grad_values, stream, params, normed_in, angle_cos, angle_sin
):
    row_count, width = stream.shape
    query_low = (
        rotate_back(grad_queries, angle_cos, angle_sin)
        .reshape(row_count, width)
        .astype(jnp.bfloat16)
    )
    key_low = (
        rotate_back(grad_keys, angle_cos, angle_sin).reshape(row_count, width).astype(jnp.bfloat16)
    )
    value_low = grad_values.reshape(row_count, width).astype(jnp.bfloat16)
    grad_query = jnp.einsum("nd,nc->dc", normed_in, query_low, preferred_element_type=jnp.float32)
    grad_key = jnp.einsum("nd,nc->dc", normed_in, key_low, preferred_element_type=jnp.float32)
    grad_value = jnp.einsum("nd,nc->dc", normed_in, value_low, preferred_element_type=jnp.float32)
    grad_normed = (
        jnp.einsum("nc,dc->nd", query_low, params[1], preferred_element_type=jnp.float32)
        + jnp.einsum("nc,dc->nd", key_low, params[2], preferred_element_type=jnp.float32)
        + jnp.einsum("nc,dc->nd", value_low, params[3], preferred_element_type=jnp.float32)
    )
    norm_value, norm_pull = jax.vjp(normalize, stream, params[0])
    grad_stream, grad_gain_attn = norm_pull(grad_normed)
    return (grad_stream, grad_gain_attn, grad_query, grad_key, grad_value)


def local_forward(stream, places, params, fetch):
    angle_cos, angle_sin = rope_table(places)
    normed_in, queries, keys_here, values_here = project(stream, params, angle_cos, angle_sin)
    row_count, width = stream.shape
    keys_local = keys_here.reshape(row_count, width)
    values_local = values_here.reshape(row_count, width)
    keys_flat, values_flat = fetch(keys_local, values_local)
    key_places = jnp.arange(keys_flat.shape[0], dtype=jnp.int32)
    attended, log_total = attend(
        queries, split_heads(keys_flat), split_heads(values_flat), places, key_places
    )
    result, finish_saved = finish(stream, attended, params)
    return (
        result,
        (
            normed_in,
            queries,
            keys_local,
            values_local,
            keys_flat,
            values_flat,
            log_total,
            angle_cos,
            angle_sin,
            finish_saved,
        ),
    )


def local_backward(grad_result, stream, places, params, saved, keys_flat, values_flat, key_sum):
    normed_in, queries = (saved[0], saved[1])
    log_total, angle_cos, angle_sin, finish_saved = (saved[6], saved[7], saved[8], saved[9])
    grad_middle, grad_attended, grad_output_w, grad_expand, grad_contract, grad_gain_ffn = (
        finish_back(grad_result, finish_saved, params)
    )
    row_count, width = stream.shape
    key_places = jnp.arange(keys_flat.shape[0], dtype=jnp.int32)
    grad_queries, grad_scores, prob_low, row_inner = attend_back(
        queries,
        split_heads(keys_flat),
        split_heads(values_flat),
        places,
        key_places,
        log_total,
        grad_attended,
    )

    def contribution(first_row, term_rows):
        grad_keys = jnp.einsum(
            "hnm,nhe->mhe", grad_scores, queries, preferred_element_type=jnp.float32
        ) * HEAD ** (-0.5)
        grad_values = jnp.einsum(
            "hnm,nhe->mhe", prob_low, grad_attended, preferred_element_type=jnp.float32
        )
        return jnp.concatenate(
            [grad_keys.reshape(term_rows, width), grad_values.reshape(term_rows, width)], axis=1
        )

    both_grads = key_sum(contribution, row_count, (queries, grad_attended, log_total, row_inner))
    grad_stream, grad_gain_attn, grad_query, grad_key, grad_value = start_back(
        grad_queries,
        split_heads(both_grads[:, :width]),
        split_heads(both_grads[:, width:]),
        stream,
        params,
        normed_in,
        angle_cos,
        angle_sin,
    )
    return (
        grad_middle + grad_stream,
        (
            grad_gain_attn,
            grad_query,
            grad_key,
            grad_value,
            grad_output_w,
            grad_gain_ffn,
            grad_expand,
            grad_contract,
        ),
    )


def whole_forward(stream, params):
    row_count, width = stream.shape
    places = jnp.arange(row_count, dtype=jnp.int32)
    angle_cos, angle_sin = rope_table(places)
    normed_in, queries, keys_here, values_here = project(stream, params, angle_cos, angle_sin)
    block_rows = 512
    block_count = row_count // block_rows

    def one_block(pieces):
        return attend(pieces[0], keys_here, values_here, pieces[1], places)

    attended, log_total = lax.map(
        one_block,
        (
            queries.reshape(block_count, block_rows, HEADS, HEAD),
            places.reshape(block_count, block_rows),
        ),
    )
    result, finish_saved = finish(stream, attended.reshape(row_count, HEADS, HEAD), params)
    return (
        result,
        (normed_in, queries, keys_here, values_here, log_total, angle_cos, angle_sin, finish_saved),
    )


def whole_backward(grad_result, stream, params, saved):
    normed_in, queries, keys_here, values_here, log_total, angle_cos, angle_sin, finish_saved = (
        saved
    )
    grad_middle, grad_attended, grad_output_w, grad_expand, grad_contract, grad_gain_ffn = (
        finish_back(grad_result, finish_saved, params)
    )
    row_count, width = stream.shape
    places = jnp.arange(row_count, dtype=jnp.int32)
    block_rows = 512
    block_count = row_count // block_rows

    def one_block(running, pieces):
        query_block, place_block, total_block, grad_block = pieces
        grad_queries, grad_scores, prob_low, row_inner = attend_back(
            query_block, keys_here, values_here, place_block, places, total_block, grad_block
        )
        grad_keys = running[0] + jnp.einsum(
            "hnm,nhe->mhe", grad_scores, query_block, preferred_element_type=jnp.float32
        ) * HEAD ** (-0.5)
        grad_values = running[1] + jnp.einsum(
            "hnm,nhe->mhe", prob_low, grad_block, preferred_element_type=jnp.float32
        )
        return ((grad_keys, grad_values), grad_queries)

    zero_grads = jnp.zeros((row_count, HEADS, HEAD), jnp.float32)
    (grad_keys, grad_values), grad_queries = lax.scan(
        one_block,
        (zero_grads, zero_grads),
        (
            queries.reshape(block_count, block_rows, HEADS, HEAD),
            places.reshape(block_count, block_rows),
            log_total,
            grad_attended.reshape(block_count, block_rows, HEADS, HEAD),
        ),
    )
    grad_stream, grad_gain_attn, grad_query, grad_key, grad_value = start_back(
        grad_queries.reshape(row_count, HEADS, HEAD),
        grad_keys,
        grad_values,
        stream,
        params,
        normed_in,
        angle_cos,
        angle_sin,
    )
    return (
        grad_middle + grad_stream,
        (
            grad_gain_attn,
            grad_query,
            grad_key,
            grad_value,
            grad_output_w,
            grad_gain_ffn,
            grad_expand,
            grad_contract,
        ),
    )


def by_rows(
    inputs,
    cotangent,
    full_gain_attn,
    full_query,
    full_key,
    full_value,
    full_output,
    full_gain_ffn,
    full_expand,
    full_contract,
    short_gain_attn,
    short_query,
    short_key,
    short_value,
    short_output,
    short_gain_ffn,
    short_expand,
    short_contract,
):
    full_params = (
        full_gain_attn,
        full_query,
        full_key,
        full_value,
        full_output,
        full_gain_ffn,
        full_expand,
        full_contract,
    )
    short_params = (
        short_gain_attn,
        short_query,
        short_key,
        short_value,
        short_output,
        short_gain_ffn,
        short_expand,
        short_contract,
    )
    stream_in = inputs[0]
    row_count, width = stream_in.shape
    own_short = row_count // 3
    position = lax.axis_index("seq")
    seq_parts = lax.axis_size("seq")
    places = position * row_count + jnp.arange(row_count, dtype=jnp.int32)

    def fetch_full(keys_local, values_local):
        return (
            lax.all_gather(keys_local, "seq", axis=0, tiled=True),
            lax.all_gather(values_local, "seq", axis=0, tiled=True),
        )

    residual, full_saved = local_forward(stream_in, places, full_params, fetch_full)
    tail_rows = from_behind(residual[row_count - 2 :], "seq", 1)
    shifted = jnp.concatenate([tail_rows, residual[: row_count - 2]], axis=0)
    pooled = jnp.mean(shifted.reshape(own_short, 3, width), axis=1)
    pooled_all = lax.all_gather(pooled, "seq", axis=0, tiled=True)
    short_all, short_saved = whole_forward(pooled_all, short_params)
    short_result = lax.dynamic_slice_in_dim(short_all, position * own_short, own_short, 0)
    output = residual + jnp.repeat(short_result, 3, axis=0)
    grad_output = cotangent[0]
    grad_short = jnp.sum(grad_output.reshape(own_short, 3, width), axis=1)
    grad_short_all = lax.all_gather(grad_short, "seq", axis=0, tiled=True)
    grad_pooled_all, short_grads = whole_backward(
        grad_short_all, pooled_all, short_params, short_saved
    )
    grad_pooled = lax.dynamic_slice_in_dim(grad_pooled_all, position * own_short, own_short, 0)
    short_grads = tuple(
        (
            lax.dynamic_slice_in_dim(
                gradient,
                position * (gradient.shape[0] // seq_parts),
                gradient.shape[0] // seq_parts,
                0,
            )
            for gradient in short_grads
        )
    )
    grad_shifted = jnp.repeat(grad_pooled / 3.0, 3, axis=0)
    carried = from_behind(grad_shifted[:2], "seq", -1)
    grad_residual = grad_output + jnp.concatenate([grad_shifted[2:], carried], axis=0)
    keys_flat, values_flat = (
        lax.all_gather(full_saved[2], "seq", axis=0, tiled=True),
        lax.all_gather(full_saved[3], "seq", axis=0, tiled=True),
    )

    def full_sum(contribution, term_rows, query_side):
        return lax.psum_scatter(
            contribution(jnp.int32(0), term_rows * lax.axis_size("seq")).astype(jnp.bfloat16),
            "seq",
            scatter_dimension=0,
            tiled=True,
        ).astype(jnp.float32)

    grad_input, full_grads = local_backward(
        grad_residual, stream_in, places, full_params, full_saved, keys_flat, values_flat, full_sum
    )
    full_shares = (
        lax.psum_scatter(
            full_grads[0].astype(jnp.bfloat16), "seq", scatter_dimension=0, tiled=True
        ).astype(jnp.float32),
        lax.psum_scatter(
            full_grads[1].astype(jnp.bfloat16), "seq", scatter_dimension=0, tiled=True
        ).astype(jnp.float32),
        lax.psum_scatter(
            full_grads[2].astype(jnp.bfloat16), "seq", scatter_dimension=0, tiled=True
        ).astype(jnp.float32),
        lax.psum_scatter(
            full_grads[3].astype(jnp.bfloat16), "seq", scatter_dimension=0, tiled=True
        ).astype(jnp.float32),
        lax.psum_scatter(
            full_grads[4].astype(jnp.bfloat16), "seq", scatter_dimension=0, tiled=True
        ).astype(jnp.float32),
        lax.psum_scatter(
            full_grads[5].astype(jnp.bfloat16), "seq", scatter_dimension=0, tiled=True
        ).astype(jnp.float32),
        lax.psum_scatter(
            full_grads[6].astype(jnp.bfloat16), "seq", scatter_dimension=0, tiled=True
        ).astype(jnp.float32),
        lax.psum_scatter(
            full_grads[7].astype(jnp.bfloat16), "seq", scatter_dimension=0, tiled=True
        ).astype(jnp.float32),
    )
    shares = tuple(full_shares) + tuple(short_grads)
    totals = (
        lax.psum(shares[0].astype(jnp.bfloat16), "batch").astype(jnp.float32),
        lax.psum(shares[1].astype(jnp.bfloat16), "batch").astype(jnp.float32),
        lax.psum(shares[2].astype(jnp.bfloat16), "batch").astype(jnp.float32),
        lax.psum(shares[3].astype(jnp.bfloat16), "batch").astype(jnp.float32),
        lax.psum(shares[4].astype(jnp.bfloat16), "batch").astype(jnp.float32),
        lax.psum(shares[5].astype(jnp.bfloat16), "batch").astype(jnp.float32),
        lax.psum(shares[6].astype(jnp.bfloat16), "batch").astype(jnp.float32),
        lax.psum(shares[7].astype(jnp.bfloat16), "batch").astype(jnp.float32),
        lax.psum(shares[8].astype(jnp.bfloat16), "batch").astype(jnp.float32),
        lax.psum(shares[9].astype(jnp.bfloat16), "batch").astype(jnp.float32),
        lax.psum(shares[10].astype(jnp.bfloat16), "batch").astype(jnp.float32),
        lax.psum(shares[11].astype(jnp.bfloat16), "batch").astype(jnp.float32),
        lax.psum(shares[12].astype(jnp.bfloat16), "batch").astype(jnp.float32),
        lax.psum(shares[13].astype(jnp.bfloat16), "batch").astype(jnp.float32),
        lax.psum(shares[14].astype(jnp.bfloat16), "batch").astype(jnp.float32),
        lax.psum(shares[15].astype(jnp.bfloat16), "batch").astype(jnp.float32),
    )
    whole = (
        lax.all_gather(totals[0].astype(jnp.bfloat16), "seq", axis=0, tiled=True).astype(
            jnp.float32
        ),
        lax.all_gather(totals[1].astype(jnp.bfloat16), "seq", axis=0, tiled=True).astype(
            jnp.float32
        ),
        lax.all_gather(totals[2].astype(jnp.bfloat16), "seq", axis=0, tiled=True).astype(
            jnp.float32
        ),
        lax.all_gather(totals[3].astype(jnp.bfloat16), "seq", axis=0, tiled=True).astype(
            jnp.float32
        ),
        lax.all_gather(totals[4].astype(jnp.bfloat16), "seq", axis=0, tiled=True).astype(
            jnp.float32
        ),
        lax.all_gather(totals[5].astype(jnp.bfloat16), "seq", axis=0, tiled=True).astype(
            jnp.float32
        ),
        lax.all_gather(totals[6].astype(jnp.bfloat16), "seq", axis=0, tiled=True).astype(
            jnp.float32
        ),
        lax.all_gather(totals[7].astype(jnp.bfloat16), "seq", axis=0, tiled=True).astype(
            jnp.float32
        ),
        lax.all_gather(totals[8].astype(jnp.bfloat16), "seq", axis=0, tiled=True).astype(
            jnp.float32
        ),
        lax.all_gather(totals[9].astype(jnp.bfloat16), "seq", axis=0, tiled=True).astype(
            jnp.float32
        ),
        lax.all_gather(totals[10].astype(jnp.bfloat16), "seq", axis=0, tiled=True).astype(
            jnp.float32
        ),
        lax.all_gather(totals[11].astype(jnp.bfloat16), "seq", axis=0, tiled=True).astype(
            jnp.float32
        ),
        lax.all_gather(totals[12].astype(jnp.bfloat16), "seq", axis=0, tiled=True).astype(
            jnp.float32
        ),
        lax.all_gather(totals[13].astype(jnp.bfloat16), "seq", axis=0, tiled=True).astype(
            jnp.float32
        ),
        lax.all_gather(totals[14].astype(jnp.bfloat16), "seq", axis=0, tiled=True).astype(
            jnp.float32
        ),
        lax.all_gather(totals[15].astype(jnp.bfloat16), "seq", axis=0, tiled=True).astype(
            jnp.float32
        ),
    )
    return (output[None], grad_input[None]) + tuple(whole)


def solution(mesh):
    sequence = P("batch", "seq", None)
    seq, batch = mesh.shape["seq"], mesh.shape["batch"]
    fits = seq == HEADS and batch == 4
    return jax.shard_map(
        by_heads if fits else by_rows,
        mesh=mesh,
        in_specs=(sequence, sequence) + (P(),) * 16,
        out_specs=(sequence, sequence) + (P(),) * 16,
        check_vma=False,
    )
```

```python
from functools import partial

import jax
import jax.numpy as jnp
import numpy as np
from jax import lax
from jax.experimental import pallas as pl
from jax.experimental.pallas import tpu as pltpu
from jax.sharding import PartitionSpec as P

HEADS = 8
HEAD = 64
LANES = 128
BLOCK = 256
FF_PARTS = 1
F32 = jnp.float32
BF16 = jnp.bfloat16


norm_eps = 1e-05


def dot_nn(left, right):
    return jnp.dot(left, right, preferred_element_type=F32)


def dot_nt(left, right):
    return lax.dot_general(left, right, (((1,), (1,)), ((), ())), preferred_element_type=F32)


def dot_tn(left, right):
    return lax.dot_general(left, right, (((0,), (0,)), ((), ())), preferred_element_type=F32)


def lower_half(rows):
    return lax.broadcasted_iota(jnp.int32, (rows, LANES), 1) < HEAD


def turn(values):
    return pltpu.roll(values, HEAD, 1)


def swap_pairs(values):
    lane = lax.broadcasted_iota(jnp.int32, values.shape, 1)
    return jnp.where(
        lane % HEAD < HEAD // 2,
        pltpu.roll(values, LANES - HEAD // 2, 1),
        pltpu.roll(values, HEAD // 2, 1),
    )


def rope(values, table):
    return values * table[:, :LANES] + swap_pairs(values) * table[:, LANES:]


def rope_back(grads, table):
    return grads * table[:, :LANES] - swap_pairs(grads) * table[:, LANES:]


def rope_constants(rows):
    frequency = np.power(
        np.float32(10000.0), -np.arange(HEAD // 2, dtype=np.float32) * np.float32(2.0 / HEAD)
    ).astype(np.float32)
    angles = np.arange(rows, dtype=np.float32)[:, None] * frequency[None, :]
    cosine, sine = np.cos(angles), np.sin(angles)
    table = np.concatenate([cosine] * 4 + [-sine, sine] * 2, axis=1)
    return jnp.asarray(table, F32)


def norm_parts(stream):
    centered = stream - jnp.mean(stream, axis=-1, keepdims=True)
    spread = jnp.mean(centered * centered, axis=-1, keepdims=True)
    scale = lax.rsqrt(spread + norm_eps)
    return centered * scale, scale


def norm_back(grad, gain, unit, scale):
    grad_unit = grad * gain
    inner = jnp.mean(grad_unit * unit, axis=-1, keepdims=True)
    return scale * (grad_unit - jnp.mean(grad_unit, axis=-1, keepdims=True) - unit * inner)


GELU_SCALE = 0.7978845608028654
GELU_CUBE = 0.044715


def gelu_both(pre):
    square = pre * pre
    half = 0.5 + 0.5 * jnp.tanh(pre * (GELU_SCALE + GELU_SCALE * GELU_CUBE * square))
    bend = pre * (2.0 * GELU_SCALE + 6.0 * GELU_SCALE * GELU_CUBE * square)
    return pre * half, half * (1.0 + (1.0 - half) * bend)


def gelu_value(pre):
    tanh = jnp.tanh(GELU_SCALE * pre * (1.0 + GELU_CUBE * pre * pre))
    return 0.5 * pre * (1.0 + tanh)


def causal(scores, first_row, first_key):
    row = lax.broadcasted_iota(jnp.int32, scores.shape, 0) + first_row
    key = lax.broadcasted_iota(jnp.int32, scores.shape, 1) + first_key
    return jnp.where(key <= row, scores, -1e30)


def fold_rows(values):
    half = values.shape[0] // 2
    return jnp.where(lower_half(half), values[:half], turn(values[half:]))


def unfold_rows(folded):
    low = lower_half(folded.shape[0])
    return jnp.where(low, folded, 0.0), jnp.where(low, turn(folded), 0.0)


def rows_at(start, size, multiple):
    return pl.ds(pl.multiple_of(start, multiple), size)


class Late:
    def __init__(self, source, target, semaphores, axis=0, parts=1):
        self.target, self.shape = target, target.shape
        size = target.shape[axis] // parts
        cuts = [(slice(None),) * axis + (pl.ds(part * size, size),) for part in range(parts)]
        self.copies = [
            pltpu.make_async_copy(source.at[cut], target.at[cut], semaphore)
            for cut, semaphore in zip(cuts, semaphores)
        ]
        self.waiting = set(range(parts))

    def ready(self, part=None):
        for at in sorted(self.waiting if part is None else self.waiting & {part}):
            self.copies[at].wait()
            self.waiting.remove(at)
        return self.target

    def __getitem__(self, index):
        return self.ready()[index]


def with_late(kernel, late, argument_count, out_count, *refs):
    arguments, outs = list(refs[:argument_count]), refs[argument_count : argument_count + out_count]
    rest = refs[argument_count + out_count :]
    first, taken, begun = len(rest) - len(late) - 1, 0, []
    for at, (place, _, part, axis, parts) in enumerate(late):
        source = arguments[place]
        source = source if part is None else part(source, refs[0][0])
        semaphores = [rest[-1].at[taken + step] for step in range(parts)]
        arguments[place] = Late(source, rest[first + at], semaphores, axis, parts)
        begun += [(part, at, copy) for part, copy in enumerate(arguments[place].copies)]
        taken += parts
    for _, _, copy in sorted(begun, key=lambda entry: entry[:2]):
        copy.start()
    kernel(*arguments, *outs, *rest[:first])


def paired(refs):
    size = refs[0].shape[0] // 2
    pairs = len(refs) // 2
    return [
        refs[step // 2].at[pl.ds(0, size), :]
        if step % 2 == 0
        else refs[pairs + step // 2].at[pl.ds(size, size), :]
        for step in range(2 * pairs)
    ]


def by_distance(share, pieces, seat):
    rows = pieces[0].shape[0]
    for step in range(len(pieces)):
        pieces[step][...] = share[rows_at((seat ^ step) * rows, rows, 16), :]


def keep_and_send(share, keep, send, seat, parts, first=0):
    rows = share.shape[0] // parts
    stride = keep.shape[0] // (parts // 2)
    for step in range(parts):
        target = keep if step % 2 == 0 else send
        at = (step // 2) * stride + first
        target[at : at + rows] = share[rows_at((seat ^ step) * rows, rows, 16), :]


def load_kernel(place, *refs):
    count = (len(refs) - 1) // 2
    copies = [
        pltpu.make_async_copy(refs[at], refs[count + at], refs[-1].at[at]) for at in range(count)
    ]
    for copy in copies:
        copy.start()
    for copy in copies:
        copy.wait()


def project_kernel(place, x, cot, gain, w_q, w_k, w_v, table, *refs):
    pieces = refs[: HEADS // 2]
    normed_out, bundle, heads, chunks = refs[HEADS // 2 :]
    rows, width = x.shape
    me = place[0]
    unit, _ = norm_parts(x[...])
    normed = (unit * gain[...]).astype(BF16)
    q = dot_nn(normed, w_q[...])
    k = dot_nn(normed, w_k[...])
    v = dot_nn(normed, w_v[...])
    low = lower_half(rows)
    low_half = lower_half(rows // 2)
    own = table[...]
    for chunk in range(width // LANES):
        cut = slice(chunk * LANES, (chunk + 1) * LANES)
        q_chunk = rope(q[:, cut], own) * HEAD**-0.5
        k_chunk = rope(k[:, cut], own)
        v_chunk = v[:, cut]
        first, later = q_chunk[: rows // 2], q_chunk[rows // 2 :]
        heads[2 * chunk, :rows] = jnp.where(low, k_chunk, turn(v_chunk)).astype(BF16)
        heads[2 * chunk + 1, :rows] = jnp.where(low, turn(k_chunk), v_chunk).astype(BF16)
        heads[2 * chunk, rows:] = jnp.where(low_half, first, turn(later)).astype(BF16)
        heads[2 * chunk + 1, rows:] = jnp.where(low_half, turn(first), later).astype(BF16)
    for step in range(HEADS):
        at = (step % 2) * heads.shape[1]
        pieces[step // 2][at : at + heads.shape[1]] = heads[me ^ step]
    normed_out[...] = normed
    bundle[:rows] = cot[...].astype(BF16)
    for chunk in range(width // LANES):
        cut = slice(chunk * LANES, (chunk + 1) * LANES)
        chunks[chunk] = cot[:, cut]
        total = sum(chunks[chunk, pl.ds(s, rows // 3, stride=3), :] for s in range(3))
        bundle[rows:, cut] = total.astype(BF16)


def attend_kernel(place, *refs):
    pieces, outs = paired(refs[:HEADS]), refs[HEADS : HEADS + HEADS // 2]
    q_all, kv_all, lse_o = refs[HEADS + HEADS // 2 :]
    me = place[0]
    rows = outs[0].shape[0]
    for step in range(HEADS):
        start = (me ^ step) * rows
        piece = pieces[step][...]
        kv_all[rows_at(start, rows, 16), :] = piece[:rows]
        first, later = unfold_rows(piece[rows:].astype(F32))
        q_all[rows_at(start, rows // 2, 16), :] = first.astype(BF16)
        q_all[rows_at(start + rows // 2, rows // 2, 16), :] = later.astype(BF16)
    low = lower_half(BLOCK)
    for block in range(q_all.shape[0] // BLOCK):
        cut = slice(block * BLOCK, (block + 1) * BLOCK)
        seen = kv_all[: (block + 1) * BLOCK]
        scores = causal(dot_nt(q_all[cut], seen), block * BLOCK, 0)
        most = jnp.max(scores, axis=-1, keepdims=True)
        weights = jnp.exp(scores - most)
        total = jnp.sum(weights, axis=-1, keepdims=True)
        attended = dot_nn(weights.astype(BF16), seen) / total
        lse_o[cut] = jnp.where(low, most + jnp.log(total), attended)
    for step in range(HEADS):
        own = lse_o[rows_at((me ^ step) * rows, rows, 16), :]
        at = (step % 2) * (rows // 2)
        outs[step // 2][at : at + rows // 2] = jnp.where(
            lower_half(rows // 2), turn(own[: rows // 2]), own[rows // 2 :]
        ).astype(BF16)


def finish_kernel(place, x, normed_a, gain, w_o, w_e, w_c, *refs):
    pieces = paired(refs[:HEADS])
    result_out, middle_out, att_out, normed_out, pooled_out, heads, chunks = refs[HEADS:]
    rows, width = x.shape
    me = place[0]
    for step in range(HEADS):
        heads[me ^ step] = pieces[step][...].astype(F32)
    low = lower_half(rows // 2)
    for chunk in range(width // LANES):
        cut = slice(chunk * LANES, (chunk + 1) * LANES)
        even, odd = heads[2 * chunk], heads[2 * chunk + 1]
        att_out[: rows // 2, cut] = jnp.where(low, even, turn(odd)).astype(BF16)
        att_out[rows // 2 :, cut] = jnp.where(low, turn(even), odd).astype(BF16)
    middle = x[...] + dot_nn(att_out[...], w_o[...])
    middle_out[...] = middle
    unit, _ = norm_parts(middle)
    normed = (unit * gain[...]).astype(BF16)
    normed_out[:rows] = normed
    normed_out[rows:] = normed_a[...]
    result = middle
    size = w_e.shape[1] // FF_PARTS
    for part in range(FF_PARTS):
        cut = slice(part * size, (part + 1) * size)
        hidden = gelu_value(dot_nn(normed, w_e.ready(part)[:, cut])).astype(BF16)
        result = result + dot_nn(hidden, w_c.ready(part)[cut, :])
    result_out[...] = result
    short = rows // 3
    for chunk in range(width // LANES):
        cut = slice(chunk * LANES, (chunk + 1) * LANES)
        chunks[chunk, :8] = jnp.zeros((8, LANES), F32)
        chunks[chunk, 8:] = result[:, cut]
        total = sum(chunks[chunk, pl.ds(s, short, stride=3), :] for s in (6, 7, 8))
        pooled_out[:short, cut] = (total / 3.0).astype(BF16)
    tail = (result[rows - 1 :] + result[rows - 2 : rows - 1]) / 3.0
    extra = pooled_out.shape[0] - short
    pooled_out[short:] = jnp.broadcast_to(tail, (extra, width)).astype(BF16)


def short_forward_kernel(
    place, residual, gathered, table, gain_a, w_q, w_k, w_v, w_o, gain_f, w_e, w_c, *refs
):
    pieces, refs = refs[:HEADS], refs[HEADS:]
    output, pooled, normed_a, q_s, k_s, v_s, o_s, lse_s, att, grad_middle = refs[:10]
    share_pieces = refs[10:-9]
    extra, middle, normed_f, hidden, grad_pre, grad_normed, grad_low, wide, share = refs[-9:]
    me, seat = place[0], place[1]
    rows, width = residual.shape
    count = pooled.shape[0]
    short = rows // 3
    chunk_count = width // LANES
    ff = w_e.shape[1]
    ff_own = ff // HEADS

    for step in range(HEADS):
        other = me ^ step
        pooled[rows_at(other * short, short, 16), :] = pieces[step][:short].astype(F32)
        extra[pl.ds(other, 1), :] = pieces[step][short:].astype(F32)[:1]
    for part in range(1, HEADS):
        at = slice(part * short, part * short + 1)
        pooled[at] = pooled[at] + extra[part - 1 : part]

    unit, _ = norm_parts(pooled[...])
    normed_a[...] = (unit * gain_a[...]).astype(BF16)
    low = lower_half(count)
    q = dot_nn(normed_a[...], w_q[...])
    turns = table[...]
    for chunk in range(chunk_count):
        q_chunk = rope(q[:, chunk * LANES : (chunk + 1) * LANES], turns) * HEAD**-0.5
        q_s[2 * chunk] = jnp.where(low, q_chunk, 0.0).astype(BF16)
        q_s[2 * chunk + 1] = jnp.where(low, 0.0, q_chunk).astype(BF16)
    k = dot_nn(normed_a[...], w_k[...])
    for chunk in range(chunk_count):
        k_s[chunk] = rope(k[:, chunk * LANES : (chunk + 1) * LANES], turns).astype(BF16)
    v = dot_nn(normed_a[...], w_v[...])
    for chunk in range(chunk_count):
        v_s[chunk] = v[:, chunk * LANES : (chunk + 1) * LANES].astype(BF16)

    low_block = lower_half(BLOCK)

    def attend_chunk(chunk, carry):
        results = []
        k_t = jnp.transpose(k_s[chunk])
        for half in range(2):
            scores = causal(dot_nn(q_s[2 * chunk + half], k_t), 0, 0)
            most = jnp.max(scores, axis=-1, keepdims=True)
            weights = jnp.exp(scores - most)
            total = jnp.sum(weights, axis=-1, keepdims=True)
            attended = dot_nn(weights.astype(BF16), v_s[chunk]) / total
            results.append((attended, most + jnp.log(total)))
        both = jnp.where(low, results[0][0], results[1][0])
        o_s[chunk] = both
        lse_s[chunk] = jnp.where(low, results[0][1], results[1][1])
        att[:, rows_at(chunk * LANES, LANES, LANES)] = both.astype(BF16)
        return carry

    lax.fori_loop(0, chunk_count, attend_chunk, 0)
    middle[...] = pooled[...] + dot_nn(att[...], w_o[...])
    unit, scale = norm_parts(middle[...])
    normed_f[...] = (unit * gain_f[...]).astype(BF16)

    for part in range(HEADS):
        grad_low[part * short : (part + 1) * short] = gathered[part]

    ff_part = ff // 4
    grad_normed[...] = jnp.zeros(grad_normed.shape, F32)
    w_e, w_c = w_e.ready(), w_c.ready()

    def feed_forward(part, carry):
        cut = rows_at(part * ff_part, ff_part, ff_part)
        pre = dot_nn(normed_f[...], w_e[:, cut])
        value, slope = gelu_both(pre)
        hidden[:, cut] = value.astype(BF16)
        grad_hidden = dot_nt(grad_low[...], w_c[cut, :])
        low_grad = (grad_hidden * slope).astype(BF16)
        grad_pre[:, cut] = low_grad
        grad_normed[...] += dot_nt(low_grad, w_e[:, cut])
        return carry

    lax.fori_loop(0, 4, feed_forward, 0)

    own_ff = rows_at(me * ff_own, ff_own, ff_own)
    share[:ff_own] = dot_tn(hidden[:, own_ff], grad_low[...]).astype(BF16)
    expand = dot_tn(normed_f[...], grad_pre[:, own_ff]).astype(BF16)
    share[ff_own : 2 * ff_own, : width // 2] = expand[: width // 2]
    share[ff_own : 2 * ff_own, width // 2 :] = expand[width // 2 :]
    by_distance(share, share_pieces, seat)

    mine = rows_at(me * short, short, 16)
    short_out = middle[mine, :] + dot_nn(hidden[mine, :], w_c[...])
    for chunk in range(chunk_count):
        cut = slice(chunk * LANES, (chunk + 1) * LANES)
        for s in range(3):
            wide[chunk, pl.ds(s, short, stride=3), :] = short_out[:, cut]
        output[:, cut] = residual[:, cut] + wide[chunk]

    unit, scale = norm_parts(middle[...])
    grad_middle[...] = grad_low[...].astype(F32) + norm_back(
        grad_normed[...], gain_f[...], unit, scale
    )


def short_back_kernel(
    place,
    cot,
    gathered,
    table,
    gain_a,
    w_q,
    w_k,
    w_v,
    w_o,
    pooled,
    normed_a,
    q_s,
    k_s,
    v_s,
    o_s,
    lse_s,
    att,
    grad_middle,
    middle,
    normed_f,
    gain_f,
    w_e,
    w_c,
    grad_all,
    share,
    full_middle,
    g1_out,
    do_s,
    dq_s,
    dk_s,
    dv_s,
    wide,
    wo_s,
    grad_own,
):
    me = place[0]
    rows, width = cot.shape
    count = pooled.shape[0]
    full = rows * HEADS
    chunk_count = width // LANES
    low = lower_half(count)
    low_block = lower_half(BLOCK)
    g1 = grad_middle[...].astype(BF16)
    d_att = dot_nt(g1, w_o[...])
    for chunk in range(chunk_count):
        do_chunk = d_att[:, chunk * LANES : (chunk + 1) * LANES]
        do_s[2 * chunk] = jnp.where(low, do_chunk, 0.0).astype(BF16)
        do_s[2 * chunk + 1] = jnp.where(low, 0.0, do_chunk).astype(BF16)
    own_chunk = rows_at((me // 2) * LANES, LANES, LANES)
    wo_s[...] = dot_tn(att[:, own_chunk], g1)
    table = table.ready()

    def attend_back(chunk, carry):
        columns = rows_at(chunk * LANES, LANES, LANES)
        dq = []
        dk = [None]
        dv = [None]
        k_t = jnp.transpose(k_s[chunk])
        v_t = jnp.transpose(v_s[chunk])
        for half in range(2):
            head = 2 * chunk + half
            lse = lse_s[chunk][:, half * HEAD : half * HEAD + 1]
            delta = jnp.sum(do_s[head].astype(F32) * o_s[chunk], axis=-1, keepdims=True)
            dq_half = None
            for key in range(1):
                cut = slice(0, count)
                rest = slice(0, count)
                k_block, v_block = k_s[chunk, cut, :], v_s[chunk, cut, :]
                q_rest, do_rest = q_s[head, rest, :], do_s[head, rest, :]
                scores = causal(dot_nn(q_rest, k_t), 0, 0)
                probs = jnp.exp(scores - lse[rest])
                grad_probs = dot_nn(do_rest, v_t)
                ds = (probs * (grad_probs - delta[rest])).astype(BF16)
                term = dot_nn(ds, k_block)
                if key == 0:
                    dq_half = term
                else:
                    dq_half = jnp.concatenate(
                        [dq_half[: key * BLOCK], dq_half[key * BLOCK :] + term]
                    )
                term = dot_tn(ds, q_rest)
                dk[key] = term if half == 0 else dk[key] + term
                term = dot_tn(probs.astype(BF16), do_rest)
                dv[key] = term if half == 0 else dv[key] + term
            dq.append(dq_half)
        both = jnp.where(lower_half(count), dq[0], dq[1]) * HEAD**-0.5
        dq_s[:, columns] = rope_back(both, table[...]).astype(BF16)
        for key in range(1):
            key_cut = slice(0, count)
            dk_s[key_cut, columns] = rope_back(dk[key], table[key_cut, :]).astype(BF16)
            dv_s[key_cut, columns] = dv[key].astype(BF16)
        return carry

    lax.fori_loop(0, chunk_count, attend_back, 0)

    odd = me % 2 == 1
    low_width = lower_half(width)
    share_q = dot_tn(normed_a[...], dq_s[:, own_chunk])
    share_k = dot_tn(normed_a[...], dk_s[:, own_chunk])
    share_v = dot_tn(normed_a[...], dv_s[:, own_chunk])
    share_q = jnp.where(odd, turn(share_q), share_q)
    share_k = jnp.where(odd, share_k, turn(share_k))
    share_v = jnp.where(odd, turn(share_v), share_v)
    head_rows = wo_s[rows_at((me % 2) * HEAD, HEAD, HEAD), :]
    pack_attention(share, jnp.where(low_width, share_q, share_k), fold_rows(share_v), head_rows)

    grad_a = dot_nt(dq_s[...], w_q[...])
    grad_a += dot_nt(dk_s[...], w_k[...])
    grad_a += dot_nt(dv_s[...], w_v[...])
    unit, scale = norm_parts(pooled[...])
    grad_pooled = grad_middle[...] + norm_back(grad_a, gain_a[...], unit, scale)
    for chunk in range(chunk_count):
        cut = slice(chunk * LANES, (chunk + 1) * LANES)
        third = grad_pooled[:, cut] / 3.0
        for s in range(3):
            wide[chunk, pl.ds(6 + s, count, stride=3), :] = third
        wide[chunk, full + 6 : full + 8] = jnp.zeros((2, LANES), F32)
        grad_own[:, cut] = cot[:, cut] + wide[chunk, rows_at(me * rows + 8, rows, 8), :]
        for part in range(HEADS):
            more = wide[chunk, 8 + part * rows : 8 + (part + 1) * rows, :]
            grad_all[part * rows : (part + 1) * rows, cut] = (
                gathered[part, :, cut].astype(F32) + more
            ).astype(BF16)
    feed_forward_back(grad_own, middle, normed_f, gain_f, w_e, w_c, full_middle, g1_out)


def feed_forward_back(grad, middle, normed, gain, w_e, w_c, grad_middle_out, g1_out):
    grad_low = grad[...].astype(BF16)
    grad_normed = 0.0
    size = w_e.shape[1] // FF_PARTS
    for part in range(FF_PARTS):
        cut = slice(part * size, (part + 1) * size)
        own_w = w_e.ready(part)[:, cut]
        _, slope = gelu_both(dot_nn(normed[...], own_w))
        grad_hidden = dot_nt(grad_low, w_c.ready(part)[cut, :])
        grad_normed += dot_nt((grad_hidden * slope).astype(BF16), own_w)
    unit, scale = norm_parts(middle[...])
    grad_middle = grad[...] + norm_back(grad_normed, gain[...], unit, scale)
    grad_middle_out[...] = grad_middle
    g1_out[...] = grad_middle.astype(BF16)


def pack_attention(share, both_qk, folded_v, head_rows):
    half = both_qk.shape[0] // 2
    share[:half, :LANES] = both_qk[:half].astype(BF16)
    share[:half, LANES : 2 * LANES] = both_qk[half:].astype(BF16)
    share[:half, 2 * LANES : 3 * LANES] = folded_v.astype(BF16)
    size = head_rows.shape[0]
    for chunk in range(head_rows.shape[1] // LANES):
        share[chunk * size : (chunk + 1) * size, 3 * LANES :] = head_rows[
            :, chunk * LANES : (chunk + 1) * LANES
        ].astype(BF16)


def feed_forward_share_kernel(parts, place, normed, grad, w_e, w_c, keep, send, share):
    seat = place[1]
    width, ff_own = w_e.shape
    normed = normed[...].reshape(-1, width)
    value, slope = gelu_both(dot_nn(normed, w_e[...]))
    grad_hidden = dot_nt(grad[...], w_c[...])
    grad_pre = (grad_hidden * slope).astype(BF16)
    share[:ff_own] = dot_tn(value.astype(BF16), grad[...]).astype(BF16)
    expand = dot_tn(normed, grad_pre).astype(BF16)
    share[ff_own:, : width // 2] = expand[: width // 2]
    share[ff_own:, width // 2 :] = expand[width // 2 :]
    keep_and_send(share, keep, send, seat, parts)


def attend_back_kernel(place, q_all, kv_all, lse_o, table, w_o, *refs):
    pieces, outs = refs[:HEADS], refs[HEADS : HEADS + HEADS // 2]
    dq_all, dkv_all, do_all, dkv_sum, dq_sum, q_t, do_t = refs[HEADS + HEADS // 2 :]
    me = place[0]
    rows = q_all.shape[0] // HEADS
    own_w = w_o[...]
    own_w = jnp.concatenate([jnp.zeros(own_w.shape, BF16), own_w])
    for step in range(HEADS):
        do_all[rows_at((me ^ step) * rows, rows, 16), :] = dot_nt(
            pieces[step][...], own_w
        ).astype(BF16)
    total = q_all.shape[0]
    lse = lse_o[...][:, :1]
    delta = jnp.sum(do_all[...].astype(F32) * lse_o[...], axis=-1, keepdims=True)
    dq_sum[...] = jnp.zeros(dq_sum.shape, F32)
    q_t[...] = jnp.transpose(q_all[...].astype(F32)).astype(BF16)
    do_t[...] = jnp.transpose(do_all[...].astype(F32)).astype(BF16)
    for block in range(total // BLOCK):
        cut = slice(block * BLOCK, (block + 1) * BLOCK)
        rest = slice(block * BLOCK, total)
        kv_block = kv_all[cut]
        scores = causal(dot_nt(q_all[rest], kv_block), 0, 0)
        probs = jnp.exp(scores - lse[rest])
        grad_probs = dot_nt(do_all[rest], kv_block)
        ds = (probs * (grad_probs - delta[rest])).astype(BF16)
        dq_sum[rest] += dot_nn(ds, kv_block)
        back = dot_nn(q_t[:, rest], ds) + dot_nn(do_t[:, rest], probs.astype(BF16))
        dkv_sum[cut] = jnp.transpose(back)
    dq_all[...] = rope_back(dq_sum[...] * HEAD**-0.5, table[...]).astype(BF16)
    low = lower_half(BLOCK)
    for block in range(q_all.shape[0] // BLOCK):
        cut = slice(block * BLOCK, (block + 1) * BLOCK)
        dkv = dkv_sum[cut]
        dkv_all[cut] = jnp.where(low, rope_back(dkv, table[cut, :]), dkv).astype(BF16)
    for step in range(HEADS):
        own = rows_at((me ^ step) * rows, rows, 16)
        at = (step % 2) * (rows + rows // 2)
        outs[step // 2][at : at + rows] = dkv_all[own, :]
        outs[step // 2][at + rows : at + rows + rows // 2] = fold_rows(
            dq_all[own, :].astype(F32)
        ).astype(BF16)


def attention_share_kernel(parts, place, gathered, dq_all, dkv_all, lse_o, more, *refs):
    pieces, keep, send, share = refs[:HEADS], refs[HEADS], refs[HEADS + 1], refs[-1]
    me, seat = place[0], place[1]
    _, rows, width = gathered.shape
    normed = gathered[...].reshape(-1, width)
    grad_q = dot_tn(normed, dq_all[...])
    grad_kv = dot_tn(normed, dkv_all[...])
    grad_o = jnp.zeros((LANES, width), F32)
    for step in range(HEADS):
        own = lse_o[rows_at((me ^ step) * rows, rows, 16), :].astype(BF16)
        grad_o += dot_tn(own, pieces[step][...])
    grad_o = grad_o[HEAD:]
    half = width // 2
    folded_v = jnp.where(lower_half(half), turn(grad_kv[:half]), grad_kv[half:])
    pack_attention(
        share, jnp.where(lower_half(width), grad_q, turn(grad_kv)), folded_v, grad_o
    )
    keep_and_send(share, keep, send, seat, parts)
    keep_and_send(more, keep, send, seat, parts, share.shape[0] // parts)


def start_back_kernel(place, x, grad_middle, gain, w_q, w_k, w_v, *refs):
    pieces = paired(refs[:HEADS])
    grad_in, heads, dq, dk, dv = refs[HEADS:]
    me = place[0]
    rows, width = x.shape
    half = rows // 2
    for step in range(HEADS):
        heads[me ^ step] = pieces[step][...]
    low, low_half = lower_half(rows), lower_half(half)
    for chunk in range(width // LANES):
        cut = slice(chunk * LANES, (chunk + 1) * LANES)
        even, odd = heads[2 * chunk].astype(F32), heads[2 * chunk + 1].astype(F32)
        dk[:, cut] = jnp.where(low, even[:rows], turn(odd[:rows])).astype(BF16)
        dv[:, cut] = jnp.where(low, turn(even[:rows]), odd[:rows]).astype(BF16)
        dq[:half, cut] = jnp.where(low_half, even[rows:], turn(odd[rows:])).astype(BF16)
        dq[half:, cut] = jnp.where(low_half, turn(even[rows:]), odd[rows:]).astype(BF16)
    grad_a = dot_nt(dq[...], w_q[...]) + dot_nt(dk[...], w_k[...]) + dot_nt(dv[...], w_v[...])
    unit, scale = norm_parts(x[...])
    grad_in[...] = grad_middle[...] + norm_back(grad_a, gain[...], unit, scale)


def column_to_row(column):
    return jnp.transpose(jnp.broadcast_to(column, (column.shape[0], LANES)))[:1]


def fold_lanes(values):
    return sum(
        values[:, at : at + LANES] for at in range(0, values.shape[1], LANES)
    )


def part_order(batch):
    order, bit = [0], batch // 2
    while bit >= 1:
        order = order + [step ^ bit for step in order]
        bit //= 2
    return order


def grads_kernel(parts, attention, feed_forward, source_count, place, *refs):
    refs = list(refs)
    sources = [refs.pop(0) for _ in range(source_count)]
    halves = source_count == 2 * HEADS
    weights = [refs.pop(0) for _ in range(4 * attention + 2 * feed_forward)]
    outs = [refs.pop(0) for _ in range(5 * attention + 3 * feed_forward)]
    me, seat = place[0], place[1]
    order = part_order(parts)
    copies = []

    def send(source, target, semaphore):
        copy = pltpu.make_async_copy(source, target, semaphore)
        copy.start()
        copies.append(copy)

    def rows_of(step):
        if source_count == 1:
            return sources[0].ready(step).at[step], step
        return sources[step], me ^ step

    def part_of(step, source, at, first, size):
        count = parts
        if halves:
            source, count, at = sources[step + (HEADS if 2 * at >= parts else 0)], parts // 2, at % (parts // 2)
        first += at * (source.shape[0] // count)
        return source[first : first + size]

    for layer in range(attention):
        w_q, w_k, w_v, gain_a = weights[4 * layer : 4 * layer + 4]
        grad_q, grad_k, grad_v, grad_o, grad_gain_a = outs[5 * layer : 5 * layer + 5]
        heads, square, over, sems_a = refs[4 * layer : 4 * layer + 4]
        width = grad_q.shape[0]
        half, at_rows = width // 2, width // 2 // parts
        for step in range(HEADS):
            source, owner = rows_of(step)
            for at, peer in enumerate(order):
                heads[owner, rows_at((seat ^ peer) * at_rows, at_rows, 16), :] = part_of(
                    step, source, at, layer * at_rows, at_rows
                )
        low = lower_half(half)
        total = None
        for chunk in range(HEADS // 2):
            cut = slice(chunk * LANES, (chunk + 1) * LANES)
            for part in range(2):
                rows = slice(part * half, (part + 1) * half)
                lanes = slice(part * LANES, (part + 1) * LANES)
                even = heads[2 * chunk, :, lanes].astype(F32)
                odd = heads[2 * chunk + 1, :, lanes].astype(F32)
                square[0, chunk, rows] = jnp.where(low, even, turn(odd))
                square[1, chunk, rows] = jnp.where(low, turn(even), odd)
            even = heads[2 * chunk, :, 2 * LANES : 3 * LANES].astype(F32)
            odd = heads[2 * chunk + 1, :, 2 * LANES : 3 * LANES].astype(F32)
            square[2, chunk, :half] = jnp.where(low, even, turn(odd))
            square[2, chunk, half:] = jnp.where(low, turn(even), odd)
            for head in (2 * chunk, 2 * chunk + 1):
                for lane in range(width // LANES):
                    over[head, :, lane * LANES : (lane + 1) * LANES] = heads[
                        head, lane * HEAD : (lane + 1) * HEAD, 3 * LANES :
                    ].astype(F32)
                send(
                    over.at[head],
                    grad_o.at[pl.ds(head * HEAD, HEAD), :],
                    sems_a.at[3 + head % 2, chunk],
                )
            for at, target in enumerate((grad_q, grad_k, grad_v)):
                send(
                    square.at[at, chunk],
                    target.at[:, pl.ds(chunk * LANES, LANES)],
                    sems_a.at[at, chunk],
                )
            term = (
                w_q[:, cut].astype(F32) * square[0, chunk]
                + w_k[:, cut].astype(F32) * square[1, chunk]
                + w_v[:, cut].astype(F32) * square[2, chunk]
            )
            total = term if total is None else total + term
        total = jnp.sum(total, axis=-1, keepdims=True)
        grad_gain_a[...] = column_to_row(total) / gain_a[...]

    if feed_forward:
        w_e, gain_f = weights[-2:]
        contract, expand, grad_gain_f = outs[-3:]
        share, acc, sems = refs[4 * attention : 4 * attention + 3]
        width = expand.shape[0]
        half = width // 2
        ff_own = contract.shape[0] // HEADS
        ff_rows = 2 * ff_own // parts
        acc[...] = jnp.zeros(acc.shape, F32)
        for step in range(HEADS):
            source, owner = rows_of(step)
            for at, peer in enumerate(order):
                share[step, rows_at((seat ^ peer) * ff_rows, ff_rows, 16), :] = part_of(
                    step, source, at, 0, ff_rows
                ).astype(F32)
            own = pl.ds(pl.multiple_of(owner * ff_own, ff_own), ff_own)
            send(share.at[step, pl.ds(0, ff_own), :], contract.at[own, :], sems.at[step, 0])
            for side in range(2):
                lanes = pl.ds(side * half, half)
                send(
                    share.at[step, pl.ds(ff_own, ff_own), lanes],
                    expand.at[pl.ds(side * half, half), own],
                    sems.at[step, 1 + side],
                )
                acc[side * half : (side + 1) * half] += fold_lanes(
                    w_e[side * half : (side + 1) * half, own].astype(F32)
                    * share[step, ff_own:, side * half : (side + 1) * half]
                )
        total = jnp.sum(acc[...], axis=-1, keepdims=True)
        grad_gain_f[...] = column_to_row(total) / gain_f[...]
    for copy in copies:
        copy.wait()


COST = 1.15e9


def call(kernel, out_shape, scratch, arguments, late=(), limit=16, in_hbm=(), kept=(), us=5):
    late = [entry if isinstance(entry, tuple) else (entry,) for entry in late]
    late = [entry + (None, None, 0, 1)[len(entry) - 1 :] for entry in late]
    specs = [pl.BlockSpec(memory_space=pltpu.SMEM)]
    specs += [pl.BlockSpec(memory_space=pltpu.VMEM)] * (len(arguments) - 1)
    buffers, arguments = [], list(arguments)
    for at, shape, *_ in late:
        specs[at] = pl.BlockSpec(memory_space=pltpu.HBM)
        buffers.append(pltpu.VMEM(shape or arguments[at].shape, arguments[at].dtype))
        arguments[at] = pltpu.with_memory_space_constraint(arguments[at], pltpu.HBM)
    body, semaphores = kernel, []
    if late:
        semaphores = [pltpu.SemaphoreType.DMA((sum(entry[4] for entry in late),))]
        body = partial(with_late, kernel, late, len(arguments), len(out_shape))
    return pl.pallas_call(
        body,
        out_shape=[
            (pltpu.HBM if at in in_hbm or at in kept else jax.ShapeDtypeStruct)(*entry)
            for at, entry in enumerate(out_shape)
        ],
        in_specs=specs,
        out_specs=[
            pl.BlockSpec(memory_space=pltpu.HBM if at in in_hbm else pltpu.VMEM)
            for at in range(len(out_shape))
        ],
        scratch_shapes=[
            pltpu.VMEM(*entry) if isinstance(entry, tuple) else entry for entry in scratch
        ]
        + buffers
        + semaphores,
        compiler_params=pltpu.CompilerParams(vmem_limit_bytes=limit * 2**20),
        cost_estimate=pl.CostEstimate(
            flops=int(us * COST), bytes_accessed=2**20, transcendentals=0
        ),
    )(*arguments)


def exchange(pieces, axis):
    devices = range(lax.axis_size(axis))
    moved = {
        step: lax.ppermute(pieces[step], axis, [(i, i ^ step) for i in devices])
        for step in reversed(range(1, len(pieces)))
    }
    return [pieces[0]] + [moved[step] for step in range(1, len(pieces))]


def after(values, *others):
    return lax.optimization_barrier((values, others))[0]


def phase(*values):
    return lax.optimization_barrier(values)


def swap(block, axis, step):
    return lax.ppermute(block, axis, [(i, i ^ step) for i in range(lax.axis_size(axis))])


def near_exchange(pairs):
    moved = {step: swap(pairs[step], "seq", 2 * step) for step in reversed(range(1, len(pairs)))}
    first = [pairs[0]] + [moved[step] for step in range(1, len(pairs))]
    return first + [swap(pair, "seq", 1) for pair in first]


def summed(pieces):
    return sum(piece.astype(F32) for piece in pieces).astype(BF16)


def sum_step(keep, arrived, bit):
    total = keep.astype(F32) + arrived.astype(F32)
    parts = lax.axis_size("batch") // (2 * bit)
    if parts <= 1:
        return total.astype(BF16), None
    total = total.reshape(parts // 2, 2, -1, total.shape[1])
    return (
        total[:, 0].reshape(-1, total.shape[-1]),
        total[:, 1].reshape(-1, total.shape[-1]).astype(BF16),
    )


def near_gather(block, *beside):
    found = {0: block}
    for step in (6, 4, 2):
        found[step] = swap(block, "seq", step)
    for step in (0, 2, 4, 6):
        found[step] = after(found[step], *beside) if beside else found[step]
        found[step + 1] = swap(found[step], "seq", 1)
    return [found[step] for step in range(HEADS)]


def gather(block):
    return lax.all_gather(block, "seq", axis=0, tiled=True)


def whole_grads(place, sources, batch, attention=(), feed_forward=None):
    width = sources[0].shape[-1]
    square, row = ((width, width), F32), ((1, width), F32)
    arguments, out_shape, scratch = [place, *sources], [], []
    late = [(1, None, None, 0, HEADS)] if len(sources) == 1 else []
    in_hbm = []
    for params in attention:
        first = len(arguments)
        arguments += [params[1], params[2], params[3], params[0]]
        late += [first, first + 1, first + 2]
        first = len(out_shape)
        in_hbm += [first, first + 1, first + 2, first + 3]
        out_shape += [square] * 4 + [row]
        scratch += [
            ((HEADS, width // 2, width), BF16),
            ((3, HEADS // 2, width, LANES), F32),
            ((HEADS, HEAD, width), F32),
            pltpu.SemaphoreType.DMA((5, HEADS // 2)),
        ]
    if feed_forward is not None:
        ff = feed_forward[6].shape[1]
        late += [len(arguments)]
        arguments += [feed_forward[6], feed_forward[5]]
        in_hbm += [len(out_shape), len(out_shape) + 1]
        out_shape += [((ff, width), F32), ((width, ff), F32), row]
        scratch += [
            ((HEADS, 2 * ff // HEADS, width), F32),
            ((width, LANES), F32),
            pltpu.SemaphoreType.DMA((HEADS, 3)),
        ]
    return call(
        partial(grads_kernel, batch, len(attention), feed_forward is not None, len(sources)),
        out_shape,
        scratch,
        tuple(arguments),
        late,
        32,
        in_hbm,
    )


def by_heads(inputs, cotangent, *weights):
    full = (weights[0][None],) + weights[1:5] + (weights[5][None],) + weights[6:8]
    brief = (weights[8][None],) + weights[9:13] + (weights[13][None],) + weights[14:16]
    x, cot = inputs[0], cotangent[0]
    rows, width = x.shape
    short, half, total = rows // 3, rows // 2, rows * HEADS
    batch = lax.axis_size("batch")
    ff = full[6].shape[1]
    ff_own = ff // HEADS
    count = short * HEADS
    chunks = width // LANES
    place = jnp.stack([lax.axis_index("seq"), lax.axis_index("batch")]).astype(jnp.int32)
    table = rope_constants(total)
    block = rows + half

    outs = call(
        project_kernel,
        [((2 * block, LANES), BF16)] * (HEADS // 2)
        + [((rows, width), BF16), ((rows + short, width), BF16)],
        [((HEADS, block, LANES), BF16), ((chunks, rows, LANES), F32)],
        (place, x, cot, full[0], full[1], full[2], full[3], table),
        (
            1,
            4,
            5,
            6,
            (7, (rows, 2 * LANES), lambda ref, me: ref.at[rows_at(me * rows, rows, 16), :]),
            2,
        ),
        kept=(HEADS // 2, HEADS // 2 + 1),
    )
    pieces, (normed_a, bundle) = near_exchange(outs[: HEADS // 2]), outs[HEADS // 2 :]
    bundles = gather(bundle).reshape(HEADS, rows + short, width)

    outs = call(
        attend_kernel,
        [((rows, LANES), BF16)] * (HEADS // 2)
        + [((total, LANES), BF16), ((total, LANES), BF16), ((total, LANES), F32)],
        [],
        (place, *pieces),
        kept=range(HEADS // 2, HEADS // 2 + 3),
    )
    pieces = near_exchange(outs[: HEADS // 2])
    q_all, kv_all, lse_o = outs[HEADS // 2 :]

    residual, middle, att, normed_f, pooled = call(
        finish_kernel,
        [
            ((rows, width), F32),
            ((rows, width), F32),
            ((rows, width), BF16),
            ((2 * rows, width), BF16),
            ((short + 16, width), BF16),
        ],
        [((HEADS, half, LANES), F32), ((chunks, rows + 8, LANES), F32)],
        (place, x, normed_a, full[5], full[4], full[6], full[7], *pieces),
        (4, 1, (5, None, None, 1, FF_PARTS), (6, None, None, 0, FF_PARTS), 2),
        kept=range(4),
    )
    pieces = near_gather(pooled)
    normed_all = gather(normed_f).reshape(HEADS, 2 * rows, width)

    outs = call(
        short_forward_kernel,
        [
            ((rows, width), F32),
            ((count, width), F32),
            ((count, width), BF16),
            ((HEADS, count, LANES), BF16),
            ((chunks, count, LANES), BF16),
            ((chunks, count, LANES), BF16),
            ((chunks, count, LANES), F32),
            ((chunks, count, LANES), F32),
            ((count, width), BF16),
            ((count, width), F32),
        ]
        + [((2 * ff_own // batch, width), BF16)] * batch,
        [
            ((HEADS, width), F32),
            ((count, width), F32),
            ((count, width), BF16),
            ((count, ff), BF16),
            ((count, ff), BF16),
            ((count, width), F32),
            ((count, width), BF16),
            ((chunks, rows, LANES), F32),
            ((2 * ff_own, width), BF16),
        ],
        (place, residual, bundles, table[:count]) + brief + tuple(pieces),
        (
            5,
            3,
            6,
            7,
            8,
            10,
            11,
            (2, (HEADS, short, width), lambda ref, me: ref.at[:, pl.ds(rows, short), :]),
            1,
        ),
        22,
        kept=(0,),
        us=16,
    )
    output, saved = outs[0], outs[1:10]
    a_at, saved = phase(outs[10:], saved)
    a_at = exchange(a_at, "batch")
    outs = call(
        short_back_kernel,
        [
            ((total, width), BF16),
            ((width // 2, width), BF16),
            ((rows, width), F32),
            ((rows, width), BF16),
        ],
        [
            ((HEADS, count, LANES), BF16),
            ((count, width), BF16),
            ((count, width), BF16),
            ((count, width), BF16),
            ((chunks, total + 16, LANES), F32),
            ((LANES, width), F32),
            ((rows, width), F32),
        ],
        (place, cot, bundles, table[:count])
        + brief[:5]
        + tuple(saved)
        + (middle, normed_f, full[5], full[6], full[7]),
        (
            8,
            3,
            5,
            6,
            7,
            (2, (HEADS, rows, width), lambda ref, me: ref.at[:, pl.ds(0, rows), :]),
            1,
            21,
            22,
            (19, (rows, width), lambda ref, me: ref.at[pl.ds(0, rows), :]),
            18,
        ),
        25,
        kept=range(3),
        us=18,
    )
    a_at, (grad_all, short_share, grad_middle, g1) = phase(a_at, outs)

    a_all, g1, grad_all = phase(summed(a_at), g1, grad_all)
    a_at = swap(a_all, "batch", 2)
    outs = call(
        partial(feed_forward_share_kernel, batch),
        [((ff_own, width), BF16)] * 2,
        [((2 * ff_own, width), BF16)],
        (place, normed_all, grad_all, full[6], full[7]),
        (
            (1, (HEADS, rows, width), lambda ref, me: ref.at[:, pl.ds(0, rows), :]),
            (3, (width, ff_own), lambda ref, me: ref.at[:, rows_at(me * ff_own, ff_own, ff_own)]),
            2,
            (4, (ff_own, width), lambda ref, me: ref.at[rows_at(me * ff_own, ff_own, ff_own), :]),
        ),
        22,
    )
    g1_all = near_gather(g1, outs[1], a_at)
    a_at, g1_all, (b_keep, b_send) = phase(a_at, g1_all, outs)

    a_all = jnp.concatenate([a_all, a_at])
    a_all, g1_all, b_send = phase(a_all, g1_all, b_send)
    a_at = swap(a_all, "batch", 1)
    b_at = swap(b_send, "batch", 1)
    outs = call(
        attend_back_kernel,
        [((2 * block, LANES), BF16)] * (HEADS // 2)
        + [((total, LANES), BF16), ((total, LANES), BF16)],
        [
            ((total, LANES), BF16),
            ((total, LANES), F32),
            ((total, LANES), F32),
            ((LANES, total), BF16),
            ((LANES, total), BF16),
        ],
        (place, q_all, kv_all, lse_o, table, full[4], *g1_all),
        (
            (5, (HEAD, width), lambda ref, me: ref.at[rows_at(me * HEAD, HEAD, HEAD), :]),
            1,
            2,
            3,
            4,
        ),
        us=7,
    )
    a_at, b_at, outs = phase(a_at, b_at, outs)
    a_shares = gather(jnp.concatenate([a_all, a_at])[None])
    pieces, (dq_all, dkv_all) = outs[: HEADS // 2], outs[HEADS // 2 :]

    b_keep, b_send = sum_step(b_keep, b_at, 1)
    b_send, dq_all = phase(b_send, dq_all)
    b_at = swap(b_send, "batch", 2)
    outs = call(
        partial(attention_share_kernel, batch),
        [((width // 2, width), BF16)] * 2,
        [((width // 2, width), BF16)],
        (place, normed_all, dq_all, dkv_all, lse_o, short_share, *g1_all),
        ((1, (HEADS, rows, width), lambda ref, me: ref.at[:, pl.ds(rows, rows), :]), 4, 5),
        us=3,
    )
    b_at, pieces, (c_keep, c_send) = phase(b_at, pieces, outs)

    b_all, _ = sum_step(b_keep, b_at, 2)
    b_all, pieces, c_send = phase(b_all, pieces, c_send)
    b_at = swap(b_all, "batch", 2)
    c_at = swap(c_send, "batch", 1)
    pieces = {step: pieces[step] for step in range(HEADS // 2)}
    moved = {step: swap(pieces[step], "seq", 2 * step) for step in (3, 2)}
    b_at, c_at, moved, pieces = phase(b_at, c_at, moved, pieces)

    b_all = jnp.concatenate([b_all, b_at])
    c_keep, c_send = sum_step(c_keep, c_at, 1)
    b_all, c_send, pieces = phase(b_all, c_send, pieces)
    b_at = swap(b_all, "batch", 1)
    c_at = swap(c_send, "batch", 2)
    moved |= {0: pieces[0], 1: swap(pieces[1], "seq", 2)}
    b_at, c_at, moved, pieces = phase(b_at, c_at, moved, pieces)

    b_all = jnp.concatenate([b_all, b_at])
    c_all, _ = sum_step(c_keep, c_at, 2)
    b_all, c_all, moved = phase(b_all, c_all, moved)
    b_shares = gather(b_all[None])
    c_at = swap(c_all, "batch", 2)
    across = {step: swap(moved[step], "seq", 1) for step in range(HEADS // 2)}
    c_at, moved, across = phase(c_at, moved, across)

    c_all, moved, across = phase(jnp.concatenate([c_all, c_at]), moved, across)
    first = {0: c_all, 2: swap(c_all, "seq", 2), 4: swap(c_all, "seq", 4)}
    c_at = swap(c_all, "batch", 1)
    pieces = [side[step] for side in (moved, across) for step in range(HEADS // 2)]
    (grad_in,) = call(
        start_back_kernel,
        [((rows, width), F32)],
        [((HEADS, block, LANES), BF16)] + [((rows, width), BF16)] * 3,
        (place, x, grad_middle, full[0], full[1], full[2], full[3], *pieces),
        (4, 5, 6, 1, 2),
        us=4,
    )
    c_at, first, grad_in = phase(c_at, first, grad_in)
    other = {0: c_at, 2: swap(c_at, "seq", 2), 4: swap(c_at, "seq", 4)}
    first |= {6: swap(first[2], "seq", 4)}
    other |= {6: swap(other[4], "seq", 2)}
    short_ff_grads = whole_grads(place, [after(a_shares, grad_in)], batch, (), brief)
    first = after(first, grad_in, short_ff_grads[0])
    other = after(other, grad_in, short_ff_grads[0])
    found = [
        half | {step + 1: swap(half[step], "seq", 1) for step in (0, 2, 4, 6)}
        for half in (first, other)
    ]
    c_shares = [half[step] for half in found for step in range(HEADS)]
    at_grads = whole_grads(place, c_shares, batch, (full, brief))
    full_ff_grads = whole_grads(place, [after(b_shares, at_grads[0])], batch, (), full)

    def arranged(attention, feed_forward):
        grad_q, grad_k, grad_v, grad_o, grad_gain_a = attention
        contract, expand, grad_gain_f = feed_forward
        return (grad_gain_a[0], grad_q, grad_k, grad_v, grad_o, grad_gain_f[0], expand, contract)

    return (
        (output[None], grad_in[None])
        + arranged(at_grads[:5], full_ff_grads)
        + arranged(at_grads[5:], short_ff_grads)
    )


def from_behind(block, axis, distance):
    devices = range(lax.axis_size(axis))
    route = [(i - distance, i) for i in devices if i - distance in devices]
    return lax.ppermute(block, axis, route)


def normalize(stream, gain):
    row_mean = jnp.mean(stream, axis=-1, keepdims=True)
    centered = stream - row_mean
    spread = jnp.mean(centered * centered, axis=-1, keepdims=True)
    return centered * lax.rsqrt(spread + norm_eps) * gain


def rope_table(positions):
    half_size = HEAD // 2
    frequency = jnp.power(10000.0, -jnp.arange(half_size, dtype=jnp.float32) * 2.0 / HEAD)
    angles = positions.astype(jnp.float32)[:, None] * frequency[None, :]
    return (jnp.cos(angles)[:, None, :], jnp.sin(angles)[:, None, :])


def rotate(values, angle_cos, angle_sin):
    first_half, second_half = jnp.split(values, 2, axis=-1)
    return jnp.concatenate(
        [
            first_half * angle_cos - second_half * angle_sin,
            first_half * angle_sin + second_half * angle_cos,
        ],
        axis=-1,
    )


def rotate_back(grads, angle_cos, angle_sin):
    first_half, second_half = jnp.split(grads, 2, axis=-1)
    return jnp.concatenate(
        [
            first_half * angle_cos + second_half * angle_sin,
            second_half * angle_cos - first_half * angle_sin,
        ],
        axis=-1,
    )


def split_heads(matrix):
    return matrix.reshape(matrix.shape[0], HEADS, HEAD)


def project(stream, params, angle_cos, angle_sin):
    normed_in = normalize(stream, params[0]).astype(jnp.bfloat16)

    def heads_of(matrix):
        return split_heads(jnp.dot(normed_in, matrix, preferred_element_type=jnp.float32))

    queries = rotate(heads_of(params[1]), angle_cos, angle_sin).astype(jnp.bfloat16)
    keys_here = rotate(heads_of(params[2]), angle_cos, angle_sin).astype(jnp.bfloat16)
    values_here = heads_of(params[3]).astype(jnp.bfloat16)
    return (normed_in, queries, keys_here, values_here)


def masked_scores(queries, keys_all, query_places, key_places):
    scores = jnp.einsum(
        "nhe,mhe->hnm", queries, keys_all, preferred_element_type=jnp.float32
    ) * HEAD ** (-0.5)
    allowed = key_places[None, None, :] <= query_places[None, :, None]
    return jnp.where(allowed, scores, -1e30)


def attend(queries, keys_all, values_all, query_places, key_places):
    scores = masked_scores(queries, keys_all, query_places, key_places)
    highest_score = jnp.max(scores, axis=-1, keepdims=True)
    log_total = highest_score + jnp.log(
        jnp.sum(jnp.exp(scores - highest_score), axis=-1, keepdims=True)
    )
    prob_low = jnp.exp(scores - log_total).astype(jnp.bfloat16)
    attended = jnp.einsum("hnm,mhe->nhe", prob_low, values_all, preferred_element_type=jnp.float32)
    return (attended, log_total)


def attend_back(queries, keys_all, values_all, query_places, key_places, log_total, grad_attended):
    scores = masked_scores(queries, keys_all, query_places, key_places)
    probs_full = jnp.exp(scores - log_total)
    grad_probs = jnp.einsum(
        "nhe,mhe->hnm", grad_attended, values_all, preferred_element_type=jnp.float32
    )
    row_inner = jnp.sum(probs_full * grad_probs, axis=-1, keepdims=True)
    grad_scores = (probs_full * (grad_probs - row_inner)).astype(jnp.bfloat16)
    grad_queries = jnp.einsum(
        "hnm,mhe->nhe", grad_scores, keys_all, preferred_element_type=jnp.float32
    ) * HEAD ** (-0.5)
    return (grad_queries, grad_scores, probs_full.astype(jnp.bfloat16), row_inner)


def finish(stream, attended, params):
    row_count, width = stream.shape
    attended_low = attended.reshape(row_count, width).astype(jnp.bfloat16)
    middle = stream + jnp.dot(attended_low, params[4], preferred_element_type=jnp.float32)
    normed_mid = normalize(middle, params[5]).astype(jnp.bfloat16)
    hidden_pre = jnp.dot(normed_mid, params[6], preferred_element_type=jnp.float32)
    hidden_low = jax.nn.gelu(hidden_pre, approximate=True).astype(jnp.bfloat16)
    result = middle + jnp.dot(hidden_low, params[7], preferred_element_type=jnp.float32)
    return (result, (attended_low, middle, normed_mid, hidden_pre, hidden_low))


def finish_back(grad_result, finish_saved, params):
    attended_low, middle, normed_mid, hidden_pre, hidden_low = finish_saved
    grad_low = grad_result.astype(jnp.bfloat16)
    grad_contract = jnp.einsum(
        "nf,nd->fd", hidden_low, grad_low, preferred_element_type=jnp.float32
    )
    grad_hidden = jnp.einsum("nd,fd->nf", grad_low, params[7], preferred_element_type=jnp.float32)
    gelu_value, gelu_pull = jax.vjp(partial(jax.nn.gelu, approximate=True), hidden_pre)
    grad_pre = gelu_pull(grad_hidden)[0].astype(jnp.bfloat16)
    grad_expand = jnp.einsum("nd,nf->df", normed_mid, grad_pre, preferred_element_type=jnp.float32)
    grad_normed = jnp.einsum("nf,df->nd", grad_pre, params[6], preferred_element_type=jnp.float32)
    norm_value, norm_pull = jax.vjp(normalize, middle, params[5])
    grad_norm_in, grad_gain_ffn = norm_pull(grad_normed)
    grad_middle = grad_result + grad_norm_in
    middle_low = grad_middle.astype(jnp.bfloat16)
    grad_output_w = jnp.einsum(
        "nc,nd->cd", attended_low, middle_low, preferred_element_type=jnp.float32
    )
    grad_attended = split_heads(
        jnp.einsum("nd,cd->nc", middle_low, params[4], preferred_element_type=jnp.float32).astype(
            jnp.bfloat16
        )
    )
    return (grad_middle, grad_attended, grad_output_w, grad_expand, grad_contract, grad_gain_ffn)


def start_back(
    grad_queries, grad_keys, grad_values, stream, params, normed_in, angle_cos, angle_sin
):
    row_count, width = stream.shape
    query_low = (
        rotate_back(grad_queries, angle_cos, angle_sin)
        .reshape(row_count, width)
        .astype(jnp.bfloat16)
    )
    key_low = (
        rotate_back(grad_keys, angle_cos, angle_sin).reshape(row_count, width).astype(jnp.bfloat16)
    )
    value_low = grad_values.reshape(row_count, width).astype(jnp.bfloat16)
    grad_query = jnp.einsum("nd,nc->dc", normed_in, query_low, preferred_element_type=jnp.float32)
    grad_key = jnp.einsum("nd,nc->dc", normed_in, key_low, preferred_element_type=jnp.float32)
    grad_value = jnp.einsum("nd,nc->dc", normed_in, value_low, preferred_element_type=jnp.float32)
    grad_normed = (
        jnp.einsum("nc,dc->nd", query_low, params[1], preferred_element_type=jnp.float32)
        + jnp.einsum("nc,dc->nd", key_low, params[2], preferred_element_type=jnp.float32)
        + jnp.einsum("nc,dc->nd", value_low, params[3], preferred_element_type=jnp.float32)
    )
    norm_value, norm_pull = jax.vjp(normalize, stream, params[0])
    grad_stream, grad_gain_attn = norm_pull(grad_normed)
    return (grad_stream, grad_gain_attn, grad_query, grad_key, grad_value)


def local_forward(stream, places, params, fetch):
    angle_cos, angle_sin = rope_table(places)
    normed_in, queries, keys_here, values_here = project(stream, params, angle_cos, angle_sin)
    row_count, width = stream.shape
    keys_local = keys_here.reshape(row_count, width)
    values_local = values_here.reshape(row_count, width)
    keys_flat, values_flat = fetch(keys_local, values_local)
    key_places = jnp.arange(keys_flat.shape[0], dtype=jnp.int32)
    attended, log_total = attend(
        queries, split_heads(keys_flat), split_heads(values_flat), places, key_places
    )
    result, finish_saved = finish(stream, attended, params)
    return (
        result,
        (
            normed_in,
            queries,
            keys_local,
            values_local,
            keys_flat,
            values_flat,
            log_total,
            angle_cos,
            angle_sin,
            finish_saved,
        ),
    )


def local_backward(grad_result, stream, places, params, saved, keys_flat, values_flat, key_sum):
    normed_in, queries = (saved[0], saved[1])
    log_total, angle_cos, angle_sin, finish_saved = (saved[6], saved[7], saved[8], saved[9])
    grad_middle, grad_attended, grad_output_w, grad_expand, grad_contract, grad_gain_ffn = (
        finish_back(grad_result, finish_saved, params)
    )
    row_count, width = stream.shape
    key_places = jnp.arange(keys_flat.shape[0], dtype=jnp.int32)
    grad_queries, grad_scores, prob_low, row_inner = attend_back(
        queries,
        split_heads(keys_flat),
        split_heads(values_flat),
        places,
        key_places,
        log_total,
        grad_attended,
    )

    def contribution(first_row, term_rows):
        grad_keys = jnp.einsum(
            "hnm,nhe->mhe", grad_scores, queries, preferred_element_type=jnp.float32
        ) * HEAD ** (-0.5)
        grad_values = jnp.einsum(
            "hnm,nhe->mhe", prob_low, grad_attended, preferred_element_type=jnp.float32
        )
        return jnp.concatenate(
            [grad_keys.reshape(term_rows, width), grad_values.reshape(term_rows, width)], axis=1
        )

    both_grads = key_sum(contribution, row_count, (queries, grad_attended, log_total, row_inner))
    grad_stream, grad_gain_attn, grad_query, grad_key, grad_value = start_back(
        grad_queries,
        split_heads(both_grads[:, :width]),
        split_heads(both_grads[:, width:]),
        stream,
        params,
        normed_in,
        angle_cos,
        angle_sin,
    )
    return (
        grad_middle + grad_stream,
        (
            grad_gain_attn,
            grad_query,
            grad_key,
            grad_value,
            grad_output_w,
            grad_gain_ffn,
            grad_expand,
            grad_contract,
        ),
    )


def whole_forward(stream, params):
    row_count, width = stream.shape
    places = jnp.arange(row_count, dtype=jnp.int32)
    angle_cos, angle_sin = rope_table(places)
    normed_in, queries, keys_here, values_here = project(stream, params, angle_cos, angle_sin)
    block_rows = 512
    block_count = row_count // block_rows

    def one_block(pieces):
        return attend(pieces[0], keys_here, values_here, pieces[1], places)

    attended, log_total = lax.map(
        one_block,
        (
            queries.reshape(block_count, block_rows, HEADS, HEAD),
            places.reshape(block_count, block_rows),
        ),
    )
    result, finish_saved = finish(stream, attended.reshape(row_count, HEADS, HEAD), params)
    return (
        result,
        (normed_in, queries, keys_here, values_here, log_total, angle_cos, angle_sin, finish_saved),
    )


def whole_backward(grad_result, stream, params, saved):
    normed_in, queries, keys_here, values_here, log_total, angle_cos, angle_sin, finish_saved = (
        saved
    )
    grad_middle, grad_attended, grad_output_w, grad_expand, grad_contract, grad_gain_ffn = (
        finish_back(grad_result, finish_saved, params)
    )
    row_count, width = stream.shape
    places = jnp.arange(row_count, dtype=jnp.int32)
    block_rows = 512
    block_count = row_count // block_rows

    def one_block(running, pieces):
        query_block, place_block, total_block, grad_block = pieces
        grad_queries, grad_scores, prob_low, row_inner = attend_back(
            query_block, keys_here, values_here, place_block, places, total_block, grad_block
        )
        grad_keys = running[0] + jnp.einsum(
            "hnm,nhe->mhe", grad_scores, query_block, preferred_element_type=jnp.float32
        ) * HEAD ** (-0.5)
        grad_values = running[1] + jnp.einsum(
            "hnm,nhe->mhe", prob_low, grad_block, preferred_element_type=jnp.float32
        )
        return ((grad_keys, grad_values), grad_queries)

    zero_grads = jnp.zeros((row_count, HEADS, HEAD), jnp.float32)
    (grad_keys, grad_values), grad_queries = lax.scan(
        one_block,
        (zero_grads, zero_grads),
        (
            queries.reshape(block_count, block_rows, HEADS, HEAD),
            places.reshape(block_count, block_rows),
            log_total,
            grad_attended.reshape(block_count, block_rows, HEADS, HEAD),
        ),
    )
    grad_stream, grad_gain_attn, grad_query, grad_key, grad_value = start_back(
        grad_queries.reshape(row_count, HEADS, HEAD),
        grad_keys,
        grad_values,
        stream,
        params,
        normed_in,
        angle_cos,
        angle_sin,
    )
    return (
        grad_middle + grad_stream,
        (
            grad_gain_attn,
            grad_query,
            grad_key,
            grad_value,
            grad_output_w,
            grad_gain_ffn,
            grad_expand,
            grad_contract,
        ),
    )


def by_rows(
    inputs,
    cotangent,
    full_gain_attn,
    full_query,
    full_key,
    full_value,
    full_output,
    full_gain_ffn,
    full_expand,
    full_contract,
    short_gain_attn,
    short_query,
    short_key,
    short_value,
    short_output,
    short_gain_ffn,
    short_expand,
    short_contract,
):
    full_params = (
        full_gain_attn,
        full_query,
        full_key,
        full_value,
        full_output,
        full_gain_ffn,
        full_expand,
        full_contract,
    )
    short_params = (
        short_gain_attn,
        short_query,
        short_key,
        short_value,
        short_output,
        short_gain_ffn,
        short_expand,
        short_contract,
    )
    stream_in = inputs[0]
    row_count, width = stream_in.shape
    own_short = row_count // 3
    position = lax.axis_index("seq")
    seq_parts = lax.axis_size("seq")
    places = position * row_count + jnp.arange(row_count, dtype=jnp.int32)

    def fetch_full(keys_local, values_local):
        return (
            lax.all_gather(keys_local, "seq", axis=0, tiled=True),
            lax.all_gather(values_local, "seq", axis=0, tiled=True),
        )

    residual, full_saved = local_forward(stream_in, places, full_params, fetch_full)
    tail_rows = from_behind(residual[row_count - 2 :], "seq", 1)
    shifted = jnp.concatenate([tail_rows, residual[: row_count - 2]], axis=0)
    pooled = jnp.mean(shifted.reshape(own_short, 3, width), axis=1)
    pooled_all = lax.all_gather(pooled, "seq", axis=0, tiled=True)
    short_all, short_saved = whole_forward(pooled_all, short_params)
    short_result = lax.dynamic_slice_in_dim(short_all, position * own_short, own_short, 0)
    output = residual + jnp.repeat(short_result, 3, axis=0)
    grad_output = cotangent[0]
    grad_short = jnp.sum(grad_output.reshape(own_short, 3, width), axis=1)
    grad_short_all = lax.all_gather(grad_short, "seq", axis=0, tiled=True)
    grad_pooled_all, short_grads = whole_backward(
        grad_short_all, pooled_all, short_params, short_saved
    )
    grad_pooled = lax.dynamic_slice_in_dim(grad_pooled_all, position * own_short, own_short, 0)
    short_grads = tuple(
        (
            lax.dynamic_slice_in_dim(
                gradient,
                position * (gradient.shape[0] // seq_parts),
                gradient.shape[0] // seq_parts,
                0,
            )
            for gradient in short_grads
        )
    )
    grad_shifted = jnp.repeat(grad_pooled / 3.0, 3, axis=0)
    carried = from_behind(grad_shifted[:2], "seq", -1)
    grad_residual = grad_output + jnp.concatenate([grad_shifted[2:], carried], axis=0)
    keys_flat, values_flat = (
        lax.all_gather(full_saved[2], "seq", axis=0, tiled=True),
        lax.all_gather(full_saved[3], "seq", axis=0, tiled=True),
    )

    def full_sum(contribution, term_rows, query_side):
        return lax.psum_scatter(
            contribution(jnp.int32(0), term_rows * lax.axis_size("seq")).astype(jnp.bfloat16),
            "seq",
            scatter_dimension=0,
            tiled=True,
        ).astype(jnp.float32)

    grad_input, full_grads = local_backward(
        grad_residual, stream_in, places, full_params, full_saved, keys_flat, values_flat, full_sum
    )
    full_shares = (
        lax.psum_scatter(
            full_grads[0].astype(jnp.bfloat16), "seq", scatter_dimension=0, tiled=True
        ).astype(jnp.float32),
        lax.psum_scatter(
            full_grads[1].astype(jnp.bfloat16), "seq", scatter_dimension=0, tiled=True
        ).astype(jnp.float32),
        lax.psum_scatter(
            full_grads[2].astype(jnp.bfloat16), "seq", scatter_dimension=0, tiled=True
        ).astype(jnp.float32),
        lax.psum_scatter(
            full_grads[3].astype(jnp.bfloat16), "seq", scatter_dimension=0, tiled=True
        ).astype(jnp.float32),
        lax.psum_scatter(
            full_grads[4].astype(jnp.bfloat16), "seq", scatter_dimension=0, tiled=True
        ).astype(jnp.float32),
        lax.psum_scatter(
            full_grads[5].astype(jnp.bfloat16), "seq", scatter_dimension=0, tiled=True
        ).astype(jnp.float32),
        lax.psum_scatter(
            full_grads[6].astype(jnp.bfloat16), "seq", scatter_dimension=0, tiled=True
        ).astype(jnp.float32),
        lax.psum_scatter(
            full_grads[7].astype(jnp.bfloat16), "seq", scatter_dimension=0, tiled=True
        ).astype(jnp.float32),
    )
    shares = tuple(full_shares) + tuple(short_grads)
    totals = (
        lax.psum(shares[0].astype(jnp.bfloat16), "batch").astype(jnp.float32),
        lax.psum(shares[1].astype(jnp.bfloat16), "batch").astype(jnp.float32),
        lax.psum(shares[2].astype(jnp.bfloat16), "batch").astype(jnp.float32),
        lax.psum(shares[3].astype(jnp.bfloat16), "batch").astype(jnp.float32),
        lax.psum(shares[4].astype(jnp.bfloat16), "batch").astype(jnp.float32),
        lax.psum(shares[5].astype(jnp.bfloat16), "batch").astype(jnp.float32),
        lax.psum(shares[6].astype(jnp.bfloat16), "batch").astype(jnp.float32),
        lax.psum(shares[7].astype(jnp.bfloat16), "batch").astype(jnp.float32),
        lax.psum(shares[8].astype(jnp.bfloat16), "batch").astype(jnp.float32),
        lax.psum(shares[9].astype(jnp.bfloat16), "batch").astype(jnp.float32),
        lax.psum(shares[10].astype(jnp.bfloat16), "batch").astype(jnp.float32),
        lax.psum(shares[11].astype(jnp.bfloat16), "batch").astype(jnp.float32),
        lax.psum(shares[12].astype(jnp.bfloat16), "batch").astype(jnp.float32),
        lax.psum(shares[13].astype(jnp.bfloat16), "batch").astype(jnp.float32),
        lax.psum(shares[14].astype(jnp.bfloat16), "batch").astype(jnp.float32),
        lax.psum(shares[15].astype(jnp.bfloat16), "batch").astype(jnp.float32),
    )
    whole = (
        lax.all_gather(totals[0].astype(jnp.bfloat16), "seq", axis=0, tiled=True).astype(
            jnp.float32
        ),
        lax.all_gather(totals[1].astype(jnp.bfloat16), "seq", axis=0, tiled=True).astype(
            jnp.float32
        ),
        lax.all_gather(totals[2].astype(jnp.bfloat16), "seq", axis=0, tiled=True).astype(
            jnp.float32
        ),
        lax.all_gather(totals[3].astype(jnp.bfloat16), "seq", axis=0, tiled=True).astype(
            jnp.float32
        ),
        lax.all_gather(totals[4].astype(jnp.bfloat16), "seq", axis=0, tiled=True).astype(
            jnp.float32
        ),
        lax.all_gather(totals[5].astype(jnp.bfloat16), "seq", axis=0, tiled=True).astype(
            jnp.float32
        ),
        lax.all_gather(totals[6].astype(jnp.bfloat16), "seq", axis=0, tiled=True).astype(
            jnp.float32
        ),
        lax.all_gather(totals[7].astype(jnp.bfloat16), "seq", axis=0, tiled=True).astype(
            jnp.float32
        ),
        lax.all_gather(totals[8].astype(jnp.bfloat16), "seq", axis=0, tiled=True).astype(
            jnp.float32
        ),
        lax.all_gather(totals[9].astype(jnp.bfloat16), "seq", axis=0, tiled=True).astype(
            jnp.float32
        ),
        lax.all_gather(totals[10].astype(jnp.bfloat16), "seq", axis=0, tiled=True).astype(
            jnp.float32
        ),
        lax.all_gather(totals[11].astype(jnp.bfloat16), "seq", axis=0, tiled=True).astype(
            jnp.float32
        ),
        lax.all_gather(totals[12].astype(jnp.bfloat16), "seq", axis=0, tiled=True).astype(
            jnp.float32
        ),
        lax.all_gather(totals[13].astype(jnp.bfloat16), "seq", axis=0, tiled=True).astype(
            jnp.float32
        ),
        lax.all_gather(totals[14].astype(jnp.bfloat16), "seq", axis=0, tiled=True).astype(
            jnp.float32
        ),
        lax.all_gather(totals[15].astype(jnp.bfloat16), "seq", axis=0, tiled=True).astype(
            jnp.float32
        ),
    )
    return (output[None], grad_input[None]) + tuple(whole)


def solution(mesh):
    sequence = P("batch", "seq", None)
    seq, batch = mesh.shape["seq"], mesh.shape["batch"]
    fits = seq == HEADS and batch == 4
    return jax.shard_map(
        by_heads if fits else by_rows,
        mesh=mesh,
        in_specs=(sequence, sequence) + (P(),) * 16,
        out_specs=(sequence, sequence) + (P(),) * 16,
        check_vma=False,
    )
```

```python
from functools import partial

import jax
import jax.numpy as jnp
import numpy as np
from jax import lax
from jax.experimental import pallas as pl
from jax.experimental.pallas import tpu as pltpu
from jax.sharding import PartitionSpec as P

HEADS = 8
HEAD = 64
LANES = 128
BLOCK = 256
FF_PARTS = 1
F32 = jnp.float32
BF16 = jnp.bfloat16


norm_eps = 1e-05


def dot_nn(left, right):
    return jnp.dot(left, right, preferred_element_type=F32)


def dot_nt(left, right):
    return lax.dot_general(left, right, (((1,), (1,)), ((), ())), preferred_element_type=F32)


def dot_tn(left, right):
    return lax.dot_general(left, right, (((0,), (0,)), ((), ())), preferred_element_type=F32)


def lower_half(rows):
    return lax.broadcasted_iota(jnp.int32, (rows, LANES), 1) < HEAD


def turn(values):
    return pltpu.roll(values, HEAD, 1)


def swap_pairs(values):
    lane = lax.broadcasted_iota(jnp.int32, values.shape, 1)
    return jnp.where(
        lane % HEAD < HEAD // 2,
        pltpu.roll(values, LANES - HEAD // 2, 1),
        pltpu.roll(values, HEAD // 2, 1),
    )


def rope(values, table):
    return values * table[:, :LANES] + swap_pairs(values) * table[:, LANES:]


def rope_back(grads, table):
    return grads * table[:, :LANES] - swap_pairs(grads) * table[:, LANES:]


def rope_constants(rows):
    frequency = np.power(
        np.float32(10000.0), -np.arange(HEAD // 2, dtype=np.float32) * np.float32(2.0 / HEAD)
    ).astype(np.float32)
    angles = np.arange(rows, dtype=np.float32)[:, None] * frequency[None, :]
    cosine, sine = np.cos(angles), np.sin(angles)
    table = np.concatenate([cosine] * 4 + [-sine, sine] * 2, axis=1)
    return jnp.asarray(table, F32)


def norm_parts(stream):
    centered = stream - jnp.mean(stream, axis=-1, keepdims=True)
    spread = jnp.mean(centered * centered, axis=-1, keepdims=True)
    scale = lax.rsqrt(spread + norm_eps)
    return centered * scale, scale


def norm_back(grad, gain, unit, scale):
    grad_unit = grad * gain
    inner = jnp.mean(grad_unit * unit, axis=-1, keepdims=True)
    return scale * (grad_unit - jnp.mean(grad_unit, axis=-1, keepdims=True) - unit * inner)


GELU_SCALE = 0.7978845608028654
GELU_CUBE = 0.044715


def gelu_both(pre):
    square = pre * pre
    half = 0.5 + 0.5 * jnp.tanh(pre * (GELU_SCALE + GELU_SCALE * GELU_CUBE * square))
    bend = pre * (2.0 * GELU_SCALE + 6.0 * GELU_SCALE * GELU_CUBE * square)
    return pre * half, half * (1.0 + (1.0 - half) * bend)


def gelu_value(pre):
    tanh = jnp.tanh(GELU_SCALE * pre * (1.0 + GELU_CUBE * pre * pre))
    return 0.5 * pre * (1.0 + tanh)


def causal(scores, first_row, first_key):
    row = lax.broadcasted_iota(jnp.int32, scores.shape, 0) + first_row
    key = lax.broadcasted_iota(jnp.int32, scores.shape, 1) + first_key
    return jnp.where(key <= row, scores, -1e30)


def fold_rows(values):
    half = values.shape[0] // 2
    return jnp.where(lower_half(half), values[:half], turn(values[half:]))


def unfold_rows(folded):
    low = lower_half(folded.shape[0])
    return jnp.where(low, folded, 0.0), jnp.where(low, turn(folded), 0.0)


def rows_at(start, size, multiple):
    return pl.ds(pl.multiple_of(start, multiple), size)


class Late:
    def __init__(self, source, target, semaphores, axis=0, parts=1):
        self.target, self.shape = target, target.shape
        size = target.shape[axis] // parts
        cuts = [(slice(None),) * axis + (pl.ds(part * size, size),) for part in range(parts)]
        self.copies = [
            pltpu.make_async_copy(source.at[cut], target.at[cut], semaphore)
            for cut, semaphore in zip(cuts, semaphores)
        ]
        self.waiting = set(range(parts))

    def ready(self, part=None):
        for at in sorted(self.waiting if part is None else self.waiting & {part}):
            self.copies[at].wait()
            self.waiting.remove(at)
        return self.target

    def __getitem__(self, index):
        return self.ready()[index]


def with_late(kernel, late, argument_count, out_count, *refs):
    arguments, outs = list(refs[:argument_count]), refs[argument_count : argument_count + out_count]
    rest = refs[argument_count + out_count :]
    first, taken, begun = len(rest) - len(late) - 1, 0, []
    for at, (place, _, part, axis, parts) in enumerate(late):
        source = arguments[place]
        source = source if part is None else part(source, refs[0][0])
        semaphores = [rest[-1].at[taken + step] for step in range(parts)]
        arguments[place] = Late(source, rest[first + at], semaphores, axis, parts)
        begun += [(part, at, copy) for part, copy in enumerate(arguments[place].copies)]
        taken += parts
    for _, _, copy in sorted(begun, key=lambda entry: entry[:2]):
        copy.start()
    kernel(*arguments, *outs, *rest[:first])


def paired(refs):
    size = refs[0].shape[0] // 2
    pairs = len(refs) // 2
    return [
        refs[step // 2].at[pl.ds(0, size), :]
        if step % 2 == 0
        else refs[pairs + step // 2].at[pl.ds(size, size), :]
        for step in range(2 * pairs)
    ]


def by_distance(share, pieces, seat):
    rows = pieces[0].shape[0]
    for step in range(len(pieces)):
        pieces[step][...] = share[rows_at((seat ^ step) * rows, rows, 16), :]


def keep_and_send(share, keep, send, seat, parts, first=0):
    rows = share.shape[0] // parts
    stride = keep.shape[0] // (parts // 2)
    for step in range(parts):
        target = keep if step % 2 == 0 else send
        at = (step // 2) * stride + first
        target[at : at + rows] = share[rows_at((seat ^ step) * rows, rows, 16), :]


def load_kernel(place, *refs):
    count = (len(refs) - 1) // 2
    copies = [
        pltpu.make_async_copy(refs[at], refs[count + at], refs[-1].at[at]) for at in range(count)
    ]
    for copy in copies:
        copy.start()
    for copy in copies:
        copy.wait()


def project_kernel(place, x, cot, gain, w_q, w_k, w_v, table, *refs):
    pieces = refs[: HEADS // 2]
    normed_out, bundle, heads, chunks = refs[HEADS // 2 :]
    rows, width = x.shape
    me = place[0]
    unit, _ = norm_parts(x[...])
    normed = (unit * gain[...]).astype(BF16)
    q = dot_nn(normed, w_q[...])
    k = dot_nn(normed, w_k[...])
    v = dot_nn(normed, w_v[...])
    low = lower_half(rows)
    low_half = lower_half(rows // 2)
    own = table[...]
    for chunk in range(width // LANES):
        cut = slice(chunk * LANES, (chunk + 1) * LANES)
        q_chunk = rope(q[:, cut], own) * HEAD**-0.5
        k_chunk = rope(k[:, cut], own)
        v_chunk = v[:, cut]
        first, later = q_chunk[: rows // 2], q_chunk[rows // 2 :]
        heads[2 * chunk, :rows] = jnp.where(low, k_chunk, turn(v_chunk)).astype(BF16)
        heads[2 * chunk + 1, :rows] = jnp.where(low, turn(k_chunk), v_chunk).astype(BF16)
        heads[2 * chunk, rows:] = jnp.where(low_half, first, turn(later)).astype(BF16)
        heads[2 * chunk + 1, rows:] = jnp.where(low_half, turn(first), later).astype(BF16)
    for step in range(HEADS):
        at = (step % 2) * heads.shape[1]
        pieces[step // 2][at : at + heads.shape[1]] = heads[me ^ step]
    normed_out[...] = normed
    bundle[:rows] = cot[...].astype(BF16)
    for chunk in range(width // LANES):
        cut = slice(chunk * LANES, (chunk + 1) * LANES)
        chunks[chunk] = cot[:, cut]
        total = sum(chunks[chunk, pl.ds(s, rows // 3, stride=3), :] for s in range(3))
        bundle[rows:, cut] = total.astype(BF16)


def attend_kernel(place, *refs):
    pieces, outs = paired(refs[:HEADS]), refs[HEADS : HEADS + HEADS // 2]
    q_all, kv_all, lse_o = refs[HEADS + HEADS // 2 :]
    me = place[0]
    rows = outs[0].shape[0]
    for step in range(HEADS):
        start = (me ^ step) * rows
        piece = pieces[step][...]
        kv_all[rows_at(start, rows, 16), :] = piece[:rows]
        first, later = unfold_rows(piece[rows:].astype(F32))
        q_all[rows_at(start, rows // 2, 16), :] = first.astype(BF16)
        q_all[rows_at(start + rows // 2, rows // 2, 16), :] = later.astype(BF16)
    low = lower_half(BLOCK)
    for block in range(q_all.shape[0] // BLOCK):
        cut = slice(block * BLOCK, (block + 1) * BLOCK)
        seen = kv_all[: (block + 1) * BLOCK]
        scores = causal(dot_nt(q_all[cut], seen), block * BLOCK, 0)
        most = jnp.max(scores, axis=-1, keepdims=True)
        weights = jnp.exp(scores - most)
        total = jnp.sum(weights, axis=-1, keepdims=True)
        attended = dot_nn(weights.astype(BF16), seen) / total
        lse_o[cut] = jnp.where(low, most + jnp.log(total), attended)
    for step in range(HEADS):
        own = lse_o[rows_at((me ^ step) * rows, rows, 16), :]
        at = (step % 2) * (rows // 2)
        outs[step // 2][at : at + rows // 2] = jnp.where(
            lower_half(rows // 2), turn(own[: rows // 2]), own[rows // 2 :]
        ).astype(BF16)


def finish_kernel(place, x, normed_a, gain, w_o, w_e, w_c, *refs):
    pieces = paired(refs[:HEADS])
    result_out, middle_out, att_out, normed_out, pooled_out, heads, chunks = refs[HEADS:]
    rows, width = x.shape
    me = place[0]
    for step in range(HEADS):
        heads[me ^ step] = pieces[step][...].astype(F32)
    low = lower_half(rows // 2)
    for chunk in range(width // LANES):
        cut = slice(chunk * LANES, (chunk + 1) * LANES)
        even, odd = heads[2 * chunk], heads[2 * chunk + 1]
        att_out[: rows // 2, cut] = jnp.where(low, even, turn(odd)).astype(BF16)
        att_out[rows // 2 :, cut] = jnp.where(low, turn(even), odd).astype(BF16)
    middle = x[...] + dot_nn(att_out[...], w_o[...])
    middle_out[...] = middle
    unit, _ = norm_parts(middle)
    normed = (unit * gain[...]).astype(BF16)
    normed_out[:rows] = normed
    normed_out[rows:] = normed_a[...]
    result = middle
    size = w_e.shape[1] // FF_PARTS
    for part in range(FF_PARTS):
        cut = slice(part * size, (part + 1) * size)
        hidden = gelu_value(dot_nn(normed, w_e.ready(part)[:, cut])).astype(BF16)
        result = result + dot_nn(hidden, w_c.ready(part)[cut, :])
    result_out[...] = result
    short = rows // 3
    for chunk in range(width // LANES):
        cut = slice(chunk * LANES, (chunk + 1) * LANES)
        chunks[chunk, :8] = jnp.zeros((8, LANES), F32)
        chunks[chunk, 8:] = result[:, cut]
        total = sum(chunks[chunk, pl.ds(s, short, stride=3), :] for s in (6, 7, 8))
        pooled_out[:short, cut] = (total / 3.0).astype(BF16)
    tail = (result[rows - 1 :] + result[rows - 2 : rows - 1]) / 3.0
    extra = pooled_out.shape[0] - short
    pooled_out[short:] = jnp.broadcast_to(tail, (extra, width)).astype(BF16)


def short_forward_kernel(
    place, gathered, table, gain_a, w_q, w_k, w_v, w_o, gain_f, w_e, w_c, *refs
):
    pieces, refs = refs[:HEADS], refs[HEADS:]
    own_middle, own_hidden = refs[:2]
    pooled, normed_a, q_s, k_s, v_s, o_s, lse_s, att, grad_middle = refs[2:11]
    share_pieces = refs[11:-8]
    extra, middle, normed_f, hidden, grad_pre, grad_normed, grad_low, share = refs[-8:]
    me, seat = place[0], place[1]
    count, width = pooled.shape
    short = count // HEADS
    chunk_count = width // LANES
    ff = w_e.shape[1]
    ff_own = ff // HEADS

    for step in range(HEADS):
        other = me ^ step
        pooled[rows_at(other * short, short, 16), :] = pieces[step][:short].astype(F32)
        extra[pl.ds(other, 1), :] = pieces[step][short:].astype(F32)[:1]
    for part in range(1, HEADS):
        at = slice(part * short, part * short + 1)
        pooled[at] = pooled[at] + extra[part - 1 : part]

    unit, _ = norm_parts(pooled[...])
    normed_a[...] = (unit * gain_a[...]).astype(BF16)
    low = lower_half(count)
    q = dot_nn(normed_a[...], w_q[...])
    turns = table[...]
    for chunk in range(chunk_count):
        q_chunk = rope(q[:, chunk * LANES : (chunk + 1) * LANES], turns) * HEAD**-0.5
        q_s[2 * chunk] = jnp.where(low, q_chunk, 0.0).astype(BF16)
        q_s[2 * chunk + 1] = jnp.where(low, 0.0, q_chunk).astype(BF16)
    k = dot_nn(normed_a[...], w_k[...])
    for chunk in range(chunk_count):
        k_s[chunk] = rope(k[:, chunk * LANES : (chunk + 1) * LANES], turns).astype(BF16)
    v = dot_nn(normed_a[...], w_v[...])
    for chunk in range(chunk_count):
        v_s[chunk] = v[:, chunk * LANES : (chunk + 1) * LANES].astype(BF16)

    low_block = lower_half(BLOCK)

    def attend_chunk(chunk, carry):
        results = []
        k_t = jnp.transpose(k_s[chunk])
        for half in range(2):
            scores = causal(dot_nn(q_s[2 * chunk + half], k_t), 0, 0)
            most = jnp.max(scores, axis=-1, keepdims=True)
            weights = jnp.exp(scores - most)
            total = jnp.sum(weights, axis=-1, keepdims=True)
            attended = dot_nn(weights.astype(BF16), v_s[chunk]) / total
            results.append((attended, most + jnp.log(total)))
        both = jnp.where(low, results[0][0], results[1][0])
        o_s[chunk] = both
        lse_s[chunk] = jnp.where(low, results[0][1], results[1][1])
        att[:, rows_at(chunk * LANES, LANES, LANES)] = both.astype(BF16)
        return carry

    lax.fori_loop(0, chunk_count, attend_chunk, 0)
    middle[...] = pooled[...] + dot_nn(att[...], w_o[...])
    unit, scale = norm_parts(middle[...])
    normed_f[...] = (unit * gain_f[...]).astype(BF16)

    for part in range(HEADS):
        grad_low[part * short : (part + 1) * short] = gathered[part]

    ff_part = ff // 4
    grad_normed[...] = jnp.zeros(grad_normed.shape, F32)
    w_e, w_c = w_e.ready(), w_c.ready()

    def feed_forward(part, carry):
        cut = rows_at(part * ff_part, ff_part, ff_part)
        pre = dot_nn(normed_f[...], w_e[:, cut])
        value, slope = gelu_both(pre)
        hidden[:, cut] = value.astype(BF16)
        grad_hidden = dot_nt(grad_low[...], w_c[cut, :])
        low_grad = (grad_hidden * slope).astype(BF16)
        grad_pre[:, cut] = low_grad
        grad_normed[...] += dot_nt(low_grad, w_e[:, cut])
        return carry

    lax.fori_loop(0, 4, feed_forward, 0)

    own_ff = rows_at(me * ff_own, ff_own, ff_own)
    share[:ff_own] = dot_tn(hidden[:, own_ff], grad_low[...]).astype(BF16)
    expand = dot_tn(normed_f[...], grad_pre[:, own_ff]).astype(BF16)
    share[ff_own : 2 * ff_own, : width // 2] = expand[: width // 2]
    share[ff_own : 2 * ff_own, width // 2 :] = expand[width // 2 :]
    by_distance(share, share_pieces, seat)

    mine = rows_at(me * short, short, 16)
    own_middle[...] = middle[mine, :]
    own_hidden[...] = hidden[mine, :]

    unit, scale = norm_parts(middle[...])
    grad_middle[...] = grad_low[...].astype(F32) + norm_back(
        grad_normed[...], gain_f[...], unit, scale
    )


def output_kernel(place, residual, middle, hidden, w_c, output, wide):
    rows, width = residual.shape
    short_out = middle[...] + dot_nn(hidden[...], w_c[...])
    for chunk in range(width // LANES):
        cut = slice(chunk * LANES, (chunk + 1) * LANES)
        for s in range(3):
            wide[chunk, pl.ds(s, rows // 3, stride=3), :] = short_out[:, cut]
        output[:, cut] = residual[:, cut] + wide[chunk]


def short_back_kernel(
    place,
    cot,
    gathered,
    table,
    gain_a,
    w_q,
    w_k,
    w_v,
    w_o,
    pooled,
    normed_a,
    q_s,
    k_s,
    v_s,
    o_s,
    lse_s,
    att,
    grad_middle,
    middle,
    normed_f,
    gain_f,
    w_e,
    w_c,
    grad_all,
    share,
    full_middle,
    g1_out,
    do_s,
    dq_s,
    dk_s,
    dv_s,
    wide,
    wo_s,
    grad_own,
):
    me = place[0]
    rows, width = cot.shape
    count = pooled.shape[0]
    full = rows * HEADS
    chunk_count = width // LANES
    low = lower_half(count)
    low_block = lower_half(BLOCK)
    g1 = grad_middle[...].astype(BF16)
    d_att = dot_nt(g1, w_o[...])
    for chunk in range(chunk_count):
        do_chunk = d_att[:, chunk * LANES : (chunk + 1) * LANES]
        do_s[2 * chunk] = jnp.where(low, do_chunk, 0.0).astype(BF16)
        do_s[2 * chunk + 1] = jnp.where(low, 0.0, do_chunk).astype(BF16)
    own_chunk = rows_at((me // 2) * LANES, LANES, LANES)
    wo_s[...] = dot_tn(att[:, own_chunk], g1)
    table = table.ready()

    def attend_back(chunk, carry):
        columns = rows_at(chunk * LANES, LANES, LANES)
        dq = []
        dk = [None]
        dv = [None]
        k_t = jnp.transpose(k_s[chunk])
        v_t = jnp.transpose(v_s[chunk])
        for half in range(2):
            head = 2 * chunk + half
            lse = lse_s[chunk][:, half * HEAD : half * HEAD + 1]
            delta = jnp.sum(do_s[head].astype(F32) * o_s[chunk], axis=-1, keepdims=True)
            dq_half = None
            for key in range(1):
                cut = slice(0, count)
                rest = slice(0, count)
                k_block, v_block = k_s[chunk, cut, :], v_s[chunk, cut, :]
                q_rest, do_rest = q_s[head, rest, :], do_s[head, rest, :]
                scores = causal(dot_nn(q_rest, k_t), 0, 0)
                probs = jnp.exp(scores - lse[rest])
                grad_probs = dot_nn(do_rest, v_t)
                ds = (probs * (grad_probs - delta[rest])).astype(BF16)
                term = dot_nn(ds, k_block)
                if key == 0:
                    dq_half = term
                else:
                    dq_half = jnp.concatenate(
                        [dq_half[: key * BLOCK], dq_half[key * BLOCK :] + term]
                    )
                term = dot_tn(ds, q_rest)
                dk[key] = term if half == 0 else dk[key] + term
                term = dot_tn(probs.astype(BF16), do_rest)
                dv[key] = term if half == 0 else dv[key] + term
            dq.append(dq_half)
        both = jnp.where(lower_half(count), dq[0], dq[1]) * HEAD**-0.5
        dq_s[:, columns] = rope_back(both, table[...]).astype(BF16)
        for key in range(1):
            key_cut = slice(0, count)
            dk_s[key_cut, columns] = rope_back(dk[key], table[key_cut, :]).astype(BF16)
            dv_s[key_cut, columns] = dv[key].astype(BF16)
        return carry

    lax.fori_loop(0, chunk_count, attend_back, 0)

    odd = me % 2 == 1
    low_width = lower_half(width)
    share_q = dot_tn(normed_a[...], dq_s[:, own_chunk])
    share_k = dot_tn(normed_a[...], dk_s[:, own_chunk])
    share_v = dot_tn(normed_a[...], dv_s[:, own_chunk])
    share_q = jnp.where(odd, turn(share_q), share_q)
    share_k = jnp.where(odd, share_k, turn(share_k))
    share_v = jnp.where(odd, turn(share_v), share_v)
    head_rows = wo_s[rows_at((me % 2) * HEAD, HEAD, HEAD), :]
    pack_attention(share, jnp.where(low_width, share_q, share_k), fold_rows(share_v), head_rows)

    grad_a = dot_nt(dq_s[...], w_q[...])
    grad_a += dot_nt(dk_s[...], w_k[...])
    grad_a += dot_nt(dv_s[...], w_v[...])
    unit, scale = norm_parts(pooled[...])
    grad_pooled = grad_middle[...] + norm_back(grad_a, gain_a[...], unit, scale)
    for chunk in range(chunk_count):
        cut = slice(chunk * LANES, (chunk + 1) * LANES)
        third = grad_pooled[:, cut] / 3.0
        for s in range(3):
            wide[chunk, pl.ds(6 + s, count, stride=3), :] = third
        wide[chunk, full + 6 : full + 8] = jnp.zeros((2, LANES), F32)
        grad_own[:, cut] = cot[:, cut] + wide[chunk, rows_at(me * rows + 8, rows, 8), :]
        for part in range(HEADS):
            more = wide[chunk, 8 + part * rows : 8 + (part + 1) * rows, :]
            grad_all[part * rows : (part + 1) * rows, cut] = (
                gathered[part, :, cut].astype(F32) + more
            ).astype(BF16)
    feed_forward_back(grad_own, middle, normed_f, gain_f, w_e, w_c, full_middle, g1_out)


def feed_forward_back(grad, middle, normed, gain, w_e, w_c, grad_middle_out, g1_out):
    grad_low = grad[...].astype(BF16)
    grad_normed = 0.0
    size = w_e.shape[1] // FF_PARTS
    for part in range(FF_PARTS):
        cut = slice(part * size, (part + 1) * size)
        own_w = w_e.ready(part)[:, cut]
        _, slope = gelu_both(dot_nn(normed[...], own_w))
        grad_hidden = dot_nt(grad_low, w_c.ready(part)[cut, :])
        grad_normed += dot_nt((grad_hidden * slope).astype(BF16), own_w)
    unit, scale = norm_parts(middle[...])
    grad_middle = grad[...] + norm_back(grad_normed, gain[...], unit, scale)
    grad_middle_out[...] = grad_middle
    g1_out[...] = grad_middle.astype(BF16)


def pack_attention(share, both_qk, folded_v, head_rows):
    half = both_qk.shape[0] // 2
    share[:half, :LANES] = both_qk[:half].astype(BF16)
    share[:half, LANES : 2 * LANES] = both_qk[half:].astype(BF16)
    share[:half, 2 * LANES : 3 * LANES] = folded_v.astype(BF16)
    size = head_rows.shape[0]
    for chunk in range(head_rows.shape[1] // LANES):
        share[chunk * size : (chunk + 1) * size, 3 * LANES :] = head_rows[
            :, chunk * LANES : (chunk + 1) * LANES
        ].astype(BF16)


def feed_forward_share_kernel(parts, place, normed, grad, w_e, w_c, keep, send, share):
    seat = place[1]
    width, ff_own = w_e.shape
    normed = normed[...].reshape(-1, width)
    value, slope = gelu_both(dot_nn(normed, w_e[...]))
    grad_hidden = dot_nt(grad[...], w_c[...])
    grad_pre = (grad_hidden * slope).astype(BF16)
    share[:ff_own] = dot_tn(value.astype(BF16), grad[...]).astype(BF16)
    expand = dot_tn(normed, grad_pre).astype(BF16)
    share[ff_own:, : width // 2] = expand[: width // 2]
    share[ff_own:, width // 2 :] = expand[width // 2 :]
    keep_and_send(share, keep, send, seat, parts)


def attend_back_kernel(place, q_all, kv_all, lse_o, table, w_o, *refs):
    pieces, outs = refs[:HEADS], refs[HEADS : HEADS + HEADS // 2]
    dq_all, dkv_all, do_all, dkv_sum, dq_sum, q_t, do_t = refs[HEADS + HEADS // 2 :]
    me = place[0]
    rows = q_all.shape[0] // HEADS
    own_w = w_o[...]
    own_w = jnp.concatenate([jnp.zeros(own_w.shape, BF16), own_w])
    for step in range(HEADS):
        do_all[rows_at((me ^ step) * rows, rows, 16), :] = dot_nt(
            pieces[step][...], own_w
        ).astype(BF16)
    total = q_all.shape[0]
    lse = lse_o[...][:, :1]
    delta = jnp.sum(do_all[...].astype(F32) * lse_o[...], axis=-1, keepdims=True)
    dq_sum[...] = jnp.zeros(dq_sum.shape, F32)
    q_t[...] = jnp.transpose(q_all[...].astype(F32)).astype(BF16)
    do_t[...] = jnp.transpose(do_all[...].astype(F32)).astype(BF16)
    for block in range(total // BLOCK):
        cut = slice(block * BLOCK, (block + 1) * BLOCK)
        rest = slice(block * BLOCK, total)
        kv_block = kv_all[cut]
        scores = causal(dot_nt(q_all[rest], kv_block), 0, 0)
        probs = jnp.exp(scores - lse[rest])
        grad_probs = dot_nt(do_all[rest], kv_block)
        ds = (probs * (grad_probs - delta[rest])).astype(BF16)
        dq_sum[rest] += dot_nn(ds, kv_block)
        back = dot_nn(q_t[:, rest], ds) + dot_nn(do_t[:, rest], probs.astype(BF16))
        dkv_sum[cut] = jnp.transpose(back)
    dq_all[...] = rope_back(dq_sum[...] * HEAD**-0.5, table[...]).astype(BF16)
    low = lower_half(BLOCK)
    for block in range(q_all.shape[0] // BLOCK):
        cut = slice(block * BLOCK, (block + 1) * BLOCK)
        dkv = dkv_sum[cut]
        dkv_all[cut] = jnp.where(low, rope_back(dkv, table[cut, :]), dkv).astype(BF16)
    for step in range(HEADS):
        own = rows_at((me ^ step) * rows, rows, 16)
        at = (step % 2) * (rows + rows // 2)
        outs[step // 2][at : at + rows] = dkv_all[own, :]
        outs[step // 2][at + rows : at + rows + rows // 2] = fold_rows(
            dq_all[own, :].astype(F32)
        ).astype(BF16)


def attention_share_kernel(parts, place, gathered, dq_all, dkv_all, lse_o, more, *refs):
    pieces, keep, send, share = refs[:HEADS], refs[HEADS], refs[HEADS + 1], refs[-1]
    me, seat = place[0], place[1]
    _, rows, width = gathered.shape
    normed = gathered[...].reshape(-1, width)
    grad_q = dot_tn(normed, dq_all[...])
    grad_kv = dot_tn(normed, dkv_all[...])
    grad_o = jnp.zeros((LANES, width), F32)
    for step in range(HEADS):
        own = lse_o[rows_at((me ^ step) * rows, rows, 16), :].astype(BF16)
        grad_o += dot_tn(own, pieces[step][...])
    grad_o = grad_o[HEAD:]
    half = width // 2
    folded_v = jnp.where(lower_half(half), turn(grad_kv[:half]), grad_kv[half:])
    pack_attention(
        share, jnp.where(lower_half(width), grad_q, turn(grad_kv)), folded_v, grad_o
    )
    keep_and_send(share, keep, send, seat, parts)
    keep_and_send(more, keep, send, seat, parts, share.shape[0] // parts)


def start_back_kernel(place, x, grad_middle, gain, w_q, w_k, w_v, *refs):
    pieces = paired(refs[:HEADS])
    grad_in, heads, dq, dk, dv = refs[HEADS:]
    me = place[0]
    rows, width = x.shape
    half = rows // 2
    for step in range(HEADS):
        heads[me ^ step] = pieces[step][...]
    low, low_half = lower_half(rows), lower_half(half)
    for chunk in range(width // LANES):
        cut = slice(chunk * LANES, (chunk + 1) * LANES)
        even, odd = heads[2 * chunk].astype(F32), heads[2 * chunk + 1].astype(F32)
        dk[:, cut] = jnp.where(low, even[:rows], turn(odd[:rows])).astype(BF16)
        dv[:, cut] = jnp.where(low, turn(even[:rows]), odd[:rows]).astype(BF16)
        dq[:half, cut] = jnp.where(low_half, even[rows:], turn(odd[rows:])).astype(BF16)
        dq[half:, cut] = jnp.where(low_half, turn(even[rows:]), odd[rows:]).astype(BF16)
    grad_a = dot_nt(dq[...], w_q[...]) + dot_nt(dk[...], w_k[...]) + dot_nt(dv[...], w_v[...])
    unit, scale = norm_parts(x[...])
    grad_in[...] = grad_middle[...] + norm_back(grad_a, gain[...], unit, scale)


def column_to_row(column):
    return jnp.transpose(jnp.broadcast_to(column, (column.shape[0], LANES)))[:1]


def fold_lanes(values):
    return sum(
        values[:, at : at + LANES] for at in range(0, values.shape[1], LANES)
    )


def part_order(batch):
    order, bit = [0], batch // 2
    while bit >= 1:
        order = order + [step ^ bit for step in order]
        bit //= 2
    return order


def grads_kernel(parts, attention, feed_forward, source_count, place, *refs):
    refs = list(refs)
    sources = [refs.pop(0) for _ in range(source_count)]
    halves = source_count == 2 * HEADS
    weights = [refs.pop(0) for _ in range(4 * attention + 2 * feed_forward)]
    outs = [refs.pop(0) for _ in range(5 * attention + 3 * feed_forward)]
    me, seat = place[0], place[1]
    order = part_order(parts)
    copies = []

    def send(source, target, semaphore):
        copy = pltpu.make_async_copy(source, target, semaphore)
        copy.start()
        copies.append(copy)

    def rows_of(step):
        if source_count == 1:
            return sources[0].ready(step).at[step], step
        return sources[step], me ^ step

    def part_of(step, source, at, first, size):
        count = parts
        if halves:
            source, count, at = sources[step + (HEADS if 2 * at >= parts else 0)], parts // 2, at % (parts // 2)
        first += at * (source.shape[0] // count)
        return source[first : first + size]

    for layer in range(attention):
        w_q, w_k, w_v, gain_a = weights[4 * layer : 4 * layer + 4]
        grad_q, grad_k, grad_v, grad_o, grad_gain_a = outs[5 * layer : 5 * layer + 5]
        heads, square, over, sems_a = refs[4 * layer : 4 * layer + 4]
        width = grad_q.shape[0]
        half, at_rows = width // 2, width // 2 // parts
        for step in range(HEADS):
            source, owner = rows_of(step)
            for at, peer in enumerate(order):
                heads[owner, rows_at((seat ^ peer) * at_rows, at_rows, 16), :] = part_of(
                    step, source, at, layer * at_rows, at_rows
                )
        low = lower_half(half)
        total = None
        for chunk in range(HEADS // 2):
            cut = slice(chunk * LANES, (chunk + 1) * LANES)
            for part in range(2):
                rows = slice(part * half, (part + 1) * half)
                lanes = slice(part * LANES, (part + 1) * LANES)
                even = heads[2 * chunk, :, lanes].astype(F32)
                odd = heads[2 * chunk + 1, :, lanes].astype(F32)
                square[0, chunk, rows] = jnp.where(low, even, turn(odd))
                square[1, chunk, rows] = jnp.where(low, turn(even), odd)
            even = heads[2 * chunk, :, 2 * LANES : 3 * LANES].astype(F32)
            odd = heads[2 * chunk + 1, :, 2 * LANES : 3 * LANES].astype(F32)
            square[2, chunk, :half] = jnp.where(low, even, turn(odd))
            square[2, chunk, half:] = jnp.where(low, turn(even), odd)
            for head in (2 * chunk, 2 * chunk + 1):
                for lane in range(width // LANES):
                    over[head, :, lane * LANES : (lane + 1) * LANES] = heads[
                        head, lane * HEAD : (lane + 1) * HEAD, 3 * LANES :
                    ].astype(F32)
                send(
                    over.at[head],
                    grad_o.at[pl.ds(head * HEAD, HEAD), :],
                    sems_a.at[3 + head % 2, chunk],
                )
            for at, target in enumerate((grad_q, grad_k, grad_v)):
                send(
                    square.at[at, chunk],
                    target.at[:, pl.ds(chunk * LANES, LANES)],
                    sems_a.at[at, chunk],
                )
            term = (
                w_q[:, cut].astype(F32) * square[0, chunk]
                + w_k[:, cut].astype(F32) * square[1, chunk]
                + w_v[:, cut].astype(F32) * square[2, chunk]
            )
            total = term if total is None else total + term
        total = jnp.sum(total, axis=-1, keepdims=True)
        grad_gain_a[...] = column_to_row(total) / gain_a[...]

    if feed_forward:
        w_e, gain_f = weights[-2:]
        contract, expand, grad_gain_f = outs[-3:]
        share, acc, sems = refs[4 * attention : 4 * attention + 3]
        width = expand.shape[0]
        half = width // 2
        ff_own = contract.shape[0] // HEADS
        ff_rows = 2 * ff_own // parts
        acc[...] = jnp.zeros(acc.shape, F32)
        for step in range(HEADS):
            source, owner = rows_of(step)
            for at, peer in enumerate(order):
                share[step, rows_at((seat ^ peer) * ff_rows, ff_rows, 16), :] = part_of(
                    step, source, at, 0, ff_rows
                ).astype(F32)
            own = pl.ds(pl.multiple_of(owner * ff_own, ff_own), ff_own)
            send(share.at[step, pl.ds(0, ff_own), :], contract.at[own, :], sems.at[step, 0])
            for side in range(2):
                lanes = pl.ds(side * half, half)
                send(
                    share.at[step, pl.ds(ff_own, ff_own), lanes],
                    expand.at[pl.ds(side * half, half), own],
                    sems.at[step, 1 + side],
                )
                acc[side * half : (side + 1) * half] += fold_lanes(
                    w_e[side * half : (side + 1) * half, own].astype(F32)
                    * share[step, ff_own:, side * half : (side + 1) * half]
                )
        total = jnp.sum(acc[...], axis=-1, keepdims=True)
        grad_gain_f[...] = column_to_row(total) / gain_f[...]
    for copy in copies:
        copy.wait()


COST = 1.15e9


def call(kernel, out_shape, scratch, arguments, late=(), limit=16, in_hbm=(), kept=(), us=5):
    late = [entry if isinstance(entry, tuple) else (entry,) for entry in late]
    late = [entry + (None, None, 0, 1)[len(entry) - 1 :] for entry in late]
    specs = [pl.BlockSpec(memory_space=pltpu.SMEM)]
    specs += [pl.BlockSpec(memory_space=pltpu.VMEM)] * (len(arguments) - 1)
    buffers, arguments = [], list(arguments)
    for at, shape, *_ in late:
        specs[at] = pl.BlockSpec(memory_space=pltpu.HBM)
        buffers.append(pltpu.VMEM(shape or arguments[at].shape, arguments[at].dtype))
        arguments[at] = pltpu.with_memory_space_constraint(arguments[at], pltpu.HBM)
    body, semaphores = kernel, []
    if late:
        semaphores = [pltpu.SemaphoreType.DMA((sum(entry[4] for entry in late),))]
        body = partial(with_late, kernel, late, len(arguments), len(out_shape))
    return pl.pallas_call(
        body,
        out_shape=[
            (pltpu.HBM if at in in_hbm or at in kept else jax.ShapeDtypeStruct)(*entry)
            for at, entry in enumerate(out_shape)
        ],
        in_specs=specs,
        out_specs=[
            pl.BlockSpec(memory_space=pltpu.HBM if at in in_hbm else pltpu.VMEM)
            for at in range(len(out_shape))
        ],
        scratch_shapes=[
            pltpu.VMEM(*entry) if isinstance(entry, tuple) else entry for entry in scratch
        ]
        + buffers
        + semaphores,
        compiler_params=pltpu.CompilerParams(vmem_limit_bytes=limit * 2**20),
        cost_estimate=pl.CostEstimate(
            flops=int(us * COST), bytes_accessed=2**20, transcendentals=0
        ),
    )(*arguments)


def exchange(pieces, axis):
    devices = range(lax.axis_size(axis))
    moved = {
        step: lax.ppermute(pieces[step], axis, [(i, i ^ step) for i in devices])
        for step in reversed(range(1, len(pieces)))
    }
    return [pieces[0]] + [moved[step] for step in range(1, len(pieces))]


def after(values, *others):
    return lax.optimization_barrier((values, others))[0]


def phase(*values):
    return lax.optimization_barrier(values)


def swap(block, axis, step):
    return lax.ppermute(block, axis, [(i, i ^ step) for i in range(lax.axis_size(axis))])


def near_exchange(pairs):
    moved = {step: swap(pairs[step], "seq", 2 * step) for step in reversed(range(1, len(pairs)))}
    first = [pairs[0]] + [moved[step] for step in range(1, len(pairs))]
    return first + [swap(pair, "seq", 1) for pair in first]


def summed(pieces):
    return sum(piece.astype(F32) for piece in pieces).astype(BF16)


def sum_step(keep, arrived, bit):
    total = keep.astype(F32) + arrived.astype(F32)
    parts = lax.axis_size("batch") // (2 * bit)
    if parts <= 1:
        return total.astype(BF16), None
    total = total.reshape(parts // 2, 2, -1, total.shape[1])
    return (
        total[:, 0].reshape(-1, total.shape[-1]),
        total[:, 1].reshape(-1, total.shape[-1]).astype(BF16),
    )


def near_gather(block, *beside):
    found = {0: block}
    for step in (6, 4, 2):
        found[step] = swap(block, "seq", step)
    for step in (0, 2, 4, 6):
        found[step] = after(found[step], *beside) if beside else found[step]
        found[step + 1] = swap(found[step], "seq", 1)
    return [found[step] for step in range(HEADS)]


def gather(block):
    return lax.all_gather(block, "seq", axis=0, tiled=True)


def whole_grads(place, sources, batch, attention=(), feed_forward=None):
    width = sources[0].shape[-1]
    square, row = ((width, width), F32), ((1, width), F32)
    arguments, out_shape, scratch = [place, *sources], [], []
    late = [(1, None, None, 0, HEADS)] if len(sources) == 1 else []
    in_hbm = []
    for params in attention:
        first = len(arguments)
        arguments += [params[1], params[2], params[3], params[0]]
        late += [first, first + 1, first + 2]
        first = len(out_shape)
        in_hbm += [first, first + 1, first + 2, first + 3]
        out_shape += [square] * 4 + [row]
        scratch += [
            ((HEADS, width // 2, width), BF16),
            ((3, HEADS // 2, width, LANES), F32),
            ((HEADS, HEAD, width), F32),
            pltpu.SemaphoreType.DMA((5, HEADS // 2)),
        ]
    if feed_forward is not None:
        ff = feed_forward[6].shape[1]
        late += [len(arguments)]
        arguments += [feed_forward[6], feed_forward[5]]
        in_hbm += [len(out_shape), len(out_shape) + 1]
        out_shape += [((ff, width), F32), ((width, ff), F32), row]
        scratch += [
            ((HEADS, 2 * ff // HEADS, width), F32),
            ((width, LANES), F32),
            pltpu.SemaphoreType.DMA((HEADS, 3)),
        ]
    return call(
        partial(grads_kernel, batch, len(attention), feed_forward is not None, len(sources)),
        out_shape,
        scratch,
        tuple(arguments),
        late,
        32,
        in_hbm,
    )


def by_heads(inputs, cotangent, *weights):
    full = (weights[0][None],) + weights[1:5] + (weights[5][None],) + weights[6:8]
    brief = (weights[8][None],) + weights[9:13] + (weights[13][None],) + weights[14:16]
    x, cot = inputs[0], cotangent[0]
    rows, width = x.shape
    short, half, total = rows // 3, rows // 2, rows * HEADS
    batch = lax.axis_size("batch")
    ff = full[6].shape[1]
    ff_own = ff // HEADS
    count = short * HEADS
    chunks = width // LANES
    place = jnp.stack([lax.axis_index("seq"), lax.axis_index("batch")]).astype(jnp.int32)
    table = rope_constants(total)
    block = rows + half

    outs = call(
        project_kernel,
        [((2 * block, LANES), BF16)] * (HEADS // 2)
        + [((rows, width), BF16), ((rows + short, width), BF16)],
        [((HEADS, block, LANES), BF16), ((chunks, rows, LANES), F32)],
        (place, x, cot, full[0], full[1], full[2], full[3], table),
        (
            1,
            3,
            4,
            5,
            6,
            (7, (rows, 2 * LANES), lambda ref, me: ref.at[rows_at(me * rows, rows, 16), :]),
            2,
        ),
        kept=(HEADS // 2, HEADS // 2 + 1),
    )
    pieces, (normed_a, bundle) = near_exchange(outs[: HEADS // 2]), outs[HEADS // 2 :]
    bundles = gather(bundle).reshape(HEADS, rows + short, width)

    outs = call(
        attend_kernel,
        [((rows, LANES), BF16)] * (HEADS // 2)
        + [((total, LANES), BF16), ((total, LANES), BF16), ((total, LANES), F32)],
        [],
        (place, *pieces),
        kept=range(HEADS // 2, HEADS // 2 + 3),
    )
    pieces = near_exchange(outs[: HEADS // 2])
    q_all, kv_all, lse_o = outs[HEADS // 2 :]

    residual, middle, att, normed_f, pooled = call(
        finish_kernel,
        [
            ((rows, width), F32),
            ((rows, width), F32),
            ((rows, width), BF16),
            ((2 * rows, width), BF16),
            ((short + 16, width), BF16),
        ],
        [((HEADS, half, LANES), F32), ((chunks, rows + 8, LANES), F32)],
        (place, x, normed_a, full[5], full[4], full[6], full[7], *pieces),
        (4, 1, (5, None, None, 1, FF_PARTS), (6, None, None, 0, FF_PARTS), 2),
        kept=range(4),
    )
    pieces = near_gather(pooled)
    normed_all = gather(normed_f).reshape(HEADS, 2 * rows, width)

    outs = call(
        short_forward_kernel,
        [
            ((short, width), F32),
            ((short, ff), BF16),
            ((count, width), F32),
            ((count, width), BF16),
            ((HEADS, count, LANES), BF16),
            ((chunks, count, LANES), BF16),
            ((chunks, count, LANES), BF16),
            ((chunks, count, LANES), F32),
            ((chunks, count, LANES), F32),
            ((count, width), BF16),
            ((count, width), F32),
        ]
        + [((2 * ff_own // batch, width), BF16)] * batch,
        [
            ((HEADS, width), F32),
            ((count, width), F32),
            ((count, width), BF16),
            ((count, ff), BF16),
            ((count, ff), BF16),
            ((count, width), F32),
            ((count, width), BF16),
            ((2 * ff_own, width), BF16),
        ],
        (place, bundles, table[:count]) + brief + tuple(pieces),
        (
            4,
            2,
            5,
            6,
            7,
            9,
            10,
            (1, (HEADS, short, width), lambda ref, me: ref.at[:, pl.ds(rows, short), :]),
        ),
        22,
        kept=(0, 1),
        us=16,
    )
    own_short, saved = outs[:2], outs[2:11]
    a_at, saved = phase(outs[11:], saved)
    a_at = exchange(a_at, "batch")
    outs = call(
        short_back_kernel,
        [
            ((total, width), BF16),
            ((width // 2, width), BF16),
            ((rows, width), F32),
            ((rows, width), BF16),
        ],
        [
            ((HEADS, count, LANES), BF16),
            ((count, width), BF16),
            ((count, width), BF16),
            ((count, width), BF16),
            ((chunks, total + 16, LANES), F32),
            ((LANES, width), F32),
            ((rows, width), F32),
        ],
        (place, cot, bundles, table[:count])
        + brief[:5]
        + tuple(saved)
        + (middle, normed_f, full[5], full[6], full[7]),
        (
            8,
            3,
            5,
            6,
            7,
            (2, (HEADS, rows, width), lambda ref, me: ref.at[:, pl.ds(0, rows), :]),
            1,
            21,
            22,
            (19, (rows, width), lambda ref, me: ref.at[pl.ds(0, rows), :]),
            18,
        ),
        25,
        kept=range(3),
        us=18,
    )
    a_at, (grad_all, short_share, grad_middle, g1) = phase(a_at, outs)

    a_all, g1, grad_all = phase(summed(a_at), g1, grad_all)
    a_at = swap(a_all, "batch", 2)
    outs = call(
        partial(feed_forward_share_kernel, batch),
        [((ff_own, width), BF16)] * 2,
        [((2 * ff_own, width), BF16)],
        (place, normed_all, grad_all, full[6], full[7]),
        (
            (1, (HEADS, rows, width), lambda ref, me: ref.at[:, pl.ds(0, rows), :]),
            (3, (width, ff_own), lambda ref, me: ref.at[:, rows_at(me * ff_own, ff_own, ff_own)]),
            2,
            (4, (ff_own, width), lambda ref, me: ref.at[rows_at(me * ff_own, ff_own, ff_own), :]),
        ),
        22,
    )
    g1_all = near_gather(g1, outs[1], a_at)
    a_all = jnp.concatenate([a_all, a_at])
    a_at = swap(a_all, "batch", 1)
    a_all, a_at, g1_all, (b_keep, b_send) = phase(a_all, a_at, g1_all, outs)

    a_shares = gather(jnp.concatenate([a_all, a_at])[None])
    b_at = swap(b_send, "batch", 1)
    outs = call(
        attend_back_kernel,
        [((2 * block, LANES), BF16)] * (HEADS // 2)
        + [((total, LANES), BF16), ((total, LANES), BF16)],
        [
            ((total, LANES), BF16),
            ((total, LANES), F32),
            ((total, LANES), F32),
            ((LANES, total), BF16),
            ((LANES, total), BF16),
        ],
        (place, q_all, kv_all, lse_o, table, full[4], *g1_all),
        (
            (5, (HEAD, width), lambda ref, me: ref.at[rows_at(me * HEAD, HEAD, HEAD), :]),
            1,
            2,
            3,
            4,
        ),
        us=7,
    )
    b_at, outs = phase(b_at, outs)
    pieces, (dq_all, dkv_all) = outs[: HEADS // 2], outs[HEADS // 2 :]

    b_keep, b_send = sum_step(b_keep, b_at, 1)
    b_send, dq_all = phase(b_send, dq_all)
    b_at = swap(b_send, "batch", 2)
    outs = call(
        partial(attention_share_kernel, batch),
        [((width // 2, width), BF16)] * 2,
        [((width // 2, width), BF16)],
        (place, normed_all, dq_all, dkv_all, lse_o, short_share, *g1_all),
        ((1, (HEADS, rows, width), lambda ref, me: ref.at[:, pl.ds(rows, rows), :]), 4, 5),
        us=3,
    )
    b_at, pieces, (c_keep, c_send) = phase(b_at, pieces, outs)

    b_all, _ = sum_step(b_keep, b_at, 2)
    b_all, pieces, c_send = phase(b_all, pieces, c_send)
    b_at = swap(b_all, "batch", 2)
    c_at = swap(c_send, "batch", 1)
    pieces = {step: pieces[step] for step in range(HEADS // 2)}
    moved = {step: swap(pieces[step], "seq", 2 * step) for step in (3, 2)}
    b_at, c_at, moved, pieces = phase(b_at, c_at, moved, pieces)

    b_all = jnp.concatenate([b_all, b_at])
    c_keep, c_send = sum_step(c_keep, c_at, 1)
    b_all, c_send, pieces = phase(b_all, c_send, pieces)
    b_at = swap(b_all, "batch", 1)
    c_at = swap(c_send, "batch", 2)
    moved |= {0: pieces[0], 1: swap(pieces[1], "seq", 2)}
    b_at, c_at, moved, pieces = phase(b_at, c_at, moved, pieces)

    b_all = jnp.concatenate([b_all, b_at])
    c_all, _ = sum_step(c_keep, c_at, 2)
    b_all, c_all, moved = phase(b_all, c_all, moved)
    b_shares = gather(b_all[None])
    c_at = swap(c_all, "batch", 2)
    across = {step: swap(moved[step], "seq", 1) for step in range(HEADS // 2)}
    (output,) = call(
        output_kernel,
        [((rows, width), F32)],
        [((chunks, rows, LANES), F32)],
        (place, residual, *own_short, brief[7]),
        (4, 3, 2, 1),
        us=3,
    )
    c_at, moved, across, output = phase(c_at, moved, across, output)

    c_all, moved, across, a_shares = phase(
        jnp.concatenate([c_all, c_at]), moved, across, a_shares
    )
    first = {0: c_all, 2: swap(c_all, "seq", 2), 4: swap(c_all, "seq", 4)}
    c_at = swap(c_all, "batch", 1)
    pieces = [side[step] for side in (moved, across) for step in range(HEADS // 2)]
    short_ff_grads = whole_grads(place, [a_shares], batch, (), brief)
    (grad_in,) = call(
        start_back_kernel,
        [((rows, width), F32)],
        [((HEADS, block, LANES), BF16)] + [((rows, width), BF16)] * 3,
        (place, x, grad_middle, full[0], full[1], full[2], full[3], *pieces),
        (4, 5, 6, 1, 2),
        us=4,
    )
    c_at, first, short_ff_grads, grad_in = phase(c_at, first, short_ff_grads, grad_in)
    other = {0: c_at, 2: swap(c_at, "seq", 2), 4: swap(c_at, "seq", 4)}
    first |= {6: swap(first[2], "seq", 4)}
    other |= {6: swap(other[4], "seq", 2)}
    found = [
        half | {step + 1: swap(half[step], "seq", 1) for step in (0, 2, 4, 6)}
        for half in (first, other)
    ]
    c_shares = [half[step] for half in found for step in range(HEADS)]
    at_grads = whole_grads(place, c_shares, batch, (full, brief))
    full_ff_grads = whole_grads(place, [after(b_shares, at_grads[0])], batch, (), full)

    def arranged(attention, feed_forward):
        grad_q, grad_k, grad_v, grad_o, grad_gain_a = attention
        contract, expand, grad_gain_f = feed_forward
        return (grad_gain_a[0], grad_q, grad_k, grad_v, grad_o, grad_gain_f[0], expand, contract)

    return (
        (output[None], grad_in[None])
        + arranged(at_grads[:5], full_ff_grads)
        + arranged(at_grads[5:], short_ff_grads)
    )


def from_behind(block, axis, distance):
    devices = range(lax.axis_size(axis))
    route = [(i - distance, i) for i in devices if i - distance in devices]
    return lax.ppermute(block, axis, route)


def normalize(stream, gain):
    row_mean = jnp.mean(stream, axis=-1, keepdims=True)
    centered = stream - row_mean
    spread = jnp.mean(centered * centered, axis=-1, keepdims=True)
    return centered * lax.rsqrt(spread + norm_eps) * gain


def rope_table(positions):
    half_size = HEAD // 2
    frequency = jnp.power(10000.0, -jnp.arange(half_size, dtype=jnp.float32) * 2.0 / HEAD)
    angles = positions.astype(jnp.float32)[:, None] * frequency[None, :]
    return (jnp.cos(angles)[:, None, :], jnp.sin(angles)[:, None, :])


def rotate(values, angle_cos, angle_sin):
    first_half, second_half = jnp.split(values, 2, axis=-1)
    return jnp.concatenate(
        [
            first_half * angle_cos - second_half * angle_sin,
            first_half * angle_sin + second_half * angle_cos,
        ],
        axis=-1,
    )


def rotate_back(grads, angle_cos, angle_sin):
    first_half, second_half = jnp.split(grads, 2, axis=-1)
    return jnp.concatenate(
        [
            first_half * angle_cos + second_half * angle_sin,
            second_half * angle_cos - first_half * angle_sin,
        ],
        axis=-1,
    )


def split_heads(matrix):
    return matrix.reshape(matrix.shape[0], HEADS, HEAD)


def project(stream, params, angle_cos, angle_sin):
    normed_in = normalize(stream, params[0]).astype(jnp.bfloat16)

    def heads_of(matrix):
        return split_heads(jnp.dot(normed_in, matrix, preferred_element_type=jnp.float32))

    queries = rotate(heads_of(params[1]), angle_cos, angle_sin).astype(jnp.bfloat16)
    keys_here = rotate(heads_of(params[2]), angle_cos, angle_sin).astype(jnp.bfloat16)
    values_here = heads_of(params[3]).astype(jnp.bfloat16)
    return (normed_in, queries, keys_here, values_here)


def masked_scores(queries, keys_all, query_places, key_places):
    scores = jnp.einsum(
        "nhe,mhe->hnm", queries, keys_all, preferred_element_type=jnp.float32
    ) * HEAD ** (-0.5)
    allowed = key_places[None, None, :] <= query_places[None, :, None]
    return jnp.where(allowed, scores, -1e30)


def attend(queries, keys_all, values_all, query_places, key_places):
    scores = masked_scores(queries, keys_all, query_places, key_places)
    highest_score = jnp.max(scores, axis=-1, keepdims=True)
    log_total = highest_score + jnp.log(
        jnp.sum(jnp.exp(scores - highest_score), axis=-1, keepdims=True)
    )
    prob_low = jnp.exp(scores - log_total).astype(jnp.bfloat16)
    attended = jnp.einsum("hnm,mhe->nhe", prob_low, values_all, preferred_element_type=jnp.float32)
    return (attended, log_total)


def attend_back(queries, keys_all, values_all, query_places, key_places, log_total, grad_attended):
    scores = masked_scores(queries, keys_all, query_places, key_places)
    probs_full = jnp.exp(scores - log_total)
    grad_probs = jnp.einsum(
        "nhe,mhe->hnm", grad_attended, values_all, preferred_element_type=jnp.float32
    )
    row_inner = jnp.sum(probs_full * grad_probs, axis=-1, keepdims=True)
    grad_scores = (probs_full * (grad_probs - row_inner)).astype(jnp.bfloat16)
    grad_queries = jnp.einsum(
        "hnm,mhe->nhe", grad_scores, keys_all, preferred_element_type=jnp.float32
    ) * HEAD ** (-0.5)
    return (grad_queries, grad_scores, probs_full.astype(jnp.bfloat16), row_inner)


def finish(stream, attended, params):
    row_count, width = stream.shape
    attended_low = attended.reshape(row_count, width).astype(jnp.bfloat16)
    middle = stream + jnp.dot(attended_low, params[4], preferred_element_type=jnp.float32)
    normed_mid = normalize(middle, params[5]).astype(jnp.bfloat16)
    hidden_pre = jnp.dot(normed_mid, params[6], preferred_element_type=jnp.float32)
    hidden_low = jax.nn.gelu(hidden_pre, approximate=True).astype(jnp.bfloat16)
    result = middle + jnp.dot(hidden_low, params[7], preferred_element_type=jnp.float32)
    return (result, (attended_low, middle, normed_mid, hidden_pre, hidden_low))


def finish_back(grad_result, finish_saved, params):
    attended_low, middle, normed_mid, hidden_pre, hidden_low = finish_saved
    grad_low = grad_result.astype(jnp.bfloat16)
    grad_contract = jnp.einsum(
        "nf,nd->fd", hidden_low, grad_low, preferred_element_type=jnp.float32
    )
    grad_hidden = jnp.einsum("nd,fd->nf", grad_low, params[7], preferred_element_type=jnp.float32)
    gelu_value, gelu_pull = jax.vjp(partial(jax.nn.gelu, approximate=True), hidden_pre)
    grad_pre = gelu_pull(grad_hidden)[0].astype(jnp.bfloat16)
    grad_expand = jnp.einsum("nd,nf->df", normed_mid, grad_pre, preferred_element_type=jnp.float32)
    grad_normed = jnp.einsum("nf,df->nd", grad_pre, params[6], preferred_element_type=jnp.float32)
    norm_value, norm_pull = jax.vjp(normalize, middle, params[5])
    grad_norm_in, grad_gain_ffn = norm_pull(grad_normed)
    grad_middle = grad_result + grad_norm_in
    middle_low = grad_middle.astype(jnp.bfloat16)
    grad_output_w = jnp.einsum(
        "nc,nd->cd", attended_low, middle_low, preferred_element_type=jnp.float32
    )
    grad_attended = split_heads(
        jnp.einsum("nd,cd->nc", middle_low, params[4], preferred_element_type=jnp.float32).astype(
            jnp.bfloat16
        )
    )
    return (grad_middle, grad_attended, grad_output_w, grad_expand, grad_contract, grad_gain_ffn)


def start_back(
    grad_queries, grad_keys, grad_values, stream, params, normed_in, angle_cos, angle_sin
):
    row_count, width = stream.shape
    query_low = (
        rotate_back(grad_queries, angle_cos, angle_sin)
        .reshape(row_count, width)
        .astype(jnp.bfloat16)
    )
    key_low = (
        rotate_back(grad_keys, angle_cos, angle_sin).reshape(row_count, width).astype(jnp.bfloat16)
    )
    value_low = grad_values.reshape(row_count, width).astype(jnp.bfloat16)
    grad_query = jnp.einsum("nd,nc->dc", normed_in, query_low, preferred_element_type=jnp.float32)
    grad_key = jnp.einsum("nd,nc->dc", normed_in, key_low, preferred_element_type=jnp.float32)
    grad_value = jnp.einsum("nd,nc->dc", normed_in, value_low, preferred_element_type=jnp.float32)
    grad_normed = (
        jnp.einsum("nc,dc->nd", query_low, params[1], preferred_element_type=jnp.float32)
        + jnp.einsum("nc,dc->nd", key_low, params[2], preferred_element_type=jnp.float32)
        + jnp.einsum("nc,dc->nd", value_low, params[3], preferred_element_type=jnp.float32)
    )
    norm_value, norm_pull = jax.vjp(normalize, stream, params[0])
    grad_stream, grad_gain_attn = norm_pull(grad_normed)
    return (grad_stream, grad_gain_attn, grad_query, grad_key, grad_value)


def local_forward(stream, places, params, fetch):
    angle_cos, angle_sin = rope_table(places)
    normed_in, queries, keys_here, values_here = project(stream, params, angle_cos, angle_sin)
    row_count, width = stream.shape
    keys_local = keys_here.reshape(row_count, width)
    values_local = values_here.reshape(row_count, width)
    keys_flat, values_flat = fetch(keys_local, values_local)
    key_places = jnp.arange(keys_flat.shape[0], dtype=jnp.int32)
    attended, log_total = attend(
        queries, split_heads(keys_flat), split_heads(values_flat), places, key_places
    )
    result, finish_saved = finish(stream, attended, params)
    return (
        result,
        (
            normed_in,
            queries,
            keys_local,
            values_local,
            keys_flat,
            values_flat,
            log_total,
            angle_cos,
            angle_sin,
            finish_saved,
        ),
    )


def local_backward(grad_result, stream, places, params, saved, keys_flat, values_flat, key_sum):
    normed_in, queries = (saved[0], saved[1])
    log_total, angle_cos, angle_sin, finish_saved = (saved[6], saved[7], saved[8], saved[9])
    grad_middle, grad_attended, grad_output_w, grad_expand, grad_contract, grad_gain_ffn = (
        finish_back(grad_result, finish_saved, params)
    )
    row_count, width = stream.shape
    key_places = jnp.arange(keys_flat.shape[0], dtype=jnp.int32)
    grad_queries, grad_scores, prob_low, row_inner = attend_back(
        queries,
        split_heads(keys_flat),
        split_heads(values_flat),
        places,
        key_places,
        log_total,
        grad_attended,
    )

    def contribution(first_row, term_rows):
        grad_keys = jnp.einsum(
            "hnm,nhe->mhe", grad_scores, queries, preferred_element_type=jnp.float32
        ) * HEAD ** (-0.5)
        grad_values = jnp.einsum(
            "hnm,nhe->mhe", prob_low, grad_attended, preferred_element_type=jnp.float32
        )
        return jnp.concatenate(
            [grad_keys.reshape(term_rows, width), grad_values.reshape(term_rows, width)], axis=1
        )

    both_grads = key_sum(contribution, row_count, (queries, grad_attended, log_total, row_inner))
    grad_stream, grad_gain_attn, grad_query, grad_key, grad_value = start_back(
        grad_queries,
        split_heads(both_grads[:, :width]),
        split_heads(both_grads[:, width:]),
        stream,
        params,
        normed_in,
        angle_cos,
        angle_sin,
    )
    return (
        grad_middle + grad_stream,
        (
            grad_gain_attn,
            grad_query,
            grad_key,
            grad_value,
            grad_output_w,
            grad_gain_ffn,
            grad_expand,
            grad_contract,
        ),
    )


def whole_forward(stream, params):
    row_count, width = stream.shape
    places = jnp.arange(row_count, dtype=jnp.int32)
    angle_cos, angle_sin = rope_table(places)
    normed_in, queries, keys_here, values_here = project(stream, params, angle_cos, angle_sin)
    block_rows = 512
    block_count = row_count // block_rows

    def one_block(pieces):
        return attend(pieces[0], keys_here, values_here, pieces[1], places)

    attended, log_total = lax.map(
        one_block,
        (
            queries.reshape(block_count, block_rows, HEADS, HEAD),
            places.reshape(block_count, block_rows),
        ),
    )
    result, finish_saved = finish(stream, attended.reshape(row_count, HEADS, HEAD), params)
    return (
        result,
        (normed_in, queries, keys_here, values_here, log_total, angle_cos, angle_sin, finish_saved),
    )


def whole_backward(grad_result, stream, params, saved):
    normed_in, queries, keys_here, values_here, log_total, angle_cos, angle_sin, finish_saved = (
        saved
    )
    grad_middle, grad_attended, grad_output_w, grad_expand, grad_contract, grad_gain_ffn = (
        finish_back(grad_result, finish_saved, params)
    )
    row_count, width = stream.shape
    places = jnp.arange(row_count, dtype=jnp.int32)
    block_rows = 512
    block_count = row_count // block_rows

    def one_block(running, pieces):
        query_block, place_block, total_block, grad_block = pieces
        grad_queries, grad_scores, prob_low, row_inner = attend_back(
            query_block, keys_here, values_here, place_block, places, total_block, grad_block
        )
        grad_keys = running[0] + jnp.einsum(
            "hnm,nhe->mhe", grad_scores, query_block, preferred_element_type=jnp.float32
        ) * HEAD ** (-0.5)
        grad_values = running[1] + jnp.einsum(
            "hnm,nhe->mhe", prob_low, grad_block, preferred_element_type=jnp.float32
        )
        return ((grad_keys, grad_values), grad_queries)

    zero_grads = jnp.zeros((row_count, HEADS, HEAD), jnp.float32)
    (grad_keys, grad_values), grad_queries = lax.scan(
        one_block,
        (zero_grads, zero_grads),
        (
            queries.reshape(block_count, block_rows, HEADS, HEAD),
            places.reshape(block_count, block_rows),
            log_total,
            grad_attended.reshape(block_count, block_rows, HEADS, HEAD),
        ),
    )
    grad_stream, grad_gain_attn, grad_query, grad_key, grad_value = start_back(
        grad_queries.reshape(row_count, HEADS, HEAD),
        grad_keys,
        grad_values,
        stream,
        params,
        normed_in,
        angle_cos,
        angle_sin,
    )
    return (
        grad_middle + grad_stream,
        (
            grad_gain_attn,
            grad_query,
            grad_key,
            grad_value,
            grad_output_w,
            grad_gain_ffn,
            grad_expand,
            grad_contract,
        ),
    )


def by_rows(
    inputs,
    cotangent,
    full_gain_attn,
    full_query,
    full_key,
    full_value,
    full_output,
    full_gain_ffn,
    full_expand,
    full_contract,
    short_gain_attn,
    short_query,
    short_key,
    short_value,
    short_output,
    short_gain_ffn,
    short_expand,
    short_contract,
):
    full_params = (
        full_gain_attn,
        full_query,
        full_key,
        full_value,
        full_output,
        full_gain_ffn,
        full_expand,
        full_contract,
    )
    short_params = (
        short_gain_attn,
        short_query,
        short_key,
        short_value,
        short_output,
        short_gain_ffn,
        short_expand,
        short_contract,
    )
    stream_in = inputs[0]
    row_count, width = stream_in.shape
    own_short = row_count // 3
    position = lax.axis_index("seq")
    seq_parts = lax.axis_size("seq")
    places = position * row_count + jnp.arange(row_count, dtype=jnp.int32)

    def fetch_full(keys_local, values_local):
        return (
            lax.all_gather(keys_local, "seq", axis=0, tiled=True),
            lax.all_gather(values_local, "seq", axis=0, tiled=True),
        )

    residual, full_saved = local_forward(stream_in, places, full_params, fetch_full)
    tail_rows = from_behind(residual[row_count - 2 :], "seq", 1)
    shifted = jnp.concatenate([tail_rows, residual[: row_count - 2]], axis=0)
    pooled = jnp.mean(shifted.reshape(own_short, 3, width), axis=1)
    pooled_all = lax.all_gather(pooled, "seq", axis=0, tiled=True)
    short_all, short_saved = whole_forward(pooled_all, short_params)
    short_result = lax.dynamic_slice_in_dim(short_all, position * own_short, own_short, 0)
    output = residual + jnp.repeat(short_result, 3, axis=0)
    grad_output = cotangent[0]
    grad_short = jnp.sum(grad_output.reshape(own_short, 3, width), axis=1)
    grad_short_all = lax.all_gather(grad_short, "seq", axis=0, tiled=True)
    grad_pooled_all, short_grads = whole_backward(
        grad_short_all, pooled_all, short_params, short_saved
    )
    grad_pooled = lax.dynamic_slice_in_dim(grad_pooled_all, position * own_short, own_short, 0)
    short_grads = tuple(
        (
            lax.dynamic_slice_in_dim(
                gradient,
                position * (gradient.shape[0] // seq_parts),
                gradient.shape[0] // seq_parts,
                0,
            )
            for gradient in short_grads
        )
    )
    grad_shifted = jnp.repeat(grad_pooled / 3.0, 3, axis=0)
    carried = from_behind(grad_shifted[:2], "seq", -1)
    grad_residual = grad_output + jnp.concatenate([grad_shifted[2:], carried], axis=0)
    keys_flat, values_flat = (
        lax.all_gather(full_saved[2], "seq", axis=0, tiled=True),
        lax.all_gather(full_saved[3], "seq", axis=0, tiled=True),
    )

    def full_sum(contribution, term_rows, query_side):
        return lax.psum_scatter(
            contribution(jnp.int32(0), term_rows * lax.axis_size("seq")).astype(jnp.bfloat16),
            "seq",
            scatter_dimension=0,
            tiled=True,
        ).astype(jnp.float32)

    grad_input, full_grads = local_backward(
        grad_residual, stream_in, places, full_params, full_saved, keys_flat, values_flat, full_sum
    )
    full_shares = (
        lax.psum_scatter(
            full_grads[0].astype(jnp.bfloat16), "seq", scatter_dimension=0, tiled=True
        ).astype(jnp.float32),
        lax.psum_scatter(
            full_grads[1].astype(jnp.bfloat16), "seq", scatter_dimension=0, tiled=True
        ).astype(jnp.float32),
        lax.psum_scatter(
            full_grads[2].astype(jnp.bfloat16), "seq", scatter_dimension=0, tiled=True
        ).astype(jnp.float32),
        lax.psum_scatter(
            full_grads[3].astype(jnp.bfloat16), "seq", scatter_dimension=0, tiled=True
        ).astype(jnp.float32),
        lax.psum_scatter(
            full_grads[4].astype(jnp.bfloat16), "seq", scatter_dimension=0, tiled=True
        ).astype(jnp.float32),
        lax.psum_scatter(
            full_grads[5].astype(jnp.bfloat16), "seq", scatter_dimension=0, tiled=True
        ).astype(jnp.float32),
        lax.psum_scatter(
            full_grads[6].astype(jnp.bfloat16), "seq", scatter_dimension=0, tiled=True
        ).astype(jnp.float32),
        lax.psum_scatter(
            full_grads[7].astype(jnp.bfloat16), "seq", scatter_dimension=0, tiled=True
        ).astype(jnp.float32),
    )
    shares = tuple(full_shares) + tuple(short_grads)
    totals = (
        lax.psum(shares[0].astype(jnp.bfloat16), "batch").astype(jnp.float32),
        lax.psum(shares[1].astype(jnp.bfloat16), "batch").astype(jnp.float32),
        lax.psum(shares[2].astype(jnp.bfloat16), "batch").astype(jnp.float32),
        lax.psum(shares[3].astype(jnp.bfloat16), "batch").astype(jnp.float32),
        lax.psum(shares[4].astype(jnp.bfloat16), "batch").astype(jnp.float32),
        lax.psum(shares[5].astype(jnp.bfloat16), "batch").astype(jnp.float32),
        lax.psum(shares[6].astype(jnp.bfloat16), "batch").astype(jnp.float32),
        lax.psum(shares[7].astype(jnp.bfloat16), "batch").astype(jnp.float32),
        lax.psum(shares[8].astype(jnp.bfloat16), "batch").astype(jnp.float32),
        lax.psum(shares[9].astype(jnp.bfloat16), "batch").astype(jnp.float32),
        lax.psum(shares[10].astype(jnp.bfloat16), "batch").astype(jnp.float32),
        lax.psum(shares[11].astype(jnp.bfloat16), "batch").astype(jnp.float32),
        lax.psum(shares[12].astype(jnp.bfloat16), "batch").astype(jnp.float32),
        lax.psum(shares[13].astype(jnp.bfloat16), "batch").astype(jnp.float32),
        lax.psum(shares[14].astype(jnp.bfloat16), "batch").astype(jnp.float32),
        lax.psum(shares[15].astype(jnp.bfloat16), "batch").astype(jnp.float32),
    )
    whole = (
        lax.all_gather(totals[0].astype(jnp.bfloat16), "seq", axis=0, tiled=True).astype(
            jnp.float32
        ),
        lax.all_gather(totals[1].astype(jnp.bfloat16), "seq", axis=0, tiled=True).astype(
            jnp.float32
        ),
        lax.all_gather(totals[2].astype(jnp.bfloat16), "seq", axis=0, tiled=True).astype(
            jnp.float32
        ),
        lax.all_gather(totals[3].astype(jnp.bfloat16), "seq", axis=0, tiled=True).astype(
            jnp.float32
        ),
        lax.all_gather(totals[4].astype(jnp.bfloat16), "seq", axis=0, tiled=True).astype(
            jnp.float32
        ),
        lax.all_gather(totals[5].astype(jnp.bfloat16), "seq", axis=0, tiled=True).astype(
            jnp.float32
        ),
        lax.all_gather(totals[6].astype(jnp.bfloat16), "seq", axis=0, tiled=True).astype(
            jnp.float32
        ),
        lax.all_gather(totals[7].astype(jnp.bfloat16), "seq", axis=0, tiled=True).astype(
            jnp.float32
        ),
        lax.all_gather(totals[8].astype(jnp.bfloat16), "seq", axis=0, tiled=True).astype(
            jnp.float32
        ),
        lax.all_gather(totals[9].astype(jnp.bfloat16), "seq", axis=0, tiled=True).astype(
            jnp.float32
        ),
        lax.all_gather(totals[10].astype(jnp.bfloat16), "seq", axis=0, tiled=True).astype(
            jnp.float32
        ),
        lax.all_gather(totals[11].astype(jnp.bfloat16), "seq", axis=0, tiled=True).astype(
            jnp.float32
        ),
        lax.all_gather(totals[12].astype(jnp.bfloat16), "seq", axis=0, tiled=True).astype(
            jnp.float32
        ),
        lax.all_gather(totals[13].astype(jnp.bfloat16), "seq", axis=0, tiled=True).astype(
            jnp.float32
        ),
        lax.all_gather(totals[14].astype(jnp.bfloat16), "seq", axis=0, tiled=True).astype(
            jnp.float32
        ),
        lax.all_gather(totals[15].astype(jnp.bfloat16), "seq", axis=0, tiled=True).astype(
            jnp.float32
        ),
    )
    return (output[None], grad_input[None]) + tuple(whole)


def solution(mesh):
    sequence = P("batch", "seq", None)
    seq, batch = mesh.shape["seq"], mesh.shape["batch"]
    fits = seq == HEADS and batch == 4
    return jax.shard_map(
        by_heads if fits else by_rows,
        mesh=mesh,
        in_specs=(sequence, sequence) + (P(),) * 16,
        out_specs=(sequence, sequence) + (P(),) * 16,
        check_vma=False,
    )
```

```python
from functools import partial

import jax
import jax.numpy as jnp
import numpy as np
from jax import lax
from jax.experimental import pallas as pl
from jax.experimental.pallas import tpu as pltpu
from jax.sharding import PartitionSpec as P

HEADS = 8
HEAD = 64
LANES = 128
BLOCK = 256
FF_PARTS = 1
F32 = jnp.float32
BF16 = jnp.bfloat16


norm_eps = 1e-05


def dot_nn(left, right):
    return jnp.dot(left, right, preferred_element_type=F32)


def dot_nt(left, right):
    return lax.dot_general(left, right, (((1,), (1,)), ((), ())), preferred_element_type=F32)


def dot_tn(left, right):
    return lax.dot_general(left, right, (((0,), (0,)), ((), ())), preferred_element_type=F32)


def lower_half(rows):
    return lax.broadcasted_iota(jnp.int32, (rows, LANES), 1) < HEAD


def turn(values):
    return pltpu.roll(values, HEAD, 1)


def swap_pairs(values):
    lane = lax.broadcasted_iota(jnp.int32, values.shape, 1)
    return jnp.where(
        lane % HEAD < HEAD // 2,
        pltpu.roll(values, LANES - HEAD // 2, 1),
        pltpu.roll(values, HEAD // 2, 1),
    )


def rope(values, table):
    return values * table[:, :LANES] + swap_pairs(values) * table[:, LANES:]


def rope_back(grads, table):
    return grads * table[:, :LANES] - swap_pairs(grads) * table[:, LANES:]


def rope_constants(rows):
    frequency = np.power(
        np.float32(10000.0), -np.arange(HEAD // 2, dtype=np.float32) * np.float32(2.0 / HEAD)
    ).astype(np.float32)
    angles = np.arange(rows, dtype=np.float32)[:, None] * frequency[None, :]
    cosine, sine = np.cos(angles), np.sin(angles)
    table = np.concatenate([cosine] * 4 + [-sine, sine] * 2, axis=1)
    return jnp.asarray(table, F32)


def norm_parts(stream):
    centered = stream - jnp.mean(stream, axis=-1, keepdims=True)
    spread = jnp.mean(centered * centered, axis=-1, keepdims=True)
    scale = lax.rsqrt(spread + norm_eps)
    return centered * scale, scale


def norm_back(grad, gain, unit, scale):
    grad_unit = grad * gain
    inner = jnp.mean(grad_unit * unit, axis=-1, keepdims=True)
    return scale * (grad_unit - jnp.mean(grad_unit, axis=-1, keepdims=True) - unit * inner)


GELU_SCALE = 0.7978845608028654
GELU_CUBE = 0.044715


def gelu_both(pre):
    square = pre * pre
    half = 0.5 + 0.5 * jnp.tanh(pre * (GELU_SCALE + GELU_SCALE * GELU_CUBE * square))
    bend = pre * (2.0 * GELU_SCALE + 6.0 * GELU_SCALE * GELU_CUBE * square)
    return pre * half, half * (1.0 + (1.0 - half) * bend)


def gelu_value(pre):
    tanh = jnp.tanh(GELU_SCALE * pre * (1.0 + GELU_CUBE * pre * pre))
    return 0.5 * pre * (1.0 + tanh)


def causal(scores, first_row, first_key):
    row = lax.broadcasted_iota(jnp.int32, scores.shape, 0) + first_row
    key = lax.broadcasted_iota(jnp.int32, scores.shape, 1) + first_key
    return jnp.where(key <= row, scores, -1e30)


def fold_rows(values):
    half = values.shape[0] // 2
    return jnp.where(lower_half(half), values[:half], turn(values[half:]))


def unfold_rows(folded):
    low = lower_half(folded.shape[0])
    return jnp.where(low, folded, 0.0), jnp.where(low, turn(folded), 0.0)


def rows_at(start, size, multiple):
    return pl.ds(pl.multiple_of(start, multiple), size)


class Late:
    def __init__(self, source, target, semaphores, axis=0, parts=1):
        self.target, self.shape = target, target.shape
        size = target.shape[axis] // parts
        cuts = [(slice(None),) * axis + (pl.ds(part * size, size),) for part in range(parts)]
        self.copies = [
            pltpu.make_async_copy(source.at[cut], target.at[cut], semaphore)
            for cut, semaphore in zip(cuts, semaphores)
        ]
        self.waiting = set(range(parts))

    def ready(self, part=None):
        for at in sorted(self.waiting if part is None else self.waiting & {part}):
            self.copies[at].wait()
            self.waiting.remove(at)
        return self.target

    def __getitem__(self, index):
        return self.ready()[index]


def with_late(kernel, late, argument_count, out_count, *refs):
    arguments, outs = list(refs[:argument_count]), refs[argument_count : argument_count + out_count]
    rest = refs[argument_count + out_count :]
    first, taken, begun = len(rest) - len(late) - 1, 0, []
    for at, (place, _, part, axis, parts) in enumerate(late):
        source = arguments[place]
        source = source if part is None else part(source, refs[0][0])
        semaphores = [rest[-1].at[taken + step] for step in range(parts)]
        arguments[place] = Late(source, rest[first + at], semaphores, axis, parts)
        begun += [(part, at, copy) for part, copy in enumerate(arguments[place].copies)]
        taken += parts
    for _, _, copy in sorted(begun, key=lambda entry: entry[:2]):
        copy.start()
    kernel(*arguments, *outs, *rest[:first])


class Departures:
    def __init__(self, semaphores):
        self.semaphores, self.copies = semaphores, []

    def send(self, source, target):
        copy = pltpu.make_async_copy(source, target, self.semaphores.at[len(self.copies)])
        copy.start()
        self.copies.append(copy)

    def wait(self):
        for copy in self.copies:
            copy.wait()


def paired(refs):
    size = refs[0].shape[0] // 2
    pairs = len(refs) // 2
    return [
        refs[step // 2].at[pl.ds(0, size), :]
        if step % 2 == 0
        else refs[pairs + step // 2].at[pl.ds(size, size), :]
        for step in range(2 * pairs)
    ]


def by_distance(share, pieces, seat):
    rows = pieces[0].shape[0]
    for step in range(len(pieces)):
        pieces[step][...] = share[rows_at((seat ^ step) * rows, rows, 16), :]


def keep_and_send(share, keep, send, seat, parts, first=0):
    rows = share.shape[0] // parts
    stride = keep.shape[0] // (parts // 2)
    for step in range(parts):
        target = keep if step % 2 == 0 else send
        at = (step // 2) * stride + first
        target[at : at + rows] = share[rows_at((seat ^ step) * rows, rows, 16), :]


def load_kernel(place, *refs):
    count = (len(refs) - 1) // 2
    copies = [
        pltpu.make_async_copy(refs[at], refs[count + at], refs[-1].at[at]) for at in range(count)
    ]
    for copy in copies:
        copy.start()
    for copy in copies:
        copy.wait()


def project_kernel(place, x, cot, gain, w_q, w_k, w_v, table, *refs):
    pieces = refs[: HEADS // 2]
    normed_out, bundle, heads, chunks = refs[HEADS // 2 :]
    rows, width = x.shape
    me = place[0]
    unit, _ = norm_parts(x[...])
    normed = (unit * gain[...]).astype(BF16)
    q = dot_nn(normed, w_q[...])
    k = dot_nn(normed, w_k[...])
    v = dot_nn(normed, w_v[...])
    low = lower_half(rows)
    low_half = lower_half(rows // 2)
    own = table[...]
    for chunk in range(width // LANES):
        cut = slice(chunk * LANES, (chunk + 1) * LANES)
        q_chunk = rope(q[:, cut], own) * HEAD**-0.5
        k_chunk = rope(k[:, cut], own)
        v_chunk = v[:, cut]
        first, later = q_chunk[: rows // 2], q_chunk[rows // 2 :]
        heads[2 * chunk, :rows] = jnp.where(low, k_chunk, turn(v_chunk)).astype(BF16)
        heads[2 * chunk + 1, :rows] = jnp.where(low, turn(k_chunk), v_chunk).astype(BF16)
        heads[2 * chunk, rows:] = jnp.where(low_half, first, turn(later)).astype(BF16)
        heads[2 * chunk + 1, rows:] = jnp.where(low_half, turn(first), later).astype(BF16)
    for step in range(HEADS):
        at = (step % 2) * heads.shape[1]
        pieces[step // 2][at : at + heads.shape[1]] = heads[me ^ step]
    normed_out[...] = normed
    bundle[:rows] = cot[...].astype(BF16)
    for chunk in range(width // LANES):
        cut = slice(chunk * LANES, (chunk + 1) * LANES)
        chunks[chunk] = cot[:, cut]
        total = sum(chunks[chunk, pl.ds(s, rows // 3, stride=3), :] for s in range(3))
        bundle[rows:, cut] = total.astype(BF16)


def attend_kernel(place, *refs):
    pieces, outs = paired(refs[:HEADS]), refs[HEADS : HEADS + HEADS // 2]
    q_out, kv_out, lse_out, q_all, kv_all, lse_o, semaphores = refs[HEADS + HEADS // 2 :]
    departures = Departures(semaphores)
    me = place[0]
    rows = outs[0].shape[0]
    for step in range(HEADS):
        start = (me ^ step) * rows
        piece = pieces[step][...]
        kv_all[rows_at(start, rows, 16), :] = piece[:rows]
        first, later = unfold_rows(piece[rows:].astype(F32))
        q_all[rows_at(start, rows // 2, 16), :] = first.astype(BF16)
        q_all[rows_at(start + rows // 2, rows // 2, 16), :] = later.astype(BF16)
    departures.send(q_all, q_out)
    departures.send(kv_all, kv_out)
    low = lower_half(BLOCK)
    for block in range(q_all.shape[0] // BLOCK):
        cut = slice(block * BLOCK, (block + 1) * BLOCK)
        seen = kv_all[: (block + 1) * BLOCK]
        scores = causal(dot_nt(q_all[cut], seen), block * BLOCK, 0)
        most = jnp.max(scores, axis=-1, keepdims=True)
        weights = jnp.exp(scores - most)
        total = jnp.sum(weights, axis=-1, keepdims=True)
        attended = dot_nn(weights.astype(BF16), seen) / total
        lse_o[cut] = jnp.where(low, most + jnp.log(total), attended)
    departures.send(lse_o, lse_out)
    for step in range(HEADS):
        own = lse_o[rows_at((me ^ step) * rows, rows, 16), :]
        at = (step % 2) * (rows // 2)
        outs[step // 2][at : at + rows // 2] = jnp.where(
            lower_half(rows // 2), turn(own[: rows // 2]), own[rows // 2 :]
        ).astype(BF16)
    departures.wait()


def finish_kernel(place, x, normed_a, gain, w_o, w_e, w_c, *refs):
    pieces = paired(refs[:HEADS])
    result_hbm, middle_hbm, normed_hbm, pooled_out = refs[HEADS : HEADS + 4]
    result_out, middle_out, normed_out, att_out, heads, chunks, semaphores = refs[HEADS + 4 :]
    departures = Departures(semaphores)
    rows, width = x.shape
    me = place[0]
    for step in range(HEADS):
        heads[me ^ step] = pieces[step][...].astype(F32)
    low = lower_half(rows // 2)
    for chunk in range(width // LANES):
        cut = slice(chunk * LANES, (chunk + 1) * LANES)
        even, odd = heads[2 * chunk], heads[2 * chunk + 1]
        att_out[: rows // 2, cut] = jnp.where(low, even, turn(odd)).astype(BF16)
        att_out[rows // 2 :, cut] = jnp.where(low, turn(even), odd).astype(BF16)
    middle = x[...] + dot_nn(att_out[...], w_o[...])
    middle_out[...] = middle
    unit, _ = norm_parts(middle)
    normed = (unit * gain[...]).astype(BF16)
    normed_out[:rows] = normed
    normed_out[rows:] = normed_a[...]
    departures.send(middle_out, middle_hbm)
    departures.send(normed_out, normed_hbm)
    result = middle
    size = w_e.shape[1] // FF_PARTS
    for part in range(FF_PARTS):
        cut = slice(part * size, (part + 1) * size)
        hidden = gelu_value(dot_nn(normed, w_e.ready(part)[:, cut])).astype(BF16)
        result = result + dot_nn(hidden, w_c.ready(part)[cut, :])
    result_out[...] = result
    departures.send(result_out, result_hbm)
    short = rows // 3
    for chunk in range(width // LANES):
        cut = slice(chunk * LANES, (chunk + 1) * LANES)
        chunks[chunk, :8] = jnp.zeros((8, LANES), F32)
        chunks[chunk, 8:] = result[:, cut]
        total = sum(chunks[chunk, pl.ds(s, short, stride=3), :] for s in (6, 7, 8))
        pooled_out[:short, cut] = (total / 3.0).astype(BF16)
    tail = (result[rows - 1 :] + result[rows - 2 : rows - 1]) / 3.0
    extra = pooled_out.shape[0] - short
    pooled_out[short:] = jnp.broadcast_to(tail, (extra, width)).astype(BF16)
    departures.wait()


def short_forward_kernel(
    place, gathered, table, gain_a, w_q, w_k, w_v, w_o, gain_f, w_e, w_c, *refs
):
    pieces, refs = refs[:HEADS], refs[HEADS:]
    own_middle, own_hidden = refs[:2]
    pooled, normed_a, q_s, k_s, v_s, o_s, lse_s, att, grad_middle = refs[2:11]
    share_pieces = refs[11:-8]
    extra, middle, normed_f, hidden, grad_pre, grad_normed, grad_low, share = refs[-8:]
    me, seat = place[0], place[1]
    count, width = pooled.shape
    short = count // HEADS
    chunk_count = width // LANES
    ff = w_e.shape[1]
    ff_own = ff // HEADS

    for step in range(HEADS):
        other = me ^ step
        pooled[rows_at(other * short, short, 16), :] = pieces[step][:short].astype(F32)
        extra[pl.ds(other, 1), :] = pieces[step][short:].astype(F32)[:1]
    for part in range(1, HEADS):
        at = slice(part * short, part * short + 1)
        pooled[at] = pooled[at] + extra[part - 1 : part]

    unit, _ = norm_parts(pooled[...])
    normed_a[...] = (unit * gain_a[...]).astype(BF16)
    low = lower_half(count)
    q = dot_nn(normed_a[...], w_q[...])
    turns = table[...]
    for chunk in range(chunk_count):
        q_chunk = rope(q[:, chunk * LANES : (chunk + 1) * LANES], turns) * HEAD**-0.5
        q_s[2 * chunk] = jnp.where(low, q_chunk, 0.0).astype(BF16)
        q_s[2 * chunk + 1] = jnp.where(low, 0.0, q_chunk).astype(BF16)
    k = dot_nn(normed_a[...], w_k[...])
    for chunk in range(chunk_count):
        k_s[chunk] = rope(k[:, chunk * LANES : (chunk + 1) * LANES], turns).astype(BF16)
    v = dot_nn(normed_a[...], w_v[...])
    for chunk in range(chunk_count):
        v_s[chunk] = v[:, chunk * LANES : (chunk + 1) * LANES].astype(BF16)

    low_block = lower_half(BLOCK)

    def attend_chunk(chunk, carry):
        results = []
        k_t = jnp.transpose(k_s[chunk])
        for half in range(2):
            scores = causal(dot_nn(q_s[2 * chunk + half], k_t), 0, 0)
            most = jnp.max(scores, axis=-1, keepdims=True)
            weights = jnp.exp(scores - most)
            total = jnp.sum(weights, axis=-1, keepdims=True)
            attended = dot_nn(weights.astype(BF16), v_s[chunk]) / total
            results.append((attended, most + jnp.log(total)))
        both = jnp.where(low, results[0][0], results[1][0])
        o_s[chunk] = both
        lse_s[chunk] = jnp.where(low, results[0][1], results[1][1])
        att[:, rows_at(chunk * LANES, LANES, LANES)] = both.astype(BF16)
        return carry

    lax.fori_loop(0, chunk_count, attend_chunk, 0)
    middle[...] = pooled[...] + dot_nn(att[...], w_o[...])
    unit, scale = norm_parts(middle[...])
    normed_f[...] = (unit * gain_f[...]).astype(BF16)

    for part in range(HEADS):
        grad_low[part * short : (part + 1) * short] = gathered[part]

    ff_part = ff // 4
    grad_normed[...] = jnp.zeros(grad_normed.shape, F32)
    w_e, w_c = w_e.ready(), w_c.ready()

    def feed_forward(part, carry):
        cut = rows_at(part * ff_part, ff_part, ff_part)
        pre = dot_nn(normed_f[...], w_e[:, cut])
        value, slope = gelu_both(pre)
        hidden[:, cut] = value.astype(BF16)
        grad_hidden = dot_nt(grad_low[...], w_c[cut, :])
        low_grad = (grad_hidden * slope).astype(BF16)
        grad_pre[:, cut] = low_grad
        grad_normed[...] += dot_nt(low_grad, w_e[:, cut])
        return carry

    lax.fori_loop(0, 4, feed_forward, 0)

    own_ff = rows_at(me * ff_own, ff_own, ff_own)
    share[:ff_own] = dot_tn(hidden[:, own_ff], grad_low[...]).astype(BF16)
    expand = dot_tn(normed_f[...], grad_pre[:, own_ff]).astype(BF16)
    share[ff_own : 2 * ff_own, : width // 2] = expand[: width // 2]
    share[ff_own : 2 * ff_own, width // 2 :] = expand[width // 2 :]
    by_distance(share, share_pieces, seat)

    mine = rows_at(me * short, short, 16)
    own_middle[...] = middle[mine, :]
    own_hidden[...] = hidden[mine, :]

    unit, scale = norm_parts(middle[...])
    grad_middle[...] = grad_low[...].astype(F32) + norm_back(
        grad_normed[...], gain_f[...], unit, scale
    )


def output_kernel(place, residual, middle, hidden, w_c, output, wide):
    rows, width = residual.shape
    short_out = middle[...] + dot_nn(hidden[...], w_c[...])
    for chunk in range(width // LANES):
        cut = slice(chunk * LANES, (chunk + 1) * LANES)
        for s in range(3):
            wide[chunk, pl.ds(s, rows // 3, stride=3), :] = short_out[:, cut]
        output[:, cut] = residual[:, cut] + wide[chunk]


def short_back_kernel(
    place,
    cot,
    gathered,
    table,
    gain_a,
    w_q,
    w_k,
    w_v,
    w_o,
    pooled,
    normed_a,
    q_s,
    k_s,
    v_s,
    o_s,
    lse_s,
    att,
    grad_middle,
    middle,
    normed_f,
    gain_f,
    w_e,
    w_c,
    all_hbm,
    share_hbm,
    middle_hbm,
    g1_out,
    grad_all,
    share,
    full_middle,
    semaphores,
    do_s,
    dq_s,
    dk_s,
    dv_s,
    wide,
    wo_s,
    grad_own,
):
    me = place[0]
    rows, width = cot.shape
    count = pooled.shape[0]
    full = rows * HEADS
    chunk_count = width // LANES
    low = lower_half(count)
    low_block = lower_half(BLOCK)
    g1 = grad_middle[...].astype(BF16)
    d_att = dot_nt(g1, w_o[...])
    for chunk in range(chunk_count):
        do_chunk = d_att[:, chunk * LANES : (chunk + 1) * LANES]
        do_s[2 * chunk] = jnp.where(low, do_chunk, 0.0).astype(BF16)
        do_s[2 * chunk + 1] = jnp.where(low, 0.0, do_chunk).astype(BF16)
    own_chunk = rows_at((me // 2) * LANES, LANES, LANES)
    wo_s[...] = dot_tn(att[:, own_chunk], g1)
    table = table.ready()

    def attend_back(chunk, carry):
        columns = rows_at(chunk * LANES, LANES, LANES)
        dq = []
        dk = [None]
        dv = [None]
        k_t = jnp.transpose(k_s[chunk])
        v_t = jnp.transpose(v_s[chunk])
        for half in range(2):
            head = 2 * chunk + half
            lse = lse_s[chunk][:, half * HEAD : half * HEAD + 1]
            delta = jnp.sum(do_s[head].astype(F32) * o_s[chunk], axis=-1, keepdims=True)
            dq_half = None
            for key in range(1):
                cut = slice(0, count)
                rest = slice(0, count)
                k_block, v_block = k_s[chunk, cut, :], v_s[chunk, cut, :]
                q_rest, do_rest = q_s[head, rest, :], do_s[head, rest, :]
                scores = causal(dot_nn(q_rest, k_t), 0, 0)
                probs = jnp.exp(scores - lse[rest])
                grad_probs = dot_nn(do_rest, v_t)
                ds = (probs * (grad_probs - delta[rest])).astype(BF16)
                term = dot_nn(ds, k_block)
                if key == 0:
                    dq_half = term
                else:
                    dq_half = jnp.concatenate(
                        [dq_half[: key * BLOCK], dq_half[key * BLOCK :] + term]
                    )
                term = dot_tn(ds, q_rest)
                dk[key] = term if half == 0 else dk[key] + term
                term = dot_tn(probs.astype(BF16), do_rest)
                dv[key] = term if half == 0 else dv[key] + term
            dq.append(dq_half)
        both = jnp.where(lower_half(count), dq[0], dq[1]) * HEAD**-0.5
        dq_s[:, columns] = rope_back(both, table[...]).astype(BF16)
        for key in range(1):
            key_cut = slice(0, count)
            dk_s[key_cut, columns] = rope_back(dk[key], table[key_cut, :]).astype(BF16)
            dv_s[key_cut, columns] = dv[key].astype(BF16)
        return carry

    lax.fori_loop(0, chunk_count, attend_back, 0)

    odd = me % 2 == 1
    low_width = lower_half(width)
    share_q = dot_tn(normed_a[...], dq_s[:, own_chunk])
    share_k = dot_tn(normed_a[...], dk_s[:, own_chunk])
    share_v = dot_tn(normed_a[...], dv_s[:, own_chunk])
    share_q = jnp.where(odd, turn(share_q), share_q)
    share_k = jnp.where(odd, share_k, turn(share_k))
    share_v = jnp.where(odd, turn(share_v), share_v)
    head_rows = wo_s[rows_at((me % 2) * HEAD, HEAD, HEAD), :]
    pack_attention(share, jnp.where(low_width, share_q, share_k), fold_rows(share_v), head_rows)

    grad_a = dot_nt(dq_s[...], w_q[...])
    grad_a += dot_nt(dk_s[...], w_k[...])
    grad_a += dot_nt(dv_s[...], w_v[...])
    unit, scale = norm_parts(pooled[...])
    grad_pooled = grad_middle[...] + norm_back(grad_a, gain_a[...], unit, scale)
    for chunk in range(chunk_count):
        cut = slice(chunk * LANES, (chunk + 1) * LANES)
        third = grad_pooled[:, cut] / 3.0
        for s in range(3):
            wide[chunk, pl.ds(6 + s, count, stride=3), :] = third
        wide[chunk, full + 6 : full + 8] = jnp.zeros((2, LANES), F32)
        grad_own[:, cut] = cot[:, cut] + wide[chunk, rows_at(me * rows + 8, rows, 8), :]
        for part in range(HEADS):
            more = wide[chunk, 8 + part * rows : 8 + (part + 1) * rows, :]
            grad_all[part * rows : (part + 1) * rows, cut] = (
                gathered[part, :, cut].astype(F32) + more
            ).astype(BF16)
    departures = Departures(semaphores)
    departures.send(share, share_hbm)
    departures.send(grad_all, all_hbm)
    feed_forward_back(grad_own, middle, normed_f, gain_f, w_e, w_c, full_middle, g1_out)
    departures.send(full_middle, middle_hbm)
    departures.wait()


def feed_forward_back(grad, middle, normed, gain, w_e, w_c, grad_middle_out, g1_out):
    grad_low = grad[...].astype(BF16)
    grad_normed = 0.0
    size = w_e.shape[1] // FF_PARTS
    for part in range(FF_PARTS):
        cut = slice(part * size, (part + 1) * size)
        own_w = w_e.ready(part)[:, cut]
        _, slope = gelu_both(dot_nn(normed[...], own_w))
        grad_hidden = dot_nt(grad_low, w_c.ready(part)[cut, :])
        grad_normed += dot_nt((grad_hidden * slope).astype(BF16), own_w)
    unit, scale = norm_parts(middle[...])
    grad_middle = grad[...] + norm_back(grad_normed, gain[...], unit, scale)
    grad_middle_out[...] = grad_middle
    g1_out[...] = grad_middle.astype(BF16)


def pack_attention(share, both_qk, folded_v, head_rows):
    half = both_qk.shape[0] // 2
    share[:half, :LANES] = both_qk[:half].astype(BF16)
    share[:half, LANES : 2 * LANES] = both_qk[half:].astype(BF16)
    share[:half, 2 * LANES : 3 * LANES] = folded_v.astype(BF16)
    size = head_rows.shape[0]
    for chunk in range(head_rows.shape[1] // LANES):
        share[chunk * size : (chunk + 1) * size, 3 * LANES :] = head_rows[
            :, chunk * LANES : (chunk + 1) * LANES
        ].astype(BF16)


def feed_forward_share_kernel(place, normed, grad, w_e, w_c, *refs):
    pieces, share = refs[:-1], refs[-1]
    seat = place[1]
    width, ff_own = w_e.shape
    normed = normed[...].reshape(-1, width)
    value, slope = gelu_both(dot_nn(normed, w_e[...]))
    grad_hidden = dot_nt(grad[...], w_c[...])
    grad_pre = (grad_hidden * slope).astype(BF16)
    share[:ff_own] = dot_tn(value.astype(BF16), grad[...]).astype(BF16)
    expand = dot_tn(normed, grad_pre).astype(BF16)
    share[ff_own:, : width // 2] = expand[: width // 2]
    share[ff_own:, width // 2 :] = expand[width // 2 :]
    by_distance(share, pieces, seat)


def attend_back_kernel(place, q_all, kv_all, lse_o, table, w_o, *refs):
    pieces, outs = refs[:HEADS], refs[HEADS : HEADS + HEADS // 2]
    dq_all, dkv_all, do_all, dkv_sum, dq_sum, q_t, do_t = refs[HEADS + HEADS // 2 :]
    me = place[0]
    rows = q_all.shape[0] // HEADS
    own_w = w_o[...]
    own_w = jnp.concatenate([jnp.zeros(own_w.shape, BF16), own_w])
    for step in range(HEADS):
        do_all[rows_at((me ^ step) * rows, rows, 16), :] = dot_nt(
            pieces[step][...], own_w
        ).astype(BF16)
    total = q_all.shape[0]
    lse = lse_o[...][:, :1]
    delta = jnp.sum(do_all[...].astype(F32) * lse_o[...], axis=-1, keepdims=True)
    dq_sum[...] = jnp.zeros(dq_sum.shape, F32)
    q_t[...] = jnp.transpose(q_all[...].astype(F32)).astype(BF16)
    do_t[...] = jnp.transpose(do_all[...].astype(F32)).astype(BF16)
    for block in range(total // BLOCK):
        cut = slice(block * BLOCK, (block + 1) * BLOCK)
        rest = slice(block * BLOCK, total)
        kv_block = kv_all[cut]
        scores = causal(dot_nt(q_all[rest], kv_block), 0, 0)
        probs = jnp.exp(scores - lse[rest])
        grad_probs = dot_nt(do_all[rest], kv_block)
        ds = (probs * (grad_probs - delta[rest])).astype(BF16)
        dq_sum[rest] += dot_nn(ds, kv_block)
        back = dot_nn(q_t[:, rest], ds) + dot_nn(do_t[:, rest], probs.astype(BF16))
        dkv_sum[cut] = jnp.transpose(back)
    dq_all[...] = rope_back(dq_sum[...] * HEAD**-0.5, table[...]).astype(BF16)
    low = lower_half(BLOCK)
    for block in range(q_all.shape[0] // BLOCK):
        cut = slice(block * BLOCK, (block + 1) * BLOCK)
        dkv = dkv_sum[cut]
        dkv_all[cut] = jnp.where(low, rope_back(dkv, table[cut, :]), dkv).astype(BF16)
    for step in range(HEADS):
        own = rows_at((me ^ step) * rows, rows, 16)
        at = (step % 2) * (rows + rows // 2)
        outs[step // 2][at : at + rows] = dkv_all[own, :]
        outs[step // 2][at + rows : at + rows + rows // 2] = fold_rows(
            dq_all[own, :].astype(F32)
        ).astype(BF16)


def attention_share_kernel(parts, place, gathered, dq_all, dkv_all, lse_o, more, *refs):
    pieces, keep, send, share = refs[:HEADS], refs[HEADS], refs[HEADS + 1], refs[-1]
    me, seat = place[0], place[1]
    _, rows, width = gathered.shape
    normed = gathered[...].reshape(-1, width)
    grad_q = dot_tn(normed, dq_all[...])
    grad_kv = dot_tn(normed, dkv_all[...])
    grad_o = jnp.zeros((LANES, width), F32)
    for step in range(HEADS):
        own = lse_o[rows_at((me ^ step) * rows, rows, 16), :].astype(BF16)
        grad_o += dot_tn(own, pieces[step][...])
    grad_o = grad_o[HEAD:]
    half = width // 2
    folded_v = jnp.where(lower_half(half), turn(grad_kv[:half]), grad_kv[half:])
    pack_attention(
        share, jnp.where(lower_half(width), grad_q, turn(grad_kv)), folded_v, grad_o
    )
    keep_and_send(share, keep, send, seat, parts)
    keep_and_send(more, keep, send, seat, parts, share.shape[0] // parts)


def start_back_kernel(place, x, grad_middle, gain, w_q, w_k, w_v, *refs):
    pieces = paired(refs[:HEADS])
    grad_in, heads, dq, dk, dv = refs[HEADS:]
    me = place[0]
    rows, width = x.shape
    half = rows // 2
    for step in range(HEADS):
        heads[me ^ step] = pieces[step][...]
    low, low_half = lower_half(rows), lower_half(half)
    for chunk in range(width // LANES):
        cut = slice(chunk * LANES, (chunk + 1) * LANES)
        even, odd = heads[2 * chunk].astype(F32), heads[2 * chunk + 1].astype(F32)
        dk[:, cut] = jnp.where(low, even[:rows], turn(odd[:rows])).astype(BF16)
        dv[:, cut] = jnp.where(low, turn(even[:rows]), odd[:rows]).astype(BF16)
        dq[:half, cut] = jnp.where(low_half, even[rows:], turn(odd[rows:])).astype(BF16)
        dq[half:, cut] = jnp.where(low_half, turn(even[rows:]), odd[rows:]).astype(BF16)
    grad_a = dot_nt(dq[...], w_q[...]) + dot_nt(dk[...], w_k[...]) + dot_nt(dv[...], w_v[...])
    unit, scale = norm_parts(x[...])
    grad_in[...] = grad_middle[...] + norm_back(grad_a, gain[...], unit, scale)


def column_to_row(column):
    return jnp.transpose(jnp.broadcast_to(column, (column.shape[0], LANES)))[:1]


def fold_lanes(values):
    return sum(
        values[:, at : at + LANES] for at in range(0, values.shape[1], LANES)
    )


def part_order(batch):
    order, bit = [0], batch // 2
    while bit >= 1:
        order = order + [step ^ bit for step in order]
        bit //= 2
    return order


def grads_kernel(parts, attention, feed_forward, source_count, place, *refs):
    refs = list(refs)
    sources = [refs.pop(0) for _ in range(source_count)]
    halves = source_count == 2 * HEADS
    weights = [refs.pop(0) for _ in range(4 * attention + 2 * feed_forward)]
    outs = [refs.pop(0) for _ in range(5 * attention + 3 * feed_forward)]
    me, seat = place[0], place[1]
    order = part_order(parts)
    copies = []

    def send(source, target, semaphore):
        copy = pltpu.make_async_copy(source, target, semaphore)
        copy.start()
        copies.append(copy)

    def rows_of(step):
        if source_count == 1:
            return sources[0].ready(step).at[step], step
        return sources[step], me ^ step

    def part_of(step, source, at, first, size):
        count = parts
        if halves:
            source, count, at = sources[step + (HEADS if 2 * at >= parts else 0)], parts // 2, at % (parts // 2)
        first += at * (source.shape[0] // count)
        return source[first : first + size]

    for layer in range(attention):
        w_q, w_k, w_v, gain_a = weights[4 * layer : 4 * layer + 4]
        grad_q, grad_k, grad_v, grad_o, grad_gain_a = outs[5 * layer : 5 * layer + 5]
        heads, square, over, sems_a = refs[4 * layer : 4 * layer + 4]
        width = grad_q.shape[0]
        half, at_rows = width // 2, width // 2 // parts
        for step in range(HEADS):
            source, owner = rows_of(step)
            for at, peer in enumerate(order):
                heads[owner, rows_at((seat ^ peer) * at_rows, at_rows, 16), :] = part_of(
                    step, source, at, layer * at_rows, at_rows
                )
        low = lower_half(half)
        total = None
        for chunk in range(HEADS // 2):
            cut = slice(chunk * LANES, (chunk + 1) * LANES)
            for part in range(2):
                rows = slice(part * half, (part + 1) * half)
                lanes = slice(part * LANES, (part + 1) * LANES)
                even = heads[2 * chunk, :, lanes].astype(F32)
                odd = heads[2 * chunk + 1, :, lanes].astype(F32)
                square[0, chunk, rows] = jnp.where(low, even, turn(odd))
                square[1, chunk, rows] = jnp.where(low, turn(even), odd)
            even = heads[2 * chunk, :, 2 * LANES : 3 * LANES].astype(F32)
            odd = heads[2 * chunk + 1, :, 2 * LANES : 3 * LANES].astype(F32)
            square[2, chunk, :half] = jnp.where(low, even, turn(odd))
            square[2, chunk, half:] = jnp.where(low, turn(even), odd)
            for head in (2 * chunk, 2 * chunk + 1):
                for lane in range(width // LANES):
                    over[head, :, lane * LANES : (lane + 1) * LANES] = heads[
                        head, lane * HEAD : (lane + 1) * HEAD, 3 * LANES :
                    ].astype(F32)
                send(
                    over.at[head],
                    grad_o.at[pl.ds(head * HEAD, HEAD), :],
                    sems_a.at[3 + head % 2, chunk],
                )
            for at, target in enumerate((grad_q, grad_k, grad_v)):
                send(
                    square.at[at, chunk],
                    target.at[:, pl.ds(chunk * LANES, LANES)],
                    sems_a.at[at, chunk],
                )
            term = (
                w_q[:, cut].astype(F32) * square[0, chunk]
                + w_k[:, cut].astype(F32) * square[1, chunk]
                + w_v[:, cut].astype(F32) * square[2, chunk]
            )
            total = term if total is None else total + term
        total = jnp.sum(total, axis=-1, keepdims=True)
        grad_gain_a[...] = column_to_row(total) / gain_a[...]

    if feed_forward:
        w_e, gain_f = weights[-2:]
        contract, expand, grad_gain_f = outs[-3:]
        share, acc, sems = refs[4 * attention : 4 * attention + 3]
        width = expand.shape[0]
        half = width // 2
        ff_own = contract.shape[0] // HEADS
        ff_rows = 2 * ff_own // parts
        acc[...] = jnp.zeros(acc.shape, F32)
        for step in range(HEADS):
            source, owner = rows_of(step)
            for at, peer in enumerate(order):
                share[step, rows_at((seat ^ peer) * ff_rows, ff_rows, 16), :] = part_of(
                    step, source, at, 0, ff_rows
                ).astype(F32)
            own = pl.ds(pl.multiple_of(owner * ff_own, ff_own), ff_own)
            send(share.at[step, pl.ds(0, ff_own), :], contract.at[own, :], sems.at[step, 0])
            for side in range(2):
                lanes = pl.ds(side * half, half)
                send(
                    share.at[step, pl.ds(ff_own, ff_own), lanes],
                    expand.at[pl.ds(side * half, half), own],
                    sems.at[step, 1 + side],
                )
                acc[side * half : (side + 1) * half] += fold_lanes(
                    w_e[side * half : (side + 1) * half, own].astype(F32)
                    * share[step, ff_own:, side * half : (side + 1) * half]
                )
        total = jnp.sum(acc[...], axis=-1, keepdims=True)
        grad_gain_f[...] = column_to_row(total) / gain_f[...]
    for copy in copies:
        copy.wait()


COST = 1.15e9


def call(kernel, out_shape, scratch, arguments, late=(), limit=16, in_hbm=(), kept=(), us=5):
    late = [entry if isinstance(entry, tuple) else (entry,) for entry in late]
    late = [entry + (None, None, 0, 1)[len(entry) - 1 :] for entry in late]
    specs = [pl.BlockSpec(memory_space=pltpu.SMEM)]
    specs += [pl.BlockSpec(memory_space=pltpu.VMEM)] * (len(arguments) - 1)
    buffers, arguments = [], list(arguments)
    for at, shape, *_ in late:
        specs[at] = pl.BlockSpec(memory_space=pltpu.HBM)
        buffers.append(pltpu.VMEM(shape or arguments[at].shape, arguments[at].dtype))
        arguments[at] = pltpu.with_memory_space_constraint(arguments[at], pltpu.HBM)
    body, semaphores = kernel, []
    if late:
        semaphores = [pltpu.SemaphoreType.DMA((sum(entry[4] for entry in late),))]
        body = partial(with_late, kernel, late, len(arguments), len(out_shape))
    return pl.pallas_call(
        body,
        out_shape=[
            (pltpu.HBM if at in in_hbm or at in kept else jax.ShapeDtypeStruct)(*entry)
            for at, entry in enumerate(out_shape)
        ],
        in_specs=specs,
        out_specs=[
            pl.BlockSpec(memory_space=pltpu.HBM if at in in_hbm else pltpu.VMEM)
            for at in range(len(out_shape))
        ],
        scratch_shapes=[
            pltpu.VMEM(*entry) if isinstance(entry, tuple) else entry for entry in scratch
        ]
        + buffers
        + semaphores,
        compiler_params=pltpu.CompilerParams(vmem_limit_bytes=limit * 2**20),
        cost_estimate=pl.CostEstimate(
            flops=int(us * COST), bytes_accessed=2**20, transcendentals=0
        ),
    )(*arguments)


def exchange(pieces, axis):
    devices = range(lax.axis_size(axis))
    moved = {
        step: lax.ppermute(pieces[step], axis, [(i, i ^ step) for i in devices])
        for step in reversed(range(1, len(pieces)))
    }
    return [pieces[0]] + [moved[step] for step in range(1, len(pieces))]


def after(values, *others):
    return lax.optimization_barrier((values, others))[0]


def phase(*values):
    return lax.optimization_barrier(values)


def swap(block, axis, step):
    return lax.ppermute(block, axis, [(i, i ^ step) for i in range(lax.axis_size(axis))])


def near_exchange(pairs):
    moved = {step: swap(pairs[step], "seq", 2 * step) for step in reversed(range(1, len(pairs)))}
    first = [pairs[0]] + [moved[step] for step in range(1, len(pairs))]
    return first + [swap(pair, "seq", 1) for pair in first]


def summed(pieces):
    return sum(piece.astype(F32) for piece in pieces).astype(BF16)


def sum_step(keep, arrived, bit):
    total = keep.astype(F32) + arrived.astype(F32)
    parts = lax.axis_size("batch") // (2 * bit)
    if parts <= 1:
        return total.astype(BF16), None
    total = total.reshape(parts // 2, 2, -1, total.shape[1])
    return (
        total[:, 0].reshape(-1, total.shape[-1]),
        total[:, 1].reshape(-1, total.shape[-1]).astype(BF16),
    )


def near_gather(block, *beside):
    found = {0: block}
    for step in (6, 4, 2):
        found[step] = swap(block, "seq", step)
    for step in (0, 2, 4, 6):
        found[step] = after(found[step], *beside) if beside else found[step]
        found[step + 1] = swap(found[step], "seq", 1)
    return [found[step] for step in range(HEADS)]


def gather(block):
    return lax.all_gather(block, "seq", axis=0, tiled=True)


def whole_grads(place, sources, batch, attention=(), feed_forward=None):
    width = sources[0].shape[-1]
    square, row = ((width, width), F32), ((1, width), F32)
    arguments, out_shape, scratch = [place, *sources], [], []
    late = [(1, None, None, 0, HEADS)] if len(sources) == 1 else []
    in_hbm = []
    for params in attention:
        first = len(arguments)
        arguments += [params[1], params[2], params[3], params[0]]
        late += [first, first + 1, first + 2]
        first = len(out_shape)
        in_hbm += [first, first + 1, first + 2, first + 3]
        out_shape += [square] * 4 + [row]
        scratch += [
            ((HEADS, width // 2, width), BF16),
            ((3, HEADS // 2, width, LANES), F32),
            ((HEADS, HEAD, width), F32),
            pltpu.SemaphoreType.DMA((5, HEADS // 2)),
        ]
    if feed_forward is not None:
        ff = feed_forward[6].shape[1]
        late += [len(arguments)]
        arguments += [feed_forward[6], feed_forward[5]]
        in_hbm += [len(out_shape), len(out_shape) + 1]
        out_shape += [((ff, width), F32), ((width, ff), F32), row]
        scratch += [
            ((HEADS, 2 * ff // HEADS, width), F32),
            ((width, LANES), F32),
            pltpu.SemaphoreType.DMA((HEADS, 3)),
        ]
    return call(
        partial(grads_kernel, batch, len(attention), feed_forward is not None, len(sources)),
        out_shape,
        scratch,
        tuple(arguments),
        late,
        32,
        in_hbm,
    )


def by_heads(inputs, cotangent, *weights):
    full = (weights[0][None],) + weights[1:5] + (weights[5][None],) + weights[6:8]
    brief = (weights[8][None],) + weights[9:13] + (weights[13][None],) + weights[14:16]
    x, cot = inputs[0], cotangent[0]
    rows, width = x.shape
    short, half, total = rows // 3, rows // 2, rows * HEADS
    batch = lax.axis_size("batch")
    ff = full[6].shape[1]
    ff_own = ff // HEADS
    count = short * HEADS
    chunks = width // LANES
    place = jnp.stack([lax.axis_index("seq"), lax.axis_index("batch")]).astype(jnp.int32)
    table = rope_constants(total)
    block = rows + half

    outs = call(
        project_kernel,
        [((2 * block, LANES), BF16)] * (HEADS // 2)
        + [((rows, width), BF16), ((rows + short, width), BF16)],
        [((HEADS, block, LANES), BF16), ((chunks, rows, LANES), F32)],
        (place, x, cot, full[0], full[1], full[2], full[3], table),
        (
            1,
            3,
            4,
            5,
            6,
            (7, (rows, 2 * LANES), lambda ref, me: ref.at[rows_at(me * rows, rows, 16), :]),
            2,
        ),
        kept=(HEADS // 2, HEADS // 2 + 1),
    )
    pieces, (normed_a, bundle) = near_exchange(outs[: HEADS // 2]), outs[HEADS // 2 :]
    bundles = gather(bundle).reshape(HEADS, rows + short, width)

    outs = call(
        attend_kernel,
        [((rows, LANES), BF16)] * (HEADS // 2)
        + [((total, LANES), BF16), ((total, LANES), BF16), ((total, LANES), F32)],
        [
            ((total, LANES), BF16),
            ((total, LANES), BF16),
            ((total, LANES), F32),
            pltpu.SemaphoreType.DMA((3,)),
        ],
        (place, *pieces),
        in_hbm=range(HEADS // 2, HEADS // 2 + 3),
    )
    pieces = near_exchange(outs[: HEADS // 2])
    q_all, kv_all, lse_o = outs[HEADS // 2 :]

    residual, middle, normed_f, pooled = call(
        finish_kernel,
        [
            ((rows, width), F32),
            ((rows, width), F32),
            ((2 * rows, width), BF16),
            ((short + 16, width), BF16),
        ],
        [
            ((rows, width), F32),
            ((rows, width), F32),
            ((2 * rows, width), BF16),
            ((rows, width), BF16),
            ((HEADS, half, LANES), F32),
            ((chunks, rows + 8, LANES), F32),
            pltpu.SemaphoreType.DMA((3,)),
        ],
        (place, x, normed_a, full[5], full[4], full[6], full[7], *pieces),
        (4, 1, (5, None, None, 1, FF_PARTS), (6, None, None, 0, FF_PARTS), 2),
        in_hbm=range(3),
    )
    pieces = near_gather(pooled)
    normed_all = gather(normed_f).reshape(HEADS, 2 * rows, width)

    outs = call(
        short_forward_kernel,
        [
            ((short, width), F32),
            ((short, ff), BF16),
            ((count, width), F32),
            ((count, width), BF16),
            ((HEADS, count, LANES), BF16),
            ((chunks, count, LANES), BF16),
            ((chunks, count, LANES), BF16),
            ((chunks, count, LANES), F32),
            ((chunks, count, LANES), F32),
            ((count, width), BF16),
            ((count, width), F32),
        ]
        + [((2 * ff_own // batch, width), BF16)] * batch,
        [
            ((HEADS, width), F32),
            ((count, width), F32),
            ((count, width), BF16),
            ((count, ff), BF16),
            ((count, ff), BF16),
            ((count, width), F32),
            ((count, width), BF16),
            ((2 * ff_own, width), BF16),
        ],
        (place, bundles, table[:count]) + brief + tuple(pieces),
        (
            4,
            2,
            5,
            6,
            7,
            9,
            10,
            (1, (HEADS, short, width), lambda ref, me: ref.at[:, pl.ds(rows, short), :]),
        ),
        22,
        kept=(0, 1),
        us=16,
    )
    own_short, saved = outs[:2], outs[2:11]
    a_at, saved = phase(outs[11:], saved)
    a_at = exchange(a_at, "batch")
    outs = call(
        short_back_kernel,
        [
            ((total, width), BF16),
            ((width // 2, width), BF16),
            ((rows, width), F32),
            ((rows, width), BF16),
        ],
        [
            ((total, width), BF16),
            ((width // 2, width), BF16),
            ((rows, width), F32),
            pltpu.SemaphoreType.DMA((3,)),
            ((HEADS, count, LANES), BF16),
            ((count, width), BF16),
            ((count, width), BF16),
            ((count, width), BF16),
            ((chunks, total + 16, LANES), F32),
            ((LANES, width), F32),
            ((rows, width), F32),
        ],
        (place, cot, bundles, table[:count])
        + brief[:5]
        + tuple(saved)
        + (middle, normed_f, full[5], full[6], full[7]),
        (
            8,
            3,
            5,
            6,
            7,
            (2, (HEADS, rows, width), lambda ref, me: ref.at[:, pl.ds(0, rows), :]),
            1,
            21,
            22,
            (19, (rows, width), lambda ref, me: ref.at[pl.ds(0, rows), :]),
            18,
        ),
        25,
        in_hbm=range(3),
        us=18,
    )
    a_at, (grad_all, short_share, grad_middle, g1) = phase(a_at, outs)

    a_all, g1, grad_all = phase(summed(a_at), g1, grad_all)
    a_at = swap(a_all, "batch", 2)
    outs = call(
        feed_forward_share_kernel,
        [((2 * ff_own // batch, width), BF16)] * batch,
        [((2 * ff_own, width), BF16)],
        (place, normed_all, grad_all, full[6], full[7]),
        (
            (1, (HEADS, rows, width), lambda ref, me: ref.at[:, pl.ds(0, rows), :]),
            (3, (width, ff_own), lambda ref, me: ref.at[:, rows_at(me * ff_own, ff_own, ff_own)]),
            2,
            (4, (ff_own, width), lambda ref, me: ref.at[rows_at(me * ff_own, ff_own, ff_own), :]),
        ),
        22,
    )
    g1_all = near_gather(g1, outs[1], a_at)
    a_all = jnp.concatenate([a_all, a_at])
    a_at = swap(a_all, "batch", 1)
    a_all, a_at, g1_all, b_at = phase(a_all, a_at, g1_all, outs)

    a_shares = gather(jnp.concatenate([a_all, a_at])[None])
    b_at = exchange(b_at, "batch")
    outs = call(
        attend_back_kernel,
        [((2 * block, LANES), BF16)] * (HEADS // 2)
        + [((total, LANES), BF16), ((total, LANES), BF16)],
        [
            ((total, LANES), BF16),
            ((total, LANES), F32),
            ((total, LANES), F32),
            ((LANES, total), BF16),
            ((LANES, total), BF16),
        ],
        (place, q_all, kv_all, lse_o, table, full[4], *g1_all),
        (
            (5, (HEAD, width), lambda ref, me: ref.at[rows_at(me * HEAD, HEAD, HEAD), :]),
            1,
            2,
            3,
            4,
        ),
        us=7,
    )
    pieces, (dq_all, dkv_all) = outs[: HEADS // 2], outs[HEADS // 2 :]
    outs = call(
        partial(attention_share_kernel, batch),
        [((width // 2, width), BF16)] * 2,
        [((width // 2, width), BF16)],
        (place, normed_all, dq_all, dkv_all, lse_o, short_share, *g1_all),
        ((1, (HEADS, rows, width), lambda ref, me: ref.at[:, pl.ds(rows, rows), :]), 4, 5),
        us=3,
    )
    b_at, pieces, (c_keep, c_send) = phase(b_at, pieces, outs)

    b_all, pieces, c_send = phase(summed(b_at), pieces, c_send)
    b_at = swap(b_all, "batch", 2)
    c_at = swap(c_send, "batch", 1)
    pieces = {step: pieces[step] for step in range(HEADS // 2)}
    moved = {step: swap(pieces[step], "seq", 2 * step) for step in (3, 2)}
    b_at, c_at, moved, pieces = phase(b_at, c_at, moved, pieces)

    b_all = jnp.concatenate([b_all, b_at])
    c_keep, c_send = sum_step(c_keep, c_at, 1)
    b_all, c_send, pieces = phase(b_all, c_send, pieces)
    b_at = swap(b_all, "batch", 1)
    c_at = swap(c_send, "batch", 2)
    moved |= {0: pieces[0], 1: swap(pieces[1], "seq", 2)}
    b_at, c_at, moved, pieces = phase(b_at, c_at, moved, pieces)

    b_all = jnp.concatenate([b_all, b_at])
    c_all, _ = sum_step(c_keep, c_at, 2)
    b_all, c_all, moved = phase(b_all, c_all, moved)
    b_shares = gather(b_all[None])
    c_at = swap(c_all, "batch", 2)
    across = {step: swap(moved[step], "seq", 1) for step in range(HEADS // 2)}
    (output,) = call(
        output_kernel,
        [((rows, width), F32)],
        [((chunks, rows, LANES), F32)],
        (place, residual, *own_short, brief[7]),
        (4, 3, 2, 1),
        us=3,
    )
    c_at, moved, across, output = phase(c_at, moved, across, output)

    c_all, moved, across, a_shares = phase(
        jnp.concatenate([c_all, c_at]), moved, across, a_shares
    )
    first = {0: c_all, 2: swap(c_all, "seq", 2), 4: swap(c_all, "seq", 4)}
    c_at = swap(c_all, "batch", 1)
    pieces = [side[step] for side in (moved, across) for step in range(HEADS // 2)]
    short_ff_grads = whole_grads(place, [a_shares], batch, (), brief)
    (grad_in,) = call(
        start_back_kernel,
        [((rows, width), F32)],
        [((HEADS, block, LANES), BF16)] + [((rows, width), BF16)] * 3,
        (place, x, grad_middle, full[0], full[1], full[2], full[3], *pieces),
        (4, 5, 6, 1, 2),
        us=4,
    )
    c_at, first, short_ff_grads, grad_in = phase(c_at, first, short_ff_grads, grad_in)
    other = {0: c_at, 2: swap(c_at, "seq", 2), 4: swap(c_at, "seq", 4)}
    first |= {6: swap(first[2], "seq", 4)}
    other |= {6: swap(other[4], "seq", 2)}
    found = [
        half | {step + 1: swap(half[step], "seq", 1) for step in (0, 2, 4, 6)}
        for half in (first, other)
    ]
    c_shares = [half[step] for half in found for step in range(HEADS)]
    at_grads = whole_grads(place, c_shares, batch, (full, brief))
    full_ff_grads = whole_grads(place, [after(b_shares, at_grads[0])], batch, (), full)

    def arranged(attention, feed_forward):
        grad_q, grad_k, grad_v, grad_o, grad_gain_a = attention
        contract, expand, grad_gain_f = feed_forward
        return (grad_gain_a[0], grad_q, grad_k, grad_v, grad_o, grad_gain_f[0], expand, contract)

    return (
        (output[None], grad_in[None])
        + arranged(at_grads[:5], full_ff_grads)
        + arranged(at_grads[5:], short_ff_grads)
    )


def from_behind(block, axis, distance):
    devices = range(lax.axis_size(axis))
    route = [(i - distance, i) for i in devices if i - distance in devices]
    return lax.ppermute(block, axis, route)


def normalize(stream, gain):
    row_mean = jnp.mean(stream, axis=-1, keepdims=True)
    centered = stream - row_mean
    spread = jnp.mean(centered * centered, axis=-1, keepdims=True)
    return centered * lax.rsqrt(spread + norm_eps) * gain


def rope_table(positions):
    half_size = HEAD // 2
    frequency = jnp.power(10000.0, -jnp.arange(half_size, dtype=jnp.float32) * 2.0 / HEAD)
    angles = positions.astype(jnp.float32)[:, None] * frequency[None, :]
    return (jnp.cos(angles)[:, None, :], jnp.sin(angles)[:, None, :])


def rotate(values, angle_cos, angle_sin):
    first_half, second_half = jnp.split(values, 2, axis=-1)
    return jnp.concatenate(
        [
            first_half * angle_cos - second_half * angle_sin,
            first_half * angle_sin + second_half * angle_cos,
        ],
        axis=-1,
    )


def rotate_back(grads, angle_cos, angle_sin):
    first_half, second_half = jnp.split(grads, 2, axis=-1)
    return jnp.concatenate(
        [
            first_half * angle_cos + second_half * angle_sin,
            second_half * angle_cos - first_half * angle_sin,
        ],
        axis=-1,
    )


def split_heads(matrix):
    return matrix.reshape(matrix.shape[0], HEADS, HEAD)


def project(stream, params, angle_cos, angle_sin):
    normed_in = normalize(stream, params[0]).astype(jnp.bfloat16)

    def heads_of(matrix):
        return split_heads(jnp.dot(normed_in, matrix, preferred_element_type=jnp.float32))

    queries = rotate(heads_of(params[1]), angle_cos, angle_sin).astype(jnp.bfloat16)
    keys_here = rotate(heads_of(params[2]), angle_cos, angle_sin).astype(jnp.bfloat16)
    values_here = heads_of(params[3]).astype(jnp.bfloat16)
    return (normed_in, queries, keys_here, values_here)


def masked_scores(queries, keys_all, query_places, key_places):
    scores = jnp.einsum(
        "nhe,mhe->hnm", queries, keys_all, preferred_element_type=jnp.float32
    ) * HEAD ** (-0.5)
    allowed = key_places[None, None, :] <= query_places[None, :, None]
    return jnp.where(allowed, scores, -1e30)


def attend(queries, keys_all, values_all, query_places, key_places):
    scores = masked_scores(queries, keys_all, query_places, key_places)
    highest_score = jnp.max(scores, axis=-1, keepdims=True)
    log_total = highest_score + jnp.log(
        jnp.sum(jnp.exp(scores - highest_score), axis=-1, keepdims=True)
    )
    prob_low = jnp.exp(scores - log_total).astype(jnp.bfloat16)
    attended = jnp.einsum("hnm,mhe->nhe", prob_low, values_all, preferred_element_type=jnp.float32)
    return (attended, log_total)


def attend_back(queries, keys_all, values_all, query_places, key_places, log_total, grad_attended):
    scores = masked_scores(queries, keys_all, query_places, key_places)
    probs_full = jnp.exp(scores - log_total)
    grad_probs = jnp.einsum(
        "nhe,mhe->hnm", grad_attended, values_all, preferred_element_type=jnp.float32
    )
    row_inner = jnp.sum(probs_full * grad_probs, axis=-1, keepdims=True)
    grad_scores = (probs_full * (grad_probs - row_inner)).astype(jnp.bfloat16)
    grad_queries = jnp.einsum(
        "hnm,mhe->nhe", grad_scores, keys_all, preferred_element_type=jnp.float32
    ) * HEAD ** (-0.5)
    return (grad_queries, grad_scores, probs_full.astype(jnp.bfloat16), row_inner)


def finish(stream, attended, params):
    row_count, width = stream.shape
    attended_low = attended.reshape(row_count, width).astype(jnp.bfloat16)
    middle = stream + jnp.dot(attended_low, params[4], preferred_element_type=jnp.float32)
    normed_mid = normalize(middle, params[5]).astype(jnp.bfloat16)
    hidden_pre = jnp.dot(normed_mid, params[6], preferred_element_type=jnp.float32)
    hidden_low = jax.nn.gelu(hidden_pre, approximate=True).astype(jnp.bfloat16)
    result = middle + jnp.dot(hidden_low, params[7], preferred_element_type=jnp.float32)
    return (result, (attended_low, middle, normed_mid, hidden_pre, hidden_low))


def finish_back(grad_result, finish_saved, params):
    attended_low, middle, normed_mid, hidden_pre, hidden_low = finish_saved
    grad_low = grad_result.astype(jnp.bfloat16)
    grad_contract = jnp.einsum(
        "nf,nd->fd", hidden_low, grad_low, preferred_element_type=jnp.float32
    )
    grad_hidden = jnp.einsum("nd,fd->nf", grad_low, params[7], preferred_element_type=jnp.float32)
    gelu_value, gelu_pull = jax.vjp(partial(jax.nn.gelu, approximate=True), hidden_pre)
    grad_pre = gelu_pull(grad_hidden)[0].astype(jnp.bfloat16)
    grad_expand = jnp.einsum("nd,nf->df", normed_mid, grad_pre, preferred_element_type=jnp.float32)
    grad_normed = jnp.einsum("nf,df->nd", grad_pre, params[6], preferred_element_type=jnp.float32)
    norm_value, norm_pull = jax.vjp(normalize, middle, params[5])
    grad_norm_in, grad_gain_ffn = norm_pull(grad_normed)
    grad_middle = grad_result + grad_norm_in
    middle_low = grad_middle.astype(jnp.bfloat16)
    grad_output_w = jnp.einsum(
        "nc,nd->cd", attended_low, middle_low, preferred_element_type=jnp.float32
    )
    grad_attended = split_heads(
        jnp.einsum("nd,cd->nc", middle_low, params[4], preferred_element_type=jnp.float32).astype(
            jnp.bfloat16
        )
    )
    return (grad_middle, grad_attended, grad_output_w, grad_expand, grad_contract, grad_gain_ffn)


def start_back(
    grad_queries, grad_keys, grad_values, stream, params, normed_in, angle_cos, angle_sin
):
    row_count, width = stream.shape
    query_low = (
        rotate_back(grad_queries, angle_cos, angle_sin)
        .reshape(row_count, width)
        .astype(jnp.bfloat16)
    )
    key_low = (
        rotate_back(grad_keys, angle_cos, angle_sin).reshape(row_count, width).astype(jnp.bfloat16)
    )
    value_low = grad_values.reshape(row_count, width).astype(jnp.bfloat16)
    grad_query = jnp.einsum("nd,nc->dc", normed_in, query_low, preferred_element_type=jnp.float32)
    grad_key = jnp.einsum("nd,nc->dc", normed_in, key_low, preferred_element_type=jnp.float32)
    grad_value = jnp.einsum("nd,nc->dc", normed_in, value_low, preferred_element_type=jnp.float32)
    grad_normed = (
        jnp.einsum("nc,dc->nd", query_low, params[1], preferred_element_type=jnp.float32)
        + jnp.einsum("nc,dc->nd", key_low, params[2], preferred_element_type=jnp.float32)
        + jnp.einsum("nc,dc->nd", value_low, params[3], preferred_element_type=jnp.float32)
    )
    norm_value, norm_pull = jax.vjp(normalize, stream, params[0])
    grad_stream, grad_gain_attn = norm_pull(grad_normed)
    return (grad_stream, grad_gain_attn, grad_query, grad_key, grad_value)


def local_forward(stream, places, params, fetch):
    angle_cos, angle_sin = rope_table(places)
    normed_in, queries, keys_here, values_here = project(stream, params, angle_cos, angle_sin)
    row_count, width = stream.shape
    keys_local = keys_here.reshape(row_count, width)
    values_local = values_here.reshape(row_count, width)
    keys_flat, values_flat = fetch(keys_local, values_local)
    key_places = jnp.arange(keys_flat.shape[0], dtype=jnp.int32)
    attended, log_total = attend(
        queries, split_heads(keys_flat), split_heads(values_flat), places, key_places
    )
    result, finish_saved = finish(stream, attended, params)
    return (
        result,
        (
            normed_in,
            queries,
            keys_local,
            values_local,
            keys_flat,
            values_flat,
            log_total,
            angle_cos,
            angle_sin,
            finish_saved,
        ),
    )


def local_backward(grad_result, stream, places, params, saved, keys_flat, values_flat, key_sum):
    normed_in, queries = (saved[0], saved[1])
    log_total, angle_cos, angle_sin, finish_saved = (saved[6], saved[7], saved[8], saved[9])
    grad_middle, grad_attended, grad_output_w, grad_expand, grad_contract, grad_gain_ffn = (
        finish_back(grad_result, finish_saved, params)
    )
    row_count, width = stream.shape
    key_places = jnp.arange(keys_flat.shape[0], dtype=jnp.int32)
    grad_queries, grad_scores, prob_low, row_inner = attend_back(
        queries,
        split_heads(keys_flat),
        split_heads(values_flat),
        places,
        key_places,
        log_total,
        grad_attended,
    )

    def contribution(first_row, term_rows):
        grad_keys = jnp.einsum(
            "hnm,nhe->mhe", grad_scores, queries, preferred_element_type=jnp.float32
        ) * HEAD ** (-0.5)
        grad_values = jnp.einsum(
            "hnm,nhe->mhe", prob_low, grad_attended, preferred_element_type=jnp.float32
        )
        return jnp.concatenate(
            [grad_keys.reshape(term_rows, width), grad_values.reshape(term_rows, width)], axis=1
        )

    both_grads = key_sum(contribution, row_count, (queries, grad_attended, log_total, row_inner))
    grad_stream, grad_gain_attn, grad_query, grad_key, grad_value = start_back(
        grad_queries,
        split_heads(both_grads[:, :width]),
        split_heads(both_grads[:, width:]),
        stream,
        params,
        normed_in,
        angle_cos,
        angle_sin,
    )
    return (
        grad_middle + grad_stream,
        (
            grad_gain_attn,
            grad_query,
            grad_key,
            grad_value,
            grad_output_w,
            grad_gain_ffn,
            grad_expand,
            grad_contract,
        ),
    )


def whole_forward(stream, params):
    row_count, width = stream.shape
    places = jnp.arange(row_count, dtype=jnp.int32)
    angle_cos, angle_sin = rope_table(places)
    normed_in, queries, keys_here, values_here = project(stream, params, angle_cos, angle_sin)
    block_rows = 512
    block_count = row_count // block_rows

    def one_block(pieces):
        return attend(pieces[0], keys_here, values_here, pieces[1], places)

    attended, log_total = lax.map(
        one_block,
        (
            queries.reshape(block_count, block_rows, HEADS, HEAD),
            places.reshape(block_count, block_rows),
        ),
    )
    result, finish_saved = finish(stream, attended.reshape(row_count, HEADS, HEAD), params)
    return (
        result,
        (normed_in, queries, keys_here, values_here, log_total, angle_cos, angle_sin, finish_saved),
    )


def whole_backward(grad_result, stream, params, saved):
    normed_in, queries, keys_here, values_here, log_total, angle_cos, angle_sin, finish_saved = (
        saved
    )
    grad_middle, grad_attended, grad_output_w, grad_expand, grad_contract, grad_gain_ffn = (
        finish_back(grad_result, finish_saved, params)
    )
    row_count, width = stream.shape
    places = jnp.arange(row_count, dtype=jnp.int32)
    block_rows = 512
    block_count = row_count // block_rows

    def one_block(running, pieces):
        query_block, place_block, total_block, grad_block = pieces
        grad_queries, grad_scores, prob_low, row_inner = attend_back(
            query_block, keys_here, values_here, place_block, places, total_block, grad_block
        )
        grad_keys = running[0] + jnp.einsum(
            "hnm,nhe->mhe", grad_scores, query_block, preferred_element_type=jnp.float32
        ) * HEAD ** (-0.5)
        grad_values = running[1] + jnp.einsum(
            "hnm,nhe->mhe", prob_low, grad_block, preferred_element_type=jnp.float32
        )
        return ((grad_keys, grad_values), grad_queries)

    zero_grads = jnp.zeros((row_count, HEADS, HEAD), jnp.float32)
    (grad_keys, grad_values), grad_queries = lax.scan(
        one_block,
        (zero_grads, zero_grads),
        (
            queries.reshape(block_count, block_rows, HEADS, HEAD),
            places.reshape(block_count, block_rows),
            log_total,
            grad_attended.reshape(block_count, block_rows, HEADS, HEAD),
        ),
    )
    grad_stream, grad_gain_attn, grad_query, grad_key, grad_value = start_back(
        grad_queries.reshape(row_count, HEADS, HEAD),
        grad_keys,
        grad_values,
        stream,
        params,
        normed_in,
        angle_cos,
        angle_sin,
    )
    return (
        grad_middle + grad_stream,
        (
            grad_gain_attn,
            grad_query,
            grad_key,
            grad_value,
            grad_output_w,
            grad_gain_ffn,
            grad_expand,
            grad_contract,
        ),
    )


def by_rows(
    inputs,
    cotangent,
    full_gain_attn,
    full_query,
    full_key,
    full_value,
    full_output,
    full_gain_ffn,
    full_expand,
    full_contract,
    short_gain_attn,
    short_query,
    short_key,
    short_value,
    short_output,
    short_gain_ffn,
    short_expand,
    short_contract,
):
    full_params = (
        full_gain_attn,
        full_query,
        full_key,
        full_value,
        full_output,
        full_gain_ffn,
        full_expand,
        full_contract,
    )
    short_params = (
        short_gain_attn,
        short_query,
        short_key,
        short_value,
        short_output,
        short_gain_ffn,
        short_expand,
        short_contract,
    )
    stream_in = inputs[0]
    row_count, width = stream_in.shape
    own_short = row_count // 3
    position = lax.axis_index("seq")
    seq_parts = lax.axis_size("seq")
    places = position * row_count + jnp.arange(row_count, dtype=jnp.int32)

    def fetch_full(keys_local, values_local):
        return (
            lax.all_gather(keys_local, "seq", axis=0, tiled=True),
            lax.all_gather(values_local, "seq", axis=0, tiled=True),
        )

    residual, full_saved = local_forward(stream_in, places, full_params, fetch_full)
    tail_rows = from_behind(residual[row_count - 2 :], "seq", 1)
    shifted = jnp.concatenate([tail_rows, residual[: row_count - 2]], axis=0)
    pooled = jnp.mean(shifted.reshape(own_short, 3, width), axis=1)
    pooled_all = lax.all_gather(pooled, "seq", axis=0, tiled=True)
    short_all, short_saved = whole_forward(pooled_all, short_params)
    short_result = lax.dynamic_slice_in_dim(short_all, position * own_short, own_short, 0)
    output = residual + jnp.repeat(short_result, 3, axis=0)
    grad_output = cotangent[0]
    grad_short = jnp.sum(grad_output.reshape(own_short, 3, width), axis=1)
    grad_short_all = lax.all_gather(grad_short, "seq", axis=0, tiled=True)
    grad_pooled_all, short_grads = whole_backward(
        grad_short_all, pooled_all, short_params, short_saved
    )
    grad_pooled = lax.dynamic_slice_in_dim(grad_pooled_all, position * own_short, own_short, 0)
    short_grads = tuple(
        (
            lax.dynamic_slice_in_dim(
                gradient,
                position * (gradient.shape[0] // seq_parts),
                gradient.shape[0] // seq_parts,
                0,
            )
            for gradient in short_grads
        )
    )
    grad_shifted = jnp.repeat(grad_pooled / 3.0, 3, axis=0)
    carried = from_behind(grad_shifted[:2], "seq", -1)
    grad_residual = grad_output + jnp.concatenate([grad_shifted[2:], carried], axis=0)
    keys_flat, values_flat = (
        lax.all_gather(full_saved[2], "seq", axis=0, tiled=True),
        lax.all_gather(full_saved[3], "seq", axis=0, tiled=True),
    )

    def full_sum(contribution, term_rows, query_side):
        return lax.psum_scatter(
            contribution(jnp.int32(0), term_rows * lax.axis_size("seq")).astype(jnp.bfloat16),
            "seq",
            scatter_dimension=0,
            tiled=True,
        ).astype(jnp.float32)

    grad_input, full_grads = local_backward(
        grad_residual, stream_in, places, full_params, full_saved, keys_flat, values_flat, full_sum
    )
    full_shares = (
        lax.psum_scatter(
            full_grads[0].astype(jnp.bfloat16), "seq", scatter_dimension=0, tiled=True
        ).astype(jnp.float32),
        lax.psum_scatter(
            full_grads[1].astype(jnp.bfloat16), "seq", scatter_dimension=0, tiled=True
        ).astype(jnp.float32),
        lax.psum_scatter(
            full_grads[2].astype(jnp.bfloat16), "seq", scatter_dimension=0, tiled=True
        ).astype(jnp.float32),
        lax.psum_scatter(
            full_grads[3].astype(jnp.bfloat16), "seq", scatter_dimension=0, tiled=True
        ).astype(jnp.float32),
        lax.psum_scatter(
            full_grads[4].astype(jnp.bfloat16), "seq", scatter_dimension=0, tiled=True
        ).astype(jnp.float32),
        lax.psum_scatter(
            full_grads[5].astype(jnp.bfloat16), "seq", scatter_dimension=0, tiled=True
        ).astype(jnp.float32),
        lax.psum_scatter(
            full_grads[6].astype(jnp.bfloat16), "seq", scatter_dimension=0, tiled=True
        ).astype(jnp.float32),
        lax.psum_scatter(
            full_grads[7].astype(jnp.bfloat16), "seq", scatter_dimension=0, tiled=True
        ).astype(jnp.float32),
    )
    shares = tuple(full_shares) + tuple(short_grads)
    totals = (
        lax.psum(shares[0].astype(jnp.bfloat16), "batch").astype(jnp.float32),
        lax.psum(shares[1].astype(jnp.bfloat16), "batch").astype(jnp.float32),
        lax.psum(shares[2].astype(jnp.bfloat16), "batch").astype(jnp.float32),
        lax.psum(shares[3].astype(jnp.bfloat16), "batch").astype(jnp.float32),
        lax.psum(shares[4].astype(jnp.bfloat16), "batch").astype(jnp.float32),
        lax.psum(shares[5].astype(jnp.bfloat16), "batch").astype(jnp.float32),
        lax.psum(shares[6].astype(jnp.bfloat16), "batch").astype(jnp.float32),
        lax.psum(shares[7].astype(jnp.bfloat16), "batch").astype(jnp.float32),
        lax.psum(shares[8].astype(jnp.bfloat16), "batch").astype(jnp.float32),
        lax.psum(shares[9].astype(jnp.bfloat16), "batch").astype(jnp.float32),
        lax.psum(shares[10].astype(jnp.bfloat16), "batch").astype(jnp.float32),
        lax.psum(shares[11].astype(jnp.bfloat16), "batch").astype(jnp.float32),
        lax.psum(shares[12].astype(jnp.bfloat16), "batch").astype(jnp.float32),
        lax.psum(shares[13].astype(jnp.bfloat16), "batch").astype(jnp.float32),
        lax.psum(shares[14].astype(jnp.bfloat16), "batch").astype(jnp.float32),
        lax.psum(shares[15].astype(jnp.bfloat16), "batch").astype(jnp.float32),
    )
    whole = (
        lax.all_gather(totals[0].astype(jnp.bfloat16), "seq", axis=0, tiled=True).astype(
            jnp.float32
        ),
        lax.all_gather(totals[1].astype(jnp.bfloat16), "seq", axis=0, tiled=True).astype(
            jnp.float32
        ),
        lax.all_gather(totals[2].astype(jnp.bfloat16), "seq", axis=0, tiled=True).astype(
            jnp.float32
        ),
        lax.all_gather(totals[3].astype(jnp.bfloat16), "seq", axis=0, tiled=True).astype(
            jnp.float32
        ),
        lax.all_gather(totals[4].astype(jnp.bfloat16), "seq", axis=0, tiled=True).astype(
            jnp.float32
        ),
        lax.all_gather(totals[5].astype(jnp.bfloat16), "seq", axis=0, tiled=True).astype(
            jnp.float32
        ),
        lax.all_gather(totals[6].astype(jnp.bfloat16), "seq", axis=0, tiled=True).astype(
            jnp.float32
        ),
        lax.all_gather(totals[7].astype(jnp.bfloat16), "seq", axis=0, tiled=True).astype(
            jnp.float32
        ),
        lax.all_gather(totals[8].astype(jnp.bfloat16), "seq", axis=0, tiled=True).astype(
            jnp.float32
        ),
        lax.all_gather(totals[9].astype(jnp.bfloat16), "seq", axis=0, tiled=True).astype(
            jnp.float32
        ),
        lax.all_gather(totals[10].astype(jnp.bfloat16), "seq", axis=0, tiled=True).astype(
            jnp.float32
        ),
        lax.all_gather(totals[11].astype(jnp.bfloat16), "seq", axis=0, tiled=True).astype(
            jnp.float32
        ),
        lax.all_gather(totals[12].astype(jnp.bfloat16), "seq", axis=0, tiled=True).astype(
            jnp.float32
        ),
        lax.all_gather(totals[13].astype(jnp.bfloat16), "seq", axis=0, tiled=True).astype(
            jnp.float32
        ),
        lax.all_gather(totals[14].astype(jnp.bfloat16), "seq", axis=0, tiled=True).astype(
            jnp.float32
        ),
        lax.all_gather(totals[15].astype(jnp.bfloat16), "seq", axis=0, tiled=True).astype(
            jnp.float32
        ),
    )
    return (output[None], grad_input[None]) + tuple(whole)


def solution(mesh):
    sequence = P("batch", "seq", None)
    seq, batch = mesh.shape["seq"], mesh.shape["batch"]
    fits = seq == HEADS and batch == 4
    return jax.shard_map(
        by_heads if fits else by_rows,
        mesh=mesh,
        in_specs=(sequence, sequence) + (P(),) * 16,
        out_specs=(sequence, sequence) + (P(),) * 16,
        check_vma=False,
    )
```

```python
from functools import partial

import jax
import jax.numpy as jnp
import numpy as np
from jax import lax
from jax.experimental import pallas as pl
from jax.experimental.pallas import tpu as pltpu
from jax.sharding import PartitionSpec as P

HEADS = 8
HEAD = 64
LANES = 128
BLOCK = 256
F32 = jnp.float32
BF16 = jnp.bfloat16


norm_eps = 1e-05


def dot_nn(left, right):
    return jnp.dot(left, right, preferred_element_type=F32)


def dot_nt(left, right):
    return lax.dot_general(left, right, (((1,), (1,)), ((), ())), preferred_element_type=F32)


def dot_tn(left, right):
    return lax.dot_general(left, right, (((0,), (0,)), ((), ())), preferred_element_type=F32)


def lower_half(rows):
    return lax.broadcasted_iota(jnp.int32, (rows, LANES), 1) < HEAD


def turn(values):
    return pltpu.roll(values, HEAD, 1)


def swap_pairs(values):
    lane = lax.broadcasted_iota(jnp.int32, values.shape, 1)
    return jnp.where(
        lane % HEAD < HEAD // 2,
        pltpu.roll(values, LANES - HEAD // 2, 1),
        pltpu.roll(values, HEAD // 2, 1),
    )


def rope(values, table):
    return values * table[:, :LANES] + swap_pairs(values) * table[:, LANES:]


def rope_back(grads, table):
    return grads * table[:, :LANES] - swap_pairs(grads) * table[:, LANES:]


def rope_constants(rows):
    frequency = np.power(
        np.float32(10000.0), -np.arange(HEAD // 2, dtype=np.float32) * np.float32(2.0 / HEAD)
    ).astype(np.float32)
    angles = np.arange(rows, dtype=np.float32)[:, None] * frequency[None, :]
    cosine, sine = np.cos(angles), np.sin(angles)
    table = np.concatenate([cosine] * 4 + [-sine, sine] * 2, axis=1)
    return jnp.asarray(table, F32)


def norm_parts(stream):
    centered = stream - jnp.mean(stream, axis=-1, keepdims=True)
    spread = jnp.mean(centered * centered, axis=-1, keepdims=True)
    scale = lax.rsqrt(spread + norm_eps)
    return centered * scale, scale


def norm_back(grad, gain, unit, scale):
    grad_unit = grad * gain
    inner = jnp.mean(grad_unit * unit, axis=-1, keepdims=True)
    return scale * (grad_unit - jnp.mean(grad_unit, axis=-1, keepdims=True) - unit * inner)


GELU_SCALE = 0.7978845608028654
GELU_CUBE = 0.044715


def gelu_both(pre):
    square = pre * pre
    half = 0.5 + 0.5 * jnp.tanh(pre * (GELU_SCALE + GELU_SCALE * GELU_CUBE * square))
    bend = pre * (2.0 * GELU_SCALE + 6.0 * GELU_SCALE * GELU_CUBE * square)
    return pre * half, half * (1.0 + (1.0 - half) * bend)


def gelu_value(pre):
    tanh = jnp.tanh(GELU_SCALE * pre * (1.0 + GELU_CUBE * pre * pre))
    return 0.5 * pre * (1.0 + tanh)


def causal(scores, first_row, first_key):
    row = lax.broadcasted_iota(jnp.int32, scores.shape, 0) + first_row
    key = lax.broadcasted_iota(jnp.int32, scores.shape, 1) + first_key
    return jnp.where(key <= row, scores, -1e30)


def fold_rows(values):
    half = values.shape[0] // 2
    return jnp.where(lower_half(half), values[:half], turn(values[half:]))


def unfold_rows(folded):
    low = lower_half(folded.shape[0])
    return jnp.where(low, folded, 0.0), jnp.where(low, turn(folded), 0.0)


def rows_at(start, size, multiple):
    return pl.ds(pl.multiple_of(start, multiple), size)


class Late:
    def __init__(self, source, target, semaphores, axis=0, parts=1):
        self.target, self.shape = target, target.shape
        size = target.shape[axis] // parts
        cuts = [(slice(None),) * axis + (pl.ds(part * size, size),) for part in range(parts)]
        self.copies = [
            pltpu.make_async_copy(source.at[cut], target.at[cut], semaphore)
            for cut, semaphore in zip(cuts, semaphores)
        ]
        self.waiting = set(range(parts))

    def ready(self, part=None):
        for at in sorted(self.waiting if part is None else self.waiting & {part}):
            self.copies[at].wait()
            self.waiting.remove(at)
        return self.target

    def __getitem__(self, index):
        return self.ready()[index]


def with_late(kernel, late, argument_count, out_count, *refs):
    arguments, outs = list(refs[:argument_count]), refs[argument_count : argument_count + out_count]
    rest = refs[argument_count + out_count :]
    first, taken, begun = len(rest) - len(late) - 1, 0, []
    for at, (place, _, part, axis, parts) in enumerate(late):
        source = arguments[place]
        source = source if part is None else part(source, refs[0][0])
        semaphores = [rest[-1].at[taken + step] for step in range(parts)]
        arguments[place] = Late(source, rest[first + at], semaphores, axis, parts)
        begun += [(part, at, copy) for part, copy in enumerate(arguments[place].copies)]
        taken += parts
    for _, _, copy in sorted(begun, key=lambda entry: entry[:2]):
        copy.start()
    kernel(*arguments, *outs, *rest[:first])


class Departures:
    def __init__(self, semaphores):
        self.semaphores, self.copies = semaphores, []

    def send(self, source, target):
        copy = pltpu.make_async_copy(source, target, self.semaphores.at[len(self.copies)])
        copy.start()
        self.copies.append(copy)

    def wait(self):
        for copy in self.copies:
            copy.wait()


def paired(refs):
    size = refs[0].shape[0] // 2
    pairs = len(refs) // 2
    return [
        refs[step // 2].at[pl.ds(0, size), :]
        if step % 2 == 0
        else refs[pairs + step // 2].at[pl.ds(size, size), :]
        for step in range(2 * pairs)
    ]


def by_distance(share, pieces, seat):
    rows = pieces[0].shape[0]
    for step in range(len(pieces)):
        pieces[step][...] = share[rows_at((seat ^ step) * rows, rows, 16), :]


def keep_and_send(share, keep, send, seat, parts, first=0):
    rows = share.shape[0] // parts
    stride = keep.shape[0] // (parts // 2)
    for step in range(parts):
        target = keep if step % 2 == 0 else send
        at = (step // 2) * stride + first
        target[at : at + rows] = share[rows_at((seat ^ step) * rows, rows, 16), :]


def project_kernel(place, x, cot, gain, w_q, w_k, w_v, table, *refs):
    pieces = refs[: HEADS // 2]
    normed_out, bundle, heads, chunks = refs[HEADS // 2 :]
    rows, width = x.shape
    me = place[0]
    unit, _ = norm_parts(x[...])
    normed = (unit * gain[...]).astype(BF16)
    q = dot_nn(normed, w_q[...])
    k = dot_nn(normed, w_k[...])
    v = dot_nn(normed, w_v[...])
    low = lower_half(rows)
    low_half = lower_half(rows // 2)
    own = table[...]
    for chunk in range(width // LANES):
        cut = slice(chunk * LANES, (chunk + 1) * LANES)
        q_chunk = rope(q[:, cut], own) * HEAD**-0.5
        k_chunk = rope(k[:, cut], own)
        v_chunk = v[:, cut]
        first, later = q_chunk[: rows // 2], q_chunk[rows // 2 :]
        heads[2 * chunk, :rows] = jnp.where(low, k_chunk, turn(v_chunk)).astype(BF16)
        heads[2 * chunk + 1, :rows] = jnp.where(low, turn(k_chunk), v_chunk).astype(BF16)
        heads[2 * chunk, rows:] = jnp.where(low_half, first, turn(later)).astype(BF16)
        heads[2 * chunk + 1, rows:] = jnp.where(low_half, turn(first), later).astype(BF16)
    for step in range(HEADS):
        at = (step % 2) * heads.shape[1]
        pieces[step // 2][at : at + heads.shape[1]] = heads[me ^ step]
    normed_out[...] = normed
    bundle[:rows] = cot[...].astype(BF16)
    for chunk in range(width // LANES):
        cut = slice(chunk * LANES, (chunk + 1) * LANES)
        chunks[chunk] = cot[:, cut]
        total = sum(chunks[chunk, pl.ds(s, rows // 3, stride=3), :] for s in range(3))
        bundle[rows:, cut] = total.astype(BF16)


def attend_kernel(place, *refs):
    pieces, outs = paired(refs[:HEADS]), refs[HEADS : HEADS + HEADS // 2]
    q_out, kv_out, lse_out, q_all, kv_all, lse_o, semaphores = refs[HEADS + HEADS // 2 :]
    departures = Departures(semaphores)
    me = place[0]
    rows = outs[0].shape[0]
    for step in range(HEADS):
        start = (me ^ step) * rows
        piece = pieces[step][...]
        kv_all[rows_at(start, rows, 16), :] = piece[:rows]
        first, later = unfold_rows(piece[rows:].astype(F32))
        q_all[rows_at(start, rows // 2, 16), :] = first.astype(BF16)
        q_all[rows_at(start + rows // 2, rows // 2, 16), :] = later.astype(BF16)
    departures.send(q_all, q_out)
    departures.send(kv_all, kv_out)
    low = lower_half(BLOCK)
    for block in range(q_all.shape[0] // BLOCK):
        cut = slice(block * BLOCK, (block + 1) * BLOCK)
        seen = kv_all[: (block + 1) * BLOCK]
        scores = causal(dot_nt(q_all[cut], seen), block * BLOCK, 0)
        most = jnp.max(scores, axis=-1, keepdims=True)
        weights = jnp.exp(scores - most)
        total = jnp.sum(weights, axis=-1, keepdims=True)
        attended = dot_nn(weights.astype(BF16), seen) / total
        lse_o[cut] = jnp.where(low, most + jnp.log(total), attended)
    departures.send(lse_o, lse_out)
    for step in range(HEADS):
        own = lse_o[rows_at((me ^ step) * rows, rows, 16), :]
        at = (step % 2) * (rows // 2)
        outs[step // 2][at : at + rows // 2] = jnp.where(
            lower_half(rows // 2), turn(own[: rows // 2]), own[rows // 2 :]
        ).astype(BF16)
    departures.wait()


def finish_kernel(place, x, normed_a, gain, w_o, w_e, w_c, *refs):
    pieces = paired(refs[:HEADS])
    result_hbm, middle_hbm, normed_hbm, pooled_out = refs[HEADS : HEADS + 4]
    result_out, middle_out, normed_out, att_out, heads, chunks, semaphores = refs[HEADS + 4 :]
    departures = Departures(semaphores)
    rows, width = x.shape
    me = place[0]
    for step in range(HEADS):
        heads[me ^ step] = pieces[step][...].astype(F32)
    low = lower_half(rows // 2)
    for chunk in range(width // LANES):
        cut = slice(chunk * LANES, (chunk + 1) * LANES)
        even, odd = heads[2 * chunk], heads[2 * chunk + 1]
        att_out[: rows // 2, cut] = jnp.where(low, even, turn(odd)).astype(BF16)
        att_out[rows // 2 :, cut] = jnp.where(low, turn(even), odd).astype(BF16)
    middle = x[...] + dot_nn(att_out[...], w_o[...])
    middle_out[...] = middle
    unit, _ = norm_parts(middle)
    normed = (unit * gain[...]).astype(BF16)
    normed_out[:rows] = normed
    normed_out[rows:] = normed_a[...]
    departures.send(middle_out, middle_hbm)
    departures.send(normed_out, normed_hbm)
    hidden = gelu_value(dot_nn(normed, w_e[...])).astype(BF16)
    result = middle + dot_nn(hidden, w_c[...])
    result_out[...] = result
    departures.send(result_out, result_hbm)
    short = rows // 3
    for chunk in range(width // LANES):
        cut = slice(chunk * LANES, (chunk + 1) * LANES)
        chunks[chunk, :8] = jnp.zeros((8, LANES), F32)
        chunks[chunk, 8:] = result[:, cut]
        total = sum(chunks[chunk, pl.ds(s, short, stride=3), :] for s in (6, 7, 8))
        pooled_out[:short, cut] = (total / 3.0).astype(BF16)
    tail = (result[rows - 1 :] + result[rows - 2 : rows - 1]) / 3.0
    extra = pooled_out.shape[0] - short
    pooled_out[short:] = jnp.broadcast_to(tail, (extra, width)).astype(BF16)
    departures.wait()


def short_forward_kernel(
    place, gathered, table, gain_a, w_q, w_k, w_v, w_o, gain_f, w_e, w_c, *refs
):
    pieces, refs = refs[:HEADS], refs[HEADS:]
    own_middle, own_hidden = refs[:2]
    pooled, normed_a, q_s, k_s, v_s, o_s, lse_s, att, grad_middle = refs[2:11]
    share_pieces = refs[11:-8]
    extra, middle, normed_f, hidden, grad_pre, grad_normed, grad_low, share = refs[-8:]
    me, seat = place[0], place[1]
    count, width = pooled.shape
    short = count // HEADS
    chunk_count = width // LANES
    ff = w_e.shape[1]
    ff_own = ff // HEADS

    for step in range(HEADS):
        other = me ^ step
        pooled[rows_at(other * short, short, 16), :] = pieces[step][:short].astype(F32)
        extra[pl.ds(other, 1), :] = pieces[step][short:].astype(F32)[:1]
    for part in range(1, HEADS):
        at = slice(part * short, part * short + 1)
        pooled[at] = pooled[at] + extra[part - 1 : part]

    unit, _ = norm_parts(pooled[...])
    normed_a[...] = (unit * gain_a[...]).astype(BF16)
    low = lower_half(count)
    q = dot_nn(normed_a[...], w_q[...])
    turns = table[...]
    for chunk in range(chunk_count):
        q_chunk = rope(q[:, chunk * LANES : (chunk + 1) * LANES], turns) * HEAD**-0.5
        q_s[2 * chunk] = jnp.where(low, q_chunk, 0.0).astype(BF16)
        q_s[2 * chunk + 1] = jnp.where(low, 0.0, q_chunk).astype(BF16)
    k = dot_nn(normed_a[...], w_k[...])
    for chunk in range(chunk_count):
        k_s[chunk] = rope(k[:, chunk * LANES : (chunk + 1) * LANES], turns).astype(BF16)
    v = dot_nn(normed_a[...], w_v[...])
    for chunk in range(chunk_count):
        v_s[chunk] = v[:, chunk * LANES : (chunk + 1) * LANES].astype(BF16)


    def attend_chunk(chunk, carry):
        results = []
        k_t = jnp.transpose(k_s[chunk])
        for half in range(2):
            scores = causal(dot_nn(q_s[2 * chunk + half], k_t), 0, 0)
            most = jnp.max(scores, axis=-1, keepdims=True)
            weights = jnp.exp(scores - most)
            total = jnp.sum(weights, axis=-1, keepdims=True)
            attended = dot_nn(weights.astype(BF16), v_s[chunk]) / total
            results.append((attended, most + jnp.log(total)))
        both = jnp.where(low, results[0][0], results[1][0])
        o_s[chunk] = both
        lse_s[chunk] = jnp.where(low, results[0][1], results[1][1])
        att[:, rows_at(chunk * LANES, LANES, LANES)] = both.astype(BF16)
        return carry

    lax.fori_loop(0, chunk_count, attend_chunk, 0)
    middle[...] = pooled[...] + dot_nn(att[...], w_o[...])
    unit, scale = norm_parts(middle[...])
    normed_f[...] = (unit * gain_f[...]).astype(BF16)

    for part in range(HEADS):
        grad_low[part * short : (part + 1) * short] = gathered[part]

    ff_part = ff // 4
    grad_normed[...] = jnp.zeros(grad_normed.shape, F32)
    w_e, w_c = w_e.ready(), w_c.ready()

    def feed_forward(part, carry):
        cut = rows_at(part * ff_part, ff_part, ff_part)
        pre = dot_nn(normed_f[...], w_e[:, cut])
        value, slope = gelu_both(pre)
        hidden[:, cut] = value.astype(BF16)
        grad_hidden = dot_nt(grad_low[...], w_c[cut, :])
        low_grad = (grad_hidden * slope).astype(BF16)
        grad_pre[:, cut] = low_grad
        grad_normed[...] += dot_nt(low_grad, w_e[:, cut])
        return carry

    lax.fori_loop(0, 4, feed_forward, 0)

    own_ff = rows_at(me * ff_own, ff_own, ff_own)
    share[:ff_own] = dot_tn(hidden[:, own_ff], grad_low[...]).astype(BF16)
    expand = dot_tn(normed_f[...], grad_pre[:, own_ff]).astype(BF16)
    share[ff_own : 2 * ff_own, : width // 2] = expand[: width // 2]
    share[ff_own : 2 * ff_own, width // 2 :] = expand[width // 2 :]
    by_distance(share, share_pieces, seat)

    mine = rows_at(me * short, short, 16)
    own_middle[...] = middle[mine, :]
    own_hidden[...] = hidden[mine, :]

    unit, scale = norm_parts(middle[...])
    grad_middle[...] = grad_low[...].astype(F32) + norm_back(
        grad_normed[...], gain_f[...], unit, scale
    )


def output_kernel(place, residual, middle, hidden, w_c, output, wide):
    rows, width = residual.shape
    short_out = middle[...] + dot_nn(hidden[...], w_c[...])
    for chunk in range(width // LANES):
        cut = slice(chunk * LANES, (chunk + 1) * LANES)
        for s in range(3):
            wide[chunk, pl.ds(s, rows // 3, stride=3), :] = short_out[:, cut]
        output[:, cut] = residual[:, cut] + wide[chunk]


def short_back_kernel(
    place,
    cot,
    gathered,
    table,
    gain_a,
    w_q,
    w_k,
    w_v,
    w_o,
    pooled,
    normed_a,
    q_s,
    k_s,
    v_s,
    o_s,
    lse_s,
    att,
    grad_middle,
    middle,
    normed_f,
    gain_f,
    w_e,
    w_c,
    all_hbm,
    share_hbm,
    middle_hbm,
    g1_out,
    grad_all,
    share,
    full_middle,
    semaphores,
    do_s,
    dq_s,
    dk_s,
    dv_s,
    wide,
    wo_s,
    grad_own,
):
    me = place[0]
    rows, width = cot.shape
    count = pooled.shape[0]
    full = rows * HEADS
    chunk_count = width // LANES
    low = lower_half(count)
    g1 = grad_middle[...].astype(BF16)
    d_att = dot_nt(g1, w_o[...])
    for chunk in range(chunk_count):
        do_chunk = d_att[:, chunk * LANES : (chunk + 1) * LANES]
        do_s[2 * chunk] = jnp.where(low, do_chunk, 0.0).astype(BF16)
        do_s[2 * chunk + 1] = jnp.where(low, 0.0, do_chunk).astype(BF16)
    own_chunk = rows_at((me // 2) * LANES, LANES, LANES)
    wo_s[...] = dot_tn(att[:, own_chunk], g1)
    table = table.ready()

    def attend_back(chunk, carry):
        columns = rows_at(chunk * LANES, LANES, LANES)
        k_t = jnp.transpose(k_s[chunk])
        v_t = jnp.transpose(v_s[chunk])
        dq, dk, dv = [], [], []
        for half in range(2):
            q_half, do_half = q_s[2 * chunk + half], do_s[2 * chunk + half]
            lse = lse_s[chunk][:, half * HEAD : half * HEAD + 1]
            delta = jnp.sum(do_half.astype(F32) * o_s[chunk], axis=-1, keepdims=True)
            probs = jnp.exp(causal(dot_nn(q_half, k_t), 0, 0) - lse)
            ds = (probs * (dot_nn(do_half, v_t) - delta)).astype(BF16)
            dq.append(dot_nn(ds, k_s[chunk]))
            dk.append(dot_tn(ds, q_half))
            dv.append(dot_tn(probs.astype(BF16), do_half))
        both = jnp.where(low, dq[0], dq[1]) * HEAD**-0.5
        dq_s[:, columns] = rope_back(both, table[...]).astype(BF16)
        dk_s[:, columns] = rope_back(dk[0] + dk[1], table[...]).astype(BF16)
        dv_s[:, columns] = (dv[0] + dv[1]).astype(BF16)
        return carry

    lax.fori_loop(0, chunk_count, attend_back, 0)

    odd = me % 2 == 1
    low_width = lower_half(width)
    share_q = dot_tn(normed_a[...], dq_s[:, own_chunk])
    share_k = dot_tn(normed_a[...], dk_s[:, own_chunk])
    share_v = dot_tn(normed_a[...], dv_s[:, own_chunk])
    share_q = jnp.where(odd, turn(share_q), share_q)
    share_k = jnp.where(odd, share_k, turn(share_k))
    share_v = jnp.where(odd, turn(share_v), share_v)
    head_rows = wo_s[rows_at((me % 2) * HEAD, HEAD, HEAD), :]
    pack_attention(share, jnp.where(low_width, share_q, share_k), fold_rows(share_v), head_rows)

    grad_a = dot_nt(dq_s[...], w_q[...])
    grad_a += dot_nt(dk_s[...], w_k[...])
    grad_a += dot_nt(dv_s[...], w_v[...])
    unit, scale = norm_parts(pooled[...])
    grad_pooled = grad_middle[...] + norm_back(grad_a, gain_a[...], unit, scale)
    for chunk in range(chunk_count):
        cut = slice(chunk * LANES, (chunk + 1) * LANES)
        third = grad_pooled[:, cut] / 3.0
        for s in range(3):
            wide[chunk, pl.ds(6 + s, count, stride=3), :] = third
        wide[chunk, full + 6 : full + 8] = jnp.zeros((2, LANES), F32)
        grad_own[:, cut] = cot[:, cut] + wide[chunk, rows_at(me * rows + 8, rows, 8), :]
        for part in range(HEADS):
            more = wide[chunk, 8 + part * rows : 8 + (part + 1) * rows, :]
            grad_all[part * rows : (part + 1) * rows, cut] = (
                gathered[part, :, cut].astype(F32) + more
            ).astype(BF16)
    departures = Departures(semaphores)
    departures.send(share, share_hbm)
    departures.send(grad_all, all_hbm)
    feed_forward_back(grad_own, middle, normed_f, gain_f, w_e, w_c, full_middle, g1_out)
    departures.send(full_middle, middle_hbm)
    departures.wait()


def feed_forward_back(grad, middle, normed, gain, w_e, w_c, grad_middle_out, g1_out):
    _, slope = gelu_both(dot_nn(normed[...], w_e[...]))
    grad_hidden = dot_nt(grad[...].astype(BF16), w_c[...])
    grad_normed = dot_nt((grad_hidden * slope).astype(BF16), w_e[...])
    unit, scale = norm_parts(middle[...])
    grad_middle = grad[...] + norm_back(grad_normed, gain[...], unit, scale)
    grad_middle_out[...] = grad_middle
    g1_out[...] = grad_middle.astype(BF16)


def pack_attention(share, both_qk, folded_v, head_rows):
    half = both_qk.shape[0] // 2
    share[:half, :LANES] = both_qk[:half].astype(BF16)
    share[:half, LANES : 2 * LANES] = both_qk[half:].astype(BF16)
    share[:half, 2 * LANES : 3 * LANES] = folded_v.astype(BF16)
    size = head_rows.shape[0]
    for chunk in range(head_rows.shape[1] // LANES):
        share[chunk * size : (chunk + 1) * size, 3 * LANES :] = head_rows[
            :, chunk * LANES : (chunk + 1) * LANES
        ].astype(BF16)


def feed_forward_share_kernel(place, normed, grad, w_e, w_c, *refs):
    pieces, share = refs[:-1], refs[-1]
    seat = place[1]
    width, ff_own = w_e.shape
    normed = normed[...].reshape(-1, width)
    value, slope = gelu_both(dot_nn(normed, w_e[...]))
    grad_hidden = dot_nt(grad[...], w_c[...])
    grad_pre = (grad_hidden * slope).astype(BF16)
    share[:ff_own] = dot_tn(value.astype(BF16), grad[...]).astype(BF16)
    expand = dot_tn(normed, grad_pre).astype(BF16)
    share[ff_own:, : width // 2] = expand[: width // 2]
    share[ff_own:, width // 2 :] = expand[width // 2 :]
    by_distance(share, pieces, seat)


def attend_back_kernel(place, q_all, kv_all, lse_o, table, w_o, *refs):
    pieces, outs = refs[:HEADS], refs[HEADS : HEADS + HEADS // 2]
    dq_all, dkv_all, do_all, dkv_sum, dq_sum, q_t, do_t = refs[HEADS + HEADS // 2 :]
    me = place[0]
    rows = q_all.shape[0] // HEADS
    own_w = w_o[...]
    own_w = jnp.concatenate([jnp.zeros(own_w.shape, BF16), own_w])
    for step in range(HEADS):
        do_all[rows_at((me ^ step) * rows, rows, 16), :] = dot_nt(
            pieces[step][...], own_w
        ).astype(BF16)
    total = q_all.shape[0]
    lse = lse_o[...][:, :1]
    delta = jnp.sum(do_all[...].astype(F32) * lse_o[...], axis=-1, keepdims=True)
    dq_sum[...] = jnp.zeros(dq_sum.shape, F32)
    q_t[...] = jnp.transpose(q_all[...].astype(F32)).astype(BF16)
    do_t[...] = jnp.transpose(do_all[...].astype(F32)).astype(BF16)
    for block in range(total // BLOCK):
        cut = slice(block * BLOCK, (block + 1) * BLOCK)
        rest = slice(block * BLOCK, total)
        kv_block = kv_all[cut]
        scores = causal(dot_nt(q_all[rest], kv_block), 0, 0)
        probs = jnp.exp(scores - lse[rest])
        grad_probs = dot_nt(do_all[rest], kv_block)
        ds = (probs * (grad_probs - delta[rest])).astype(BF16)
        dq_sum[rest] += dot_nn(ds, kv_block)
        back = dot_nn(q_t[:, rest], ds) + dot_nn(do_t[:, rest], probs.astype(BF16))
        dkv_sum[cut] = jnp.transpose(back)
    dq_all[...] = rope_back(dq_sum[...] * HEAD**-0.5, table[...]).astype(BF16)
    low = lower_half(BLOCK)
    for block in range(q_all.shape[0] // BLOCK):
        cut = slice(block * BLOCK, (block + 1) * BLOCK)
        dkv = dkv_sum[cut]
        dkv_all[cut] = jnp.where(low, rope_back(dkv, table[cut, :]), dkv).astype(BF16)
    for step in range(HEADS):
        own = rows_at((me ^ step) * rows, rows, 16)
        at = (step % 2) * (rows + rows // 2)
        outs[step // 2][at : at + rows] = dkv_all[own, :]
        outs[step // 2][at + rows : at + rows + rows // 2] = fold_rows(
            dq_all[own, :].astype(F32)
        ).astype(BF16)


def attention_share_kernel(parts, place, gathered, dq_all, dkv_all, lse_o, more, *refs):
    pieces, keep, send, share = refs[:HEADS], refs[HEADS], refs[HEADS + 1], refs[-1]
    me, seat = place[0], place[1]
    _, rows, width = gathered.shape
    normed = gathered[...].reshape(-1, width)
    grad_q = dot_tn(normed, dq_all[...])
    grad_kv = dot_tn(normed, dkv_all[...])
    grad_o = jnp.zeros((LANES, width), F32)
    for step in range(HEADS):
        own = lse_o[rows_at((me ^ step) * rows, rows, 16), :].astype(BF16)
        grad_o += dot_tn(own, pieces[step][...])
    grad_o = grad_o[HEAD:]
    half = width // 2
    folded_v = jnp.where(lower_half(half), turn(grad_kv[:half]), grad_kv[half:])
    pack_attention(
        share, jnp.where(lower_half(width), grad_q, turn(grad_kv)), folded_v, grad_o
    )
    keep_and_send(share, keep, send, seat, parts)
    keep_and_send(more, keep, send, seat, parts, share.shape[0] // parts)


def start_back_kernel(place, x, grad_middle, gain, w_q, w_k, w_v, *refs):
    pieces = paired(refs[:HEADS])
    grad_in, heads, dq, dk, dv = refs[HEADS:]
    me = place[0]
    rows, width = x.shape
    half = rows // 2
    for step in range(HEADS):
        heads[me ^ step] = pieces[step][...]
    low, low_half = lower_half(rows), lower_half(half)
    for chunk in range(width // LANES):
        cut = slice(chunk * LANES, (chunk + 1) * LANES)
        even, odd = heads[2 * chunk].astype(F32), heads[2 * chunk + 1].astype(F32)
        dk[:, cut] = jnp.where(low, even[:rows], turn(odd[:rows])).astype(BF16)
        dv[:, cut] = jnp.where(low, turn(even[:rows]), odd[:rows]).astype(BF16)
        dq[:half, cut] = jnp.where(low_half, even[rows:], turn(odd[rows:])).astype(BF16)
        dq[half:, cut] = jnp.where(low_half, turn(even[rows:]), odd[rows:]).astype(BF16)
    grad_a = dot_nt(dq[...], w_q[...]) + dot_nt(dk[...], w_k[...]) + dot_nt(dv[...], w_v[...])
    unit, scale = norm_parts(x[...])
    grad_in[...] = grad_middle[...] + norm_back(grad_a, gain[...], unit, scale)


def column_to_row(column):
    return jnp.transpose(jnp.broadcast_to(column, (column.shape[0], LANES)))[:1]


def fold_lanes(values):
    return sum(
        values[:, at : at + LANES] for at in range(0, values.shape[1], LANES)
    )


def part_order(batch):
    order, bit = [0], batch // 2
    while bit >= 1:
        order = order + [step ^ bit for step in order]
        bit //= 2
    return order


def grads_kernel(parts, attention, feed_forward, place, *refs):
    refs = list(refs)
    sources = [refs.pop(0) for _ in range(2 * HEADS if attention else 0)]
    weights = [refs.pop(0) for _ in range(4 * attention)]
    if feed_forward:
        gathered, w_e, gain_f = [refs.pop(0) for _ in range(3)]
    outs = [refs.pop(0) for _ in range(5 * attention + 3 * feed_forward)]
    me, seat = place[0], place[1]
    order = part_order(parts)
    copies = []

    def send(source, target, semaphore):
        copy = pltpu.make_async_copy(source, target, semaphore)
        copy.start()
        copies.append(copy)

    for layer in range(attention):
        w_q, w_k, w_v, gain_a = weights[4 * layer : 4 * layer + 4]
        grad_q, grad_k, grad_v, grad_o, grad_gain_a = outs[5 * layer : 5 * layer + 5]
        heads, square, over, sems_a = refs[4 * layer : 4 * layer + 4]
        width = grad_q.shape[0]
        half, at_rows = width // 2, width // 2 // parts
        for at, peer in enumerate(order):
            half_parts = parts // 2
            first = ((at % half_parts) * attention + layer) * at_rows
            for step in range(HEADS):
                source = sources[at // half_parts * HEADS + step]
                heads[me ^ step, rows_at((seat ^ peer) * at_rows, at_rows, 16), :] = source[
                    first : first + at_rows
                ]
        low = lower_half(half)
        total = None
        for chunk in range(HEADS // 2):
            cut = slice(chunk * LANES, (chunk + 1) * LANES)
            for part in range(2):
                rows = slice(part * half, (part + 1) * half)
                lanes = slice(part * LANES, (part + 1) * LANES)
                even = heads[2 * chunk, :, lanes].astype(F32)
                odd = heads[2 * chunk + 1, :, lanes].astype(F32)
                square[0, chunk, rows] = jnp.where(low, even, turn(odd))
                square[1, chunk, rows] = jnp.where(low, turn(even), odd)
            even = heads[2 * chunk, :, 2 * LANES : 3 * LANES].astype(F32)
            odd = heads[2 * chunk + 1, :, 2 * LANES : 3 * LANES].astype(F32)
            square[2, chunk, :half] = jnp.where(low, even, turn(odd))
            square[2, chunk, half:] = jnp.where(low, turn(even), odd)
            for head in (2 * chunk, 2 * chunk + 1):
                for lane in range(width // LANES):
                    over[head, :, lane * LANES : (lane + 1) * LANES] = heads[
                        head, lane * HEAD : (lane + 1) * HEAD, 3 * LANES :
                    ].astype(F32)
                send(
                    over.at[head],
                    grad_o.at[pl.ds(head * HEAD, HEAD), :],
                    sems_a.at[3 + head % 2, chunk],
                )
            for at, target in enumerate((grad_q, grad_k, grad_v)):
                send(
                    square.at[at, chunk],
                    target.at[:, pl.ds(chunk * LANES, LANES)],
                    sems_a.at[at, chunk],
                )
            term = (
                w_q[:, cut].astype(F32) * square[0, chunk]
                + w_k[:, cut].astype(F32) * square[1, chunk]
                + w_v[:, cut].astype(F32) * square[2, chunk]
            )
            total = term if total is None else total + term
        total = jnp.sum(total, axis=-1, keepdims=True)
        grad_gain_a[...] = column_to_row(total) / gain_a[...]

    if feed_forward:
        contract, expand, grad_gain_f = outs[-3:]
        share, acc, sems = refs[4 * attention : 4 * attention + 3]
        width = expand.shape[0]
        half = width // 2
        ff_own = contract.shape[0] // HEADS
        ff_rows = 2 * ff_own // parts
        acc[...] = jnp.zeros(acc.shape, F32)
        for owner in range(HEADS):
            source = gathered.ready(owner)
            for at, peer in enumerate(order):
                share[owner, rows_at((seat ^ peer) * ff_rows, ff_rows, 16), :] = source[
                    owner, at * ff_rows : (at + 1) * ff_rows
                ].astype(F32)
            own = slice(owner * ff_own, (owner + 1) * ff_own)
            send(share.at[owner, pl.ds(0, ff_own), :], contract.at[own, :], sems.at[owner, 0])
            for side in range(2):
                lanes = slice(side * half, (side + 1) * half)
                send(
                    share.at[owner, pl.ds(ff_own, ff_own), lanes],
                    expand.at[lanes, own],
                    sems.at[owner, 1 + side],
                )
                acc[lanes] += fold_lanes(
                    w_e[lanes, own].astype(F32) * share[owner, ff_own:, lanes]
                )
        total = jnp.sum(acc[...], axis=-1, keepdims=True)
        grad_gain_f[...] = column_to_row(total) / gain_f[...]
    for copy in copies:
        copy.wait()


COST = 1.15e9


def call(kernel, out_shape, scratch, arguments, late=(), limit=16, in_hbm=(), kept=(), us=5):
    late = [entry if isinstance(entry, tuple) else (entry,) for entry in late]
    late = [entry + (None, None, 0, 1)[len(entry) - 1 :] for entry in late]
    specs = [pl.BlockSpec(memory_space=pltpu.SMEM)]
    specs += [pl.BlockSpec(memory_space=pltpu.VMEM)] * (len(arguments) - 1)
    buffers, arguments = [], list(arguments)
    for at, shape, *_ in late:
        specs[at] = pl.BlockSpec(memory_space=pltpu.HBM)
        buffers.append(pltpu.VMEM(shape or arguments[at].shape, arguments[at].dtype))
        arguments[at] = pltpu.with_memory_space_constraint(arguments[at], pltpu.HBM)
    body, semaphores = kernel, []
    if late:
        semaphores = [pltpu.SemaphoreType.DMA((sum(entry[4] for entry in late),))]
        body = partial(with_late, kernel, late, len(arguments), len(out_shape))
    return pl.pallas_call(
        body,
        out_shape=[
            (pltpu.HBM if at in in_hbm or at in kept else jax.ShapeDtypeStruct)(*entry)
            for at, entry in enumerate(out_shape)
        ],
        in_specs=specs,
        out_specs=[
            pl.BlockSpec(memory_space=pltpu.HBM if at in in_hbm else pltpu.VMEM)
            for at in range(len(out_shape))
        ],
        scratch_shapes=[
            pltpu.VMEM(*entry) if isinstance(entry, tuple) else entry for entry in scratch
        ]
        + buffers
        + semaphores,
        compiler_params=pltpu.CompilerParams(vmem_limit_bytes=limit * 2**20),
        cost_estimate=pl.CostEstimate(
            flops=int(us * COST), bytes_accessed=2**20, transcendentals=0
        ),
    )(*arguments)


def exchange(pieces, axis):
    devices = range(lax.axis_size(axis))
    moved = {
        step: lax.ppermute(pieces[step], axis, [(i, i ^ step) for i in devices])
        for step in reversed(range(1, len(pieces)))
    }
    return [pieces[0]] + [moved[step] for step in range(1, len(pieces))]


def after(values, *others):
    return lax.optimization_barrier((values, others))[0]


def phase(*values):
    return lax.optimization_barrier(values)


def swap(block, axis, step):
    return lax.ppermute(block, axis, [(i, i ^ step) for i in range(lax.axis_size(axis))])


def near_exchange(pairs):
    moved = {step: swap(pairs[step], "seq", 2 * step) for step in reversed(range(1, len(pairs)))}
    first = [pairs[0]] + [moved[step] for step in range(1, len(pairs))]
    return first + [swap(pair, "seq", 1) for pair in first]


def summed(pieces):
    return sum(piece.astype(F32) for piece in pieces).astype(BF16)


def sum_step(keep, arrived, bit):
    total = keep.astype(F32) + arrived.astype(F32)
    parts = lax.axis_size("batch") // (2 * bit)
    if parts <= 1:
        return total.astype(BF16), None
    total = total.reshape(parts // 2, 2, -1, total.shape[1])
    return (
        total[:, 0].reshape(-1, total.shape[-1]),
        total[:, 1].reshape(-1, total.shape[-1]).astype(BF16),
    )


def near_gather(block, *beside):
    found = {0: block}
    for step in (6, 4, 2):
        found[step] = swap(block, "seq", step)
    for step in (0, 2, 4, 6):
        found[step] = after(found[step], *beside) if beside else found[step]
        found[step + 1] = swap(found[step], "seq", 1)
    return [found[step] for step in range(HEADS)]


def gather(block):
    return lax.all_gather(block, "seq", axis=0, tiled=True)


def whole_grads(place, batch, sources=(), attention=(), gathered=None, feed_forward=None):
    arguments, out_shape, scratch, late, in_hbm = [place, *sources], [], [], [], []
    width = (attention or (feed_forward,))[0][1].shape[0]
    square, row = ((width, width), F32), ((1, width), F32)
    for params in attention:
        first = len(arguments)
        arguments += [params[1], params[2], params[3], params[0]]
        late += [first, first + 1, first + 2]
        first = len(out_shape)
        in_hbm += [first, first + 1, first + 2, first + 3]
        out_shape += [square] * 4 + [row]
        scratch += [
            ((HEADS, width // 2, width), BF16),
            ((3, HEADS // 2, width, LANES), F32),
            ((HEADS, HEAD, width), F32),
            pltpu.SemaphoreType.DMA((5, HEADS // 2)),
        ]
    if feed_forward is not None:
        ff = feed_forward[6].shape[1]
        late += [(len(arguments), None, None, 0, HEADS), len(arguments) + 1]
        arguments += [gathered, feed_forward[6], feed_forward[5]]
        in_hbm += [len(out_shape), len(out_shape) + 1]
        out_shape += [((ff, width), F32), ((width, ff), F32), row]
        scratch += [
            ((HEADS, 2 * ff // HEADS, width), F32),
            ((width, LANES), F32),
            pltpu.SemaphoreType.DMA((HEADS, 3)),
        ]
    return call(
        partial(grads_kernel, batch, len(attention), feed_forward is not None),
        out_shape,
        scratch,
        tuple(arguments),
        late,
        40 if attention else 24,
        in_hbm,
    )


def by_heads(inputs, cotangent, *weights):
    full = (weights[0][None],) + weights[1:5] + (weights[5][None],) + weights[6:8]
    brief = (weights[8][None],) + weights[9:13] + (weights[13][None],) + weights[14:16]
    x, cot = inputs[0], cotangent[0]
    rows, width = x.shape
    short, half, total = rows // 3, rows // 2, rows * HEADS
    batch = lax.axis_size("batch")
    ff = full[6].shape[1]
    ff_own = ff // HEADS
    count = short * HEADS
    chunks = width // LANES
    place = jnp.stack([lax.axis_index("seq"), lax.axis_index("batch")]).astype(jnp.int32)
    table = rope_constants(total)
    block = rows + half

    outs = call(
        project_kernel,
        [((2 * block, LANES), BF16)] * (HEADS // 2)
        + [((rows, width), BF16), ((rows + short, width), BF16)],
        [((HEADS, block, LANES), BF16), ((chunks, rows, LANES), F32)],
        (place, x, cot, full[0], full[1], full[2], full[3], table),
        (
            1,
            3,
            4,
            5,
            6,
            (7, (rows, 2 * LANES), lambda ref, me: ref.at[rows_at(me * rows, rows, 16), :]),
            2,
        ),
        kept=(HEADS // 2, HEADS // 2 + 1),
    )
    pieces, (normed_a, bundle) = near_exchange(outs[: HEADS // 2]), outs[HEADS // 2 :]
    bundles = gather(bundle).reshape(HEADS, rows + short, width)

    outs = call(
        attend_kernel,
        [((rows, LANES), BF16)] * (HEADS // 2)
        + [((total, LANES), BF16), ((total, LANES), BF16), ((total, LANES), F32)],
        [
            ((total, LANES), BF16),
            ((total, LANES), BF16),
            ((total, LANES), F32),
            pltpu.SemaphoreType.DMA((3,)),
        ],
        (place, *pieces),
        in_hbm=range(HEADS // 2, HEADS // 2 + 3),
    )
    pieces = near_exchange(outs[: HEADS // 2])
    q_all, kv_all, lse_o = outs[HEADS // 2 :]

    residual, middle, normed_f, pooled = call(
        finish_kernel,
        [
            ((rows, width), F32),
            ((rows, width), F32),
            ((2 * rows, width), BF16),
            ((short + 16, width), BF16),
        ],
        [
            ((rows, width), F32),
            ((rows, width), F32),
            ((2 * rows, width), BF16),
            ((rows, width), BF16),
            ((HEADS, half, LANES), F32),
            ((chunks, rows + 8, LANES), F32),
            pltpu.SemaphoreType.DMA((3,)),
        ],
        (place, x, normed_a, full[5], full[4], full[6], full[7], *pieces),
        (4, 1, 5, 6, 2),
        in_hbm=range(3),
    )
    pieces = near_gather(pooled)
    normed_all = gather(normed_f).reshape(HEADS, 2 * rows, width)

    outs = call(
        short_forward_kernel,
        [
            ((short, width), F32),
            ((short, ff), BF16),
            ((count, width), F32),
            ((count, width), BF16),
            ((HEADS, count, LANES), BF16),
            ((chunks, count, LANES), BF16),
            ((chunks, count, LANES), BF16),
            ((chunks, count, LANES), F32),
            ((chunks, count, LANES), F32),
            ((count, width), BF16),
            ((count, width), F32),
        ]
        + [((2 * ff_own // batch, width), BF16)] * batch,
        [
            ((HEADS, width), F32),
            ((count, width), F32),
            ((count, width), BF16),
            ((count, ff), BF16),
            ((count, ff), BF16),
            ((count, width), F32),
            ((count, width), BF16),
            ((2 * ff_own, width), BF16),
        ],
        (place, bundles, table[:count]) + brief + tuple(pieces),
        (
            4,
            2,
            5,
            6,
            7,
            9,
            10,
            (1, (HEADS, short, width), lambda ref, me: ref.at[:, pl.ds(rows, short), :]),
        ),
        22,
        kept=(0, 1),
        us=16,
    )
    own_short, saved = outs[:2], outs[2:11]
    a_at, saved = phase(outs[11:], saved)
    a_at = exchange(a_at, "batch")
    outs = call(
        short_back_kernel,
        [
            ((total, width), BF16),
            ((width // 2, width), BF16),
            ((rows, width), F32),
            ((rows, width), BF16),
        ],
        [
            ((total, width), BF16),
            ((width // 2, width), BF16),
            ((rows, width), F32),
            pltpu.SemaphoreType.DMA((3,)),
            ((HEADS, count, LANES), BF16),
            ((count, width), BF16),
            ((count, width), BF16),
            ((count, width), BF16),
            ((chunks, total + 16, LANES), F32),
            ((LANES, width), F32),
            ((rows, width), F32),
        ],
        (place, cot, bundles, table[:count])
        + brief[:5]
        + tuple(saved)
        + (middle, normed_f, full[5], full[6], full[7]),
        (
            8,
            3,
            5,
            6,
            7,
            (2, (HEADS, rows, width), lambda ref, me: ref.at[:, pl.ds(0, rows), :]),
            1,
            21,
            22,
            (19, (rows, width), lambda ref, me: ref.at[pl.ds(0, rows), :]),
            18,
        ),
        25,
        in_hbm=range(3),
        us=18,
    )
    a_at, (grad_all, short_share, grad_middle, g1) = phase(a_at, outs)

    a_all, g1, grad_all = phase(summed(a_at), g1, grad_all)
    a_at = swap(a_all, "batch", 2)
    outs = call(
        feed_forward_share_kernel,
        [((2 * ff_own // batch, width), BF16)] * batch,
        [((2 * ff_own, width), BF16)],
        (place, normed_all, grad_all, full[6], full[7]),
        (
            (1, (HEADS, rows, width), lambda ref, me: ref.at[:, pl.ds(0, rows), :]),
            (3, (width, ff_own), lambda ref, me: ref.at[:, rows_at(me * ff_own, ff_own, ff_own)]),
            2,
            (4, (ff_own, width), lambda ref, me: ref.at[rows_at(me * ff_own, ff_own, ff_own), :]),
        ),
        22,
    )
    g1_all = near_gather(g1, outs[1], a_at)
    a_all = jnp.concatenate([a_all, a_at])
    a_at = swap(a_all, "batch", 1)
    a_all, a_at, g1_all, b_at = phase(a_all, a_at, g1_all, outs)

    a_shares = gather(jnp.concatenate([a_all, a_at])[None])
    b_at = exchange(b_at, "batch")
    outs = call(
        attend_back_kernel,
        [((2 * block, LANES), BF16)] * (HEADS // 2)
        + [((total, LANES), BF16), ((total, LANES), BF16)],
        [
            ((total, LANES), BF16),
            ((total, LANES), F32),
            ((total, LANES), F32),
            ((LANES, total), BF16),
            ((LANES, total), BF16),
        ],
        (place, q_all, kv_all, lse_o, table, full[4], *g1_all),
        (
            (5, (HEAD, width), lambda ref, me: ref.at[rows_at(me * HEAD, HEAD, HEAD), :]),
            1,
            2,
            3,
            4,
        ),
        us=7,
    )
    pieces, (dq_all, dkv_all) = outs[: HEADS // 2], outs[HEADS // 2 :]
    outs = call(
        partial(attention_share_kernel, batch),
        [((width // 2, width), BF16)] * 2,
        [((width // 2, width), BF16)],
        (place, normed_all, dq_all, dkv_all, lse_o, short_share, *g1_all),
        ((1, (HEADS, rows, width), lambda ref, me: ref.at[:, pl.ds(rows, rows), :]), 4, 5),
        us=3,
    )
    b_at, pieces, (c_keep, c_send) = phase(b_at, pieces, outs)

    b_all, pieces, c_send = phase(summed(b_at), pieces, c_send)
    b_at = swap(b_all, "batch", 2)
    c_at = swap(c_send, "batch", 1)
    pieces = {step: pieces[step] for step in range(HEADS // 2)}
    moved = {step: swap(pieces[step], "seq", 2 * step) for step in (3, 2)}
    b_at, c_at, moved, pieces = phase(b_at, c_at, moved, pieces)

    b_all = jnp.concatenate([b_all, b_at])
    c_keep, c_send = sum_step(c_keep, c_at, 1)
    b_all, c_send, pieces = phase(b_all, c_send, pieces)
    b_at = swap(b_all, "batch", 1)
    c_at = swap(c_send, "batch", 2)
    moved |= {0: pieces[0], 1: swap(pieces[1], "seq", 2)}
    b_at, c_at, moved, pieces = phase(b_at, c_at, moved, pieces)

    b_all = jnp.concatenate([b_all, b_at])
    c_all, _ = sum_step(c_keep, c_at, 2)
    b_all, c_all, moved = phase(b_all, c_all, moved)
    b_shares = gather(b_all[None])
    c_at = swap(c_all, "batch", 2)
    across = {step: swap(moved[step], "seq", 1) for step in range(HEADS // 2)}
    (output,) = call(
        output_kernel,
        [((rows, width), F32)],
        [((chunks, rows, LANES), F32)],
        (place, residual, *own_short, brief[7]),
        (4, 3, 2, 1),
        us=3,
    )
    c_at, moved, across, output = phase(c_at, moved, across, output)

    c_all, moved, across, a_shares = phase(
        jnp.concatenate([c_all, c_at]), moved, across, a_shares
    )
    first = {0: c_all, 2: swap(c_all, "seq", 2), 4: swap(c_all, "seq", 4)}
    c_at = swap(c_all, "batch", 1)
    pieces = [side[step] for side in (moved, across) for step in range(HEADS // 2)]
    short_ff_grads = whole_grads(place, batch, gathered=a_shares, feed_forward=brief)
    (grad_in,) = call(
        start_back_kernel,
        [((rows, width), F32)],
        [((HEADS, block, LANES), BF16)] + [((rows, width), BF16)] * 3,
        (place, x, grad_middle, full[0], full[1], full[2], full[3], *pieces),
        (4, 5, 6, 1, 2),
        us=4,
    )
    c_at, first, short_ff_grads, grad_in = phase(c_at, first, short_ff_grads, grad_in)
    other = {0: c_at, 2: swap(c_at, "seq", 2), 4: swap(c_at, "seq", 4)}
    first |= {6: swap(first[2], "seq", 4)}
    other |= {6: swap(other[4], "seq", 2)}
    found = [
        half | {step + 1: swap(half[step], "seq", 1) for step in (0, 2, 4, 6)}
        for half in (first, other)
    ]
    c_shares = [half[step] for half in found for step in range(HEADS)]
    both_grads = whole_grads(place, batch, c_shares, (full, brief), b_shares, full)
    at_grads, full_ff_grads = both_grads[:10], both_grads[10:]

    def arranged(attention, feed_forward):
        grad_q, grad_k, grad_v, grad_o, grad_gain_a = attention
        contract, expand, grad_gain_f = feed_forward
        return (grad_gain_a[0], grad_q, grad_k, grad_v, grad_o, grad_gain_f[0], expand, contract)

    return (
        (output[None], grad_in[None])
        + arranged(at_grads[:5], full_ff_grads)
        + arranged(at_grads[5:], short_ff_grads)
    )


def from_behind(block, axis, distance):
    devices = range(lax.axis_size(axis))
    route = [(i - distance, i) for i in devices if i - distance in devices]
    return lax.ppermute(block, axis, route)


def normalize(stream, gain):
    row_mean = jnp.mean(stream, axis=-1, keepdims=True)
    centered = stream - row_mean
    spread = jnp.mean(centered * centered, axis=-1, keepdims=True)
    return centered * lax.rsqrt(spread + norm_eps) * gain


def rope_table(positions):
    half_size = HEAD // 2
    frequency = jnp.power(10000.0, -jnp.arange(half_size, dtype=jnp.float32) * 2.0 / HEAD)
    angles = positions.astype(jnp.float32)[:, None] * frequency[None, :]
    return (jnp.cos(angles)[:, None, :], jnp.sin(angles)[:, None, :])


def rotate(values, angle_cos, angle_sin):
    first_half, second_half = jnp.split(values, 2, axis=-1)
    return jnp.concatenate(
        [
            first_half * angle_cos - second_half * angle_sin,
            first_half * angle_sin + second_half * angle_cos,
        ],
        axis=-1,
    )


def rotate_back(grads, angle_cos, angle_sin):
    first_half, second_half = jnp.split(grads, 2, axis=-1)
    return jnp.concatenate(
        [
            first_half * angle_cos + second_half * angle_sin,
            second_half * angle_cos - first_half * angle_sin,
        ],
        axis=-1,
    )


def split_heads(matrix):
    return matrix.reshape(matrix.shape[0], HEADS, HEAD)


def project(stream, params, angle_cos, angle_sin):
    normed_in = normalize(stream, params[0]).astype(jnp.bfloat16)

    def heads_of(matrix):
        return split_heads(jnp.dot(normed_in, matrix, preferred_element_type=jnp.float32))

    queries = rotate(heads_of(params[1]), angle_cos, angle_sin).astype(jnp.bfloat16)
    keys_here = rotate(heads_of(params[2]), angle_cos, angle_sin).astype(jnp.bfloat16)
    values_here = heads_of(params[3]).astype(jnp.bfloat16)
    return (normed_in, queries, keys_here, values_here)


def masked_scores(queries, keys_all, query_places, key_places):
    scores = jnp.einsum(
        "nhe,mhe->hnm", queries, keys_all, preferred_element_type=jnp.float32
    ) * HEAD ** (-0.5)
    allowed = key_places[None, None, :] <= query_places[None, :, None]
    return jnp.where(allowed, scores, -1e30)


def attend(queries, keys_all, values_all, query_places, key_places):
    scores = masked_scores(queries, keys_all, query_places, key_places)
    highest_score = jnp.max(scores, axis=-1, keepdims=True)
    log_total = highest_score + jnp.log(
        jnp.sum(jnp.exp(scores - highest_score), axis=-1, keepdims=True)
    )
    prob_low = jnp.exp(scores - log_total).astype(jnp.bfloat16)
    attended = jnp.einsum("hnm,mhe->nhe", prob_low, values_all, preferred_element_type=jnp.float32)
    return (attended, log_total)


def attend_back(queries, keys_all, values_all, query_places, key_places, log_total, grad_attended):
    scores = masked_scores(queries, keys_all, query_places, key_places)
    probs_full = jnp.exp(scores - log_total)
    grad_probs = jnp.einsum(
        "nhe,mhe->hnm", grad_attended, values_all, preferred_element_type=jnp.float32
    )
    row_inner = jnp.sum(probs_full * grad_probs, axis=-1, keepdims=True)
    grad_scores = (probs_full * (grad_probs - row_inner)).astype(jnp.bfloat16)
    grad_queries = jnp.einsum(
        "hnm,mhe->nhe", grad_scores, keys_all, preferred_element_type=jnp.float32
    ) * HEAD ** (-0.5)
    return (grad_queries, grad_scores, probs_full.astype(jnp.bfloat16), row_inner)


def finish(stream, attended, params):
    row_count, width = stream.shape
    attended_low = attended.reshape(row_count, width).astype(jnp.bfloat16)
    middle = stream + jnp.dot(attended_low, params[4], preferred_element_type=jnp.float32)
    normed_mid = normalize(middle, params[5]).astype(jnp.bfloat16)
    hidden_pre = jnp.dot(normed_mid, params[6], preferred_element_type=jnp.float32)
    hidden_low = jax.nn.gelu(hidden_pre, approximate=True).astype(jnp.bfloat16)
    result = middle + jnp.dot(hidden_low, params[7], preferred_element_type=jnp.float32)
    return (result, (attended_low, middle, normed_mid, hidden_pre, hidden_low))


def finish_back(grad_result, finish_saved, params):
    attended_low, middle, normed_mid, hidden_pre, hidden_low = finish_saved
    grad_low = grad_result.astype(jnp.bfloat16)
    grad_contract = jnp.einsum(
        "nf,nd->fd", hidden_low, grad_low, preferred_element_type=jnp.float32
    )
    grad_hidden = jnp.einsum("nd,fd->nf", grad_low, params[7], preferred_element_type=jnp.float32)
    gelu_value, gelu_pull = jax.vjp(partial(jax.nn.gelu, approximate=True), hidden_pre)
    grad_pre = gelu_pull(grad_hidden)[0].astype(jnp.bfloat16)
    grad_expand = jnp.einsum("nd,nf->df", normed_mid, grad_pre, preferred_element_type=jnp.float32)
    grad_normed = jnp.einsum("nf,df->nd", grad_pre, params[6], preferred_element_type=jnp.float32)
    norm_value, norm_pull = jax.vjp(normalize, middle, params[5])
    grad_norm_in, grad_gain_ffn = norm_pull(grad_normed)
    grad_middle = grad_result + grad_norm_in
    middle_low = grad_middle.astype(jnp.bfloat16)
    grad_output_w = jnp.einsum(
        "nc,nd->cd", attended_low, middle_low, preferred_element_type=jnp.float32
    )
    grad_attended = split_heads(
        jnp.einsum("nd,cd->nc", middle_low, params[4], preferred_element_type=jnp.float32).astype(
            jnp.bfloat16
        )
    )
    return (grad_middle, grad_attended, grad_output_w, grad_expand, grad_contract, grad_gain_ffn)


def start_back(
    grad_queries, grad_keys, grad_values, stream, params, normed_in, angle_cos, angle_sin
):
    row_count, width = stream.shape
    query_low = (
        rotate_back(grad_queries, angle_cos, angle_sin)
        .reshape(row_count, width)
        .astype(jnp.bfloat16)
    )
    key_low = (
        rotate_back(grad_keys, angle_cos, angle_sin).reshape(row_count, width).astype(jnp.bfloat16)
    )
    value_low = grad_values.reshape(row_count, width).astype(jnp.bfloat16)
    grad_query = jnp.einsum("nd,nc->dc", normed_in, query_low, preferred_element_type=jnp.float32)
    grad_key = jnp.einsum("nd,nc->dc", normed_in, key_low, preferred_element_type=jnp.float32)
    grad_value = jnp.einsum("nd,nc->dc", normed_in, value_low, preferred_element_type=jnp.float32)
    grad_normed = (
        jnp.einsum("nc,dc->nd", query_low, params[1], preferred_element_type=jnp.float32)
        + jnp.einsum("nc,dc->nd", key_low, params[2], preferred_element_type=jnp.float32)
        + jnp.einsum("nc,dc->nd", value_low, params[3], preferred_element_type=jnp.float32)
    )
    norm_value, norm_pull = jax.vjp(normalize, stream, params[0])
    grad_stream, grad_gain_attn = norm_pull(grad_normed)
    return (grad_stream, grad_gain_attn, grad_query, grad_key, grad_value)


def local_forward(stream, places, params, fetch):
    angle_cos, angle_sin = rope_table(places)
    normed_in, queries, keys_here, values_here = project(stream, params, angle_cos, angle_sin)
    row_count, width = stream.shape
    keys_local = keys_here.reshape(row_count, width)
    values_local = values_here.reshape(row_count, width)
    keys_flat, values_flat = fetch(keys_local, values_local)
    key_places = jnp.arange(keys_flat.shape[0], dtype=jnp.int32)
    attended, log_total = attend(
        queries, split_heads(keys_flat), split_heads(values_flat), places, key_places
    )
    result, finish_saved = finish(stream, attended, params)
    return (
        result,
        (
            normed_in,
            queries,
            keys_local,
            values_local,
            keys_flat,
            values_flat,
            log_total,
            angle_cos,
            angle_sin,
            finish_saved,
        ),
    )


def local_backward(grad_result, stream, places, params, saved, keys_flat, values_flat, key_sum):
    normed_in, queries = (saved[0], saved[1])
    log_total, angle_cos, angle_sin, finish_saved = (saved[6], saved[7], saved[8], saved[9])
    grad_middle, grad_attended, grad_output_w, grad_expand, grad_contract, grad_gain_ffn = (
        finish_back(grad_result, finish_saved, params)
    )
    row_count, width = stream.shape
    key_places = jnp.arange(keys_flat.shape[0], dtype=jnp.int32)
    grad_queries, grad_scores, prob_low, row_inner = attend_back(
        queries,
        split_heads(keys_flat),
        split_heads(values_flat),
        places,
        key_places,
        log_total,
        grad_attended,
    )

    def contribution(first_row, term_rows):
        grad_keys = jnp.einsum(
            "hnm,nhe->mhe", grad_scores, queries, preferred_element_type=jnp.float32
        ) * HEAD ** (-0.5)
        grad_values = jnp.einsum(
            "hnm,nhe->mhe", prob_low, grad_attended, preferred_element_type=jnp.float32
        )
        return jnp.concatenate(
            [grad_keys.reshape(term_rows, width), grad_values.reshape(term_rows, width)], axis=1
        )

    both_grads = key_sum(contribution, row_count, (queries, grad_attended, log_total, row_inner))
    grad_stream, grad_gain_attn, grad_query, grad_key, grad_value = start_back(
        grad_queries,
        split_heads(both_grads[:, :width]),
        split_heads(both_grads[:, width:]),
        stream,
        params,
        normed_in,
        angle_cos,
        angle_sin,
    )
    return (
        grad_middle + grad_stream,
        (
            grad_gain_attn,
            grad_query,
            grad_key,
            grad_value,
            grad_output_w,
            grad_gain_ffn,
            grad_expand,
            grad_contract,
        ),
    )


def whole_forward(stream, params):
    row_count, width = stream.shape
    places = jnp.arange(row_count, dtype=jnp.int32)
    angle_cos, angle_sin = rope_table(places)
    normed_in, queries, keys_here, values_here = project(stream, params, angle_cos, angle_sin)
    block_rows = 512
    block_count = row_count // block_rows

    def one_block(pieces):
        return attend(pieces[0], keys_here, values_here, pieces[1], places)

    attended, log_total = lax.map(
        one_block,
        (
            queries.reshape(block_count, block_rows, HEADS, HEAD),
            places.reshape(block_count, block_rows),
        ),
    )
    result, finish_saved = finish(stream, attended.reshape(row_count, HEADS, HEAD), params)
    return (
        result,
        (normed_in, queries, keys_here, values_here, log_total, angle_cos, angle_sin, finish_saved),
    )


def whole_backward(grad_result, stream, params, saved):
    normed_in, queries, keys_here, values_here, log_total, angle_cos, angle_sin, finish_saved = (
        saved
    )
    grad_middle, grad_attended, grad_output_w, grad_expand, grad_contract, grad_gain_ffn = (
        finish_back(grad_result, finish_saved, params)
    )
    row_count, width = stream.shape
    places = jnp.arange(row_count, dtype=jnp.int32)
    block_rows = 512
    block_count = row_count // block_rows

    def one_block(running, pieces):
        query_block, place_block, total_block, grad_block = pieces
        grad_queries, grad_scores, prob_low, row_inner = attend_back(
            query_block, keys_here, values_here, place_block, places, total_block, grad_block
        )
        grad_keys = running[0] + jnp.einsum(
            "hnm,nhe->mhe", grad_scores, query_block, preferred_element_type=jnp.float32
        ) * HEAD ** (-0.5)
        grad_values = running[1] + jnp.einsum(
            "hnm,nhe->mhe", prob_low, grad_block, preferred_element_type=jnp.float32
        )
        return ((grad_keys, grad_values), grad_queries)

    zero_grads = jnp.zeros((row_count, HEADS, HEAD), jnp.float32)
    (grad_keys, grad_values), grad_queries = lax.scan(
        one_block,
        (zero_grads, zero_grads),
        (
            queries.reshape(block_count, block_rows, HEADS, HEAD),
            places.reshape(block_count, block_rows),
            log_total,
            grad_attended.reshape(block_count, block_rows, HEADS, HEAD),
        ),
    )
    grad_stream, grad_gain_attn, grad_query, grad_key, grad_value = start_back(
        grad_queries.reshape(row_count, HEADS, HEAD),
        grad_keys,
        grad_values,
        stream,
        params,
        normed_in,
        angle_cos,
        angle_sin,
    )
    return (
        grad_middle + grad_stream,
        (
            grad_gain_attn,
            grad_query,
            grad_key,
            grad_value,
            grad_output_w,
            grad_gain_ffn,
            grad_expand,
            grad_contract,
        ),
    )


def by_rows(
    inputs,
    cotangent,
    full_gain_attn,
    full_query,
    full_key,
    full_value,
    full_output,
    full_gain_ffn,
    full_expand,
    full_contract,
    short_gain_attn,
    short_query,
    short_key,
    short_value,
    short_output,
    short_gain_ffn,
    short_expand,
    short_contract,
):
    full_params = (
        full_gain_attn,
        full_query,
        full_key,
        full_value,
        full_output,
        full_gain_ffn,
        full_expand,
        full_contract,
    )
    short_params = (
        short_gain_attn,
        short_query,
        short_key,
        short_value,
        short_output,
        short_gain_ffn,
        short_expand,
        short_contract,
    )
    stream_in = inputs[0]
    row_count, width = stream_in.shape
    own_short = row_count // 3
    position = lax.axis_index("seq")
    seq_parts = lax.axis_size("seq")
    places = position * row_count + jnp.arange(row_count, dtype=jnp.int32)

    def fetch_full(keys_local, values_local):
        return (
            lax.all_gather(keys_local, "seq", axis=0, tiled=True),
            lax.all_gather(values_local, "seq", axis=0, tiled=True),
        )

    residual, full_saved = local_forward(stream_in, places, full_params, fetch_full)
    tail_rows = from_behind(residual[row_count - 2 :], "seq", 1)
    shifted = jnp.concatenate([tail_rows, residual[: row_count - 2]], axis=0)
    pooled = jnp.mean(shifted.reshape(own_short, 3, width), axis=1)
    pooled_all = lax.all_gather(pooled, "seq", axis=0, tiled=True)
    short_all, short_saved = whole_forward(pooled_all, short_params)
    short_result = lax.dynamic_slice_in_dim(short_all, position * own_short, own_short, 0)
    output = residual + jnp.repeat(short_result, 3, axis=0)
    grad_output = cotangent[0]
    grad_short = jnp.sum(grad_output.reshape(own_short, 3, width), axis=1)
    grad_short_all = lax.all_gather(grad_short, "seq", axis=0, tiled=True)
    grad_pooled_all, short_grads = whole_backward(
        grad_short_all, pooled_all, short_params, short_saved
    )
    grad_pooled = lax.dynamic_slice_in_dim(grad_pooled_all, position * own_short, own_short, 0)
    short_grads = tuple(
        (
            lax.dynamic_slice_in_dim(
                gradient,
                position * (gradient.shape[0] // seq_parts),
                gradient.shape[0] // seq_parts,
                0,
            )
            for gradient in short_grads
        )
    )
    grad_shifted = jnp.repeat(grad_pooled / 3.0, 3, axis=0)
    carried = from_behind(grad_shifted[:2], "seq", -1)
    grad_residual = grad_output + jnp.concatenate([grad_shifted[2:], carried], axis=0)
    keys_flat, values_flat = (
        lax.all_gather(full_saved[2], "seq", axis=0, tiled=True),
        lax.all_gather(full_saved[3], "seq", axis=0, tiled=True),
    )

    def full_sum(contribution, term_rows, query_side):
        return lax.psum_scatter(
            contribution(jnp.int32(0), term_rows * lax.axis_size("seq")).astype(jnp.bfloat16),
            "seq",
            scatter_dimension=0,
            tiled=True,
        ).astype(jnp.float32)

    grad_input, full_grads = local_backward(
        grad_residual, stream_in, places, full_params, full_saved, keys_flat, values_flat, full_sum
    )
    full_shares = (
        lax.psum_scatter(
            full_grads[0].astype(jnp.bfloat16), "seq", scatter_dimension=0, tiled=True
        ).astype(jnp.float32),
        lax.psum_scatter(
            full_grads[1].astype(jnp.bfloat16), "seq", scatter_dimension=0, tiled=True
        ).astype(jnp.float32),
        lax.psum_scatter(
            full_grads[2].astype(jnp.bfloat16), "seq", scatter_dimension=0, tiled=True
        ).astype(jnp.float32),
        lax.psum_scatter(
            full_grads[3].astype(jnp.bfloat16), "seq", scatter_dimension=0, tiled=True
        ).astype(jnp.float32),
        lax.psum_scatter(
            full_grads[4].astype(jnp.bfloat16), "seq", scatter_dimension=0, tiled=True
        ).astype(jnp.float32),
        lax.psum_scatter(
            full_grads[5].astype(jnp.bfloat16), "seq", scatter_dimension=0, tiled=True
        ).astype(jnp.float32),
        lax.psum_scatter(
            full_grads[6].astype(jnp.bfloat16), "seq", scatter_dimension=0, tiled=True
        ).astype(jnp.float32),
        lax.psum_scatter(
            full_grads[7].astype(jnp.bfloat16), "seq", scatter_dimension=0, tiled=True
        ).astype(jnp.float32),
    )
    shares = tuple(full_shares) + tuple(short_grads)
    totals = (
        lax.psum(shares[0].astype(jnp.bfloat16), "batch").astype(jnp.float32),
        lax.psum(shares[1].astype(jnp.bfloat16), "batch").astype(jnp.float32),
        lax.psum(shares[2].astype(jnp.bfloat16), "batch").astype(jnp.float32),
        lax.psum(shares[3].astype(jnp.bfloat16), "batch").astype(jnp.float32),
        lax.psum(shares[4].astype(jnp.bfloat16), "batch").astype(jnp.float32),
        lax.psum(shares[5].astype(jnp.bfloat16), "batch").astype(jnp.float32),
        lax.psum(shares[6].astype(jnp.bfloat16), "batch").astype(jnp.float32),
        lax.psum(shares[7].astype(jnp.bfloat16), "batch").astype(jnp.float32),
        lax.psum(shares[8].astype(jnp.bfloat16), "batch").astype(jnp.float32),
        lax.psum(shares[9].astype(jnp.bfloat16), "batch").astype(jnp.float32),
        lax.psum(shares[10].astype(jnp.bfloat16), "batch").astype(jnp.float32),
        lax.psum(shares[11].astype(jnp.bfloat16), "batch").astype(jnp.float32),
        lax.psum(shares[12].astype(jnp.bfloat16), "batch").astype(jnp.float32),
        lax.psum(shares[13].astype(jnp.bfloat16), "batch").astype(jnp.float32),
        lax.psum(shares[14].astype(jnp.bfloat16), "batch").astype(jnp.float32),
        lax.psum(shares[15].astype(jnp.bfloat16), "batch").astype(jnp.float32),
    )
    whole = (
        lax.all_gather(totals[0].astype(jnp.bfloat16), "seq", axis=0, tiled=True).astype(
            jnp.float32
        ),
        lax.all_gather(totals[1].astype(jnp.bfloat16), "seq", axis=0, tiled=True).astype(
            jnp.float32
        ),
        lax.all_gather(totals[2].astype(jnp.bfloat16), "seq", axis=0, tiled=True).astype(
            jnp.float32
        ),
        lax.all_gather(totals[3].astype(jnp.bfloat16), "seq", axis=0, tiled=True).astype(
            jnp.float32
        ),
        lax.all_gather(totals[4].astype(jnp.bfloat16), "seq", axis=0, tiled=True).astype(
            jnp.float32
        ),
        lax.all_gather(totals[5].astype(jnp.bfloat16), "seq", axis=0, tiled=True).astype(
            jnp.float32
        ),
        lax.all_gather(totals[6].astype(jnp.bfloat16), "seq", axis=0, tiled=True).astype(
            jnp.float32
        ),
        lax.all_gather(totals[7].astype(jnp.bfloat16), "seq", axis=0, tiled=True).astype(
            jnp.float32
        ),
        lax.all_gather(totals[8].astype(jnp.bfloat16), "seq", axis=0, tiled=True).astype(
            jnp.float32
        ),
        lax.all_gather(totals[9].astype(jnp.bfloat16), "seq", axis=0, tiled=True).astype(
            jnp.float32
        ),
        lax.all_gather(totals[10].astype(jnp.bfloat16), "seq", axis=0, tiled=True).astype(
            jnp.float32
        ),
        lax.all_gather(totals[11].astype(jnp.bfloat16), "seq", axis=0, tiled=True).astype(
            jnp.float32
        ),
        lax.all_gather(totals[12].astype(jnp.bfloat16), "seq", axis=0, tiled=True).astype(
            jnp.float32
        ),
        lax.all_gather(totals[13].astype(jnp.bfloat16), "seq", axis=0, tiled=True).astype(
            jnp.float32
        ),
        lax.all_gather(totals[14].astype(jnp.bfloat16), "seq", axis=0, tiled=True).astype(
            jnp.float32
        ),
        lax.all_gather(totals[15].astype(jnp.bfloat16), "seq", axis=0, tiled=True).astype(
            jnp.float32
        ),
    )
    return (output[None], grad_input[None]) + tuple(whole)


def solution(mesh):
    sequence = P("batch", "seq", None)
    seq, batch = mesh.shape["seq"], mesh.shape["batch"]
    fits = seq == HEADS and batch == 4
    return jax.shard_map(
        by_heads if fits else by_rows,
        mesh=mesh,
        in_specs=(sequence, sequence) + (P(),) * 16,
        out_specs=(sequence, sequence) + (P(),) * 16,
        check_vma=False,
    )
```

```python
from functools import partial

import jax
import jax.numpy as jnp
import numpy as np
from jax import lax
from jax.experimental import pallas as pl
from jax.experimental.pallas import tpu as pltpu
from jax.sharding import PartitionSpec as P

HEADS = 8
HEAD = 64
LANES = 128
BLOCK = 256
F32 = jnp.float32
BF16 = jnp.bfloat16


norm_eps = 1e-05


def dot_nn(left, right):
    return jnp.dot(left, right, preferred_element_type=F32)


def dot_nt(left, right):
    return lax.dot_general(left, right, (((1,), (1,)), ((), ())), preferred_element_type=F32)


def dot_tn(left, right):
    return lax.dot_general(left, right, (((0,), (0,)), ((), ())), preferred_element_type=F32)


def lower_half(rows):
    return lax.broadcasted_iota(jnp.int32, (rows, LANES), 1) < HEAD


def turn(values):
    return pltpu.roll(values, HEAD, 1)


def swap_pairs(values):
    lane = lax.broadcasted_iota(jnp.int32, values.shape, 1)
    return jnp.where(
        lane % HEAD < HEAD // 2,
        pltpu.roll(values, LANES - HEAD // 2, 1),
        pltpu.roll(values, HEAD // 2, 1),
    )


def rope(values, table):
    return values * table[:, :LANES] + swap_pairs(values) * table[:, LANES:]


def rope_back(grads, table):
    return grads * table[:, :LANES] - swap_pairs(grads) * table[:, LANES:]


def rope_constants(rows):
    frequency = np.power(
        np.float32(10000.0), -np.arange(HEAD // 2, dtype=np.float32) * np.float32(2.0 / HEAD)
    ).astype(np.float32)
    angles = np.arange(rows, dtype=np.float32)[:, None] * frequency[None, :]
    cosine, sine = np.cos(angles), np.sin(angles)
    table = np.concatenate([cosine] * 4 + [-sine, sine] * 2, axis=1)
    return jnp.asarray(table, F32)


def norm_parts(stream):
    centered = stream - jnp.mean(stream, axis=-1, keepdims=True)
    spread = jnp.mean(centered * centered, axis=-1, keepdims=True)
    scale = lax.rsqrt(spread + norm_eps)
    return centered * scale, scale


def norm_back(grad, gain, unit, scale):
    grad_unit = grad * gain
    inner = jnp.mean(grad_unit * unit, axis=-1, keepdims=True)
    return scale * (grad_unit - jnp.mean(grad_unit, axis=-1, keepdims=True) - unit * inner)


GELU_SCALE = 0.7978845608028654
GELU_CUBE = 0.044715


def gelu_both(pre):
    square = pre * pre
    half = 0.5 + 0.5 * jnp.tanh(pre * (GELU_SCALE + GELU_SCALE * GELU_CUBE * square))
    bend = pre * (2.0 * GELU_SCALE + 6.0 * GELU_SCALE * GELU_CUBE * square)
    return pre * half, half * (1.0 + (1.0 - half) * bend)


def gelu_value(pre):
    tanh = jnp.tanh(GELU_SCALE * pre * (1.0 + GELU_CUBE * pre * pre))
    return 0.5 * pre * (1.0 + tanh)


def causal(scores, first_row, first_key):
    row = lax.broadcasted_iota(jnp.int32, scores.shape, 0) + first_row
    key = lax.broadcasted_iota(jnp.int32, scores.shape, 1) + first_key
    return jnp.where(key <= row, scores, -1e30)


def fold_rows(values):
    half = values.shape[0] // 2
    return jnp.where(lower_half(half), values[:half], turn(values[half:]))


def unfold_rows(folded):
    low = lower_half(folded.shape[0])
    return jnp.where(low, folded, 0.0), jnp.where(low, turn(folded), 0.0)


def rows_at(start, size, multiple):
    return pl.ds(pl.multiple_of(start, multiple), size)


class Late:
    def __init__(self, source, target, semaphores, axis=0, parts=1):
        self.target, self.shape = target, target.shape
        size = target.shape[axis] // parts
        cuts = [(slice(None),) * axis + (pl.ds(part * size, size),) for part in range(parts)]
        self.copies = [
            pltpu.make_async_copy(source.at[cut], target.at[cut], semaphore)
            for cut, semaphore in zip(cuts, semaphores)
        ]
        self.waiting = set(range(parts))

    def ready(self, part=None):
        for at in sorted(self.waiting if part is None else self.waiting & {part}):
            self.copies[at].wait()
            self.waiting.remove(at)
        return self.target

    def __getitem__(self, index):
        return self.ready()[index]


def with_late(kernel, late, argument_count, out_count, *refs):
    arguments, outs = list(refs[:argument_count]), refs[argument_count : argument_count + out_count]
    rest = refs[argument_count + out_count :]
    first, taken, begun = len(rest) - len(late) - 1, 0, []
    for at, (place, _, part, axis, parts) in enumerate(late):
        source = arguments[place]
        source = source if part is None else part(source, refs[0][0])
        semaphores = [rest[-1].at[taken + step] for step in range(parts)]
        arguments[place] = Late(source, rest[first + at], semaphores, axis, parts)
        begun += [(part, at, copy) for part, copy in enumerate(arguments[place].copies)]
        taken += parts
    for _, _, copy in sorted(begun, key=lambda entry: entry[:2]):
        copy.start()
    kernel(*arguments, *outs, *rest[:first])


class Departures:
    def __init__(self, semaphores):
        self.semaphores, self.copies = semaphores, []

    def send(self, source, target):
        copy = pltpu.make_async_copy(source, target, self.semaphores.at[len(self.copies)])
        copy.start()
        self.copies.append(copy)

    def wait(self):
        for copy in self.copies:
            copy.wait()


def paired(refs):
    size = refs[0].shape[0] // 2
    pairs = len(refs) // 2
    return [
        refs[step // 2].at[pl.ds(0, size), :]
        if step % 2 == 0
        else refs[pairs + step // 2].at[pl.ds(size, size), :]
        for step in range(2 * pairs)
    ]


def by_distance(share, pieces, seat):
    rows = pieces[0].shape[0]
    for step in range(len(pieces)):
        pieces[step][...] = share[rows_at((seat ^ step) * rows, rows, 16), :]


def keep_and_send(share, keep, send, seat, parts, first=0):
    rows = share.shape[0] // parts
    stride = keep.shape[0] // (parts // 2)
    for step in range(parts):
        target = keep if step % 2 == 0 else send
        at = (step // 2) * stride + first
        target[at : at + rows] = share[rows_at((seat ^ step) * rows, rows, 16), :]


def project_kernel(place, x, cot, gain, w_q, w_k, w_v, table, *refs):
    pieces = refs[: HEADS // 2]
    normed_out, bundle, heads, chunks = refs[HEADS // 2 :]
    rows, width = x.shape
    me = place[0]
    unit, _ = norm_parts(x[...])
    normed = (unit * gain[...]).astype(BF16)
    q = dot_nn(normed, w_q[...])
    k = dot_nn(normed, w_k[...])
    v = dot_nn(normed, w_v[...])
    low = lower_half(rows)
    low_half = lower_half(rows // 2)
    own = table[...]
    for chunk in range(width // LANES):
        cut = slice(chunk * LANES, (chunk + 1) * LANES)
        q_chunk = rope(q[:, cut], own) * HEAD**-0.5
        k_chunk = rope(k[:, cut], own)
        v_chunk = v[:, cut]
        first, later = q_chunk[: rows // 2], q_chunk[rows // 2 :]
        heads[2 * chunk, :rows] = jnp.where(low, k_chunk, turn(v_chunk)).astype(BF16)
        heads[2 * chunk + 1, :rows] = jnp.where(low, turn(k_chunk), v_chunk).astype(BF16)
        heads[2 * chunk, rows:] = jnp.where(low_half, first, turn(later)).astype(BF16)
        heads[2 * chunk + 1, rows:] = jnp.where(low_half, turn(first), later).astype(BF16)
    for step in range(HEADS):
        at = (step % 2) * heads.shape[1]
        pieces[step // 2][at : at + heads.shape[1]] = heads[me ^ step]
    normed_out[...] = normed
    bundle[:rows] = cot[...].astype(BF16)
    for chunk in range(width // LANES):
        cut = slice(chunk * LANES, (chunk + 1) * LANES)
        chunks[chunk] = cot[:, cut]
        total = sum(chunks[chunk, pl.ds(s, rows // 3, stride=3), :] for s in range(3))
        bundle[rows:, cut] = total.astype(BF16)


def attend_kernel(place, *refs):
    pieces, outs = paired(refs[:HEADS]), refs[HEADS : HEADS + HEADS // 2]
    q_out, kv_out, lse_out, q_all, kv_all, lse_o, semaphores = refs[HEADS + HEADS // 2 :]
    departures = Departures(semaphores)
    me = place[0]
    rows = outs[0].shape[0]
    for step in range(HEADS):
        start = (me ^ step) * rows
        piece = pieces[step][...]
        kv_all[rows_at(start, rows, 16), :] = piece[:rows]
        first, later = unfold_rows(piece[rows:].astype(F32))
        q_all[rows_at(start, rows // 2, 16), :] = first.astype(BF16)
        q_all[rows_at(start + rows // 2, rows // 2, 16), :] = later.astype(BF16)
    departures.send(q_all, q_out)
    departures.send(kv_all, kv_out)
    low = lower_half(BLOCK)
    for block in range(q_all.shape[0] // BLOCK):
        cut = slice(block * BLOCK, (block + 1) * BLOCK)
        seen = kv_all[: (block + 1) * BLOCK]
        scores = causal(dot_nt(q_all[cut], seen), block * BLOCK, 0)
        most = jnp.max(scores, axis=-1, keepdims=True)
        weights = jnp.exp(scores - most)
        total = jnp.sum(weights, axis=-1, keepdims=True)
        attended = dot_nn(weights.astype(BF16), seen) / total
        lse_o[cut] = jnp.where(low, most + jnp.log(total), attended)
    departures.send(lse_o, lse_out)
    for step in range(HEADS):
        own = lse_o[rows_at((me ^ step) * rows, rows, 16), :]
        at = (step % 2) * (rows // 2)
        outs[step // 2][at : at + rows // 2] = jnp.where(
            lower_half(rows // 2), turn(own[: rows // 2]), own[rows // 2 :]
        ).astype(BF16)
    departures.wait()


def finish_kernel(place, x, normed_a, gain, w_o, w_e, w_c, *refs):
    pieces = paired(refs[:HEADS])
    result_hbm, middle_hbm, normed_hbm, pooled_out = refs[HEADS : HEADS + 4]
    result_out, middle_out, normed_out, att_out, heads, chunks, semaphores = refs[HEADS + 4 :]
    departures = Departures(semaphores)
    rows, width = x.shape
    me = place[0]
    for step in range(HEADS):
        heads[me ^ step] = pieces[step][...].astype(F32)
    low = lower_half(rows // 2)
    for chunk in range(width // LANES):
        cut = slice(chunk * LANES, (chunk + 1) * LANES)
        even, odd = heads[2 * chunk], heads[2 * chunk + 1]
        att_out[: rows // 2, cut] = jnp.where(low, even, turn(odd)).astype(BF16)
        att_out[rows // 2 :, cut] = jnp.where(low, turn(even), odd).astype(BF16)
    middle = x[...] + dot_nn(att_out[...], w_o[...])
    middle_out[...] = middle
    unit, _ = norm_parts(middle)
    normed = (unit * gain[...]).astype(BF16)
    normed_out[:rows] = normed
    normed_out[rows:] = normed_a[...]
    departures.send(middle_out, middle_hbm)
    departures.send(normed_out, normed_hbm)
    hidden = gelu_value(dot_nn(normed, w_e[...])).astype(BF16)
    result = middle + dot_nn(hidden, w_c[...])
    result_out[...] = result
    departures.send(result_out, result_hbm)
    short = rows // 3
    for chunk in range(width // LANES):
        cut = slice(chunk * LANES, (chunk + 1) * LANES)
        chunks[chunk, :8] = jnp.zeros((8, LANES), F32)
        chunks[chunk, 8:] = result[:, cut]
        total = sum(chunks[chunk, pl.ds(s, short, stride=3), :] for s in (6, 7, 8))
        pooled_out[:short, cut] = (total / 3.0).astype(BF16)
    tail = (result[rows - 1 :] + result[rows - 2 : rows - 1]) / 3.0
    extra = pooled_out.shape[0] - short
    pooled_out[short:] = jnp.broadcast_to(tail, (extra, width)).astype(BF16)
    departures.wait()


def short_forward_kernel(
    place, gathered, table, gain_a, w_q, w_k, w_v, w_o, gain_f, w_e, w_c, *refs
):
    pieces, refs = refs[:HEADS], refs[HEADS:]
    own_middle, own_hidden = refs[:2]
    pooled, normed_a, q_s, k_s, v_s, o_s, lse_s, att, grad_middle = refs[2:11]
    share_pieces = refs[11:-8]
    extra, middle, normed_f, hidden, grad_pre, grad_normed, grad_low, share = refs[-8:]
    me, seat = place[0], place[1]
    count, width = pooled.shape
    short = count // HEADS
    chunk_count = width // LANES
    ff = w_e.shape[1]
    ff_own = ff // HEADS

    for step in range(HEADS):
        other = me ^ step
        pooled[rows_at(other * short, short, 16), :] = pieces[step][:short].astype(F32)
        extra[pl.ds(other, 1), :] = pieces[step][short:].astype(F32)[:1]
    for part in range(1, HEADS):
        at = slice(part * short, part * short + 1)
        pooled[at] = pooled[at] + extra[part - 1 : part]

    unit, _ = norm_parts(pooled[...])
    normed_a[...] = (unit * gain_a[...]).astype(BF16)
    low = lower_half(count)
    q = dot_nn(normed_a[...], w_q[...])
    turns = table[...]
    for chunk in range(chunk_count):
        q_chunk = rope(q[:, chunk * LANES : (chunk + 1) * LANES], turns) * HEAD**-0.5
        q_s[2 * chunk] = jnp.where(low, q_chunk, 0.0).astype(BF16)
        q_s[2 * chunk + 1] = jnp.where(low, 0.0, q_chunk).astype(BF16)
    k = dot_nn(normed_a[...], w_k[...])
    for chunk in range(chunk_count):
        k_s[chunk] = rope(k[:, chunk * LANES : (chunk + 1) * LANES], turns).astype(BF16)
    v = dot_nn(normed_a[...], w_v[...])
    for chunk in range(chunk_count):
        v_s[chunk] = v[:, chunk * LANES : (chunk + 1) * LANES].astype(BF16)


    def attend_chunk(chunk, carry):
        results = []
        k_t = jnp.transpose(k_s[chunk])
        for half in range(2):
            scores = causal(dot_nn(q_s[2 * chunk + half], k_t), 0, 0)
            most = jnp.max(scores, axis=-1, keepdims=True)
            weights = jnp.exp(scores - most)
            total = jnp.sum(weights, axis=-1, keepdims=True)
            attended = dot_nn(weights.astype(BF16), v_s[chunk]) / total
            results.append((attended, most + jnp.log(total)))
        both = jnp.where(low, results[0][0], results[1][0])
        o_s[chunk] = both
        lse_s[chunk] = jnp.where(low, results[0][1], results[1][1])
        att[:, rows_at(chunk * LANES, LANES, LANES)] = both.astype(BF16)
        return carry

    lax.fori_loop(0, chunk_count, attend_chunk, 0)
    middle[...] = pooled[...] + dot_nn(att[...], w_o[...])
    unit, scale = norm_parts(middle[...])
    normed_f[...] = (unit * gain_f[...]).astype(BF16)

    for part in range(HEADS):
        grad_low[part * short : (part + 1) * short] = gathered[part]

    ff_part = ff // 4
    grad_normed[...] = jnp.zeros(grad_normed.shape, F32)
    w_e, w_c = w_e.ready(), w_c.ready()

    def feed_forward(part, carry):
        cut = rows_at(part * ff_part, ff_part, ff_part)
        pre = dot_nn(normed_f[...], w_e[:, cut])
        value, slope = gelu_both(pre)
        hidden[:, cut] = value.astype(BF16)
        grad_hidden = dot_nt(grad_low[...], w_c[cut, :])
        low_grad = (grad_hidden * slope).astype(BF16)
        grad_pre[:, cut] = low_grad
        grad_normed[...] += dot_nt(low_grad, w_e[:, cut])
        return carry

    lax.fori_loop(0, 4, feed_forward, 0)

    own_ff = rows_at(me * ff_own, ff_own, ff_own)
    share[:ff_own] = dot_tn(hidden[:, own_ff], grad_low[...]).astype(BF16)
    expand = dot_tn(normed_f[...], grad_pre[:, own_ff]).astype(BF16)
    share[ff_own : 2 * ff_own, : width // 2] = expand[: width // 2]
    share[ff_own : 2 * ff_own, width // 2 :] = expand[width // 2 :]
    by_distance(share, share_pieces, seat)

    mine = rows_at(me * short, short, 16)
    own_middle[...] = middle[mine, :]
    own_hidden[...] = hidden[mine, :]

    unit, scale = norm_parts(middle[...])
    grad_middle[...] = grad_low[...].astype(F32) + norm_back(
        grad_normed[...], gain_f[...], unit, scale
    )


def output_kernel(place, residual, middle, hidden, w_c, output, wide):
    rows, width = residual.shape
    short_out = middle[...] + dot_nn(hidden[...], w_c[...])
    for chunk in range(width // LANES):
        cut = slice(chunk * LANES, (chunk + 1) * LANES)
        for s in range(3):
            wide[chunk, pl.ds(s, rows // 3, stride=3), :] = short_out[:, cut]
        output[:, cut] = residual[:, cut] + wide[chunk]


def short_back_kernel(
    place,
    cot,
    gathered,
    table,
    gain_a,
    w_q,
    w_k,
    w_v,
    w_o,
    pooled,
    normed_a,
    q_s,
    k_s,
    v_s,
    o_s,
    lse_s,
    att,
    grad_middle,
    middle,
    normed_f,
    gain_f,
    w_e,
    w_c,
    all_hbm,
    share_hbm,
    middle_hbm,
    g1_out,
    grad_all,
    share,
    full_middle,
    semaphores,
    do_s,
    dq_s,
    dk_s,
    dv_s,
    wide,
    wo_s,
    grad_own,
):
    me = place[0]
    rows, width = cot.shape
    count = pooled.shape[0]
    full = rows * HEADS
    chunk_count = width // LANES
    low = lower_half(count)
    g1 = grad_middle[...].astype(BF16)
    d_att = dot_nt(g1, w_o[...])
    for chunk in range(chunk_count):
        do_chunk = d_att[:, chunk * LANES : (chunk + 1) * LANES]
        do_s[2 * chunk] = jnp.where(low, do_chunk, 0.0).astype(BF16)
        do_s[2 * chunk + 1] = jnp.where(low, 0.0, do_chunk).astype(BF16)
    own_chunk = rows_at((me // 2) * LANES, LANES, LANES)
    wo_s[...] = dot_tn(att[:, own_chunk], g1)
    table = table.ready()

    def attend_back(chunk, carry):
        columns = rows_at(chunk * LANES, LANES, LANES)
        k_t = jnp.transpose(k_s[chunk])
        v_t = jnp.transpose(v_s[chunk])
        dq, dk, dv = [], [], []
        for half in range(2):
            q_half, do_half = q_s[2 * chunk + half], do_s[2 * chunk + half]
            lse = lse_s[chunk][:, half * HEAD : half * HEAD + 1]
            delta = jnp.sum(do_half.astype(F32) * o_s[chunk], axis=-1, keepdims=True)
            probs = jnp.exp(causal(dot_nn(q_half, k_t), 0, 0) - lse)
            ds = (probs * (dot_nn(do_half, v_t) - delta)).astype(BF16)
            dq.append(dot_nn(ds, k_s[chunk]))
            dk.append(dot_tn(ds, q_half))
            dv.append(dot_tn(probs.astype(BF16), do_half))
        both = jnp.where(low, dq[0], dq[1]) * HEAD**-0.5
        dq_s[:, columns] = rope_back(both, table[...]).astype(BF16)
        dk_s[:, columns] = rope_back(dk[0] + dk[1], table[...]).astype(BF16)
        dv_s[:, columns] = (dv[0] + dv[1]).astype(BF16)
        return carry

    lax.fori_loop(0, chunk_count, attend_back, 0)

    odd = me % 2 == 1
    low_width = lower_half(width)
    share_q = dot_tn(normed_a[...], dq_s[:, own_chunk])
    share_k = dot_tn(normed_a[...], dk_s[:, own_chunk])
    share_v = dot_tn(normed_a[...], dv_s[:, own_chunk])
    share_q = jnp.where(odd, turn(share_q), share_q)
    share_k = jnp.where(odd, share_k, turn(share_k))
    share_v = jnp.where(odd, turn(share_v), share_v)
    head_rows = wo_s[rows_at((me % 2) * HEAD, HEAD, HEAD), :]
    pack_attention(share, jnp.where(low_width, share_q, share_k), fold_rows(share_v), head_rows)

    grad_a = dot_nt(dq_s[...], w_q[...])
    grad_a += dot_nt(dk_s[...], w_k[...])
    grad_a += dot_nt(dv_s[...], w_v[...])
    unit, scale = norm_parts(pooled[...])
    grad_pooled = grad_middle[...] + norm_back(grad_a, gain_a[...], unit, scale)
    for chunk in range(chunk_count):
        cut = slice(chunk * LANES, (chunk + 1) * LANES)
        third = grad_pooled[:, cut] / 3.0
        for s in range(3):
            wide[chunk, pl.ds(6 + s, count, stride=3), :] = third
        wide[chunk, full + 6 : full + 8] = jnp.zeros((2, LANES), F32)
        grad_own[:, cut] = cot[:, cut] + wide[chunk, rows_at(me * rows + 8, rows, 8), :]
        for part in range(HEADS):
            more = wide[chunk, 8 + part * rows : 8 + (part + 1) * rows, :]
            grad_all[part * rows : (part + 1) * rows, cut] = (
                gathered[part, :, cut].astype(F32) + more
            ).astype(BF16)
    departures = Departures(semaphores)
    departures.send(share, share_hbm)
    departures.send(grad_all, all_hbm)
    feed_forward_back(grad_own, middle, normed_f, gain_f, w_e, w_c, full_middle, g1_out)
    departures.send(full_middle, middle_hbm)
    departures.wait()


def feed_forward_back(grad, middle, normed, gain, w_e, w_c, grad_middle_out, g1_out):
    _, slope = gelu_both(dot_nn(normed[...], w_e[...]))
    grad_hidden = dot_nt(grad[...].astype(BF16), w_c[...])
    grad_normed = dot_nt((grad_hidden * slope).astype(BF16), w_e[...])
    unit, scale = norm_parts(middle[...])
    grad_middle = grad[...] + norm_back(grad_normed, gain[...], unit, scale)
    grad_middle_out[...] = grad_middle
    g1_out[...] = grad_middle.astype(BF16)


def pack_attention(share, both_qk, folded_v, head_rows):
    half = both_qk.shape[0] // 2
    share[:half, :LANES] = both_qk[:half].astype(BF16)
    share[:half, LANES : 2 * LANES] = both_qk[half:].astype(BF16)
    share[:half, 2 * LANES : 3 * LANES] = folded_v.astype(BF16)
    size = head_rows.shape[0]
    for chunk in range(head_rows.shape[1] // LANES):
        share[chunk * size : (chunk + 1) * size, 3 * LANES :] = head_rows[
            :, chunk * LANES : (chunk + 1) * LANES
        ].astype(BF16)


def feed_forward_share_kernel(place, normed, grad, w_e, w_c, *refs):
    pieces, share = refs[:-1], refs[-1]
    seat = place[1]
    width, ff_own = w_e.shape
    normed = normed[...].reshape(-1, width)
    value, slope = gelu_both(dot_nn(normed, w_e[...]))
    grad_hidden = dot_nt(grad[...], w_c[...])
    grad_pre = (grad_hidden * slope).astype(BF16)
    share[:ff_own] = dot_tn(value.astype(BF16), grad[...]).astype(BF16)
    expand = dot_tn(normed, grad_pre).astype(BF16)
    share[ff_own:, : width // 2] = expand[: width // 2]
    share[ff_own:, width // 2 :] = expand[width // 2 :]
    by_distance(share, pieces, seat)


def attend_back_kernel(place, q_all, kv_all, lse_o, table, w_o, *refs):
    pieces, outs = refs[:HEADS], refs[HEADS : HEADS + HEADS // 2]
    dq_all, dkv_all, do_all, dkv_sum, dq_sum, q_t, do_t = refs[HEADS + HEADS // 2 :]
    me = place[0]
    rows = q_all.shape[0] // HEADS
    own_w = w_o[...]
    own_w = jnp.concatenate([jnp.zeros(own_w.shape, BF16), own_w])
    for step in range(HEADS):
        do_all[rows_at((me ^ step) * rows, rows, 16), :] = dot_nt(
            pieces[step][...], own_w
        ).astype(BF16)
    total = q_all.shape[0]
    lse = lse_o[...][:, :1]
    delta = jnp.sum(do_all[...].astype(F32) * lse_o[...], axis=-1, keepdims=True)
    dq_sum[...] = jnp.zeros(dq_sum.shape, F32)
    q_t[...] = jnp.transpose(q_all[...].astype(F32)).astype(BF16)
    do_t[...] = jnp.transpose(do_all[...].astype(F32)).astype(BF16)
    for block in range(total // BLOCK):
        cut = slice(block * BLOCK, (block + 1) * BLOCK)
        rest = slice(block * BLOCK, total)
        kv_block = kv_all[cut]
        scores = causal(dot_nt(q_all[rest], kv_block), 0, 0)
        probs = jnp.exp(scores - lse[rest])
        grad_probs = dot_nt(do_all[rest], kv_block)
        ds = (probs * (grad_probs - delta[rest])).astype(BF16)
        dq_sum[rest] += dot_nn(ds, kv_block)
        back = dot_nn(q_t[:, rest], ds) + dot_nn(do_t[:, rest], probs.astype(BF16))
        dkv_sum[cut] = jnp.transpose(back)
    dq_all[...] = rope_back(dq_sum[...] * HEAD**-0.5, table[...]).astype(BF16)
    low = lower_half(BLOCK)
    for block in range(q_all.shape[0] // BLOCK):
        cut = slice(block * BLOCK, (block + 1) * BLOCK)
        dkv = dkv_sum[cut]
        dkv_all[cut] = jnp.where(low, rope_back(dkv, table[cut, :]), dkv).astype(BF16)
    for step in range(HEADS):
        own = rows_at((me ^ step) * rows, rows, 16)
        at = (step % 2) * (rows + rows // 2)
        outs[step // 2][at : at + rows] = dkv_all[own, :]
        outs[step // 2][at + rows : at + rows + rows // 2] = fold_rows(
            dq_all[own, :].astype(F32)
        ).astype(BF16)


def attention_share_kernel(parts, place, gathered, dq_all, dkv_all, lse_o, more, *refs):
    pieces, keep, send, share = refs[:HEADS], refs[HEADS], refs[HEADS + 1], refs[-1]
    me, seat = place[0], place[1]
    _, rows, width = gathered.shape
    normed = gathered[...].reshape(-1, width)
    grad_q = dot_tn(normed, dq_all[...])
    grad_kv = dot_tn(normed, dkv_all[...])
    grad_o = jnp.zeros((LANES, width), F32)
    for step in range(HEADS):
        own = lse_o[rows_at((me ^ step) * rows, rows, 16), :].astype(BF16)
        grad_o += dot_tn(own, pieces[step][...])
    grad_o = grad_o[HEAD:]
    half = width // 2
    folded_v = jnp.where(lower_half(half), turn(grad_kv[:half]), grad_kv[half:])
    pack_attention(
        share, jnp.where(lower_half(width), grad_q, turn(grad_kv)), folded_v, grad_o
    )
    keep_and_send(share, keep, send, seat, parts)
    keep_and_send(more, keep, send, seat, parts, share.shape[0] // parts)


def start_back_kernel(place, x, grad_middle, gain, w_q, w_k, w_v, *refs):
    pieces = paired(refs[:HEADS])
    grad_in, heads, dq, dk, dv = refs[HEADS:]
    me = place[0]
    rows, width = x.shape
    half = rows // 2
    for step in range(HEADS):
        heads[me ^ step] = pieces[step][...]
    low, low_half = lower_half(rows), lower_half(half)
    for chunk in range(width // LANES):
        cut = slice(chunk * LANES, (chunk + 1) * LANES)
        even, odd = heads[2 * chunk].astype(F32), heads[2 * chunk + 1].astype(F32)
        dk[:, cut] = jnp.where(low, even[:rows], turn(odd[:rows])).astype(BF16)
        dv[:, cut] = jnp.where(low, turn(even[:rows]), odd[:rows]).astype(BF16)
        dq[:half, cut] = jnp.where(low_half, even[rows:], turn(odd[rows:])).astype(BF16)
        dq[half:, cut] = jnp.where(low_half, turn(even[rows:]), odd[rows:]).astype(BF16)
    grad_a = dot_nt(dq[...], w_q[...]) + dot_nt(dk[...], w_k[...]) + dot_nt(dv[...], w_v[...])
    unit, scale = norm_parts(x[...])
    grad_in[...] = grad_middle[...] + norm_back(grad_a, gain[...], unit, scale)


def column_to_row(column):
    return jnp.transpose(jnp.broadcast_to(column, (column.shape[0], LANES)))[:1]


def fold_lanes(values):
    return sum(
        values[:, at : at + LANES] for at in range(0, values.shape[1], LANES)
    )


def part_order(batch):
    order, bit = [0], batch // 2
    while bit >= 1:
        order = order + [step ^ bit for step in order]
        bit //= 2
    return order


def grads_kernel(parts, attention, feed_forward, place, *refs):
    refs = list(refs)
    sources = [refs.pop(0) for _ in range(2 * HEADS if attention else 0)]
    weights = [refs.pop(0) for _ in range(4 * attention)]
    if feed_forward:
        gathered, w_e, gain_f = [refs.pop(0) for _ in range(3)]
    outs = [refs.pop(0) for _ in range(5 * attention + 3 * feed_forward)]
    me, seat = place[0], place[1]
    order = part_order(parts)
    copies = []

    def send(source, target, semaphore):
        copy = pltpu.make_async_copy(source, target, semaphore)
        copy.start()
        copies.append(copy)

    for layer in range(attention):
        w_q, w_k, w_v, gain_a = weights[4 * layer : 4 * layer + 4]
        grad_q, grad_k, grad_v, grad_o, grad_gain_a = outs[5 * layer : 5 * layer + 5]
        heads, square, over, sems_a = refs[4 * layer : 4 * layer + 4]
        width = grad_q.shape[0]
        half, at_rows = width // 2, width // 2 // parts
        for at, peer in enumerate(order):
            half_parts = parts // 2
            first = ((at % half_parts) * attention + layer) * at_rows
            for step in range(HEADS):
                source = sources[at // half_parts * HEADS + step]
                heads[me ^ step, rows_at((seat ^ peer) * at_rows, at_rows, 16), :] = source[
                    first : first + at_rows
                ]
        low = lower_half(half)
        total = None
        for chunk in range(HEADS // 2):
            cut = slice(chunk * LANES, (chunk + 1) * LANES)
            for part in range(2):
                rows = slice(part * half, (part + 1) * half)
                lanes = slice(part * LANES, (part + 1) * LANES)
                even = heads[2 * chunk, :, lanes].astype(F32)
                odd = heads[2 * chunk + 1, :, lanes].astype(F32)
                square[0, chunk, rows] = jnp.where(low, even, turn(odd))
                square[1, chunk, rows] = jnp.where(low, turn(even), odd)
            even = heads[2 * chunk, :, 2 * LANES : 3 * LANES].astype(F32)
            odd = heads[2 * chunk + 1, :, 2 * LANES : 3 * LANES].astype(F32)
            square[2, chunk, :half] = jnp.where(low, even, turn(odd))
            square[2, chunk, half:] = jnp.where(low, turn(even), odd)
            for head in (2 * chunk, 2 * chunk + 1):
                for lane in range(width // LANES):
                    over[head, :, lane * LANES : (lane + 1) * LANES] = heads[
                        head, lane * HEAD : (lane + 1) * HEAD, 3 * LANES :
                    ].astype(F32)
                send(
                    over.at[head],
                    grad_o.at[pl.ds(head * HEAD, HEAD), :],
                    sems_a.at[3 + head % 2, chunk],
                )
            for at, target in enumerate((grad_q, grad_k, grad_v)):
                send(
                    square.at[at, chunk],
                    target.at[:, pl.ds(chunk * LANES, LANES)],
                    sems_a.at[at, chunk],
                )
            term = (
                w_q[:, cut].astype(F32) * square[0, chunk]
                + w_k[:, cut].astype(F32) * square[1, chunk]
                + w_v[:, cut].astype(F32) * square[2, chunk]
            )
            total = term if total is None else total + term
        total = jnp.sum(total, axis=-1, keepdims=True)
        grad_gain_a[...] = column_to_row(total) / gain_a[...]

    if feed_forward:
        contract, expand, grad_gain_f = outs[-3:]
        share, acc, sems = refs[4 * attention : 4 * attention + 3]
        width = expand.shape[0]
        half = width // 2
        ff_own = contract.shape[0] // HEADS
        ff_rows = 2 * ff_own // parts
        acc[...] = jnp.zeros(acc.shape, F32)
        for owner in range(HEADS):
            source = gathered.ready(owner)
            for at, peer in enumerate(order):
                share[owner, rows_at((seat ^ peer) * ff_rows, ff_rows, 16), :] = source[
                    owner, at * ff_rows : (at + 1) * ff_rows
                ].astype(F32)
            own = slice(owner * ff_own, (owner + 1) * ff_own)
            send(share.at[owner, pl.ds(0, ff_own), :], contract.at[own, :], sems.at[owner, 0])
            for side in range(2):
                lanes = slice(side * half, (side + 1) * half)
                send(
                    share.at[owner, pl.ds(ff_own, ff_own), lanes],
                    expand.at[lanes, own],
                    sems.at[owner, 1 + side],
                )
                acc[lanes] += fold_lanes(
                    w_e[lanes, own].astype(F32) * share[owner, ff_own:, lanes]
                )
        total = jnp.sum(acc[...], axis=-1, keepdims=True)
        grad_gain_f[...] = column_to_row(total) / gain_f[...]
    for copy in copies:
        copy.wait()


COST = 2.5e9


def call(kernel, out_shape, scratch, arguments, late=(), limit=16, in_hbm=(), kept=(), us=5):
    late = [entry if isinstance(entry, tuple) else (entry,) for entry in late]
    late = [entry + (None, None, 0, 1)[len(entry) - 1 :] for entry in late]
    specs = [pl.BlockSpec(memory_space=pltpu.SMEM)]
    specs += [pl.BlockSpec(memory_space=pltpu.VMEM)] * (len(arguments) - 1)
    buffers, arguments = [], list(arguments)
    for at, shape, *_ in late:
        specs[at] = pl.BlockSpec(memory_space=pltpu.HBM)
        buffers.append(pltpu.VMEM(shape or arguments[at].shape, arguments[at].dtype))
        arguments[at] = pltpu.with_memory_space_constraint(arguments[at], pltpu.HBM)
    body, semaphores = kernel, []
    if late:
        semaphores = [pltpu.SemaphoreType.DMA((sum(entry[4] for entry in late),))]
        body = partial(with_late, kernel, late, len(arguments), len(out_shape))
    return pl.pallas_call(
        body,
        out_shape=[
            (pltpu.HBM if at in in_hbm or at in kept else jax.ShapeDtypeStruct)(*entry)
            for at, entry in enumerate(out_shape)
        ],
        in_specs=specs,
        out_specs=[
            pl.BlockSpec(memory_space=pltpu.HBM if at in in_hbm else pltpu.VMEM)
            for at in range(len(out_shape))
        ],
        scratch_shapes=[
            pltpu.VMEM(*entry) if isinstance(entry, tuple) else entry for entry in scratch
        ]
        + buffers
        + semaphores,
        compiler_params=pltpu.CompilerParams(vmem_limit_bytes=limit * 2**20),
        cost_estimate=pl.CostEstimate(
            flops=int(us * COST), bytes_accessed=2**20, transcendentals=0
        ),
    )(*arguments)


def exchange(pieces, axis):
    devices = range(lax.axis_size(axis))
    moved = {
        step: lax.ppermute(pieces[step], axis, [(i, i ^ step) for i in devices])
        for step in reversed(range(1, len(pieces)))
    }
    return [pieces[0]] + [moved[step] for step in range(1, len(pieces))]


def after(values, *others):
    return lax.optimization_barrier((values, others))[0]


def phase(*values):
    return lax.optimization_barrier(values)


def swap(block, axis, step):
    return lax.ppermute(block, axis, [(i, i ^ step) for i in range(lax.axis_size(axis))])


def near_exchange(pairs):
    moved = {step: swap(pairs[step], "seq", 2 * step) for step in reversed(range(1, len(pairs)))}
    first = [pairs[0]] + [moved[step] for step in range(1, len(pairs))]
    return first + [swap(pair, "seq", 1) for pair in first]


def summed(pieces):
    return sum(piece.astype(F32) for piece in pieces).astype(BF16)


def sum_step(keep, arrived, bit):
    total = keep.astype(F32) + arrived.astype(F32)
    parts = lax.axis_size("batch") // (2 * bit)
    if parts <= 1:
        return total.astype(BF16), None
    total = total.reshape(parts // 2, 2, -1, total.shape[1])
    return (
        total[:, 0].reshape(-1, total.shape[-1]),
        total[:, 1].reshape(-1, total.shape[-1]).astype(BF16),
    )


def near_gather(block, *beside):
    found = {0: block}
    for step in (6, 4, 2):
        found[step] = swap(block, "seq", step)
    for step in (0, 2, 4, 6):
        found[step] = after(found[step], *beside) if beside else found[step]
        found[step + 1] = swap(found[step], "seq", 1)
    return [found[step] for step in range(HEADS)]


def gather(block):
    return lax.all_gather(block, "seq", axis=0, tiled=True)


def whole_grads(place, batch, sources=(), attention=(), gathered=None, feed_forward=None):
    arguments, out_shape, scratch, late, in_hbm = [place, *sources], [], [], [], []
    width = (attention or (feed_forward,))[0][1].shape[0]
    square, row = ((width, width), F32), ((1, width), F32)
    for params in attention:
        first = len(arguments)
        arguments += [params[1], params[2], params[3], params[0]]
        late += [first, first + 1, first + 2]
        first = len(out_shape)
        in_hbm += [first, first + 1, first + 2, first + 3]
        out_shape += [square] * 4 + [row]
        scratch += [
            ((HEADS, width // 2, width), BF16),
            ((3, HEADS // 2, width, LANES), F32),
            ((HEADS, HEAD, width), F32),
            pltpu.SemaphoreType.DMA((5, HEADS // 2)),
        ]
    if feed_forward is not None:
        ff = feed_forward[6].shape[1]
        late += [(len(arguments), None, None, 0, HEADS), len(arguments) + 1]
        arguments += [gathered, feed_forward[6], feed_forward[5]]
        in_hbm += [len(out_shape), len(out_shape) + 1]
        out_shape += [((ff, width), F32), ((width, ff), F32), row]
        scratch += [
            ((HEADS, 2 * ff // HEADS, width), F32),
            ((width, LANES), F32),
            pltpu.SemaphoreType.DMA((HEADS, 3)),
        ]
    return call(
        partial(grads_kernel, batch, len(attention), feed_forward is not None),
        out_shape,
        scratch,
        tuple(arguments),
        late,
        40 if attention else 24,
        in_hbm,
    )


def by_heads(inputs, cotangent, *weights):
    full = (weights[0][None],) + weights[1:5] + (weights[5][None],) + weights[6:8]
    brief = (weights[8][None],) + weights[9:13] + (weights[13][None],) + weights[14:16]
    x, cot = inputs[0], cotangent[0]
    rows, width = x.shape
    short, half, total = rows // 3, rows // 2, rows * HEADS
    batch = lax.axis_size("batch")
    ff = full[6].shape[1]
    ff_own = ff // HEADS
    count = short * HEADS
    chunks = width // LANES
    place = jnp.stack([lax.axis_index("seq"), lax.axis_index("batch")]).astype(jnp.int32)
    table = rope_constants(total)
    block = rows + half

    outs = call(
        project_kernel,
        [((2 * block, LANES), BF16)] * (HEADS // 2)
        + [((rows, width), BF16), ((rows + short, width), BF16)],
        [((HEADS, block, LANES), BF16), ((chunks, rows, LANES), F32)],
        (place, x, cot, full[0], full[1], full[2], full[3], table),
        (
            1,
            3,
            4,
            5,
            6,
            (7, (rows, 2 * LANES), lambda ref, me: ref.at[rows_at(me * rows, rows, 16), :]),
            2,
        ),
        kept=(HEADS // 2, HEADS // 2 + 1),
    )
    pieces, (normed_a, bundle) = near_exchange(outs[: HEADS // 2]), outs[HEADS // 2 :]
    bundles = gather(bundle).reshape(HEADS, rows + short, width)

    outs = call(
        attend_kernel,
        [((rows, LANES), BF16)] * (HEADS // 2)
        + [((total, LANES), BF16), ((total, LANES), BF16), ((total, LANES), F32)],
        [
            ((total, LANES), BF16),
            ((total, LANES), BF16),
            ((total, LANES), F32),
            pltpu.SemaphoreType.DMA((3,)),
        ],
        (place, *pieces),
        in_hbm=range(HEADS // 2, HEADS // 2 + 3),
    )
    pieces = near_exchange(outs[: HEADS // 2])
    q_all, kv_all, lse_o = outs[HEADS // 2 :]

    residual, middle, normed_f, pooled = call(
        finish_kernel,
        [
            ((rows, width), F32),
            ((rows, width), F32),
            ((2 * rows, width), BF16),
            ((short + 16, width), BF16),
        ],
        [
            ((rows, width), F32),
            ((rows, width), F32),
            ((2 * rows, width), BF16),
            ((rows, width), BF16),
            ((HEADS, half, LANES), F32),
            ((chunks, rows + 8, LANES), F32),
            pltpu.SemaphoreType.DMA((3,)),
        ],
        (place, x, normed_a, full[5], full[4], full[6], full[7], *pieces),
        (4, 1, 5, 6, 2),
        in_hbm=range(3),
    )
    pieces = near_gather(pooled)
    normed_all = gather(normed_f).reshape(HEADS, 2 * rows, width)

    outs = call(
        short_forward_kernel,
        [
            ((short, width), F32),
            ((short, ff), BF16),
            ((count, width), F32),
            ((count, width), BF16),
            ((HEADS, count, LANES), BF16),
            ((chunks, count, LANES), BF16),
            ((chunks, count, LANES), BF16),
            ((chunks, count, LANES), F32),
            ((chunks, count, LANES), F32),
            ((count, width), BF16),
            ((count, width), F32),
        ]
        + [((2 * ff_own // batch, width), BF16)] * batch,
        [
            ((HEADS, width), F32),
            ((count, width), F32),
            ((count, width), BF16),
            ((count, ff), BF16),
            ((count, ff), BF16),
            ((count, width), F32),
            ((count, width), BF16),
            ((2 * ff_own, width), BF16),
        ],
        (place, bundles, table[:count]) + brief + tuple(pieces),
        (
            4,
            2,
            5,
            6,
            7,
            9,
            10,
            (1, (HEADS, short, width), lambda ref, me: ref.at[:, pl.ds(rows, short), :]),
        ),
        22,
        kept=(0, 1),
        us=16,
    )
    own_short, saved = outs[:2], outs[2:11]
    a_at, saved = phase(outs[11:], saved)
    a_at = exchange(a_at, "batch")
    outs = call(
        short_back_kernel,
        [
            ((total, width), BF16),
            ((width // 2, width), BF16),
            ((rows, width), F32),
            ((rows, width), BF16),
        ],
        [
            ((total, width), BF16),
            ((width // 2, width), BF16),
            ((rows, width), F32),
            pltpu.SemaphoreType.DMA((3,)),
            ((HEADS, count, LANES), BF16),
            ((count, width), BF16),
            ((count, width), BF16),
            ((count, width), BF16),
            ((chunks, total + 16, LANES), F32),
            ((LANES, width), F32),
            ((rows, width), F32),
        ],
        (place, cot, bundles, table[:count])
        + brief[:5]
        + tuple(saved)
        + (middle, normed_f, full[5], full[6], full[7]),
        (
            8,
            3,
            5,
            6,
            7,
            (2, (HEADS, rows, width), lambda ref, me: ref.at[:, pl.ds(0, rows), :]),
            1,
            21,
            22,
            (19, (rows, width), lambda ref, me: ref.at[pl.ds(0, rows), :]),
            18,
        ),
        25,
        in_hbm=range(3),
        us=18,
    )
    a_at, (grad_all, short_share, grad_middle, g1) = phase(a_at, outs)

    a_all, g1, grad_all = phase(summed(a_at), g1, grad_all)
    a_at = swap(a_all, "batch", 2)
    outs = call(
        feed_forward_share_kernel,
        [((2 * ff_own // batch, width), BF16)] * batch,
        [((2 * ff_own, width), BF16)],
        (place, normed_all, grad_all, full[6], full[7]),
        (
            (1, (HEADS, rows, width), lambda ref, me: ref.at[:, pl.ds(0, rows), :]),
            (3, (width, ff_own), lambda ref, me: ref.at[:, rows_at(me * ff_own, ff_own, ff_own)]),
            2,
            (4, (ff_own, width), lambda ref, me: ref.at[rows_at(me * ff_own, ff_own, ff_own), :]),
        ),
        22,
    )
    g1_all = near_gather(g1, outs[1], a_at)
    a_all = jnp.concatenate([a_all, a_at])
    a_at = swap(a_all, "batch", 1)
    a_all, a_at, g1_all, b_at = phase(a_all, a_at, g1_all, outs)

    a_shares = gather(jnp.concatenate([a_all, a_at])[None])
    b_at = exchange(b_at, "batch")
    outs = call(
        attend_back_kernel,
        [((2 * block, LANES), BF16)] * (HEADS // 2)
        + [((total, LANES), BF16), ((total, LANES), BF16)],
        [
            ((total, LANES), BF16),
            ((total, LANES), F32),
            ((total, LANES), F32),
            ((LANES, total), BF16),
            ((LANES, total), BF16),
        ],
        (place, q_all, kv_all, lse_o, table, full[4], *g1_all),
        (
            (5, (HEAD, width), lambda ref, me: ref.at[rows_at(me * HEAD, HEAD, HEAD), :]),
            1,
            2,
            3,
            4,
        ),
        us=7,
    )
    pieces, (dq_all, dkv_all) = outs[: HEADS // 2], outs[HEADS // 2 :]
    outs = call(
        partial(attention_share_kernel, batch),
        [((width // 2, width), BF16)] * 2,
        [((width // 2, width), BF16)],
        (place, normed_all, dq_all, dkv_all, lse_o, short_share, *g1_all),
        ((1, (HEADS, rows, width), lambda ref, me: ref.at[:, pl.ds(rows, rows), :]), 4, 5),
        us=3,
    )
    b_at, pieces, (c_keep, c_send) = phase(b_at, pieces, outs)

    b_all, pieces, c_send = phase(summed(b_at), pieces, c_send)
    b_at = swap(b_all, "batch", 2)
    c_at = swap(c_send, "batch", 1)
    pieces = {step: pieces[step] for step in range(HEADS // 2)}
    moved = {step: swap(pieces[step], "seq", 2 * step) for step in (3, 2)}
    b_at, c_at, moved, pieces = phase(b_at, c_at, moved, pieces)

    b_all = jnp.concatenate([b_all, b_at])
    c_keep, c_send = sum_step(c_keep, c_at, 1)
    b_all, c_send, pieces = phase(b_all, c_send, pieces)
    b_at = swap(b_all, "batch", 1)
    c_at = swap(c_send, "batch", 2)
    moved |= {0: pieces[0], 1: swap(pieces[1], "seq", 2)}
    b_at, c_at, moved, pieces = phase(b_at, c_at, moved, pieces)

    b_all = jnp.concatenate([b_all, b_at])
    c_all, _ = sum_step(c_keep, c_at, 2)
    b_all, c_all, moved = phase(b_all, c_all, moved)
    b_shares = gather(b_all[None])
    c_at = swap(c_all, "batch", 2)
    across = {step: swap(moved[step], "seq", 1) for step in range(HEADS // 2)}
    (output,) = call(
        output_kernel,
        [((rows, width), F32)],
        [((chunks, rows, LANES), F32)],
        (place, residual, *own_short, brief[7]),
        (4, 3, 2, 1),
        us=3,
    )
    c_at, moved, across, output = phase(c_at, moved, across, output)

    c_all, moved, across, a_shares = phase(
        jnp.concatenate([c_all, c_at]), moved, across, a_shares
    )
    first = {0: c_all, 2: swap(c_all, "seq", 2), 4: swap(c_all, "seq", 4)}
    c_at = swap(c_all, "batch", 1)
    pieces = [side[step] for side in (moved, across) for step in range(HEADS // 2)]
    short_ff_grads = whole_grads(place, batch, gathered=a_shares, feed_forward=brief)
    (grad_in,) = call(
        start_back_kernel,
        [((rows, width), F32)],
        [((HEADS, block, LANES), BF16)] + [((rows, width), BF16)] * 3,
        (place, x, grad_middle, full[0], full[1], full[2], full[3], *pieces),
        (4, 5, 6, 1, 2),
        us=4,
    )
    c_at, first, short_ff_grads, grad_in = phase(c_at, first, short_ff_grads, grad_in)
    other = {0: c_at, 2: swap(c_at, "seq", 2), 4: swap(c_at, "seq", 4)}
    first |= {6: swap(first[2], "seq", 4)}
    other |= {6: swap(other[4], "seq", 2)}
    found = [
        half | {step + 1: swap(half[step], "seq", 1) for step in (0, 2, 4, 6)}
        for half in (first, other)
    ]
    c_shares = [half[step] for half in found for step in range(HEADS)]
    both_grads = whole_grads(place, batch, c_shares, (full, brief), b_shares, full)
    at_grads, full_ff_grads = both_grads[:10], both_grads[10:]

    def arranged(attention, feed_forward):
        grad_q, grad_k, grad_v, grad_o, grad_gain_a = attention
        contract, expand, grad_gain_f = feed_forward
        return (grad_gain_a[0], grad_q, grad_k, grad_v, grad_o, grad_gain_f[0], expand, contract)

    return (
        (output[None], grad_in[None])
        + arranged(at_grads[:5], full_ff_grads)
        + arranged(at_grads[5:], short_ff_grads)
    )


def from_behind(block, axis, distance):
    devices = range(lax.axis_size(axis))
    route = [(i - distance, i) for i in devices if i - distance in devices]
    return lax.ppermute(block, axis, route)


def normalize(stream, gain):
    row_mean = jnp.mean(stream, axis=-1, keepdims=True)
    centered = stream - row_mean
    spread = jnp.mean(centered * centered, axis=-1, keepdims=True)
    return centered * lax.rsqrt(spread + norm_eps) * gain


def rope_table(positions):
    half_size = HEAD // 2
    frequency = jnp.power(10000.0, -jnp.arange(half_size, dtype=jnp.float32) * 2.0 / HEAD)
    angles = positions.astype(jnp.float32)[:, None] * frequency[None, :]
    return (jnp.cos(angles)[:, None, :], jnp.sin(angles)[:, None, :])


def rotate(values, angle_cos, angle_sin):
    first_half, second_half = jnp.split(values, 2, axis=-1)
    return jnp.concatenate(
        [
            first_half * angle_cos - second_half * angle_sin,
            first_half * angle_sin + second_half * angle_cos,
        ],
        axis=-1,
    )


def rotate_back(grads, angle_cos, angle_sin):
    first_half, second_half = jnp.split(grads, 2, axis=-1)
    return jnp.concatenate(
        [
            first_half * angle_cos + second_half * angle_sin,
            second_half * angle_cos - first_half * angle_sin,
        ],
        axis=-1,
    )


def split_heads(matrix):
    return matrix.reshape(matrix.shape[0], HEADS, HEAD)


def project(stream, params, angle_cos, angle_sin):
    normed_in = normalize(stream, params[0]).astype(jnp.bfloat16)

    def heads_of(matrix):
        return split_heads(jnp.dot(normed_in, matrix, preferred_element_type=jnp.float32))

    queries = rotate(heads_of(params[1]), angle_cos, angle_sin).astype(jnp.bfloat16)
    keys_here = rotate(heads_of(params[2]), angle_cos, angle_sin).astype(jnp.bfloat16)
    values_here = heads_of(params[3]).astype(jnp.bfloat16)
    return (normed_in, queries, keys_here, values_here)


def masked_scores(queries, keys_all, query_places, key_places):
    scores = jnp.einsum(
        "nhe,mhe->hnm", queries, keys_all, preferred_element_type=jnp.float32
    ) * HEAD ** (-0.5)
    allowed = key_places[None, None, :] <= query_places[None, :, None]
    return jnp.where(allowed, scores, -1e30)


def attend(queries, keys_all, values_all, query_places, key_places):
    scores = masked_scores(queries, keys_all, query_places, key_places)
    highest_score = jnp.max(scores, axis=-1, keepdims=True)
    log_total = highest_score + jnp.log(
        jnp.sum(jnp.exp(scores - highest_score), axis=-1, keepdims=True)
    )
    prob_low = jnp.exp(scores - log_total).astype(jnp.bfloat16)
    attended = jnp.einsum("hnm,mhe->nhe", prob_low, values_all, preferred_element_type=jnp.float32)
    return (attended, log_total)


def attend_back(queries, keys_all, values_all, query_places, key_places, log_total, grad_attended):
    scores = masked_scores(queries, keys_all, query_places, key_places)
    probs_full = jnp.exp(scores - log_total)
    grad_probs = jnp.einsum(
        "nhe,mhe->hnm", grad_attended, values_all, preferred_element_type=jnp.float32
    )
    row_inner = jnp.sum(probs_full * grad_probs, axis=-1, keepdims=True)
    grad_scores = (probs_full * (grad_probs - row_inner)).astype(jnp.bfloat16)
    grad_queries = jnp.einsum(
        "hnm,mhe->nhe", grad_scores, keys_all, preferred_element_type=jnp.float32
    ) * HEAD ** (-0.5)
    return (grad_queries, grad_scores, probs_full.astype(jnp.bfloat16), row_inner)


def finish(stream, attended, params):
    row_count, width = stream.shape
    attended_low = attended.reshape(row_count, width).astype(jnp.bfloat16)
    middle = stream + jnp.dot(attended_low, params[4], preferred_element_type=jnp.float32)
    normed_mid = normalize(middle, params[5]).astype(jnp.bfloat16)
    hidden_pre = jnp.dot(normed_mid, params[6], preferred_element_type=jnp.float32)
    hidden_low = jax.nn.gelu(hidden_pre, approximate=True).astype(jnp.bfloat16)
    result = middle + jnp.dot(hidden_low, params[7], preferred_element_type=jnp.float32)
    return (result, (attended_low, middle, normed_mid, hidden_pre, hidden_low))


def finish_back(grad_result, finish_saved, params):
    attended_low, middle, normed_mid, hidden_pre, hidden_low = finish_saved
    grad_low = grad_result.astype(jnp.bfloat16)
    grad_contract = jnp.einsum(
        "nf,nd->fd", hidden_low, grad_low, preferred_element_type=jnp.float32
    )
    grad_hidden = jnp.einsum("nd,fd->nf", grad_low, params[7], preferred_element_type=jnp.float32)
    gelu_value, gelu_pull = jax.vjp(partial(jax.nn.gelu, approximate=True), hidden_pre)
    grad_pre = gelu_pull(grad_hidden)[0].astype(jnp.bfloat16)
    grad_expand = jnp.einsum("nd,nf->df", normed_mid, grad_pre, preferred_element_type=jnp.float32)
    grad_normed = jnp.einsum("nf,df->nd", grad_pre, params[6], preferred_element_type=jnp.float32)
    norm_value, norm_pull = jax.vjp(normalize, middle, params[5])
    grad_norm_in, grad_gain_ffn = norm_pull(grad_normed)
    grad_middle = grad_result + grad_norm_in
    middle_low = grad_middle.astype(jnp.bfloat16)
    grad_output_w = jnp.einsum(
        "nc,nd->cd", attended_low, middle_low, preferred_element_type=jnp.float32
    )
    grad_attended = split_heads(
        jnp.einsum("nd,cd->nc", middle_low, params[4], preferred_element_type=jnp.float32).astype(
            jnp.bfloat16
        )
    )
    return (grad_middle, grad_attended, grad_output_w, grad_expand, grad_contract, grad_gain_ffn)


def start_back(
    grad_queries, grad_keys, grad_values, stream, params, normed_in, angle_cos, angle_sin
):
    row_count, width = stream.shape
    query_low = (
        rotate_back(grad_queries, angle_cos, angle_sin)
        .reshape(row_count, width)
        .astype(jnp.bfloat16)
    )
    key_low = (
        rotate_back(grad_keys, angle_cos, angle_sin).reshape(row_count, width).astype(jnp.bfloat16)
    )
    value_low = grad_values.reshape(row_count, width).astype(jnp.bfloat16)
    grad_query = jnp.einsum("nd,nc->dc", normed_in, query_low, preferred_element_type=jnp.float32)
    grad_key = jnp.einsum("nd,nc->dc", normed_in, key_low, preferred_element_type=jnp.float32)
    grad_value = jnp.einsum("nd,nc->dc", normed_in, value_low, preferred_element_type=jnp.float32)
    grad_normed = (
        jnp.einsum("nc,dc->nd", query_low, params[1], preferred_element_type=jnp.float32)
        + jnp.einsum("nc,dc->nd", key_low, params[2], preferred_element_type=jnp.float32)
        + jnp.einsum("nc,dc->nd", value_low, params[3], preferred_element_type=jnp.float32)
    )
    norm_value, norm_pull = jax.vjp(normalize, stream, params[0])
    grad_stream, grad_gain_attn = norm_pull(grad_normed)
    return (grad_stream, grad_gain_attn, grad_query, grad_key, grad_value)


def local_forward(stream, places, params, fetch):
    angle_cos, angle_sin = rope_table(places)
    normed_in, queries, keys_here, values_here = project(stream, params, angle_cos, angle_sin)
    row_count, width = stream.shape
    keys_local = keys_here.reshape(row_count, width)
    values_local = values_here.reshape(row_count, width)
    keys_flat, values_flat = fetch(keys_local, values_local)
    key_places = jnp.arange(keys_flat.shape[0], dtype=jnp.int32)
    attended, log_total = attend(
        queries, split_heads(keys_flat), split_heads(values_flat), places, key_places
    )
    result, finish_saved = finish(stream, attended, params)
    return (
        result,
        (
            normed_in,
            queries,
            keys_local,
            values_local,
            keys_flat,
            values_flat,
            log_total,
            angle_cos,
            angle_sin,
            finish_saved,
        ),
    )


def local_backward(grad_result, stream, places, params, saved, keys_flat, values_flat, key_sum):
    normed_in, queries = (saved[0], saved[1])
    log_total, angle_cos, angle_sin, finish_saved = (saved[6], saved[7], saved[8], saved[9])
    grad_middle, grad_attended, grad_output_w, grad_expand, grad_contract, grad_gain_ffn = (
        finish_back(grad_result, finish_saved, params)
    )
    row_count, width = stream.shape
    key_places = jnp.arange(keys_flat.shape[0], dtype=jnp.int32)
    grad_queries, grad_scores, prob_low, row_inner = attend_back(
        queries,
        split_heads(keys_flat),
        split_heads(values_flat),
        places,
        key_places,
        log_total,
        grad_attended,
    )

    def contribution(first_row, term_rows):
        grad_keys = jnp.einsum(
            "hnm,nhe->mhe", grad_scores, queries, preferred_element_type=jnp.float32
        ) * HEAD ** (-0.5)
        grad_values = jnp.einsum(
            "hnm,nhe->mhe", prob_low, grad_attended, preferred_element_type=jnp.float32
        )
        return jnp.concatenate(
            [grad_keys.reshape(term_rows, width), grad_values.reshape(term_rows, width)], axis=1
        )

    both_grads = key_sum(contribution, row_count, (queries, grad_attended, log_total, row_inner))
    grad_stream, grad_gain_attn, grad_query, grad_key, grad_value = start_back(
        grad_queries,
        split_heads(both_grads[:, :width]),
        split_heads(both_grads[:, width:]),
        stream,
        params,
        normed_in,
        angle_cos,
        angle_sin,
    )
    return (
        grad_middle + grad_stream,
        (
            grad_gain_attn,
            grad_query,
            grad_key,
            grad_value,
            grad_output_w,
            grad_gain_ffn,
            grad_expand,
            grad_contract,
        ),
    )


def whole_forward(stream, params):
    row_count, width = stream.shape
    places = jnp.arange(row_count, dtype=jnp.int32)
    angle_cos, angle_sin = rope_table(places)
    normed_in, queries, keys_here, values_here = project(stream, params, angle_cos, angle_sin)
    block_rows = 512
    block_count = row_count // block_rows

    def one_block(pieces):
        return attend(pieces[0], keys_here, values_here, pieces[1], places)

    attended, log_total = lax.map(
        one_block,
        (
            queries.reshape(block_count, block_rows, HEADS, HEAD),
            places.reshape(block_count, block_rows),
        ),
    )
    result, finish_saved = finish(stream, attended.reshape(row_count, HEADS, HEAD), params)
    return (
        result,
        (normed_in, queries, keys_here, values_here, log_total, angle_cos, angle_sin, finish_saved),
    )


def whole_backward(grad_result, stream, params, saved):
    normed_in, queries, keys_here, values_here, log_total, angle_cos, angle_sin, finish_saved = (
        saved
    )
    grad_middle, grad_attended, grad_output_w, grad_expand, grad_contract, grad_gain_ffn = (
        finish_back(grad_result, finish_saved, params)
    )
    row_count, width = stream.shape
    places = jnp.arange(row_count, dtype=jnp.int32)
    block_rows = 512
    block_count = row_count // block_rows

    def one_block(running, pieces):
        query_block, place_block, total_block, grad_block = pieces
        grad_queries, grad_scores, prob_low, row_inner = attend_back(
            query_block, keys_here, values_here, place_block, places, total_block, grad_block
        )
        grad_keys = running[0] + jnp.einsum(
            "hnm,nhe->mhe", grad_scores, query_block, preferred_element_type=jnp.float32
        ) * HEAD ** (-0.5)
        grad_values = running[1] + jnp.einsum(
            "hnm,nhe->mhe", prob_low, grad_block, preferred_element_type=jnp.float32
        )
        return ((grad_keys, grad_values), grad_queries)

    zero_grads = jnp.zeros((row_count, HEADS, HEAD), jnp.float32)
    (grad_keys, grad_values), grad_queries = lax.scan(
        one_block,
        (zero_grads, zero_grads),
        (
            queries.reshape(block_count, block_rows, HEADS, HEAD),
            places.reshape(block_count, block_rows),
            log_total,
            grad_attended.reshape(block_count, block_rows, HEADS, HEAD),
        ),
    )
    grad_stream, grad_gain_attn, grad_query, grad_key, grad_value = start_back(
        grad_queries.reshape(row_count, HEADS, HEAD),
        grad_keys,
        grad_values,
        stream,
        params,
        normed_in,
        angle_cos,
        angle_sin,
    )
    return (
        grad_middle + grad_stream,
        (
            grad_gain_attn,
            grad_query,
            grad_key,
            grad_value,
            grad_output_w,
            grad_gain_ffn,
            grad_expand,
            grad_contract,
        ),
    )


def by_rows(
    inputs,
    cotangent,
    full_gain_attn,
    full_query,
    full_key,
    full_value,
    full_output,
    full_gain_ffn,
    full_expand,
    full_contract,
    short_gain_attn,
    short_query,
    short_key,
    short_value,
    short_output,
    short_gain_ffn,
    short_expand,
    short_contract,
):
    full_params = (
        full_gain_attn,
        full_query,
        full_key,
        full_value,
        full_output,
        full_gain_ffn,
        full_expand,
        full_contract,
    )
    short_params = (
        short_gain_attn,
        short_query,
        short_key,
        short_value,
        short_output,
        short_gain_ffn,
        short_expand,
        short_contract,
    )
    stream_in = inputs[0]
    row_count, width = stream_in.shape
    own_short = row_count // 3
    position = lax.axis_index("seq")
    seq_parts = lax.axis_size("seq")
    places = position * row_count + jnp.arange(row_count, dtype=jnp.int32)

    def fetch_full(keys_local, values_local):
        return (
            lax.all_gather(keys_local, "seq", axis=0, tiled=True),
            lax.all_gather(values_local, "seq", axis=0, tiled=True),
        )

    residual, full_saved = local_forward(stream_in, places, full_params, fetch_full)
    tail_rows = from_behind(residual[row_count - 2 :], "seq", 1)
    shifted = jnp.concatenate([tail_rows, residual[: row_count - 2]], axis=0)
    pooled = jnp.mean(shifted.reshape(own_short, 3, width), axis=1)
    pooled_all = lax.all_gather(pooled, "seq", axis=0, tiled=True)
    short_all, short_saved = whole_forward(pooled_all, short_params)
    short_result = lax.dynamic_slice_in_dim(short_all, position * own_short, own_short, 0)
    output = residual + jnp.repeat(short_result, 3, axis=0)
    grad_output = cotangent[0]
    grad_short = jnp.sum(grad_output.reshape(own_short, 3, width), axis=1)
    grad_short_all = lax.all_gather(grad_short, "seq", axis=0, tiled=True)
    grad_pooled_all, short_grads = whole_backward(
        grad_short_all, pooled_all, short_params, short_saved
    )
    grad_pooled = lax.dynamic_slice_in_dim(grad_pooled_all, position * own_short, own_short, 0)
    short_grads = tuple(
        (
            lax.dynamic_slice_in_dim(
                gradient,
                position * (gradient.shape[0] // seq_parts),
                gradient.shape[0] // seq_parts,
                0,
            )
            for gradient in short_grads
        )
    )
    grad_shifted = jnp.repeat(grad_pooled / 3.0, 3, axis=0)
    carried = from_behind(grad_shifted[:2], "seq", -1)
    grad_residual = grad_output + jnp.concatenate([grad_shifted[2:], carried], axis=0)
    keys_flat, values_flat = (
        lax.all_gather(full_saved[2], "seq", axis=0, tiled=True),
        lax.all_gather(full_saved[3], "seq", axis=0, tiled=True),
    )

    def full_sum(contribution, term_rows, query_side):
        return lax.psum_scatter(
            contribution(jnp.int32(0), term_rows * lax.axis_size("seq")).astype(jnp.bfloat16),
            "seq",
            scatter_dimension=0,
            tiled=True,
        ).astype(jnp.float32)

    grad_input, full_grads = local_backward(
        grad_residual, stream_in, places, full_params, full_saved, keys_flat, values_flat, full_sum
    )
    full_shares = (
        lax.psum_scatter(
            full_grads[0].astype(jnp.bfloat16), "seq", scatter_dimension=0, tiled=True
        ).astype(jnp.float32),
        lax.psum_scatter(
            full_grads[1].astype(jnp.bfloat16), "seq", scatter_dimension=0, tiled=True
        ).astype(jnp.float32),
        lax.psum_scatter(
            full_grads[2].astype(jnp.bfloat16), "seq", scatter_dimension=0, tiled=True
        ).astype(jnp.float32),
        lax.psum_scatter(
            full_grads[3].astype(jnp.bfloat16), "seq", scatter_dimension=0, tiled=True
        ).astype(jnp.float32),
        lax.psum_scatter(
            full_grads[4].astype(jnp.bfloat16), "seq", scatter_dimension=0, tiled=True
        ).astype(jnp.float32),
        lax.psum_scatter(
            full_grads[5].astype(jnp.bfloat16), "seq", scatter_dimension=0, tiled=True
        ).astype(jnp.float32),
        lax.psum_scatter(
            full_grads[6].astype(jnp.bfloat16), "seq", scatter_dimension=0, tiled=True
        ).astype(jnp.float32),
        lax.psum_scatter(
            full_grads[7].astype(jnp.bfloat16), "seq", scatter_dimension=0, tiled=True
        ).astype(jnp.float32),
    )
    shares = tuple(full_shares) + tuple(short_grads)
    totals = (
        lax.psum(shares[0].astype(jnp.bfloat16), "batch").astype(jnp.float32),
        lax.psum(shares[1].astype(jnp.bfloat16), "batch").astype(jnp.float32),
        lax.psum(shares[2].astype(jnp.bfloat16), "batch").astype(jnp.float32),
        lax.psum(shares[3].astype(jnp.bfloat16), "batch").astype(jnp.float32),
        lax.psum(shares[4].astype(jnp.bfloat16), "batch").astype(jnp.float32),
        lax.psum(shares[5].astype(jnp.bfloat16), "batch").astype(jnp.float32),
        lax.psum(shares[6].astype(jnp.bfloat16), "batch").astype(jnp.float32),
        lax.psum(shares[7].astype(jnp.bfloat16), "batch").astype(jnp.float32),
        lax.psum(shares[8].astype(jnp.bfloat16), "batch").astype(jnp.float32),
        lax.psum(shares[9].astype(jnp.bfloat16), "batch").astype(jnp.float32),
        lax.psum(shares[10].astype(jnp.bfloat16), "batch").astype(jnp.float32),
        lax.psum(shares[11].astype(jnp.bfloat16), "batch").astype(jnp.float32),
        lax.psum(shares[12].astype(jnp.bfloat16), "batch").astype(jnp.float32),
        lax.psum(shares[13].astype(jnp.bfloat16), "batch").astype(jnp.float32),
        lax.psum(shares[14].astype(jnp.bfloat16), "batch").astype(jnp.float32),
        lax.psum(shares[15].astype(jnp.bfloat16), "batch").astype(jnp.float32),
    )
    whole = (
        lax.all_gather(totals[0].astype(jnp.bfloat16), "seq", axis=0, tiled=True).astype(
            jnp.float32
        ),
        lax.all_gather(totals[1].astype(jnp.bfloat16), "seq", axis=0, tiled=True).astype(
            jnp.float32
        ),
        lax.all_gather(totals[2].astype(jnp.bfloat16), "seq", axis=0, tiled=True).astype(
            jnp.float32
        ),
        lax.all_gather(totals[3].astype(jnp.bfloat16), "seq", axis=0, tiled=True).astype(
            jnp.float32
        ),
        lax.all_gather(totals[4].astype(jnp.bfloat16), "seq", axis=0, tiled=True).astype(
            jnp.float32
        ),
        lax.all_gather(totals[5].astype(jnp.bfloat16), "seq", axis=0, tiled=True).astype(
            jnp.float32
        ),
        lax.all_gather(totals[6].astype(jnp.bfloat16), "seq", axis=0, tiled=True).astype(
            jnp.float32
        ),
        lax.all_gather(totals[7].astype(jnp.bfloat16), "seq", axis=0, tiled=True).astype(
            jnp.float32
        ),
        lax.all_gather(totals[8].astype(jnp.bfloat16), "seq", axis=0, tiled=True).astype(
            jnp.float32
        ),
        lax.all_gather(totals[9].astype(jnp.bfloat16), "seq", axis=0, tiled=True).astype(
            jnp.float32
        ),
        lax.all_gather(totals[10].astype(jnp.bfloat16), "seq", axis=0, tiled=True).astype(
            jnp.float32
        ),
        lax.all_gather(totals[11].astype(jnp.bfloat16), "seq", axis=0, tiled=True).astype(
            jnp.float32
        ),
        lax.all_gather(totals[12].astype(jnp.bfloat16), "seq", axis=0, tiled=True).astype(
            jnp.float32
        ),
        lax.all_gather(totals[13].astype(jnp.bfloat16), "seq", axis=0, tiled=True).astype(
            jnp.float32
        ),
        lax.all_gather(totals[14].astype(jnp.bfloat16), "seq", axis=0, tiled=True).astype(
            jnp.float32
        ),
        lax.all_gather(totals[15].astype(jnp.bfloat16), "seq", axis=0, tiled=True).astype(
            jnp.float32
        ),
    )
    return (output[None], grad_input[None]) + tuple(whole)


def solution(mesh):
    sequence = P("batch", "seq", None)
    seq, batch = mesh.shape["seq"], mesh.shape["batch"]
    fits = seq == HEADS and batch == 4
    return jax.shard_map(
        by_heads if fits else by_rows,
        mesh=mesh,
        in_specs=(sequence, sequence) + (P(),) * 16,
        out_specs=(sequence, sequence) + (P(),) * 16,
        check_vma=False,
    )
```
